32 devices in a mesh: row: 2 (over y), col: 16 (over z, x, core).
Axes of the slice: x: 2, y: 2, z: 4, core: 2. Of those that a mesh axis runs over, the one named last changes fastest.
Arguments:
- pixels: bfloat16 [6304, 768], P('row', 'col'), may hold values from -6 to 6
- mask_places: int32 [32, 80], P('col'), may hold values from 1 to 196, as said below
- mask_count: int32 [32], P('col'), may hold values from 40 to 80, as said below
- targets: int32 [32, 80], P('col'), may hold values from 0 to 8191
- step_count: int32 [1], replicated, may hold values from 1 to 20
- patch_weight: float32 [768, 768], P('col', 'row'), may hold values from -0.21875 to 0.21875
- vector_table: float32 [205, 768], P(None, 'row')
- input_weight: float32 [1, 768, 2304], P(None, 'row', 'col'), may hold values from -0.21875 to 0.21875
- output_weight: float32 [1, 768, 768], P(None, 'col', 'row'), may hold values from -0.625 to 0.625
- upward_weight: float32 [1, 768, 3072], P(None, 'row', 'col'), may hold values from -0.21875 to 0.21875
- downward_weight: float32 [1, 3072, 768], P(None, 'col', 'row'), may hold values from -0.109375 to 0.109375
- head_weight: float32 [768, 8192], P(None, 'row'), may hold values from -0.21875 to 0.21875
- drift_patch: float32 [768, 768], P('col', 'row'), may hold values from -4.5776367e-05 to 4.5776367e-05
- drift_table: float32 [205, 768], P(None, 'row'), may hold values from -4.5776367e-05 to 4.5776367e-05
- drift_input: float32 [1, 768, 2304], P(None, 'row', 'col'), may hold values from -4.5776367e-05 to 4.5776367e-05
- drift_output: float32 [1, 768, 768], P(None, 'col', 'row'), may hold values from -4.5776367e-05 to 4.5776367e-05
- drift_upward: float32 [1, 768, 3072], P(None, 'row', 'col'), may hold values from -4.5776367e-05 to 4.5776367e-05
- drift_downward: float32 [1, 3072, 768], P(None, 'col', 'row'), may hold values from -4.5776367e-05 to 4.5776367e-05
- drift_head: float32 [768, 8192], P(None, 'row'), may hold values from -4.5776367e-05 to 4.5776367e-05
- power_patch: float32 [768, 768], P('col', 'row'), may hold values from 2.1251565e-13 to 2.1251564e-12
- power_table: float32 [205, 768], P(None, 'row'), may hold values from 2.1251565e-13 to 2.1251564e-12
- power_input: float32 [1, 768, 2304], P(None, 'row', 'col'), may hold values from 2.1251565e-13 to 2.1251564e-12
- power_output: float32 [1, 768, 768], P(None, 'col', 'row'), may hold values from 2.1251565e-13 to 2.1251564e-12
- power_upward: float32 [1, 768, 3072], P(None, 'row', 'col'), may hold values from 2.1251565e-13 to 2.1251564e-12
- power_downward: float32 [1, 3072, 768], P(None, 'col', 'row'), may hold values from 2.1251565e-13 to 2.1251564e-12
- power_head: float32 [768, 8192], P(None, 'row'), may hold values from 2.1251565e-13 to 2.1251564e-12
Outputs:
- mean_loss: float32 [], replicated
- grad_norm: float32 [], replicated
- patch_update: float32 [768, 768], P('col', 'row')
- patch_drift: float32 [768, 768], P('col', 'row')
- patch_power: float32 [768, 768], P('col', 'row')
- table_update: float32 [205, 768], P(None, 'row')
- table_drift: float32 [205, 768], P(None, 'row')
- table_power: float32 [205, 768], P(None, 'row')
- input_update: float32 [1, 768, 2304], P(None, 'row', 'col')
- input_drift: float32 [1, 768, 2304], P(None, 'row', 'col')
- input_power: float32 [1, 768, 2304], P(None, 'row', 'col')
- output_update: float32 [1, 768, 768], P(None, 'col', 'row')
- output_drift: float32 [1, 768, 768], P(None, 'col', 'row')
- output_power: float32 [1, 768, 768], P(None, 'col', 'row')
- upward_update: float32 [1, 768, 3072], P(None, 'row', 'col')
- upward_drift: float32 [1, 768, 3072], P(None, 'row', 'col')
- upward_power: float32 [1, 768, 3072], P(None, 'row', 'col')
- downward_update: float32 [1, 3072, 768], P(None, 'col', 'row')
- downward_drift: float32 [1, 3072, 768], P(None, 'col', 'row')
- downward_power: float32 [1, 3072, 768], P(None, 'col', 'row')
- head_update: float32 [768, 8192], P(None, 'row')
- head_drift: float32 [768, 8192], P(None, 'row')
- head_power: float32 [768, 8192], P(None, 'row')
The draws below stay inside these ranges and needn't reach their ends.
Inputs may be any that keep to these rules, and one draw needn't show every extreme that they name: `mask_places`: within each image the 80 places are distinct; slot j counts when j < mask_count of that image. `mask_count`: some image has exactly 80 counted slots.
All inputs are finite; a program needn't handle non-finite values.
Results may differ from the reference program's by a relative error of at most 0.024.
Values may be sent and summed in bfloat16 or wider, within the bound.
A program may use at most 256 MiB of HBM per device.

```python
import math
import jax
import jax.numpy as jnp
from jax import lax

D = 768
HEADS = 12
HD = 64
FF = 3072
VOCAB = 8192
PIX = 768
SEQ = 197
MSLOT = 80
LAYERS = 1
IMAGES = 32
TOKENS = 6304
TABLE = 205


def draw_vector_table(key, part):
    upper = SEQ + 2
    line_index = jnp.arange(TABLE, dtype=jnp.int32)[:, None]
    norm_line = line_index >= upper
    gain_line = norm_line & ((line_index - upper) % 2 == 0)
    noise = jax.random.normal(key, (TABLE, D), jnp.float32)
    spread = jax.random.uniform(jax.random.fold_in(key, 1), (TABLE, D), jnp.float32, -0.3, 0.3)
    return jnp.where(gain_line, 1.0 + spread, jnp.where(norm_line, 0.2 * noise, 0.5 * noise))


def draw_mask_places(key, part):
    keys = jax.random.split(key, IMAGES)

    def one_image(image_key):
        return jax.random.permutation(image_key, SEQ - 1)[:MSLOT] + 1
    return jax.vmap(one_image)(keys).astype(jnp.int32)


def draw_mask_count(key, part):
    counts = jax.random.randint(key, (IMAGES,), MSLOT // 2, MSLOT + 1)
    return counts.at[0].set(MSLOT).astype(jnp.int32)


def plant(result, stream_key, smallest, top_value):
    place = [jax.random.randint(jax.random.fold_in(stream_key, axis), (), 0, length) for axis, length in enumerate(result.shape)]
    widest = result.shape.index(max(result.shape))
    neighbour = place[:widest] + [(place[widest] + 1) % result.shape[widest]] + place[widest + 1:]
    return result.at[tuple(place)].set(smallest).at[tuple(neighbour)].set(top_value)


def steps_of(rng, shape, cuts, low, largest):
    factor_of = 1.0
    for axis_at, shards_of in cuts:
        draws = jax.random.uniform(jax.random.fold_in(jax.random.fold_in(rng, 6), axis_at), (shards_of,), jnp.float32, low / len(cuts), largest / len(cuts))
        factor_of = factor_of * jnp.repeat(jnp.exp(draws), shape[axis_at] // shards_of).reshape((-1,) + (1,) * (len(shape) - 1 - axis_at))
    return factor_of


def centred(rng, dims, width, reach, cuts=(), kind=jnp.bfloat16):
    array = jax.random.normal(rng, dims, jnp.float32) * width
    if len(cuts) > 0:
        array = steps_of(rng, dims, cuts, -0.22, 0.18) * array
    return jnp.clip(array, min=-reach, max=reach).astype(kind)


def setup_inputs(seed: int = 0) -> dict:
    splits = jax.random.split(jax.random.key(seed), 27)
    return {
        "pixels": centred(splits[0], (TOKENS, PIX), 1.0, 6.0, ((0, 2), (1, 16))),
        "mask_places": draw_mask_places(jax.random.fold_in(splits[26], 71), 0),
        "mask_count": draw_mask_count(jax.random.fold_in(splits[26], 71), 0),
        "targets": plant(jax.random.randint(splits[3], (IMAGES, MSLOT), 0, VOCAB), jax.random.fold_in(splits[3], 1), 0, VOCAB - 1).astype(jnp.int32),
        "step_count": jax.random.randint(splits[4], (1,), 1, 21).astype(jnp.int32),
        "patch_weight": centred(splits[5], (PIX, D), PIX ** -0.5, 0.21875, ((0, 16), (1, 2)), jnp.float32),
        "vector_table": draw_vector_table(jax.random.fold_in(splits[26], 71), 0),
        "input_weight": centred(splits[7], (LAYERS, D, 3 * D), D ** -0.5, 0.21875, ((1, 2), (2, 16)), jnp.float32),
        "output_weight": centred(splits[8], (LAYERS, D, D), (D // 8) ** -0.5, 0.625, ((1, 16), (2, 2)), jnp.float32),
        "upward_weight": centred(splits[9], (LAYERS, D, FF), D ** -0.5, 0.21875, ((1, 2), (2, 16)), jnp.float32),
        "downward_weight": centred(splits[10], (LAYERS, FF, D), FF ** -0.5, 0.109375, ((1, 16), (2, 2)), jnp.float32),
        "head_weight": centred(splits[11], (D, VOCAB), D ** -0.5, 0.21875, ((1, 2),), jnp.float32),
        "drift_patch": centred(splits[12], (PIX, D), (0.011 / (PIX * D + TABLE * D + LAYERS * (4 * D * D + 2 * D * FF) + D * VOCAB) ** 0.5), 4.57763671875e-05, ((0, 16), (1, 2)), jnp.float32),
        "drift_table": centred(splits[13], (TABLE, D), (0.011 / (PIX * D + TABLE * D + LAYERS * (4 * D * D + 2 * D * FF) + D * VOCAB) ** 0.5), 4.57763671875e-05, ((1, 2),), jnp.float32),
        "drift_input": centred(splits[14], (LAYERS, D, 3 * D), (0.011 / (PIX * D + TABLE * D + LAYERS * (4 * D * D + 2 * D * FF) + D * VOCAB) ** 0.5), 4.57763671875e-05, ((1, 2), (2, 16)), jnp.float32),
        "drift_output": centred(splits[15], (LAYERS, D, D), (0.011 / (PIX * D + TABLE * D + LAYERS * (4 * D * D + 2 * D * FF) + D * VOCAB) ** 0.5), 4.57763671875e-05, ((1, 16), (2, 2)), jnp.float32),
        "drift_upward": centred(splits[16], (LAYERS, D, FF), (0.011 / (PIX * D + TABLE * D + LAYERS * (4 * D * D + 2 * D * FF) + D * VOCAB) ** 0.5), 4.57763671875e-05, ((1, 2), (2, 16)), jnp.float32),
        "drift_downward": centred(splits[17], (LAYERS, FF, D), (0.011 / (PIX * D + TABLE * D + LAYERS * (4 * D * D + 2 * D * FF) + D * VOCAB) ** 0.5), 4.57763671875e-05, ((1, 16), (2, 2)), jnp.float32),
        "drift_head": centred(splits[18], (D, VOCAB), (0.011 / (PIX * D + TABLE * D + LAYERS * (4 * D * D + 2 * D * FF) + D * VOCAB) ** 0.5), 4.57763671875e-05, ((1, 2),), jnp.float32),
        "power_patch": jnp.clip(jnp.exp(math.log(2.1251563876723e-12) - 2.3025851 * jax.random.uniform(splits[19], (PIX, D), jnp.float32) ** steps_of(splits[19], (PIX, D), ((0, 16), (1, 2)), -0.2, 0.2)), 2.125156468987463e-13, 2.1251563876723e-12),
        "power_table": jnp.clip(jnp.exp(math.log(2.1251563876723e-12) - 2.3025851 * jax.random.uniform(splits[20], (TABLE, D), jnp.float32) ** steps_of(splits[20], (TABLE, D), ((1, 2),), -0.2, 0.2)), 2.125156468987463e-13, 2.1251563876723e-12),
        "power_input": jnp.clip(jnp.exp(math.log(2.1251563876723e-12) - 2.3025851 * jax.random.uniform(splits[21], (LAYERS, D, 3 * D), jnp.float32) ** steps_of(splits[21], (LAYERS, D, 3 * D), ((1, 2), (2, 16)), -0.2, 0.2)), 2.125156468987463e-13, 2.1251563876723e-12),
        "power_output": jnp.clip(jnp.exp(math.log(2.1251563876723e-12) - 2.3025851 * jax.random.uniform(splits[22], (LAYERS, D, D), jnp.float32) ** steps_of(splits[22], (LAYERS, D, D), ((1, 16), (2, 2)), -0.2, 0.2)), 2.125156468987463e-13, 2.1251563876723e-12),
        "power_upward": jnp.clip(jnp.exp(math.log(2.1251563876723e-12) - 2.3025851 * jax.random.uniform(splits[23], (LAYERS, D, FF), jnp.float32) ** steps_of(splits[23], (LAYERS, D, FF), ((1, 2), (2, 16)), -0.2, 0.2)), 2.125156468987463e-13, 2.1251563876723e-12),
        "power_downward": jnp.clip(jnp.exp(math.log(2.1251563876723e-12) - 2.3025851 * jax.random.uniform(splits[24], (LAYERS, FF, D), jnp.float32) ** steps_of(splits[24], (LAYERS, FF, D), ((1, 16), (2, 2)), -0.2, 0.2)), 2.125156468987463e-13, 2.1251563876723e-12),
        "power_head": jnp.clip(jnp.exp(math.log(2.1251563876723e-12) - 2.3025851 * jax.random.uniform(splits[25], (D, VOCAB), jnp.float32) ** steps_of(splits[25], (D, VOCAB), ((1, 2),), -0.2, 0.2)), 2.125156468987463e-13, 2.1251563876723e-12),
    }


@jax.custom_vjp
def low(v):
    return lax.optimization_barrier(v.astype(jnp.bfloat16)).astype(jnp.float32)

@jax.custom_vjp
def low_back(v):
    return v

def low_keep(v):
    return (low(v), None)

def low_pass(kept, grad):
    return (grad,)

def back_keep(v):
    return (v, None)

def back_low(kept, grad):
    return (low(grad),)
low.defvjp(low_keep, low_pass)
low_back.defvjp(back_keep, back_low)
norm_eps = 1e-06
clip_limit = 0.1
learn_rate = 0.01
beta_first = 0.9
beta_second = 0.999
adam_eps = 1e-08
weight_decay = 0.05
highest = lax.Precision.HIGHEST

def layer_norm(values, gain, shift):
    center = lax.optimization_barrier(jnp.mean(values, axis=-1, keepdims=True))
    spread = lax.optimization_barrier(jnp.mean(jnp.square(values - center), axis=-1, keepdims=True))
    return (values - center) * lax.rsqrt(spread + norm_eps) * gain + shift

def attend_group(packed):
    amount = packed.shape[0]
    pieces = packed.reshape(amount, SEQ, 3, HEADS, HD)
    scores = jnp.einsum('gqhd,gkhd->ghqk', pieces[:, :, 0], pieces[:, :, 1], precision=highest)
    scores = low_back(scores * (1.0 / math.sqrt(HD)))
    attention = jax.nn.softmax(scores, axis=-1)
    mixture = jnp.einsum('ghqk,gkhd->gqhd', low(attention), pieces[:, :, 2], precision=highest)
    return mixture.reshape(amount, SEQ, HEADS * HD)

def forward(params, pixel_data, mask_places, mask_count, targets):
    patch_weight, vector_table, input_weight, output_weight, upward_weight, downward_weight, head_weight = params
    images = mask_places.shape[0]
    grouping = math.gcd(images, 16)
    patch = low_back(jnp.dot(pixel_data, low(patch_weight), precision=highest)).reshape(images, SEQ, D)
    places = jnp.arange(SEQ, dtype=jnp.int32)
    counted = jnp.arange(MSLOT, dtype=jnp.int32)[None, :] < mask_count[:, None]
    masked = jnp.any((mask_places[:, :, None] == places[None, None, :]) & counted[:, :, None], axis=1)
    opening = (places == 0)[None, :, None]
    stream = jnp.where(opening, vector_table[SEQ], jnp.where(masked[:, :, None], vector_table[SEQ + 1], patch))
    stream = (stream + vector_table[:SEQ][None]).reshape(images * SEQ, D)
    for layer_index in range(LAYERS):
        base = SEQ + 2 + 4 * layer_index
        normed = low(layer_norm(stream, vector_table[base], vector_table[base + 1]))
        packed = low(low_back(jnp.dot(normed, low(input_weight[layer_index]), precision=highest)))
        mixture = lax.map(jax.checkpoint(attend_group), packed.reshape(images // grouping, grouping, SEQ, 3 * D))
        mixture = low(low_back(mixture.reshape(images * SEQ, D)))
        stream = stream + low_back(jnp.dot(mixture, low(output_weight[layer_index]), precision=highest))
        normed = low(layer_norm(stream, vector_table[base + 2], vector_table[base + 3]))
        hidden_pre = low_back(jnp.dot(normed, low(upward_weight[layer_index]), precision=highest))
        hidden_act = low(jax.nn.gelu(hidden_pre, approximate=False))
        stream = stream + low_back(jnp.dot(hidden_act, low(downward_weight[layer_index]), precision=highest))
    last = SEQ + 2 + 4 * LAYERS
    final_out = layer_norm(stream, vector_table[last], vector_table[last + 1]).reshape(images, SEQ, D)
    picked = low(jnp.take_along_axis(final_out, mask_places[:, :, None], axis=1))
    head_low = low(head_weight)
    picked_groups = picked.reshape(images // grouping, grouping * MSLOT, D)
    target_groups = targets.reshape(images // grouping, grouping * MSLOT)
    keep_groups = counted.astype(jnp.float32).reshape(images // grouping, grouping * MSLOT)

    def head_loss(item):
        block, target_block, keep_block = item
        logits = low_back(jnp.dot(block, head_low, precision=highest))
        log_total = jax.nn.logsumexp(logits, axis=-1)
        chosen = jnp.take_along_axis(logits, target_block[:, None], axis=1)[:, 0]
        return jnp.sum((log_total - chosen) * keep_block)
    return jnp.sum(lax.map(jax.checkpoint(head_loss), (picked_groups, target_groups, keep_groups)))

def adam_step(weight, grad, drift, power, factor, step_value):
    scaled = grad * factor
    new_drift = beta_first * drift + (1.0 - beta_first) * scaled
    new_power = beta_second * power + (1.0 - beta_second) * scaled * scaled
    drift_hat = new_drift / (1.0 - jnp.power(beta_first, step_value))
    power_hat = new_power / (1.0 - jnp.power(beta_second, step_value))
    update = -learn_rate * (drift_hat / (jnp.sqrt(power_hat) + adam_eps) + weight_decay * weight)
    return (update, new_drift, new_power)

def reference(pixels, mask_places, mask_count, targets, step_count, patch_weight, vector_table, input_weight, output_weight, upward_weight, downward_weight, head_weight, drift_patch, drift_table, drift_input, drift_output, drift_upward, drift_downward, drift_head, power_patch, power_table, power_input, power_output, power_upward, power_downward, power_head):
    params = (patch_weight, vector_table, input_weight, output_weight, upward_weight, downward_weight, head_weight)
    pixel_data = pixels.astype(jnp.float32)

    def loss_of(*weights):
        return forward(weights, pixel_data, mask_places, mask_count, targets)
    loss_total, pull = jax.vjp(loss_of, *params)
    grads = pull(jnp.ones_like(loss_total))
    count_total = jnp.sum(mask_count.astype(jnp.float32))
    squares = jnp.float32(0.0)
    for grad in grads:
        squares = squares + jnp.sum(grad * grad)
    mean_loss = loss_total / count_total
    grad_norm = jnp.sqrt(squares) / count_total
    factor = jnp.minimum(1.0, clip_limit / grad_norm) / count_total
    step_value = step_count[0].astype(jnp.float32)
    drifts = (drift_patch, drift_table, drift_input, drift_output, drift_upward, drift_downward, drift_head)
    powers = (power_patch, power_table, power_input, power_output, power_upward, power_downward, power_head)
    results = [adam_step(params[index], grads[index], drifts[index], powers[index], factor, step_value) for index in range(7)]
    return (mean_loss, grad_norm, results[0][0], results[0][1], results[0][2], results[1][0], results[1][1], results[1][2], results[2][0], results[2][1], results[2][2], results[3][0], results[3][1], results[3][2], results[4][0], results[4][1], results[4][2], results[5][0], results[5][1], results[5][2], results[6][0], results[6][1], results[6][2])
```

```python
import math

import jax
import jax.numpy as jnp
from jax import lax
from jax.sharding import PartitionSpec as P

HEADS = 12
HD = 64
SEQ = 197
MSLOT = 80
BOTH = ("row", "col")

norm_eps = 1e-06
clip_limit = 0.1
learn_rate = 0.01
beta_first = 0.9
beta_second = 0.999
adam_eps = 1e-08
weight_decay = 0.05
low_type = jnp.bfloat16
wide = jnp.float32


def product(left, right):
    return jnp.dot(left, right, preferred_element_type=wide)


def product_nt(left, right):
    return jnp.einsum("ab,cb->ac", left, right, preferred_element_type=wide)


def product_tn(left, right):
    return jnp.einsum("ab,ac->bc", left, right, preferred_element_type=wide)


def norm_forward(values, gain, shift):
    center = jnp.mean(values, axis=1, keepdims=True)
    moved = values - center
    inverse = lax.rsqrt(jnp.mean(moved * moved, axis=1, keepdims=True) + norm_eps)
    scaled = moved * inverse
    return scaled * gain + shift, (scaled, inverse)


def norm_backward(upstream, kept, gain):
    scaled, inverse = kept
    inner = upstream * gain
    downstream = inverse * (
        inner
        - jnp.mean(inner, axis=1, keepdims=True)
        - scaled * jnp.mean(inner * scaled, axis=1, keepdims=True)
    )
    return downstream, jnp.sum(upstream * scaled, axis=0), jnp.sum(upstream, axis=0)


def exact_gelu(values):
    return jax.nn.gelu(values, approximate=False)


def split_heads(grouped):
    images = grouped.shape[0] // SEQ
    pieces = grouped.reshape(images, SEQ, 3, HEADS, HD)
    return pieces[:, :, 0], pieces[:, :, 1], pieces[:, :, 2]


def attention_weights(query, keys):
    scores = jnp.einsum("iqhd,ikhd->ihqk", query, keys, preferred_element_type=wide)
    return jax.nn.softmax(scores * (1.0 / math.sqrt(HD)), axis=-1)


def attend(grouped):
    query, keys, values = split_heads(grouped)
    weights_full = attention_weights(query, keys)
    mixture = jnp.einsum(
        "ihqk,ikhd->iqhd", weights_full.astype(low_type), values, preferred_element_type=wide
    )
    return mixture.reshape(grouped.shape[0], HEADS * HD), weights_full


def attend_back(grouped, weights_full, grad_mixture):
    query, keys, values = split_heads(grouped)
    images = query.shape[0]
    weights_low = weights_full.astype(low_type)
    grad_out = grad_mixture.reshape(images, SEQ, HEADS, HD)
    grad_weights = jnp.einsum("iqhd,ikhd->ihqk", grad_out, values, preferred_element_type=wide)
    grad_values = jnp.einsum("ihqk,iqhd->ikhd", weights_low, grad_out, preferred_element_type=wide)
    centered = grad_weights - jnp.sum(weights_full * grad_weights, axis=-1, keepdims=True)
    grad_scores = (weights_full * centered).astype(low_type)
    scale = 1.0 / math.sqrt(HD)
    grad_query = jnp.einsum("ihqk,ikhd->iqhd", grad_scores, keys, preferred_element_type=wide)
    grad_keys = jnp.einsum("ihqk,iqhd->ikhd", grad_scores, query, preferred_element_type=wide)
    stacked = jnp.stack([grad_query * scale, grad_keys * scale, grad_values], axis=2)
    return stacked.reshape(images * SEQ, 3 * HEADS * HD)


def adam_step(weight, grad, drift, power, factor, step_value):
    scaled = grad * factor
    new_drift = beta_first * drift + (1.0 - beta_first) * scaled
    new_power = beta_second * power + (1.0 - beta_second) * scaled * scaled
    drift_hat = new_drift / (1.0 - jnp.power(beta_first, step_value))
    power_hat = new_power / (1.0 - jnp.power(beta_second, step_value))
    update = -learn_rate * (drift_hat / (jnp.sqrt(power_hat) + adam_eps) + weight_decay * weight)
    return (update, new_drift, new_power)


def on_device(
    pixels,
    mask_places,
    mask_count,
    targets,
    step_count,
    patch_weight,
    vector_table,
    input_weight,
    output_weight,
    upward_weight,
    downward_weight,
    head_weight,
    drift_patch,
    drift_table,
    drift_input,
    drift_output,
    drift_upward,
    drift_downward,
    drift_head,
    power_patch,
    power_table,
    power_input,
    power_output,
    power_upward,
    power_downward,
    power_head,
):
    rows, cols = lax.axis_size("row"), lax.axis_size("col")
    row_index = lax.axis_index("row")
    col_index = lax.axis_index("col")
    images = mask_places.shape[0] // rows
    width = vector_table.shape[1] * rows

    blocks = [
        patch_weight.astype(low_type),
        input_weight[0].astype(low_type).T,
        output_weight[0].astype(low_type),
        upward_weight[0].astype(low_type).T,
        downward_weight[0].astype(low_type),
    ]
    heights = [block.shape[0] for block in blocks]
    gathered = lax.all_gather(jnp.concatenate(blocks, axis=0), BOTH, axis=0, tiled=False)
    gathered = gathered.reshape(rows, cols, sum(heights), -1)

    def whole(index):
        start = sum(heights[:index])
        part = gathered[:, :, start : start + heights[index]]
        return jnp.transpose(part, (1, 2, 0, 3)).reshape(cols * heights[index], width)

    patch_low, input_turned, output_low, upward_turned, downward_low = map(whole, range(5))
    table = lax.all_gather(vector_table, "row", axis=1, tiled=True)

    local_images = pixels.shape[0] // SEQ
    part = pixels.shape[1]
    grid = pixels.reshape(local_images // (rows * images), rows, images, SEQ, part)
    grid = lax.all_to_all(grid, "row", split_axis=1, concat_axis=0, tiled=True)
    grid = grid.reshape(cols, images * SEQ, part)
    grid = lax.all_to_all(grid, "col", split_axis=0, concat_axis=0, tiled=True)
    pixel_own = jnp.transpose(grid, (1, 0, 2)).reshape(images * SEQ, cols * part)

    def own(values):
        return lax.dynamic_slice_in_dim(values, row_index * images, images, axis=0)

    places_own, count_own = own(mask_places), own(mask_count)

    def gains_of(norm_index):
        return (table[SEQ + 2 + 2 * norm_index], table[SEQ + 3 + 2 * norm_index])

    patch_proj = product(pixel_own, patch_low)
    places = jnp.arange(SEQ, dtype=jnp.int32)
    counted_own = jnp.arange(MSLOT, dtype=jnp.int32)[None, :] < count_own[:, None]
    matches = places_own[:, :, None] == places[None, None, :]
    masked = jnp.any(matches & counted_own[:, :, None], axis=1)[:, :, None]
    opening = (places == 0)[None, :, None]
    stream = jnp.where(
        opening,
        table[SEQ],
        jnp.where(masked, table[SEQ + 1], patch_proj.reshape(images, SEQ, -1)),
    )
    stream = (stream + table[:SEQ][None]).reshape(images * SEQ, -1)
    gain_one, shift_one = gains_of(0)
    gain_two, shift_two = gains_of(1)
    final_gain, final_shift = gains_of(2)
    normed_one, stats_one = norm_forward(stream, gain_one, shift_one)
    normed_one = normed_one.astype(low_type)
    grouped = product_nt(normed_one, input_turned).astype(low_type)
    mixture, weights_full = attend(grouped)
    mixture = mixture.astype(low_type)
    stream_mid = stream + product(mixture, output_low)
    normed_two, stats_two = norm_forward(stream_mid, gain_two, shift_two)
    normed_two = normed_two.astype(low_type)
    hidden_pre = product_nt(normed_two, upward_turned)
    hidden_act = exact_gelu(hidden_pre).astype(low_type)
    stream_last = stream_mid + product(hidden_act, downward_low)
    final_out, final_stats = norm_forward(stream_last, final_gain, final_shift)
    selector = matches.astype(low_type)
    picked = jnp.einsum(
        "ims,isd->imd", selector, final_out.astype(low_type).reshape(images, SEQ, -1),
        preferred_element_type=wide,
    ).astype(low_type)

    picked_wide = lax.all_gather(picked.reshape(images * MSLOT, -1), "row", axis=0, tiled=True)
    head_low = head_weight.astype(low_type)
    logits = product(picked_wide, head_low)
    vocab_local = head_weight.shape[1]
    target_local = targets.reshape(-1) - row_index * vocab_local
    target_hits = target_local[:, None] == jnp.arange(vocab_local, dtype=jnp.int32)[None, :]
    chosen = jnp.sum(jnp.where(target_hits, logits, 0.0), axis=1)
    local_top = jnp.max(logits, axis=1)
    local_sum = jnp.sum(jnp.exp(logits - local_top[:, None]), axis=1)
    pair = lax.all_gather(jnp.stack([local_top, local_sum]), "row", axis=0, tiled=False)
    top_value = jnp.max(pair[:, 0], axis=0)
    exp_total = jnp.sum(pair[:, 1] * jnp.exp(pair[:, 0] - top_value), axis=0)
    log_total = top_value + jnp.log(exp_total)
    counted = jnp.arange(MSLOT, dtype=jnp.int32)[None, :] < mask_count[:, None]
    slot_weight = counted.reshape(-1).astype(wide)
    leader_row = (row_index == 0).astype(wide)
    loss_part = jnp.sum(log_total * slot_weight) * leader_row - jnp.sum(chosen * slot_weight)
    count_part = jnp.sum(mask_count.astype(wide)) * leader_row
    grad_logits = (
        (jnp.exp(logits - log_total[:, None]) - target_hits.astype(wide)) * slot_weight[:, None]
    ).astype(low_type)
    grad_head_local = product_tn(picked_wide, grad_logits)
    grad_head = lax.psum(grad_head_local.astype(low_type), "col").astype(wide)
    grad_picked = lax.psum_scatter(
        product_nt(grad_logits, head_low).astype(low_type),
        "row",
        scatter_dimension=0,
        tiled=True,
    )
    grad_final = jnp.einsum(
        "ims,imd->isd", selector, grad_picked.reshape(images, MSLOT, -1),
        preferred_element_type=wide,
    )

    grad_stream, grad_final_gain, grad_final_shift = norm_backward(
        grad_final.reshape(images * SEQ, -1), final_stats, final_gain
    )
    grad_two = grad_stream.astype(low_type)
    grad_downward = product_tn(hidden_act, grad_two)
    grad_act = product_nt(grad_two, downward_low)
    _, gelu_pull = jax.vjp(exact_gelu, hidden_pre)
    grad_pre = gelu_pull(grad_act)[0].astype(low_type)
    grad_upward_turned = product_tn(grad_pre, normed_two)
    grad_normed_two = product(grad_pre, upward_turned)
    grad_mid, grad_gain_two, grad_shift_two = norm_backward(grad_normed_two, stats_two, gain_two)
    grad_mid = grad_mid + grad_stream
    grad_one = grad_mid.astype(low_type)
    grad_output = product_tn(mixture, grad_one)
    grad_mixture = product_nt(grad_one, output_low).astype(low_type)
    grad_grouped = attend_back(grouped, weights_full, grad_mixture).astype(low_type)
    grad_input_turned = product_tn(grad_grouped, normed_one)
    grad_normed_one = product(grad_grouped, input_turned)
    grad_below, grad_gain_one, grad_shift_one = norm_backward(grad_normed_one, stats_one, gain_one)
    grad_grid = (grad_below + grad_mid).reshape(images, SEQ, -1)
    grad_patch = jnp.where(opening | masked, 0.0, grad_grid).reshape(images * SEQ, -1)
    grad_patch_weight = product_tn(pixel_own, grad_patch.astype(low_type))
    lines = [
        jnp.sum(grad_grid, axis=0),
        jnp.sum(grad_grid[:, 0], axis=0)[None],
        jnp.sum(jnp.where(masked, grad_grid, 0.0), axis=(0, 1))[None],
        jnp.stack(
            [grad_gain_one, grad_shift_one, grad_gain_two, grad_shift_two,
             grad_final_gain, grad_final_shift]
        ),
    ]
    table_local = jnp.concatenate(lines, axis=0).astype(low_type)

    def dealt(value, height):
        grid = value.astype(low_type).reshape(cols, height, rows, -1)
        return jnp.transpose(grid, (2, 0, 1, 3)).reshape(rows * cols, height, -1)

    stacked = jnp.concatenate(
        [
            dealt(value, height)
            for value, height in zip(
                [grad_patch_weight, grad_input_turned, grad_output, grad_upward_turned,
                 grad_downward],
                heights,
            )
        ],
        axis=1,
    )
    summed = lax.psum_scatter(stacked, BOTH, scatter_dimension=0, tiled=False).astype(wide)
    starts = [sum(heights[:index]) for index in range(6)]
    pieces = [summed[starts[index] : starts[index + 1]] for index in range(5)]
    grad_table = lax.psum(table_local, BOTH).astype(wide)
    grad_table = lax.dynamic_slice_in_dim(
        grad_table, row_index * vector_table.shape[1], vector_table.shape[1], axis=1
    )
    leader_col = (col_index == 0).astype(wide)
    squares_part = jnp.sum(summed * summed) + leader_col * (
        jnp.sum(grad_table * grad_table) + jnp.sum(grad_head * grad_head)
    )
    loss_total, count_total, squares_total = lax.psum((loss_part, count_part, squares_part), BOTH)
    mean_loss = loss_total / count_total
    grad_norm = jnp.sqrt(squares_total) / count_total
    factor = jnp.minimum(1.0, clip_limit / grad_norm) / count_total
    step_value = step_count[0].astype(wide)
    steps = [
        (patch_weight, pieces[0], drift_patch, power_patch),
        (vector_table, grad_table, drift_table, power_table),
        (input_weight, pieces[1].T[None], drift_input, power_input),
        (output_weight, pieces[2][None], drift_output, power_output),
        (upward_weight, pieces[3].T[None], drift_upward, power_upward),
        (downward_weight, pieces[4][None], drift_downward, power_downward),
        (head_weight, grad_head, drift_head, power_head),
    ]
    results = []
    for weight, grad, drift, power in steps:
        results.extend(adam_step(weight, grad, drift, power, factor, step_value))
    return (mean_loss, grad_norm, *results)


def solution(mesh):
    state = (
        P("col", "row"),
        P(None, "row"),
        P(None, "row", "col"),
        P(None, "col", "row"),
        P(None, "row", "col"),
        P(None, "col", "row"),
        P(None, "row"),
    )
    data = (P("row", "col"), P("col", None), P("col"), P("col", None), P())
    outs = (P(), P()) + tuple(spec for spec in state for _ in range(3))
    return jax.shard_map(
        on_device,
        mesh=mesh,
        in_specs=data + state * 3,
        out_specs=outs,
        check_vma=False,
    )
```

```python
import math

import jax
import jax.numpy as jnp
from jax import lax
from jax.experimental import pallas as pl
from jax.experimental.pallas import tpu as pltpu
from jax.sharding import PartitionSpec as P

HEADS = 12
HD = 64
SEQ = 197
MSLOT = 80
BOTH = ("row", "col")

norm_eps = 1e-06
clip_limit = 0.1
learn_rate = 0.01
beta_first = 0.9
beta_second = 0.999
adam_eps = 1e-08
weight_decay = 0.05
low_type = jnp.bfloat16
wide = jnp.float32


def product(left, right):
    return jnp.dot(left, right, preferred_element_type=wide)


def product_nt(left, right):
    return jnp.einsum("ab,cb->ac", left, right, preferred_element_type=wide)


def product_tn(left, right):
    return jnp.einsum("ab,ac->bc", left, right, preferred_element_type=wide)


def norm_forward(values, gain, shift):
    center = jnp.mean(values, axis=1, keepdims=True)
    moved = values - center
    inverse = lax.rsqrt(jnp.mean(moved * moved, axis=1, keepdims=True) + norm_eps)
    scaled = moved * inverse
    return scaled * gain + shift, (scaled, inverse)


def norm_backward(upstream, kept, gain):
    scaled, inverse = kept
    inner = upstream * gain
    downstream = inverse * (
        inner
        - jnp.mean(inner, axis=1, keepdims=True)
        - scaled * jnp.mean(inner * scaled, axis=1, keepdims=True)
    )
    return downstream, jnp.sum(upstream * scaled, axis=0), jnp.sum(upstream, axis=0)


def exact_gelu(values):
    return jax.nn.gelu(values, approximate=False)


def split_heads(grouped):
    images = grouped.shape[0] // SEQ
    pieces = grouped.reshape(images, SEQ, 3, HEADS, HD)
    return pieces[:, :, 0], pieces[:, :, 1], pieces[:, :, 2]


def attention_weights(query, keys):
    scores = jnp.einsum("iqhd,ikhd->ihqk", query, keys, preferred_element_type=wide)
    return jax.nn.softmax(scores * (1.0 / math.sqrt(HD)), axis=-1)


def attend(grouped):
    query, keys, values = split_heads(grouped)
    weights_full = attention_weights(query, keys)
    mixture = jnp.einsum(
        "ihqk,ikhd->iqhd", weights_full.astype(low_type), values, preferred_element_type=wide
    )
    return mixture.reshape(grouped.shape[0], HEADS * HD), weights_full


def attend_back(grouped, weights_full, grad_mixture):
    query, keys, values = split_heads(grouped)
    images = query.shape[0]
    weights_low = weights_full.astype(low_type)
    grad_out = grad_mixture.reshape(images, SEQ, HEADS, HD)
    grad_weights = jnp.einsum("iqhd,ikhd->ihqk", grad_out, values, preferred_element_type=wide)
    grad_values = jnp.einsum("ihqk,iqhd->ikhd", weights_low, grad_out, preferred_element_type=wide)
    centered = grad_weights - jnp.sum(weights_full * grad_weights, axis=-1, keepdims=True)
    grad_scores = (weights_full * centered).astype(low_type)
    scale = 1.0 / math.sqrt(HD)
    grad_query = jnp.einsum("ihqk,ikhd->iqhd", grad_scores, keys, preferred_element_type=wide)
    grad_keys = jnp.einsum("ihqk,iqhd->ikhd", grad_scores, query, preferred_element_type=wide)
    stacked = jnp.stack([grad_query * scale, grad_keys * scale, grad_values], axis=2)
    return stacked.reshape(images * SEQ, 3 * HEADS * HD)


def adam_step(weight, grad, drift, power, factor, step_value):
    scaled = grad * factor
    new_drift = beta_first * drift + (1.0 - beta_first) * scaled
    new_power = beta_second * power + (1.0 - beta_second) * scaled * scaled
    drift_hat = new_drift / (1.0 - jnp.power(beta_first, step_value))
    power_hat = new_power / (1.0 - jnp.power(beta_second, step_value))
    update = -learn_rate * (drift_hat / (jnp.sqrt(power_hat) + adam_eps) + weight_decay * weight)
    return (update, new_drift, new_power)


def on_device(
    pixels,
    mask_places,
    mask_count,
    targets,
    step_count,
    patch_weight,
    vector_table,
    input_weight,
    output_weight,
    upward_weight,
    downward_weight,
    head_weight,
    drift_patch,
    drift_table,
    drift_input,
    drift_output,
    drift_upward,
    drift_downward,
    drift_head,
    power_patch,
    power_table,
    power_input,
    power_output,
    power_upward,
    power_downward,
    power_head,
):
    rows, cols = lax.axis_size("row"), lax.axis_size("col")
    row_index = lax.axis_index("row")
    col_index = lax.axis_index("col")
    images = mask_places.shape[0] // rows
    width = vector_table.shape[1] * rows

    blocks = [
        patch_weight.astype(low_type),
        input_weight[0].astype(low_type).T,
        output_weight[0].astype(low_type),
        upward_weight[0].astype(low_type).T,
        downward_weight[0].astype(low_type),
    ]
    heights = [block.shape[0] for block in blocks]
    gathered = lax.all_gather(jnp.concatenate(blocks, axis=0), BOTH, axis=0, tiled=False)
    gathered = gathered.reshape(rows, cols, sum(heights), -1)

    def whole(index):
        start = sum(heights[:index])
        part = gathered[:, :, start : start + heights[index]]
        return jnp.transpose(part, (1, 2, 0, 3)).reshape(cols * heights[index], width)

    patch_low, input_turned, output_low, upward_turned, downward_low = map(whole, range(5))
    table = lax.all_gather(vector_table, "row", axis=1, tiled=True)

    local_images = pixels.shape[0] // SEQ
    part = pixels.shape[1]
    grid = pixels.reshape(local_images // (rows * images), rows, images, SEQ, part)
    grid = lax.all_to_all(grid, "row", split_axis=1, concat_axis=0, tiled=True)
    grid = grid.reshape(cols, images * SEQ, part)
    grid = lax.all_to_all(grid, "col", split_axis=0, concat_axis=0, tiled=True)
    pixel_own = jnp.transpose(grid, (1, 0, 2)).reshape(images * SEQ, cols * part)

    def own(values):
        return lax.dynamic_slice_in_dim(values, row_index * images, images, axis=0)

    places_own, count_own = own(mask_places), own(mask_count)

    def gains_of(norm_index):
        return (table[SEQ + 2 + 2 * norm_index], table[SEQ + 3 + 2 * norm_index])

    patch_proj = product(pixel_own, patch_low)
    places = jnp.arange(SEQ, dtype=jnp.int32)
    counted_own = jnp.arange(MSLOT, dtype=jnp.int32)[None, :] < count_own[:, None]
    matches = places_own[:, :, None] == places[None, None, :]
    masked = jnp.any(matches & counted_own[:, :, None], axis=1)[:, :, None]
    opening = (places == 0)[None, :, None]
    stream = jnp.where(
        opening,
        table[SEQ],
        jnp.where(masked, table[SEQ + 1], patch_proj.reshape(images, SEQ, -1)),
    )
    stream = (stream + table[:SEQ][None]).reshape(images * SEQ, -1)
    gain_one, shift_one = gains_of(0)
    gain_two, shift_two = gains_of(1)
    final_gain, final_shift = gains_of(2)
    normed_one, stats_one = norm_forward(stream, gain_one, shift_one)
    normed_one = normed_one.astype(low_type)
    grouped = product_nt(normed_one, input_turned).astype(low_type)
    mixture, weights_full = attend(grouped)
    mixture = mixture.astype(low_type)
    stream_mid = stream + product(mixture, output_low)
    normed_two, stats_two = norm_forward(stream_mid, gain_two, shift_two)
    normed_two = normed_two.astype(low_type)
    hidden_pre = product_nt(normed_two, upward_turned)
    hidden_act = exact_gelu(hidden_pre).astype(low_type)
    stream_last = stream_mid + product(hidden_act, downward_low)
    final_out, final_stats = norm_forward(stream_last, final_gain, final_shift)
    selector = matches.astype(low_type)
    picked = jnp.einsum(
        "ims,isd->imd", selector, final_out.astype(low_type).reshape(images, SEQ, -1),
        preferred_element_type=wide,
    ).astype(low_type)

    picked_wide = lax.all_gather(picked.reshape(images * MSLOT, -1), "row", axis=0, tiled=True)
    head_low = head_weight.astype(low_type)
    logits = product(picked_wide, head_low)
    vocab_local = head_weight.shape[1]
    target_local = targets.reshape(-1) - row_index * vocab_local
    target_hits = target_local[:, None] == jnp.arange(vocab_local, dtype=jnp.int32)[None, :]
    chosen = jnp.sum(jnp.where(target_hits, logits, 0.0), axis=1)
    local_top = jnp.max(logits, axis=1)
    local_sum = jnp.sum(jnp.exp(logits - local_top[:, None]), axis=1)
    pair = lax.all_gather(jnp.stack([local_top, local_sum]), "row", axis=0, tiled=False)
    top_value = jnp.max(pair[:, 0], axis=0)
    exp_total = jnp.sum(pair[:, 1] * jnp.exp(pair[:, 0] - top_value), axis=0)
    log_total = top_value + jnp.log(exp_total)
    counted = jnp.arange(MSLOT, dtype=jnp.int32)[None, :] < mask_count[:, None]
    slot_weight = counted.reshape(-1).astype(wide)
    leader_row = (row_index == 0).astype(wide)
    loss_part = jnp.sum(log_total * slot_weight) * leader_row - jnp.sum(chosen * slot_weight)
    count_part = jnp.sum(mask_count.astype(wide)) * leader_row
    grad_logits = (
        (jnp.exp(logits - log_total[:, None]) - target_hits.astype(wide)) * slot_weight[:, None]
    ).astype(low_type)
    grad_head_local = product_tn(picked_wide, grad_logits)
    grad_head = lax.psum(grad_head_local.astype(low_type), "col").astype(wide)
    grad_picked = lax.psum_scatter(
        product_nt(grad_logits, head_low).astype(low_type),
        "row",
        scatter_dimension=0,
        tiled=True,
    )
    grad_final = jnp.einsum(
        "ims,imd->isd", selector, grad_picked.reshape(images, MSLOT, -1),
        preferred_element_type=wide,
    )

    grad_stream, grad_final_gain, grad_final_shift = norm_backward(
        grad_final.reshape(images * SEQ, -1), final_stats, final_gain
    )
    grad_two = grad_stream.astype(low_type)
    grad_downward = product_tn(hidden_act, grad_two)
    grad_act = product_nt(grad_two, downward_low)
    _, gelu_pull = jax.vjp(exact_gelu, hidden_pre)
    grad_pre = gelu_pull(grad_act)[0].astype(low_type)
    grad_upward_turned = product_tn(grad_pre, normed_two)
    grad_normed_two = product(grad_pre, upward_turned)
    grad_mid, grad_gain_two, grad_shift_two = norm_backward(grad_normed_two, stats_two, gain_two)
    grad_mid = grad_mid + grad_stream
    grad_one = grad_mid.astype(low_type)
    grad_output = product_tn(mixture, grad_one)
    grad_mixture = product_nt(grad_one, output_low).astype(low_type)
    grad_grouped = attend_back(grouped, weights_full, grad_mixture).astype(low_type)
    grad_input_turned = product_tn(grad_grouped, normed_one)
    grad_normed_one = product(grad_grouped, input_turned)
    grad_below, grad_gain_one, grad_shift_one = norm_backward(grad_normed_one, stats_one, gain_one)
    grad_grid = (grad_below + grad_mid).reshape(images, SEQ, -1)
    grad_patch = jnp.where(opening | masked, 0.0, grad_grid).reshape(images * SEQ, -1)
    grad_patch_weight = product_tn(pixel_own, grad_patch.astype(low_type))
    lines = [
        jnp.sum(grad_grid, axis=0),
        jnp.sum(grad_grid[:, 0], axis=0)[None],
        jnp.sum(jnp.where(masked, grad_grid, 0.0), axis=(0, 1))[None],
        jnp.stack(
            [grad_gain_one, grad_shift_one, grad_gain_two, grad_shift_two,
             grad_final_gain, grad_final_shift]
        ),
    ]
    table_local = jnp.concatenate(lines, axis=0).astype(low_type)

    def dealt(value, height):
        grid = value.astype(low_type).reshape(cols, height, rows, -1)
        return jnp.transpose(grid, (2, 0, 1, 3)).reshape(rows * cols, height, -1)

    stacked = jnp.concatenate(
        [
            dealt(value, height)
            for value, height in zip(
                [grad_patch_weight, grad_input_turned, grad_output, grad_upward_turned,
                 grad_downward],
                heights,
            )
        ],
        axis=1,
    )
    summed = lax.psum_scatter(stacked, BOTH, scatter_dimension=0, tiled=False).astype(wide)
    starts = [sum(heights[:index]) for index in range(6)]
    pieces = [summed[starts[index] : starts[index + 1]] for index in range(5)]
    grad_table = lax.psum(table_local, BOTH).astype(wide)
    grad_table = lax.dynamic_slice_in_dim(
        grad_table, row_index * vector_table.shape[1], vector_table.shape[1], axis=1
    )
    leader_col = (col_index == 0).astype(wide)
    squares_part = jnp.sum(summed * summed) + leader_col * (
        jnp.sum(grad_table * grad_table) + jnp.sum(grad_head * grad_head)
    )
    loss_total, count_total, squares_total = lax.psum((loss_part, count_part, squares_part), BOTH)
    mean_loss = loss_total / count_total
    grad_norm = jnp.sqrt(squares_total) / count_total
    factor = jnp.minimum(1.0, clip_limit / grad_norm) / count_total
    step_value = step_count[0].astype(wide)
    steps = [
        (patch_weight, pieces[0], drift_patch, power_patch),
        (vector_table, grad_table, drift_table, power_table),
        (input_weight, pieces[1].T[None], drift_input, power_input),
        (output_weight, pieces[2][None], drift_output, power_output),
        (upward_weight, pieces[3].T[None], drift_upward, power_upward),
        (downward_weight, pieces[4][None], drift_downward, power_downward),
        (head_weight, grad_head, drift_head, power_head),
    ]
    results = []
    for weight, grad, drift, power in steps:
        results.extend(adam_step(weight, grad, drift, power, factor, step_value))
    return (mean_loss, grad_norm, *results)


VMEM_LIMIT = 62 * 2**20
TOK = 208
UNIT = 48
UNITS = 13
BANDS = 8
EYE = pl.DeviceIdType.MESH


def nn(left, right):
    return jnp.dot(left, right, preferred_element_type=wide)


def nt(left, right):
    return lax.dot_general(left, right, (((1,), (1,)), ((), ())), preferred_element_type=wide)


def tn(left, right):
    return lax.dot_general(left, right, (((0,), (0,)), ((), ())), preferred_element_type=wide)


def gelu_parts(values):
    phi_total = 0.5 * (1.0 + lax.erf(values * math.sqrt(0.5)))
    density = jnp.exp(values * values * -0.5) * (1.0 / math.sqrt(2.0 * math.pi))
    return phi_total, density


def normed(values, gain, shift):
    center = jnp.mean(values, axis=1, keepdims=True)
    moved = values - center
    inverse = lax.rsqrt(jnp.mean(moved * moved, axis=1, keepdims=True) + norm_eps)
    scaled = moved * inverse
    return scaled * gain + shift, scaled, inverse


def normed_back(upstream, scaled, inverse, gain):
    inner = upstream * gain
    down = inverse * (
        inner
        - jnp.mean(inner, axis=1, keepdims=True)
        - scaled * jnp.mean(inner * scaled, axis=1, keepdims=True)
    )
    return (
        down,
        jnp.sum(upstream * scaled, axis=0, keepdims=True),
        jnp.sum(upstream, axis=0, keepdims=True),
    )


def step_kernel(
    pix_in, blk_in, tab_in, places, info_in, counts, head_in,
    gout, gtab_out, ghead, scal_out,
    wg, px, tb, st0, st1, st2, n1, n2, mix, qkv, hpre, hact,
    hn, hbuf, pk, pkp, pp, lt, pkt, gch, colb, sq, lsb, flip, tmpa, gpk, gps, gpr, g2b, gacc, gst,
    rk, r1a, r1b, r2a, r2b, rz, tab, tabk, tabr, fin,
    ag_send, ag_recv, px_send, px_recv, tb_sem, pk_send, pk_recv, ex_send, ex_recv,
    ls_send, ls_recv, rs_send, rs_recv, tab_send, tab_recv, fin_send, fin_recv, hb_sem, gh_sem,
):
    r = lax.axis_index("row")
    c = lax.axis_index("col")
    z, x, k = c // 4, (c // 2) % 2, c % 2
    half = tb.shape[1] // 2
    d_y = (1 - r, c)
    d_x = (r, z * 4 + (1 - x) * 2 + k)
    d_k = (r, z * 4 + x * 2 + 1 - k)

    def d_z(step):
        return (r, lax.rem(z + step, 4) * 4 + x * 2 + k)

    def remote(src, dst, send, recv, device):
        return pltpu.make_async_remote_copy(
            src_ref=src, dst_ref=dst, send_sem=send, recv_sem=recv,
            device_id=device, device_id_type=EYE,
        )

    def lanes(row):
        return pl.ds(pl.multiple_of(row * half, half), half)

    sq[...] = jnp.zeros_like(sq)
    barrier = pltpu.get_barrier_semaphore()

    def greet(n, _):
        other = lax.rem(r * 16 + c + n, 32)
        pl.semaphore_signal(barrier, inc=1, device_id=(other // 16, other % 16), device_id_type=EYE)
        return 0

    lax.fori_loop(1, 32, greet, 0)

    for n in range(UNITS):
        wg[z, x, k, UNIT * n : UNIT * (n + 1), lanes(r)] = blk_in[UNIT * n : UNIT * (n + 1)]
    tb[:, lanes(r)] = tab_in[...]
    hcopy = lambda n: pltpu.make_async_copy(
        head_in.at[:, pl.ds(pl.multiple_of(n * 256, 256), 256)], hbuf.at[n % 2], hb_sem.at[n % 2]
    )
    hcopy(0).start()
    pl.semaphore_wait(barrier, 31)

    def gather_moves(buf, part, both, send, recv):
        lo, hi = pl.ds(0, 2), pl.ds(2, 2)
        every = slice(None)
        other = lax.rem

        def move(index, out_region, in_region, device):
            out_ref = buf.at[out_region]
            in_ref = buf.at[in_region]
            return (
                remote(out_ref, out_ref, send.at[index], recv.at[index], device),
                remote(in_ref, in_ref, send.at[index], recv.at[index], device),
            )

        first = [
            move(n - 1, (z, x, k) + part(r), (lax.rem(z + 4 - n, 4), x, k) + part(r), d_z(n))
            for n in (1, 2, 3)
        ]
        second = [
            move(3, (lo, x, k) + part(r), (lo, 1 - x, k) + part(r), d_x),
            move(4, (hi, x, k) + part(r), (hi, x, k) + part(1 - r), d_y),
        ]
        pair_one = [move(5, (every, x, k) + part(r), (every, x, 1 - k) + part(r), d_k)]
        third = [
            move(6, (lo, every, k) + part(r), (lo, every, k) + part(1 - r), d_y),
            move(7, (hi, x, k) + both, (hi, 1 - x, k) + both, d_x),
        ]
        pair_two = [
            move(8, (lo, 1 - x, k) + part(r), (lo, 1 - x, 1 - k) + part(r), d_k),
            move(9, (hi, x, k) + part(1 - r), (hi, x, 1 - k) + part(1 - r), d_k),
        ]
        pair_three = [
            move(10, (lo, every, k) + part(1 - r), (lo, every, 1 - k) + part(1 - r), d_k),
            move(11, (hi, 1 - x, k) + both, (hi, 1 - x, 1 - k) + both, d_k),
        ]
        return first, second, pair_one, third, pair_two, pair_three

    def begin(moves):
        for out_copy, _ in moves:
            out_copy.start()

    def landed(moves):
        for _, in_copy in moves:
            in_copy.wait_recv()

    def sent(moves):
        for out_copy, _ in moves:
            out_copy.wait_send()

    def unit_rows(n):
        return pl.ds(pl.multiple_of(n * UNIT, UNIT), UNIT)

    def weight_moves(n):
        rows = unit_rows(n)
        return gather_moves(
            wg, lambda row: (rows, lanes(row)), (rows, slice(None)), ag_send.at[n], ag_recv.at[n]
        )

    def picked_moves(n):
        cut = lanes(n)
        return gather_moves(
            pk, lambda row: (pl.ds(pl.multiple_of(row * MSLOT, 16), MSLOT), cut),
            (slice(None), cut), pk_send.at[n], pk_recv.at[n],
        )

    def px_move(n):
        target = (n % 2, 8 * r + n // 2)
        slot = pl.ds(pl.multiple_of(c * UNIT, UNIT), UNIT)
        return target, remote(pix_in.at[n], px.at[slot], px_send.at[n], px_recv.at[c], target)

    def px_in(n):
        slot = pl.ds(pl.multiple_of(n * UNIT, UNIT), UNIT)
        return remote(px.at[slot], px.at[slot], px_send.at[n], px_recv.at[n], d_y)

    def px_start(n, _):
        target, copy = px_move(n)
        mine = jnp.logical_and(target[0] == r, target[1] == c)

        @pl.when(mine)
        def _():
            px[pl.ds(pl.multiple_of(c * UNIT, UNIT), UNIT), :] = pix_in[n]

        @pl.when(jnp.logical_not(mine))
        def _():
            copy.start()

        return 0

    def px_done(n, _):
        target, copy = px_move(n)

        @pl.when(jnp.logical_not(jnp.logical_and(target[0] == r, target[1] == c)))
        def _():
            copy.wait_send()

        @pl.when(jnp.logical_not(jnp.logical_and(n == c, r == c // 8)))
        def _():
            px_in(n).wait_recv()

        return 0

    cut_rows = TOK // 2
    own_cut = pl.ds(pl.multiple_of(k * cut_rows, 8), cut_rows)
    other_cut = pl.ds(pl.multiple_of((1 - k) * cut_rows, 8), cut_rows)

    def tb_copy(rows, row, index, device):
        ref = tb.at[rows, lanes(row)]
        return remote(ref, ref, tb_sem.at[index, 0], tb_sem.at[index, 1], device)

    token = lax.broadcasted_iota(jnp.int32, (TOK, 1), 0)
    slot_hit = lax.broadcasted_iota(jnp.int32, (TOK, MSLOT), 0) == places[pl.ds(r, 1), :]
    slot_on = lax.broadcasted_iota(jnp.int32, (TOK, MSLOT), 1) < counts[r]
    selector = jnp.where(slot_hit, 1.0, 0.0)
    masked = jnp.sum(jnp.where(slot_on, selector, 0.0), axis=1, keepdims=True) > 0.5
    opening = token == 0

    def gain(n):
        return tb[SEQ + 2 + 2 * n : SEQ + 3 + 2 * n, :]

    def shift(n):
        return tb[SEQ + 3 + 2 * n : SEQ + 4 + 2 * n, :]

    def square(n):
        return wg[:, :, :, unit_rows(n), :].reshape(16 * UNIT, 2 * half)

    def set_square(n, value):
        wg[:, :, :, unit_rows(n), :] = value.astype(low_type).reshape(4, 2, 2, UNIT, 2 * half)

    def triple():
        return wg[:, :, :, UNIT : 4 * UNIT, :].reshape(48 * UNIT, 2 * half)

    lane_low = lax.broadcasted_iota(jnp.int32, (1, 2 * HD), 1) < HD
    keep_low = jnp.where(lane_low, 1.0, 0.0)
    keep_high = 1.0 - keep_low

    def twice(values):
        return jnp.concatenate(
            [values * keep_low.astype(low_type), values * keep_high.astype(low_type)], axis=0
        )

    def once(values):
        return values[:TOK] * keep_low + values[TOK:] * keep_high

    def pair_lanes(part, p):
        return pl.ds(pl.multiple_of(part * HEADS * HD + p * 2 * HD, 2 * HD), 2 * HD)

    def pair_probs(p):
        query2 = twice(qkv[:, pair_lanes(0, p)])
        key2 = qkv[:, pair_lanes(1, p)]
        scores = nt(query2, key2) * (1.0 / math.sqrt(HD))
        valid = lax.broadcasted_iota(jnp.int32, (1, TOK), 1) < SEQ
        scores = jnp.where(valid, scores, -1e30)
        lifted = jnp.exp(scores - jnp.max(scores, axis=1, keepdims=True))
        return query2, key2, lifted * (1.0 / jnp.sum(lifted, axis=1, keepdims=True))

    def do_patch():
        tb_copy(own_cut, 1 - r, 0, d_y).wait_recv()
        tb_copy(own_cut, 1 - r, 1, d_k).start()
        lax.fori_loop(0, 16, px_done, 0)
        patch = tn(px[...], square(0))[:TOK]
        tb_copy(own_cut, r, 0, d_y).wait_send()
        tb_copy(other_cut, 1 - r, 1, d_k).wait_recv()
        tb_copy(own_cut, 1 - r, 1, d_k).wait_send()
        value = jnp.where(
            opening, tb[SEQ : SEQ + 1, :], jnp.where(masked, tb[SEQ + 1 : SEQ + 2, :], patch)
        )
        value = jnp.where(token < SEQ, value + tb[...], 0.0)
        st0[...] = value
        n1[...] = normed(value, gain(0), shift(0))[0].astype(low_type)

    def do_attention():
        qkv[...] = nt(n1[...], triple()).astype(low_type)

        def one_pair(p, _):
            _, _, probs = pair_probs(p)
            mixed = nn(probs.astype(low_type), qkv[:, pair_lanes(2, p)])
            mix[:, pair_lanes(0, p)] = once(mixed).astype(low_type)
            return 0

        lax.fori_loop(0, HEADS // 2, one_pair, 0)

    def do_output():
        value = st0[...] + nn(mix[...], square(4))
        st1[...] = value
        st2[...] = value
        n2[...] = normed(value, gain(1), shift(1))[0].astype(low_type)

    def do_up(j):
        value = nt(n2[...], square(5 + j))
        hpre[j] = value
        phi_total, _ = gelu_parts(value)
        hact[j] = (value * phi_total).astype(low_type)

    def do_down(j):
        st2[...] += nn(hact[j], square(9 + j))

    begin(weight_moves(0)[0])
    lax.fori_loop(0, 16, px_start, 0)
    tb_copy(own_cut, r, 0, d_y).start()

    def tick(t, _):
        @pl.when(jnp.logical_and(t >= 1, t < UNITS))
        def _():
            begin(weight_moves(t)[0])

        @pl.when(jnp.logical_and(t >= 2, t < UNITS + 2))
        def _():
            first, second, pair_one, _, _, _ = weight_moves(t - 2)
            landed(first)
            begin(second)
            begin(pair_one)

        @pl.when(jnp.logical_and(t >= 3, t < UNITS + 3))
        def _():
            _, second, _, third, pair_two, _ = weight_moves(t - 3)
            landed(second)
            begin(third)
            begin(pair_two)

        @pl.when(jnp.logical_and(t >= 5, t < UNITS + 5))
        def _():
            _, _, _, third, _, pair_three = weight_moves(t - 5)
            landed(third)
            begin(pair_three)

        @pl.when(t >= 6)
        def _():
            _, _, pair_one, _, pair_two, pair_three = weight_moves(t - 6)
            landed(pair_one)
            landed(pair_two)
            landed(pair_three)

        @pl.when(t < 2 * BANDS)
        def _():
            @pl.when(t + 1 < 2 * BANDS)
            def _():
                hcopy(t + 1).start()

            hcopy(t).wait()
            hn[:, pl.ds(pl.multiple_of(t * 256, 256), 256)] = hbuf[t % 2].astype(low_type)

        @pl.when(t == 6)
        def _():
            do_patch()

        @pl.when(t == 9)
        def _():
            do_attention()

        @pl.when(t == 10)
        def _():
            do_output()

        @pl.when(jnp.logical_and(t >= 11, t < 15))
        def _():
            do_up(t - 11)

        @pl.when(t >= 15)
        def _():
            do_down(t - 15)

        return 0

    lax.fori_loop(0, UNITS + 6, tick, 0)

    def all_sent(n, _):
        for moves in weight_moves(n):
            sent(moves)
        return 0

    final_out, _, _ = normed(st2[...], gain(2), shift(2))
    picked = tn(selector.astype(low_type), final_out.astype(low_type)).astype(low_type)
    own_rows = pl.ds(pl.multiple_of(r * MSLOT, 16), MSLOT)
    other_rows = pl.ds(pl.multiple_of((1 - r) * MSLOT, 16), MSLOT)
    pp[own_rows, :] = picked
    pk[z, x, k, own_rows, :] = picked

    def swap(index, src, dst, device):
        return remote(src, dst, ex_send.at[index], ex_recv.at[index], device)

    swap_picked = swap(0, pp.at[own_rows, :], pkp, d_y)
    swap_picked.start()
    for n in range(2):
        begin(picked_moves(n)[0])
    lax.fori_loop(0, UNITS, all_sent, 0)
    info = jnp.transpose(info_in[...])
    target_col = info[: 2 * MSLOT, 1:2]
    weight_col = info[: 2 * MSLOT, 2:3]
    base = (r * (BANDS * 512)).astype(wide)
    band_lane = lax.broadcasted_iota(jnp.int32, (1, 512), 1).astype(wide)

    def band(v):
        return pl.ds(pl.multiple_of(v * 512, 512), 512)

    def band_hit(v, column):
        return (band_lane + (base + (v * 512).astype(wide))) == column

    swap_picked.wait()
    pp[other_rows, :] = pkp[...]

    def picked_second(n):
        first, second, pair_one, _, _, _ = picked_moves(n)
        landed(first)
        begin(second)
        begin(pair_one)

    def picked_third(n):
        _, second, _, third, pair_two, _ = picked_moves(n)
        landed(second)
        begin(third)
        begin(pair_two)

    def picked_last(n):
        _, _, _, third, _, pair_three = picked_moves(n)
        landed(third)
        begin(pair_three)

    def picked_done(n):
        _, _, pair_one, _, pair_two, pair_three = picked_moves(n)
        landed(pair_one)
        landed(pair_two)
        landed(pair_three)

    def logits_band(v, carry):
        top, chosen = carry
        value = nn(pp[...], hn[:, band(v)])
        lt[v] = value
        chosen += jnp.sum(jnp.where(band_hit(v, target_col), value, 0.0), axis=1, keepdims=True)
        return jnp.maximum(top, jnp.max(value, axis=1, keepdims=True)), chosen

    zero_col = jnp.zeros((2 * MSLOT, 1), wide)
    top, chosen = lax.fori_loop(0, BANDS, logits_band, (zero_col - 1e30, zero_col))
    picked_second(0)

    def sum_band(v, total):
        return total + jnp.sum(jnp.exp(lt[v] - top), axis=1, keepdims=True)

    total = lax.fori_loop(0, BANDS, sum_band, zero_col)
    column = lax.broadcasted_iota(jnp.int32, (1, 128), 1)
    tmpa[...] = jnp.zeros_like(tmpa)
    tmpa[0 : 2 * MSLOT, :] = jnp.where(column == 0, top, jnp.where(column == 1, total, 0.0))
    sq[0] = jnp.transpose(tmpa[...])[:8]
    swap_lse = swap(1, sq.at[0], sq.at[1], d_y)
    swap_lse.start()
    picked_second(1)
    picked_third(0)
    swap_lse.wait()
    flip[...] = jnp.zeros_like(flip)
    flip[0:8, :] = sq[1]
    theirs = jnp.transpose(flip[...])[: 2 * MSLOT]
    their_top, their_total = theirs[:, 0:1], theirs[:, 1:2]
    best = jnp.maximum(top, their_top)
    log_total = best + jnp.log(total * jnp.exp(top - best) + their_total * jnp.exp(their_top - best))

    tmpa[0 : 2 * MSLOT, :] = jnp.where(
        column == 0, log_total, jnp.where(column == 1, target_col, jnp.where(column == 2, weight_col, 0.0))
    )
    lsb[c] = jnp.transpose(tmpa[...])[:8]

    def ls_copy(n):
        other = lax.rem(c + n, 16)
        return remote(lsb.at[c], lsb.at[c], ls_send.at[n], ls_recv.at[n], (r, other))

    def ls_in(n):
        other = lax.rem(c + 16 - n, 16)
        return remote(lsb.at[other], lsb.at[other], ls_send.at[n], ls_recv.at[n], (r, other))

    def ls_start(n, _):
        ls_copy(n).start()
        return 0

    def ls_done(n, _):
        ls_copy(n).wait_send()
        ls_in(n).wait_recv()
        return 0

    lax.fori_loop(1, 16, ls_start, 0)
    gpk[...] = jnp.zeros_like(gpk)

    def grad_band(v, _):
        value = jnp.exp(lt[v] - log_total) - jnp.where(band_hit(v, target_col), 1.0, 0.0)
        gpk[...] += nt((value * weight_col).astype(low_type), hn[:, band(v)])
        return 0

    lax.fori_loop(0, BANDS, grad_band, 0)
    gps[...] = gpk[other_rows, :].astype(low_type)
    swap_grad = swap(2, gps, gpr, d_y)
    swap_grad.start()
    picked_third(1)
    picked_last(0)
    leader = jnp.where(r == 0, 1.0, 0.0)
    loss_part = jnp.sum((log_total * leader - chosen) * weight_col, axis=0, keepdims=True)
    swap_grad.wait()
    grad_picked = (gpk[own_rows, :] + gpr[...].astype(wide)).astype(low_type)
    grad_final = nn(selector.astype(low_type), grad_picked)
    _, scaled, inverse = normed(st2[...], gain(2), shift(2))
    grad_last, grad_gain, grad_shift = normed_back(grad_final, scaled, inverse, gain(2))
    st2[...] = grad_last
    g2b[...] = grad_last.astype(low_type)
    gst[4:5, :] = grad_gain
    gst[5:6, :] = grad_shift
    gacc[...] = jnp.zeros_like(gacc)
    picked_last(1)

    def pair_region(n):
        return rk.at[lax.rem(n, 4)]

    def rs_copy(n, index, src, dst, device):
        return remote(src, dst, rs_send.at[n, index], rs_recv.at[n, index], device)

    lo, hi = pl.ds(0, 2), pl.ds(2, 2)

    def sums_moves(n):
        rows = unit_rows(UNITS - 1 - n)
        zero = [rs_copy(n, 0, wg.at[:, :, 1 - k, rows, :], rk.at[lax.rem(n, 4)], d_k)]
        one = [
            rs_copy(n, 1, wg.at[lo, :, k, rows, lanes(1 - r)], r1a.at[lax.rem(n, 7)], d_y),
            rs_copy(n, 2, wg.at[hi, 1 - x, k, rows, :], r1b.at[lax.rem(n, 7)], d_x),
        ]
        two = [
            rs_copy(n, 3, wg.at[lo, 1 - x, k, rows, lanes(r)], r2a.at[lax.rem(n, 7)], d_x),
            rs_copy(n, 4, wg.at[hi, x, k, rows, lanes(1 - r)], r2b.at[lax.rem(n, 7)], d_y),
        ]
        three = [
            rs_copy(n, 4 + m, wg.at[lax.rem(z + m, 4), x, k, rows, lanes(r)], rz.at[lax.rem(n, 7), m - 1], d_z(m))
            for m in (1, 2, 3)
        ]
        return zero, one, two, three

    def sum_start(copies):
        for copy in copies:
            copy.start()

    def sum_land(copies):
        for copy in copies:
            copy.wait_recv()

    def fold(region, value):
        wg[region] = (wg[region].astype(wide) + value.astype(wide)).astype(low_type)

    def sums_one(n):
        rows = unit_rows(UNITS - 1 - n)
        zero, one, _, _ = sums_moves(n)
        sum_land(zero)
        fold((slice(None), slice(None), k, rows, slice(None)), rk[lax.rem(n, 4)])
        sum_start(one)

    def sums_two(n):
        rows = unit_rows(UNITS - 1 - n)
        _, one, two, _ = sums_moves(n)
        sum_land(one)
        fold((lo, slice(None), k, rows, lanes(r)), r1a[lax.rem(n, 7)])
        fold((hi, x, k, rows, slice(None)), r1b[lax.rem(n, 7)])
        sum_start(two)

    def sums_three(n):
        rows = unit_rows(UNITS - 1 - n)
        _, _, two, three = sums_moves(n)
        sum_land(two)
        fold((lo, x, k, rows, lanes(r)), r2a[lax.rem(n, 7)])
        fold((hi, x, k, rows, lanes(r)), r2b[lax.rem(n, 7)])
        sum_start(three)

    def sums_four(n):
        rows = unit_rows(UNITS - 1 - n)
        _, _, _, three = sums_moves(n)
        sum_land(three)
        value = wg[z, x, k, rows, lanes(r)].astype(wide)
        for m in range(3):
            value = value + rz[lax.rem(n, 7), m].astype(wide)
        gout[rows, :] = value
        sq[2, 0:1, 0:128] += jnp.sum(jnp.sum(value * value, axis=0, keepdims=True), axis=1, keepdims=True)

    def sums_sent(n, _):
        for moves in sums_moves(n):
            sent([(copy, None) for copy in moves])
        return 0

    def back_down(j):
        grad_act = nt(g2b[...], square(9 + j))
        value = hpre[j]
        phi_total, density = gelu_parts(value)
        grad_pre = (grad_act * (phi_total + value * density)).astype(low_type)
        set_square(9 + j, tn(hact[j], g2b[...]))
        hact[j] = grad_pre

    def back_up(j):
        gacc[...] += nn(hact[j], square(5 + j))
        set_square(5 + j, tn(hact[j], n2[...]))

    def back_output():
        _, scaled, inverse = normed(st1[...], gain(1), shift(1))
        down, grad_gain, grad_shift = normed_back(gacc[...], scaled, inverse, gain(1))
        gst[2:3, :] = grad_gain
        gst[3:4, :] = grad_shift
        down = down + st2[...]
        st2[...] = down
        g2b[...] = down.astype(low_type)
        grad_mix = nt(g2b[...], square(4)).astype(low_type)
        set_square(4, tn(mix[...], g2b[...]))
        mix[...] = grad_mix

    def back_attention():
        def one_pair(p, _):
            query2, key2, probs = pair_probs(p)
            value2 = qkv[:, pair_lanes(2, p)]
            upstream = twice(mix[:, pair_lanes(0, p)])
            grad_probs = nt(upstream, value2)
            centered = grad_probs - jnp.sum(probs * grad_probs, axis=1, keepdims=True)
            grad_scores = (probs * centered).astype(low_type)
            scale = 1.0 / math.sqrt(HD)
            grad_query = once(nn(grad_scores, key2)) * scale
            grad_key = tn(grad_scores, query2) * scale
            grad_value = tn(probs.astype(low_type), upstream)
            qkv[:, pair_lanes(0, p)] = grad_query.astype(low_type)
            qkv[:, pair_lanes(1, p)] = grad_key.astype(low_type)
            qkv[:, pair_lanes(2, p)] = grad_value.astype(low_type)
            return 0

        lax.fori_loop(0, HEADS // 2, one_pair, 0)
        gacc[...] = nn(qkv[...], triple())
        wg[:, :, :, UNIT : 4 * UNIT, :] = (
            tn(qkv[...], n1[...]).astype(low_type).reshape(4, 2, 2, 3 * UNIT, 2 * half)
        )

    def back_patch():
        _, scaled, inverse = normed(st0[...], gain(0), shift(0))
        down, grad_gain, grad_shift = normed_back(gacc[...], scaled, inverse, gain(0))
        grad = down + st2[...]
        grad_patch = jnp.where(jnp.logical_or(opening, masked), 0.0, grad).astype(low_type)
        set_square(0, nn(px[:, 0:TOK], grad_patch))
        lines = [
            grad[0:1],
            jnp.sum(jnp.where(masked, grad, 0.0), axis=0, keepdims=True),
            grad_gain, grad_shift, gst[2:3, :], gst[3:4, :], gst[4:5, :], gst[5:6, :],
        ]
        for n, line in enumerate(lines):
            grad = jnp.where(token == SEQ + n, line, grad)
        tab[0:TOK, :] = grad.astype(low_type)
        tab[TOK:, :] = jnp.zeros((tab.shape[0] - TOK, tab.shape[1]), low_type)

    tab_half = tab.shape[0] // 2
    rows_own = pl.ds(pl.multiple_of(k * tab_half, 16), tab_half)
    rows_other = pl.ds(pl.multiple_of((1 - k) * tab_half, 16), tab_half)
    d_z1 = (r, (z + 1 - 2 * (z % 2)) * 4 + x * 2 + k)
    d_z2 = (r, lax.rem(z + 2, 4) * 4 + x * 2 + k)
    own_part = tab.at[rows_own, lanes(r)]
    tab_moves = [
        remote(tab.at[rows_other, :], tabk, tab_send.at[0], tab_recv.at[0], d_k),
        remote(tab.at[rows_own, lanes(1 - r)], tabr.at[0], tab_send.at[1], tab_recv.at[1], d_y),
        remote(own_part, tabr.at[1], tab_send.at[2], tab_recv.at[2], d_x),
        remote(own_part, tabr.at[2], tab_send.at[3], tab_recv.at[3], d_z1),
        remote(own_part, tabr.at[3], tab_send.at[4], tab_recv.at[4], d_z2),
        remote(own_part, tabr.at[4], tab_send.at[5], tab_recv.at[5], d_k),
    ]

    def tab_step(n):
        tab_moves[n].wait()
        if n == 0:
            tab[rows_own, :] = (
                tab[rows_own, :].astype(wide) + tabk[...].astype(wide)
            ).astype(low_type)
        elif n < 5:
            tab[rows_own, lanes(r)] = (
                tab[rows_own, lanes(r)].astype(wide) + tabr[n - 1].astype(wide)
            ).astype(low_type)
        if n < 5:
            tab_moves[n + 1].start()

    def gh_copy(v):
        return pltpu.make_async_copy(hn.at[:, band(v)], ghead.at[:, band(v)], gh_sem.at[v])

    def head_band(v):
        def rows_block(n, _):
            at = pl.ds(pl.multiple_of(n * 4 * MSLOT, 16), 4 * MSLOT)
            value = nn(pk[n // 2, n % 2].reshape(4 * MSLOT, 2 * half), hn[:, band(v)])
            cols = colb[at, :]
            hit = jnp.where(band_hit(v, cols[:, 1:2]), 1.0, 0.0)
            gch[at, :] = ((jnp.exp(value - cols[:, 0:1]) - hit) * cols[:, 2:3]).astype(low_type)
            return 0

        lax.fori_loop(0, 8, rows_block, 0)
        value = nn(pkt[...], gch[...])
        sq[3, 0:1, 0:128] += jnp.sum(jnp.sum(value * value, axis=0, keepdims=True), axis=1, keepdims=True)
        hn[:, band(v)] = value.astype(low_type)
        gh_copy(v).start()

    def head_ready():
        for n in range(2):
            picked_done(n)
        lax.fori_loop(1, 16, ls_done, 0)

        def to_columns(n, _):
            flip[0:8, :] = lsb[n]
            colb[pl.ds(pl.multiple_of(n * 2 * MSLOT, 16), 2 * MSLOT), :] = jnp.transpose(flip[...])[: 2 * MSLOT]
            return 0

        lax.fori_loop(0, 16, to_columns, 0)

        def turn(n, _):
            rows = pk[n].reshape(8 * MSLOT, 2 * half)
            pkt[:, pl.ds(pl.multiple_of(n * 8 * MSLOT, 128), 8 * MSLOT)] = jnp.transpose(rows)
            return 0

        lax.fori_loop(0, 4, turn, 0)

    def back_step(s, _):
        @pl.when(s < 4)
        def _():
            back_down(3 - s)

        @pl.when(jnp.logical_and(s >= 4, s < 8))
        def _():
            back_up(7 - s)

        @pl.when(s == 8)
        def _():
            back_output()

        @pl.when(s == 9)
        def _():
            back_attention()

        @pl.when(s == 12)
        def _():
            back_patch()
            tab_moves[0].start()

        @pl.when(s < UNITS)
        def _():
            sum_start(sums_moves(s)[0])

        @pl.when(jnp.logical_and(s >= 1, s < UNITS + 1))
        def _():
            sums_one(s - 1)

        @pl.when(jnp.logical_and(s >= 3, s < UNITS + 3))
        def _():
            sums_two(s - 3)

        @pl.when(jnp.logical_and(s >= 5, s < UNITS + 5))
        def _():
            sums_three(s - 5)

        @pl.when(s >= 7)
        def _():
            sums_four(s - 7)

        for n in range(6):
            @pl.when(s == 13 + n)
            def _():
                tab_step(n)

        @pl.when(s == 2)
        def _():
            head_ready()

        @pl.when(jnp.logical_and(s >= 3, s < 7))
        def _():
            head_band(s - 3)

        @pl.when(jnp.logical_and(s >= 10, s < 12))
        def _():
            head_band(s - 6)

        @pl.when(jnp.logical_and(s >= 13, s < 15))
        def _():
            head_band(s - 7)

        return 0

    lax.fori_loop(0, UNITS + 7, back_step, 0)
    gtab_out[rows_own, :] = tab[rows_own, lanes(r)].astype(wide)
    gtab_out[rows_other, :] = tabr[4].astype(wide)
    value = gtab_out[...]
    first_col = jnp.where(c == 0, 1.0, 0.0)
    table_squares = jnp.sum(jnp.sum(value * value, axis=0, keepdims=True), axis=1, keepdims=True)
    line = lax.broadcasted_iota(jnp.int32, (8, 128), 0)
    squares = sq[2, 0:1, 0:128] + (sq[3, 0:1, 0:128] + table_squares) * first_col
    count = (counts[0] + counts[1]).astype(wide) * leader
    fin[r * 16 + c] = jnp.where(
        line == 0, loss_part, jnp.where(line == 1, count, jnp.where(line == 2, squares, 0.0))
    )

    def fin_copy(n, step):
        other = lax.rem(r * 16 + c + step, 32)
        owner = r * 16 + c if n == 0 else lax.rem(r * 16 + c + 32 - step, 32)
        ref = fin.at[owner]
        return remote(ref, ref, fin_send.at[step], fin_recv.at[step], (other // 16, other % 16))

    def fin_start(step, _):
        fin_copy(0, step).start()
        return 0

    def fin_done(step, _):
        fin_copy(0, step).wait_send()
        fin_copy(1, step).wait_recv()
        return 0

    lax.fori_loop(1, 32, fin_start, 0)
    lax.fori_loop(0, UNITS, sums_sent, 0)
    for n in range(2):
        for moves in picked_moves(n):
            sent(moves)
    for v in range(BANDS):
        gh_copy(v).wait()
    lax.fori_loop(1, 32, fin_done, 0)
    scal_out[...] = jnp.sum(fin[...], axis=0)


def step_call(pix, blk, tab, places, info, counts, head):
    half = tab.shape[1]
    full = 2 * half
    vocab = head.shape[1]
    slots = 32 * MSLOT
    vm = pltpu.VMEM
    dma = pltpu.SemaphoreType.DMA
    f32, b16 = wide, low_type
    scratch = [
        vm((4, 2, 2, UNITS * UNIT, full), b16),
        vm((16 * UNIT, 256), b16),
        vm((TOK, full), f32),
        vm((TOK, full), f32), vm((TOK, full), f32), vm((TOK, full), f32),
        vm((TOK, full), b16), vm((TOK, full), b16), vm((TOK, full), b16),
        vm((TOK, 3 * full), b16),
        vm((4, TOK, full), f32),
        vm((4, TOK, full), b16),
        vm((full, vocab), b16),
        vm((2, full, 256), f32),
        vm((4, 2, 2, 2 * MSLOT, full), b16),
        vm((MSLOT, full), b16),
        vm((2 * MSLOT, full), b16),
        vm((BANDS, 2 * MSLOT, 512), f32),
        vm((full, slots), b16),
        vm((slots, 512), b16),
        vm((slots, 128), f32),
        vm((4, 8, 256), f32),
        vm((16, 8, 256), f32),
        vm((128, 256), f32),
        vm((256, 128), f32),
        vm((2 * MSLOT, full), f32),
        vm((MSLOT, full), b16), vm((MSLOT, full), b16),
        vm((TOK, full), b16),
        vm((TOK, full), f32),
        vm((8, full), f32),
        vm((4, 4, 2, UNIT, full), b16),
        vm((7, 2, 2, UNIT, half), b16),
        vm((7, 2, UNIT, full), b16),
        vm((7, 2, UNIT, half), b16),
        vm((7, 2, UNIT, half), b16),
        vm((7, 3, UNIT, half), b16),
        vm((224, full), b16),
        vm((112, full), b16),
        vm((5, 112, half), b16),
        vm((32, 8, 128), f32),
        dma((UNITS, 12)), dma((UNITS, 12)),
        dma((16,)), dma((16,)),
        dma((2, 2)),
        dma((2, 12)), dma((2, 12)),
        dma((3,)), dma((3,)),
        dma((16,)), dma((16,)),
        dma((UNITS, 8)), dma((UNITS, 8)),
        dma((6,)), dma((6,)),
        dma((32,)), dma((32,)),
        dma((2,)),
        dma((BANDS,)),
    ]
    in_vmem = pl.BlockSpec(memory_space=pltpu.VMEM)
    return pl.pallas_call(
        step_kernel,
        out_shape=(
            jax.ShapeDtypeStruct((UNITS * UNIT, half), f32),
            jax.ShapeDtypeStruct((224, half), f32),
            jax.ShapeDtypeStruct((full, vocab), b16),
            jax.ShapeDtypeStruct((8, 128), f32),
        ),
        in_specs=[
            in_vmem, in_vmem, in_vmem, in_vmem, in_vmem,
            pl.BlockSpec(memory_space=pltpu.SMEM),
            pl.BlockSpec(memory_space=pl.ANY),
        ],
        out_specs=(in_vmem, in_vmem, pl.BlockSpec(memory_space=pl.ANY), in_vmem),
        scratch_shapes=scratch,
        compiler_params=pltpu.CompilerParams(
            collective_id=0, has_side_effects=True, vmem_limit_bytes=VMEM_LIMIT
        ),
        cost_estimate=pl.CostEstimate(flops=50_000_000_000, bytes_accessed=40_000_000, transcendentals=0),
    )(pix, blk, tab, places, info, counts, head)


def block_path(
    pixels, mask_places, mask_count, targets, step_count,
    patch_weight, vector_table, input_weight, output_weight, upward_weight, downward_weight, head_weight,
    *moments,
):
    part = pixels.shape[1]
    images = pixels.shape[0] // SEQ
    pix = jnp.transpose(pixels.reshape(images, SEQ, part), (0, 2, 1))
    pix = jnp.pad(pix, ((0, 0), (0, 0), (0, 256 - SEQ)))
    up = upward_weight[0].astype(low_type).T
    blk = jnp.concatenate(
        [
            patch_weight.astype(low_type),
            input_weight[0].astype(low_type).T,
            output_weight[0].astype(low_type),
            up,
            downward_weight[0].astype(low_type),
        ],
        axis=0,
    )
    tab = jnp.pad(vector_table, ((0, TOK - vector_table.shape[0]), (0, 0)))
    counted = jnp.arange(MSLOT, dtype=jnp.int32)[None, :] < mask_count[:, None]
    rows = jnp.stack(
        [jnp.zeros((2 * MSLOT,), wide), targets.reshape(-1).astype(wide), counted.reshape(-1).astype(wide)]
    )
    info = jnp.pad(rows, ((0, 125), (0, 256 - 2 * MSLOT)))
    gout, gtab, ghead, scal = step_call(pix, blk, tab, mask_places, info, mask_count, head_weight)
    loss_total, count_total, squares_total = scal[0, 0], scal[1, 0], scal[2, 0]
    mean_loss = loss_total / count_total
    grad_norm = jnp.sqrt(squares_total) / count_total
    factor = jnp.minimum(1.0, clip_limit / grad_norm) / count_total
    step_value = step_count[0].astype(wide)
    starts = [0, 1, 4, 5, 9, 13]
    pieces = [gout[UNIT * starts[n] : UNIT * starts[n + 1]] for n in range(5)]
    grads = [
        pieces[0], gtab[: vector_table.shape[0]], pieces[1].T[None], pieces[2][None],
        pieces[3].T[None], pieces[4][None], ghead.astype(wide),
    ]
    weights = [
        patch_weight, vector_table, input_weight, output_weight, upward_weight, downward_weight, head_weight,
    ]
    results = []
    for n in range(7):
        results.extend(adam_step(weights[n], grads[n], moments[n], moments[7 + n], factor, step_value))
    return (mean_loss, grad_norm, *results)


def solution(mesh):
    state = (
        P("col", "row"),
        P(None, "row"),
        P(None, "row", "col"),
        P(None, "col", "row"),
        P(None, "row", "col"),
        P(None, "col", "row"),
        P(None, "row"),
    )
    data = (P("row", "col"), P("col", None), P("col"), P("col", None), P())
    outs = (P(), P()) + tuple(spec for spec in state for _ in range(3))
    fits = dict(mesh.shape) == {"row": 2, "col": 16}
    return jax.shard_map(
        block_path if fits else on_device,
        mesh=mesh,
        in_specs=data + state * 3,
        out_specs=outs,
        check_vma=False,
    )
```

```python
import math

import jax
import jax.numpy as jnp
from jax import lax
from jax.experimental import pallas as pl
from jax.experimental.pallas import tpu as pltpu
from jax.sharding import PartitionSpec as P

HEADS = 12
HD = 64
SEQ = 197
MSLOT = 80
BOTH = ("row", "col")

norm_eps = 1e-06
clip_limit = 0.1
learn_rate = 0.01
beta_first = 0.9
beta_second = 0.999
adam_eps = 1e-08
weight_decay = 0.05
low_type = jnp.bfloat16
wide = jnp.float32


def product(left, right):
    return jnp.dot(left, right, preferred_element_type=wide)


def product_nt(left, right):
    return jnp.einsum("ab,cb->ac", left, right, preferred_element_type=wide)


def product_tn(left, right):
    return jnp.einsum("ab,ac->bc", left, right, preferred_element_type=wide)


def norm_forward(values, gain, shift):
    center = jnp.mean(values, axis=1, keepdims=True)
    moved = values - center
    inverse = lax.rsqrt(jnp.mean(moved * moved, axis=1, keepdims=True) + norm_eps)
    scaled = moved * inverse
    return scaled * gain + shift, (scaled, inverse)


def norm_backward(upstream, kept, gain):
    scaled, inverse = kept
    inner = upstream * gain
    downstream = inverse * (
        inner
        - jnp.mean(inner, axis=1, keepdims=True)
        - scaled * jnp.mean(inner * scaled, axis=1, keepdims=True)
    )
    return downstream, jnp.sum(upstream * scaled, axis=0), jnp.sum(upstream, axis=0)


def exact_gelu(values):
    return jax.nn.gelu(values, approximate=False)


def split_heads(grouped):
    images = grouped.shape[0] // SEQ
    pieces = grouped.reshape(images, SEQ, 3, HEADS, HD)
    return pieces[:, :, 0], pieces[:, :, 1], pieces[:, :, 2]


def attention_weights(query, keys):
    scores = jnp.einsum("iqhd,ikhd->ihqk", query, keys, preferred_element_type=wide)
    return jax.nn.softmax(scores * (1.0 / math.sqrt(HD)), axis=-1)


def attend(grouped):
    query, keys, values = split_heads(grouped)
    weights_full = attention_weights(query, keys)
    mixture = jnp.einsum(
        "ihqk,ikhd->iqhd", weights_full.astype(low_type), values, preferred_element_type=wide
    )
    return mixture.reshape(grouped.shape[0], HEADS * HD), weights_full


def attend_back(grouped, weights_full, grad_mixture):
    query, keys, values = split_heads(grouped)
    images = query.shape[0]
    weights_low = weights_full.astype(low_type)
    grad_out = grad_mixture.reshape(images, SEQ, HEADS, HD)
    grad_weights = jnp.einsum("iqhd,ikhd->ihqk", grad_out, values, preferred_element_type=wide)
    grad_values = jnp.einsum("ihqk,iqhd->ikhd", weights_low, grad_out, preferred_element_type=wide)
    centered = grad_weights - jnp.sum(weights_full * grad_weights, axis=-1, keepdims=True)
    grad_scores = (weights_full * centered).astype(low_type)
    scale = 1.0 / math.sqrt(HD)
    grad_query = jnp.einsum("ihqk,ikhd->iqhd", grad_scores, keys, preferred_element_type=wide)
    grad_keys = jnp.einsum("ihqk,iqhd->ikhd", grad_scores, query, preferred_element_type=wide)
    stacked = jnp.stack([grad_query * scale, grad_keys * scale, grad_values], axis=2)
    return stacked.reshape(images * SEQ, 3 * HEADS * HD)


def adam_step(weight, grad, drift, power, factor, step_value):
    scaled = grad * factor
    new_drift = beta_first * drift + (1.0 - beta_first) * scaled
    new_power = beta_second * power + (1.0 - beta_second) * scaled * scaled
    drift_hat = new_drift / (1.0 - jnp.power(beta_first, step_value))
    power_hat = new_power / (1.0 - jnp.power(beta_second, step_value))
    update = -learn_rate * (drift_hat / (jnp.sqrt(power_hat) + adam_eps) + weight_decay * weight)
    return (update, new_drift, new_power)


def on_device(
    pixels,
    mask_places,
    mask_count,
    targets,
    step_count,
    patch_weight,
    vector_table,
    input_weight,
    output_weight,
    upward_weight,
    downward_weight,
    head_weight,
    drift_patch,
    drift_table,
    drift_input,
    drift_output,
    drift_upward,
    drift_downward,
    drift_head,
    power_patch,
    power_table,
    power_input,
    power_output,
    power_upward,
    power_downward,
    power_head,
):
    rows, cols = lax.axis_size("row"), lax.axis_size("col")
    row_index = lax.axis_index("row")
    col_index = lax.axis_index("col")
    images = mask_places.shape[0] // rows
    width = vector_table.shape[1] * rows

    blocks = [
        patch_weight.astype(low_type),
        input_weight[0].astype(low_type).T,
        output_weight[0].astype(low_type),
        upward_weight[0].astype(low_type).T,
        downward_weight[0].astype(low_type),
    ]
    heights = [block.shape[0] for block in blocks]
    gathered = lax.all_gather(jnp.concatenate(blocks, axis=0), BOTH, axis=0, tiled=False)
    gathered = gathered.reshape(rows, cols, sum(heights), -1)

    def whole(index):
        start = sum(heights[:index])
        part = gathered[:, :, start : start + heights[index]]
        return jnp.transpose(part, (1, 2, 0, 3)).reshape(cols * heights[index], width)

    patch_low, input_turned, output_low, upward_turned, downward_low = map(whole, range(5))
    table = lax.all_gather(vector_table, "row", axis=1, tiled=True)

    local_images = pixels.shape[0] // SEQ
    part = pixels.shape[1]
    grid = pixels.reshape(local_images // (rows * images), rows, images, SEQ, part)
    grid = lax.all_to_all(grid, "row", split_axis=1, concat_axis=0, tiled=True)
    grid = grid.reshape(cols, images * SEQ, part)
    grid = lax.all_to_all(grid, "col", split_axis=0, concat_axis=0, tiled=True)
    pixel_own = jnp.transpose(grid, (1, 0, 2)).reshape(images * SEQ, cols * part)

    def own(values):
        return lax.dynamic_slice_in_dim(values, row_index * images, images, axis=0)

    places_own, count_own = own(mask_places), own(mask_count)

    def gains_of(norm_index):
        return (table[SEQ + 2 + 2 * norm_index], table[SEQ + 3 + 2 * norm_index])

    patch_proj = product(pixel_own, patch_low)
    places = jnp.arange(SEQ, dtype=jnp.int32)
    counted_own = jnp.arange(MSLOT, dtype=jnp.int32)[None, :] < count_own[:, None]
    matches = places_own[:, :, None] == places[None, None, :]
    masked = jnp.any(matches & counted_own[:, :, None], axis=1)[:, :, None]
    opening = (places == 0)[None, :, None]
    stream = jnp.where(
        opening,
        table[SEQ],
        jnp.where(masked, table[SEQ + 1], patch_proj.reshape(images, SEQ, -1)),
    )
    stream = (stream + table[:SEQ][None]).reshape(images * SEQ, -1)
    gain_one, shift_one = gains_of(0)
    gain_two, shift_two = gains_of(1)
    final_gain, final_shift = gains_of(2)
    normed_one, stats_one = norm_forward(stream, gain_one, shift_one)
    normed_one = normed_one.astype(low_type)
    grouped = product_nt(normed_one, input_turned).astype(low_type)
    mixture, weights_full = attend(grouped)
    mixture = mixture.astype(low_type)
    stream_mid = stream + product(mixture, output_low)
    normed_two, stats_two = norm_forward(stream_mid, gain_two, shift_two)
    normed_two = normed_two.astype(low_type)
    hidden_pre = product_nt(normed_two, upward_turned)
    hidden_act = exact_gelu(hidden_pre).astype(low_type)
    stream_last = stream_mid + product(hidden_act, downward_low)
    final_out, final_stats = norm_forward(stream_last, final_gain, final_shift)
    selector = matches.astype(low_type)
    picked = jnp.einsum(
        "ims,isd->imd", selector, final_out.astype(low_type).reshape(images, SEQ, -1),
        preferred_element_type=wide,
    ).astype(low_type)

    picked_wide = lax.all_gather(picked.reshape(images * MSLOT, -1), "row", axis=0, tiled=True)
    head_low = head_weight.astype(low_type)
    logits = product(picked_wide, head_low)
    vocab_local = head_weight.shape[1]
    target_local = targets.reshape(-1) - row_index * vocab_local
    target_hits = target_local[:, None] == jnp.arange(vocab_local, dtype=jnp.int32)[None, :]
    chosen = jnp.sum(jnp.where(target_hits, logits, 0.0), axis=1)
    local_top = jnp.max(logits, axis=1)
    local_sum = jnp.sum(jnp.exp(logits - local_top[:, None]), axis=1)
    pair = lax.all_gather(jnp.stack([local_top, local_sum]), "row", axis=0, tiled=False)
    top_value = jnp.max(pair[:, 0], axis=0)
    exp_total = jnp.sum(pair[:, 1] * jnp.exp(pair[:, 0] - top_value), axis=0)
    log_total = top_value + jnp.log(exp_total)
    counted = jnp.arange(MSLOT, dtype=jnp.int32)[None, :] < mask_count[:, None]
    slot_weight = counted.reshape(-1).astype(wide)
    leader_row = (row_index == 0).astype(wide)
    loss_part = jnp.sum(log_total * slot_weight) * leader_row - jnp.sum(chosen * slot_weight)
    count_part = jnp.sum(mask_count.astype(wide)) * leader_row
    grad_logits = (
        (jnp.exp(logits - log_total[:, None]) - target_hits.astype(wide)) * slot_weight[:, None]
    ).astype(low_type)
    grad_head_local = product_tn(picked_wide, grad_logits)
    grad_head = lax.psum(grad_head_local.astype(low_type), "col").astype(wide)
    grad_picked = lax.psum_scatter(
        product_nt(grad_logits, head_low).astype(low_type),
        "row",
        scatter_dimension=0,
        tiled=True,
    )
    grad_final = jnp.einsum(
        "ims,imd->isd", selector, grad_picked.reshape(images, MSLOT, -1),
        preferred_element_type=wide,
    )

    grad_stream, grad_final_gain, grad_final_shift = norm_backward(
        grad_final.reshape(images * SEQ, -1), final_stats, final_gain
    )
    grad_two = grad_stream.astype(low_type)
    grad_downward = product_tn(hidden_act, grad_two)
    grad_act = product_nt(grad_two, downward_low)
    _, gelu_pull = jax.vjp(exact_gelu, hidden_pre)
    grad_pre = gelu_pull(grad_act)[0].astype(low_type)
    grad_upward_turned = product_tn(grad_pre, normed_two)
    grad_normed_two = product(grad_pre, upward_turned)
    grad_mid, grad_gain_two, grad_shift_two = norm_backward(grad_normed_two, stats_two, gain_two)
    grad_mid = grad_mid + grad_stream
    grad_one = grad_mid.astype(low_type)
    grad_output = product_tn(mixture, grad_one)
    grad_mixture = product_nt(grad_one, output_low).astype(low_type)
    grad_grouped = attend_back(grouped, weights_full, grad_mixture).astype(low_type)
    grad_input_turned = product_tn(grad_grouped, normed_one)
    grad_normed_one = product(grad_grouped, input_turned)
    grad_below, grad_gain_one, grad_shift_one = norm_backward(grad_normed_one, stats_one, gain_one)
    grad_grid = (grad_below + grad_mid).reshape(images, SEQ, -1)
    grad_patch = jnp.where(opening | masked, 0.0, grad_grid).reshape(images * SEQ, -1)
    grad_patch_weight = product_tn(pixel_own, grad_patch.astype(low_type))
    lines = [
        jnp.sum(grad_grid, axis=0),
        jnp.sum(grad_grid[:, 0], axis=0)[None],
        jnp.sum(jnp.where(masked, grad_grid, 0.0), axis=(0, 1))[None],
        jnp.stack(
            [grad_gain_one, grad_shift_one, grad_gain_two, grad_shift_two,
             grad_final_gain, grad_final_shift]
        ),
    ]
    table_local = jnp.concatenate(lines, axis=0).astype(low_type)

    def dealt(value, height):
        grid = value.astype(low_type).reshape(cols, height, rows, -1)
        return jnp.transpose(grid, (2, 0, 1, 3)).reshape(rows * cols, height, -1)

    stacked = jnp.concatenate(
        [
            dealt(value, height)
            for value, height in zip(
                [grad_patch_weight, grad_input_turned, grad_output, grad_upward_turned,
                 grad_downward],
                heights,
            )
        ],
        axis=1,
    )
    summed = lax.psum_scatter(stacked, BOTH, scatter_dimension=0, tiled=False).astype(wide)
    starts = [sum(heights[:index]) for index in range(6)]
    pieces = [summed[starts[index] : starts[index + 1]] for index in range(5)]
    grad_table = lax.psum(table_local, BOTH).astype(wide)
    grad_table = lax.dynamic_slice_in_dim(
        grad_table, row_index * vector_table.shape[1], vector_table.shape[1], axis=1
    )
    leader_col = (col_index == 0).astype(wide)
    squares_part = jnp.sum(summed * summed) + leader_col * (
        jnp.sum(grad_table * grad_table) + jnp.sum(grad_head * grad_head)
    )
    loss_total, count_total, squares_total = lax.psum((loss_part, count_part, squares_part), BOTH)
    mean_loss = loss_total / count_total
    grad_norm = jnp.sqrt(squares_total) / count_total
    factor = jnp.minimum(1.0, clip_limit / grad_norm) / count_total
    step_value = step_count[0].astype(wide)
    steps = [
        (patch_weight, pieces[0], drift_patch, power_patch),
        (vector_table, grad_table, drift_table, power_table),
        (input_weight, pieces[1].T[None], drift_input, power_input),
        (output_weight, pieces[2][None], drift_output, power_output),
        (upward_weight, pieces[3].T[None], drift_upward, power_upward),
        (downward_weight, pieces[4][None], drift_downward, power_downward),
        (head_weight, grad_head, drift_head, power_head),
    ]
    results = []
    for weight, grad, drift, power in steps:
        results.extend(adam_step(weight, grad, drift, power, factor, step_value))
    return (mean_loss, grad_norm, *results)


VMEM_LIMIT = 62 * 2**20
TOK = 208
UNIT = 48
UNITS = 13
BANDS = 8
AHEAD = 4
LAG_A = 1
LAG_B = 3
LAG_C = 4
EYE = pl.DeviceIdType.MESH


def nn(left, right):
    return jnp.dot(left, right, preferred_element_type=wide)


def nt(left, right):
    return lax.dot_general(left, right, (((1,), (1,)), ((), ())), preferred_element_type=wide)


def tn(left, right):
    return lax.dot_general(left, right, (((0,), (0,)), ((), ())), preferred_element_type=wide)


def gelu_parts(values):
    phi_total = 0.5 * (1.0 + lax.erf(values * math.sqrt(0.5)))
    density = jnp.exp(values * values * -0.5) * (1.0 / math.sqrt(2.0 * math.pi))
    return phi_total, density


def normed(values, gain, shift):
    center = jnp.mean(values, axis=1, keepdims=True)
    moved = values - center
    inverse = lax.rsqrt(jnp.mean(moved * moved, axis=1, keepdims=True) + norm_eps)
    scaled = moved * inverse
    return scaled * gain + shift, scaled, inverse


def normed_back(upstream, scaled, inverse, gain):
    inner = upstream * gain
    down = inverse * (
        inner
        - jnp.mean(inner, axis=1, keepdims=True)
        - scaled * jnp.mean(inner * scaled, axis=1, keepdims=True)
    )
    return (
        down,
        jnp.sum(upstream * scaled, axis=0, keepdims=True),
        jnp.sum(upstream, axis=0, keepdims=True),
    )


def step_kernel(
    pix_in, patch_in, input_in, output_in, up_in, down_in, tab_in, places, targets, counts, head_in,
    gout, gtab_out, ghead, scal_out,
    wg, px_out, px_mid, px, tb, st0, st1, st2, n1, n2, mix, qkv, hpre, hact,
    hn, hbuf, pk, pkp, pp, lt, pkt, gch, colb, sq, lsb, flip, tmpa, gpk, gps, gpr, g2b, gacc, gst,
    rk, r1a, r1b, r2a, r2b, rz, tab, tabk, tabr, fin,
    ag_send, ag_recv, px_sem, px_send, px_recv, tb_sem, pk_send, pk_recv, ex_send, ex_recv,
    ls_send, ls_recv, rs_send, rs_recv, tab_send, tab_recv, fin_send, fin_recv, hb_sem, gh_sem,
):
    r = lax.axis_index("row")
    c = lax.axis_index("col")
    z, x, k = c // 4, (c // 2) % 2, c % 2
    half = tb.shape[1] // 2
    d_y = (1 - r, c)
    d_x = (r, z * 4 + (1 - x) * 2 + k)
    d_k = (r, z * 4 + x * 2 + 1 - k)

    def d_z(step):
        return (r, lax.rem(z + step, 4) * 4 + x * 2 + k)

    def remote(src, dst, send, recv, device):
        return pltpu.make_async_remote_copy(
            src_ref=src, dst_ref=dst, send_sem=send, recv_sem=recv,
            device_id=device, device_id_type=EYE,
        )

    def lanes(row):
        return pl.ds(pl.multiple_of(row * half, half), half)

    sq[...] = jnp.zeros_like(sq)
    width = px_out.shape[3]
    barrier = pltpu.get_barrier_semaphore()

    def greet(n, _):
        other = lax.rem(r * 16 + c + n, 32)
        pl.semaphore_signal(barrier, inc=1, device_id=(other // 16, other % 16), device_id_type=EYE)
        return 0

    lax.fori_loop(1, 32, greet, 0)

    for n in range(16):
        px_out[n % 2, n // 2, :, 0:SEQ] = pix_in[:, n * SEQ : (n + 1) * SEQ]
        px_out[n % 2, n // 2, :, SEQ:] = jnp.zeros((UNIT, width - SEQ), low_type)
    heights = (UNIT, 3 * UNIT, UNIT, 4 * UNIT, 4 * UNIT)
    blocks = (
        patch_in[...], input_in[...], output_in[...], up_in[...], down_in[...],
    )
    start = 0
    for height, block in zip(heights, blocks):
        wg[z, x, k, start : start + height, lanes(r)] = block.astype(low_type)
        start += height
    tb[0 : tab_in.shape[0], lanes(r)] = tab_in[...]
    tb[tab_in.shape[0] :, lanes(r)] = jnp.zeros((TOK - tab_in.shape[0], half), wide)
    hcopy = lambda n: pltpu.make_async_copy(
        head_in.at[:, pl.ds(pl.multiple_of(n * 256, 256), 256)], hbuf.at[n % 2], hb_sem.at[n % 2]
    )
    hcopy(0).start()
    pl.semaphore_wait(barrier, 31)

    def gather_moves(buf, part, both, send, recv):
        lo, hi = pl.ds(0, 2), pl.ds(2, 2)
        every = slice(None)
        other = lax.rem

        def move(index, out_region, in_region, device):
            out_ref = buf.at[out_region]
            in_ref = buf.at[in_region]
            return (
                remote(out_ref, out_ref, send.at[index], recv.at[index], device),
                remote(in_ref, in_ref, send.at[index], recv.at[index], device),
            )

        first = [
            move(n - 1, (z, x, k) + part(r), (lax.rem(z + 4 - n, 4), x, k) + part(r), d_z(n))
            for n in (1, 2, 3)
        ]
        second = [
            move(3, (lo, x, k) + part(r), (lo, 1 - x, k) + part(r), d_x),
            move(4, (hi, x, k) + part(r), (hi, x, k) + part(1 - r), d_y),
        ]
        pair_one = [move(5, (every, x, k) + part(r), (every, x, 1 - k) + part(r), d_k)]
        third = [
            move(6, (lo, every, k) + part(r), (lo, every, k) + part(1 - r), d_y),
            move(7, (hi, x, k) + both, (hi, 1 - x, k) + both, d_x),
        ]
        pair_two = [
            move(8, (lo, 1 - x, k) + part(r), (lo, 1 - x, 1 - k) + part(r), d_k),
            move(9, (hi, x, k) + part(1 - r), (hi, x, 1 - k) + part(1 - r), d_k),
        ]
        pair_three = [
            move(10, (lo, every, k) + part(1 - r), (lo, every, 1 - k) + part(1 - r), d_k),
            move(11, (hi, 1 - x, k) + both, (hi, 1 - x, 1 - k) + both, d_k),
        ]
        return first, second, pair_one, third, pair_two, pair_three

    def begin(moves):
        for out_copy, _ in moves:
            out_copy.start()

    def landed(moves):
        for _, in_copy in moves:
            in_copy.wait_recv()

    def sent(moves):
        for out_copy, _ in moves:
            out_copy.wait_send()

    def unit_rows(n):
        return pl.ds(pl.multiple_of(n * UNIT, UNIT), UNIT)

    def weight_moves(n):
        rows = unit_rows(n)
        return gather_moves(
            wg, lambda row: (rows, lanes(row)), (rows, slice(None)), ag_send.at[n], ag_recv.at[n]
        )

    def picked_moves(n):
        cut = lanes(n)
        return gather_moves(
            pk, lambda row: (pl.ds(pl.multiple_of(row * MSLOT, 16), MSLOT), cut),
            (slice(None), cut), pk_send.at[n], pk_recv.at[n],
        )

    px_swap = remote(px_out.at[1 - r], px_mid, px_sem.at[0], px_sem.at[1], d_y)

    def px_slot(n):
        return px.at[pl.ds(pl.multiple_of(n * UNIT, UNIT), UNIT)]

    def px_move(part, n):
        target = 8 * (r if part == 0 else 1 - r) + n
        src = px_out.at[r, n] if part == 0 else px_mid.at[n]
        return target, remote(src, px_slot(c), px_send.at[part, n], px_recv.at[c], (r, target))

    def px_start(part):
        def one(n, _):
            target, copy = px_move(part, n)

            @pl.when(target == c)
            def _():
                px[pl.ds(pl.multiple_of(c * UNIT, UNIT), UNIT), :] = (
                    px_out[r, n] if part == 0 else px_mid[n]
                )

            @pl.when(target != c)
            def _():
                copy.start()

            return 0

        lax.fori_loop(0, 8, one, 0)

    def px_done(n, _):
        for part in range(2):
            target, copy = px_move(part, n)

            @pl.when(target != c)
            def _():
                copy.wait_send()

        for source in (n, n + 8):

            @pl.when(source != c)
            def _():
                remote(px_slot(source), px_slot(source), px_send.at[0, n], px_recv.at[source], d_y).wait_recv()

        return 0

    cut_rows = TOK // 2
    own_cut = pl.ds(pl.multiple_of(k * cut_rows, 8), cut_rows)
    other_cut = pl.ds(pl.multiple_of((1 - k) * cut_rows, 8), cut_rows)

    def tb_copy(rows, row, index, device):
        ref = tb.at[rows, lanes(row)]
        return remote(ref, ref, tb_sem.at[index, 0], tb_sem.at[index, 1], device)

    token = lax.broadcasted_iota(jnp.int32, (TOK, 1), 0)
    slot_hit = lax.broadcasted_iota(jnp.int32, (TOK, MSLOT), 0) == places[pl.ds(r, 1), :]
    slot_on = lax.broadcasted_iota(jnp.int32, (TOK, MSLOT), 1) < counts[r]
    selector = jnp.where(slot_hit, 1.0, 0.0)
    masked = jnp.sum(jnp.where(slot_on, selector, 0.0), axis=1, keepdims=True) > 0.5
    opening = token == 0

    def gain(n):
        return tb[SEQ + 2 + 2 * n : SEQ + 3 + 2 * n, :]

    def shift(n):
        return tb[SEQ + 3 + 2 * n : SEQ + 4 + 2 * n, :]

    def square(n):
        return wg[:, :, :, unit_rows(n), :].reshape(16 * UNIT, 2 * half)

    def set_square(n, value):
        wg[:, :, :, unit_rows(n), :] = value.astype(low_type).reshape(4, 2, 2, UNIT, 2 * half)

    def triple():
        return wg[:, :, :, UNIT : 4 * UNIT, :].reshape(48 * UNIT, 2 * half)

    lane_low = lax.broadcasted_iota(jnp.int32, (1, 2 * HD), 1) < HD
    keep_low = jnp.where(lane_low, 1.0, 0.0)
    keep_high = 1.0 - keep_low

    def twice(values):
        return jnp.concatenate(
            [values * keep_low.astype(low_type), values * keep_high.astype(low_type)], axis=0
        )

    def once(values):
        return values[:TOK] * keep_low + values[TOK:] * keep_high

    def pair_lanes(part, p):
        return pl.ds(pl.multiple_of(part * HEADS * HD + p * 2 * HD, 2 * HD), 2 * HD)

    def pair_probs(p):
        query2 = twice(qkv[:, pair_lanes(0, p)])
        key2 = qkv[:, pair_lanes(1, p)]
        scores = nt(query2, key2) * (1.0 / math.sqrt(HD))
        valid = lax.broadcasted_iota(jnp.int32, (1, TOK), 1) < SEQ
        scores = jnp.where(valid, scores, -1e30)
        lifted = jnp.exp(scores - jnp.max(scores, axis=1, keepdims=True))
        return query2, key2, lifted * (1.0 / jnp.sum(lifted, axis=1, keepdims=True))

    def do_patch():
        tb_copy(own_cut, 1 - r, 0, d_y).wait_recv()
        tb_copy(own_cut, 1 - r, 1, d_k).start()
        lax.fori_loop(0, 8, px_done, 0)
        patch = tn(px[...], square(0))[:TOK]
        tb_copy(own_cut, r, 0, d_y).wait_send()
        tb_copy(other_cut, 1 - r, 1, d_k).wait_recv()
        tb_copy(own_cut, 1 - r, 1, d_k).wait_send()
        value = jnp.where(
            opening, tb[SEQ : SEQ + 1, :], jnp.where(masked, tb[SEQ + 1 : SEQ + 2, :], patch)
        )
        value = jnp.where(token < SEQ, value + tb[...], 0.0)
        st0[...] = value
        n1[...] = normed(value, gain(0), shift(0))[0].astype(low_type)

    def do_attention():
        qkv[...] = nt(n1[...], triple()).astype(low_type)

        def one_pair(p, _):
            _, _, probs = pair_probs(p)
            mixed = nn(probs.astype(low_type), qkv[:, pair_lanes(2, p)])
            mix[:, pair_lanes(0, p)] = once(mixed).astype(low_type)
            return 0

        lax.fori_loop(0, HEADS // 2, one_pair, 0)

    def do_output():
        value = st0[...] + nn(mix[...], square(4))
        st1[...] = value
        st2[...] = value
        n2[...] = normed(value, gain(1), shift(1))[0].astype(low_type)

    def do_up(j):
        value = nt(n2[...], square(5 + j))
        hpre[j] = value
        phi_total, _ = gelu_parts(value)
        hact[j] = (value * phi_total).astype(low_type)

    def do_down(j):
        st2[...] += nn(hact[j], square(9 + j))

    px_swap.start()
    begin(weight_moves(0)[0])
    begin(weight_moves(1)[0])
    px_start(0)
    for n in range(2, AHEAD):
        begin(weight_moves(n)[0])
    tb_copy(own_cut, r, 0, d_y).start()

    def tick(t, _):
        @pl.when(t < UNITS)
        def _():
            first, second, pair_one, _, _, _ = weight_moves(t)
            landed(first)
            begin(second)
            begin(pair_one)

        @pl.when(t == 0)
        def _():
            px_swap.wait()
            px_start(1)

        @pl.when(t < UNITS - AHEAD)
        def _():
            begin(weight_moves(t + AHEAD)[0])

        @pl.when(jnp.logical_and(t >= LAG_A, t < UNITS + LAG_A))
        def _():
            _, second, _, third, pair_two, _ = weight_moves(t - LAG_A)
            landed(second)
            begin(third)
            begin(pair_two)

        @pl.when(jnp.logical_and(t >= LAG_B, t < UNITS + LAG_B))
        def _():
            _, _, _, third, _, pair_three = weight_moves(t - LAG_B)
            landed(third)
            begin(pair_three)

        @pl.when(t >= LAG_C)
        def _():
            _, _, pair_one, _, pair_two, pair_three = weight_moves(t - LAG_C)
            landed(pair_one)
            landed(pair_two)
            landed(pair_three)

        @pl.when(t < 2 * BANDS)
        def _():
            @pl.when(t + 1 < 2 * BANDS)
            def _():
                hcopy(t + 1).start()

            hcopy(t).wait()
            hn[:, pl.ds(pl.multiple_of(t * 256, 256), 256)] = hbuf[t % 2].astype(low_type)

        @pl.when(t == LAG_C + 2)
        def _():
            do_patch()

        @pl.when(t == LAG_C + 3)
        def _():
            do_attention()

        @pl.when(t == LAG_C + 4)
        def _():
            do_output()

        @pl.when(jnp.logical_and(t >= LAG_C + 5, t < LAG_C + 9))
        def _():
            do_up(t - LAG_C - 5)

        @pl.when(t >= LAG_C + 9)
        def _():
            do_down(t - LAG_C - 9)

        return 0

    lax.fori_loop(0, UNITS + LAG_C, tick, 0)

    def all_sent(n, _):
        for moves in weight_moves(n):
            sent(moves)
        return 0

    final_out, _, _ = normed(st2[...], gain(2), shift(2))
    picked = tn(selector.astype(low_type), final_out.astype(low_type)).astype(low_type)
    own_rows = pl.ds(pl.multiple_of(r * MSLOT, 16), MSLOT)
    other_rows = pl.ds(pl.multiple_of((1 - r) * MSLOT, 16), MSLOT)
    pp[own_rows, :] = picked
    pk[z, x, k, own_rows, :] = picked

    def swap(index, src, dst, device):
        return remote(src, dst, ex_send.at[index], ex_recv.at[index], device)

    swap_picked = swap(0, pp.at[own_rows, :], pkp, d_y)
    swap_picked.start()
    for n in range(2):
        begin(picked_moves(n)[0])
    lax.fori_loop(0, UNITS, all_sent, 0)
    flip[...] = jnp.zeros_like(flip)
    flip[0:2, 0:MSLOT] = targets[...].astype(wide)
    info = jnp.transpose(flip[...])
    target_col = jnp.concatenate([info[:MSLOT, 0:1], info[:MSLOT, 1:2]], axis=0)
    slot_line = lax.broadcasted_iota(jnp.int32, (MSLOT, 1), 0)
    weight_col = jnp.concatenate(
        [jnp.where(slot_line < counts[0], 1.0, 0.0), jnp.where(slot_line < counts[1], 1.0, 0.0)], axis=0
    )
    base = (r * (BANDS * 512)).astype(wide)
    band_lane = lax.broadcasted_iota(jnp.int32, (1, 512), 1).astype(wide)

    def band(v):
        return pl.ds(pl.multiple_of(v * 512, 512), 512)

    def band_hit(v, column):
        return (band_lane + (base + (v * 512).astype(wide))) == column

    swap_picked.wait()
    pp[other_rows, :] = pkp[...]

    def picked_second(n):
        first, second, pair_one, _, _, _ = picked_moves(n)
        landed(first)
        begin(second)
        begin(pair_one)

    def picked_third(n):
        _, second, _, third, pair_two, _ = picked_moves(n)
        landed(second)
        begin(third)
        begin(pair_two)

    def picked_last(n):
        _, _, _, third, _, pair_three = picked_moves(n)
        landed(third)
        begin(pair_three)

    def picked_done(n):
        _, _, pair_one, _, pair_two, pair_three = picked_moves(n)
        landed(pair_one)
        landed(pair_two)
        landed(pair_three)

    def logits_band(v, carry):
        top, chosen = carry
        value = nn(pp[...], hn[:, band(v)])
        lt[v] = value
        chosen += jnp.sum(jnp.where(band_hit(v, target_col), value, 0.0), axis=1, keepdims=True)
        return jnp.maximum(top, jnp.max(value, axis=1, keepdims=True)), chosen

    zero_col = jnp.zeros((2 * MSLOT, 1), wide)
    top, chosen = lax.fori_loop(0, BANDS, logits_band, (zero_col - 1e30, zero_col))
    picked_second(0)

    def sum_band(v, total):
        return total + jnp.sum(jnp.exp(lt[v] - top), axis=1, keepdims=True)

    total = lax.fori_loop(0, BANDS, sum_band, zero_col)
    column = lax.broadcasted_iota(jnp.int32, (1, 128), 1)
    tmpa[...] = jnp.zeros_like(tmpa)
    tmpa[0 : 2 * MSLOT, :] = jnp.where(column == 0, top, jnp.where(column == 1, total, 0.0))
    sq[0] = jnp.transpose(tmpa[...])[:8]
    swap_lse = swap(1, sq.at[0], sq.at[1], d_y)
    swap_lse.start()
    picked_second(1)
    picked_third(0)
    swap_lse.wait()
    flip[...] = jnp.zeros_like(flip)
    flip[0:8, :] = sq[1]
    theirs = jnp.transpose(flip[...])[: 2 * MSLOT]
    their_top, their_total = theirs[:, 0:1], theirs[:, 1:2]
    best = jnp.maximum(top, their_top)
    log_total = best + jnp.log(total * jnp.exp(top - best) + their_total * jnp.exp(their_top - best))

    tmpa[0 : 2 * MSLOT, :] = jnp.where(
        column == 0, log_total, jnp.where(column == 1, target_col, jnp.where(column == 2, weight_col, 0.0))
    )
    lsb[c] = jnp.transpose(tmpa[...])[:8]

    def ls_copy(n):
        other = lax.rem(c + n, 16)
        return remote(lsb.at[c], lsb.at[c], ls_send.at[n], ls_recv.at[n], (r, other))

    def ls_in(n):
        other = lax.rem(c + 16 - n, 16)
        return remote(lsb.at[other], lsb.at[other], ls_send.at[n], ls_recv.at[n], (r, other))

    def ls_start(n, _):
        ls_copy(n).start()
        return 0

    def ls_done(n, _):
        ls_copy(n).wait_send()
        ls_in(n).wait_recv()
        return 0

    lax.fori_loop(1, 16, ls_start, 0)
    gpk[...] = jnp.zeros_like(gpk)

    def grad_band(v, _):
        value = jnp.exp(lt[v] - log_total) - jnp.where(band_hit(v, target_col), 1.0, 0.0)
        gpk[...] += nt((value * weight_col).astype(low_type), hn[:, band(v)])
        return 0

    lax.fori_loop(0, BANDS, grad_band, 0)
    gps[...] = gpk[other_rows, :].astype(low_type)
    swap_grad = swap(2, gps, gpr, d_y)
    swap_grad.start()
    picked_third(1)
    picked_last(0)
    leader = jnp.where(r == 0, 1.0, 0.0)
    loss_part = jnp.sum((log_total * leader - chosen) * weight_col, axis=0, keepdims=True)
    swap_grad.wait()
    grad_picked = (gpk[own_rows, :] + gpr[...].astype(wide)).astype(low_type)
    grad_final = nn(selector.astype(low_type), grad_picked)
    _, scaled, inverse = normed(st2[...], gain(2), shift(2))
    grad_last, grad_gain, grad_shift = normed_back(grad_final, scaled, inverse, gain(2))
    st2[...] = grad_last
    g2b[...] = grad_last.astype(low_type)
    gst[4:5, :] = grad_gain
    gst[5:6, :] = grad_shift
    gacc[...] = jnp.zeros_like(gacc)
    picked_last(1)

    def pair_region(n):
        return rk.at[lax.rem(n, 4)]

    def rs_copy(n, index, src, dst, device):
        return remote(src, dst, rs_send.at[n, index], rs_recv.at[n, index], device)

    lo, hi = pl.ds(0, 2), pl.ds(2, 2)

    def sums_moves(n):
        rows = unit_rows(UNITS - 1 - n)
        zero = [rs_copy(n, 0, wg.at[:, :, 1 - k, rows, :], rk.at[lax.rem(n, 4)], d_k)]
        one = [
            rs_copy(n, 1, wg.at[lo, :, k, rows, lanes(1 - r)], r1a.at[lax.rem(n, 7)], d_y),
            rs_copy(n, 2, wg.at[hi, 1 - x, k, rows, :], r1b.at[lax.rem(n, 7)], d_x),
        ]
        two = [
            rs_copy(n, 3, wg.at[lo, 1 - x, k, rows, lanes(r)], r2a.at[lax.rem(n, 7)], d_x),
            rs_copy(n, 4, wg.at[hi, x, k, rows, lanes(1 - r)], r2b.at[lax.rem(n, 7)], d_y),
        ]
        three = [
            rs_copy(n, 4 + m, wg.at[lax.rem(z + m, 4), x, k, rows, lanes(r)], rz.at[lax.rem(n, 7), m - 1], d_z(m))
            for m in (1, 2, 3)
        ]
        return zero, one, two, three

    def sum_start(copies):
        for copy in copies:
            copy.start()

    def sum_land(copies):
        for copy in copies:
            copy.wait_recv()

    def fold(region, value):
        wg[region] = (wg[region].astype(wide) + value.astype(wide)).astype(low_type)

    def sums_one(n):
        rows = unit_rows(UNITS - 1 - n)
        zero, one, _, _ = sums_moves(n)
        sum_land(zero)
        fold((slice(None), slice(None), k, rows, slice(None)), rk[lax.rem(n, 4)])
        sum_start(one)

    def sums_two(n):
        rows = unit_rows(UNITS - 1 - n)
        _, one, two, _ = sums_moves(n)
        sum_land(one)
        fold((lo, slice(None), k, rows, lanes(r)), r1a[lax.rem(n, 7)])
        fold((hi, x, k, rows, slice(None)), r1b[lax.rem(n, 7)])
        sum_start(two)

    def sums_three(n):
        rows = unit_rows(UNITS - 1 - n)
        _, _, two, three = sums_moves(n)
        sum_land(two)
        fold((lo, x, k, rows, lanes(r)), r2a[lax.rem(n, 7)])
        fold((hi, x, k, rows, lanes(r)), r2b[lax.rem(n, 7)])
        sum_start(three)

    def sums_four(n):
        rows = unit_rows(UNITS - 1 - n)
        _, _, _, three = sums_moves(n)
        sum_land(three)
        value = wg[z, x, k, rows, lanes(r)].astype(wide)
        for m in range(3):
            value = value + rz[lax.rem(n, 7), m].astype(wide)
        gout[rows, :] = value
        sq[2, 0:1, 0:128] += jnp.sum(jnp.sum(value * value, axis=0, keepdims=True), axis=1, keepdims=True)

    def sums_sent(n, _):
        for moves in sums_moves(n):
            sent([(copy, None) for copy in moves])
        return 0

    def back_down(j):
        grad_act = nt(g2b[...], square(9 + j))
        value = hpre[j]
        phi_total, density = gelu_parts(value)
        grad_pre = (grad_act * (phi_total + value * density)).astype(low_type)
        set_square(9 + j, tn(hact[j], g2b[...]))
        hact[j] = grad_pre

    def back_up(j):
        gacc[...] += nn(hact[j], square(5 + j))
        set_square(5 + j, tn(hact[j], n2[...]))

    def back_output():
        _, scaled, inverse = normed(st1[...], gain(1), shift(1))
        down, grad_gain, grad_shift = normed_back(gacc[...], scaled, inverse, gain(1))
        gst[2:3, :] = grad_gain
        gst[3:4, :] = grad_shift
        down = down + st2[...]
        st2[...] = down
        g2b[...] = down.astype(low_type)
        grad_mix = nt(g2b[...], square(4)).astype(low_type)
        set_square(4, tn(mix[...], g2b[...]))
        mix[...] = grad_mix

    def back_attention():
        def one_pair(p, _):
            query2, key2, probs = pair_probs(p)
            value2 = qkv[:, pair_lanes(2, p)]
            upstream = twice(mix[:, pair_lanes(0, p)])
            grad_probs = nt(upstream, value2)
            centered = grad_probs - jnp.sum(probs * grad_probs, axis=1, keepdims=True)
            grad_scores = (probs * centered).astype(low_type)
            scale = 1.0 / math.sqrt(HD)
            grad_query = once(nn(grad_scores, key2)) * scale
            grad_key = tn(grad_scores, query2) * scale
            grad_value = tn(probs.astype(low_type), upstream)
            qkv[:, pair_lanes(0, p)] = grad_query.astype(low_type)
            qkv[:, pair_lanes(1, p)] = grad_key.astype(low_type)
            qkv[:, pair_lanes(2, p)] = grad_value.astype(low_type)
            return 0

        lax.fori_loop(0, HEADS // 2, one_pair, 0)
        gacc[...] = nn(qkv[...], triple())
        wg[:, :, :, UNIT : 4 * UNIT, :] = (
            tn(qkv[...], n1[...]).astype(low_type).reshape(4, 2, 2, 3 * UNIT, 2 * half)
        )

    def back_patch():
        _, scaled, inverse = normed(st0[...], gain(0), shift(0))
        down, grad_gain, grad_shift = normed_back(gacc[...], scaled, inverse, gain(0))
        grad = down + st2[...]
        grad_patch = jnp.where(jnp.logical_or(opening, masked), 0.0, grad).astype(low_type)
        set_square(0, nn(px[:, 0:TOK], grad_patch))
        lines = [
            grad[0:1],
            jnp.sum(jnp.where(masked, grad, 0.0), axis=0, keepdims=True),
            grad_gain, grad_shift, gst[2:3, :], gst[3:4, :], gst[4:5, :], gst[5:6, :],
        ]
        for n, line in enumerate(lines):
            grad = jnp.where(token == SEQ + n, line, grad)
        tab[0:TOK, :] = grad.astype(low_type)
        tab[TOK:, :] = jnp.zeros((tab.shape[0] - TOK, tab.shape[1]), low_type)

    tab_half = tab.shape[0] // 2
    rows_own = pl.ds(pl.multiple_of(k * tab_half, 16), tab_half)
    rows_other = pl.ds(pl.multiple_of((1 - k) * tab_half, 16), tab_half)
    d_z1 = (r, (z + 1 - 2 * (z % 2)) * 4 + x * 2 + k)
    d_z2 = (r, lax.rem(z + 2, 4) * 4 + x * 2 + k)
    own_part = tab.at[rows_own, lanes(r)]
    tab_moves = [
        remote(tab.at[rows_other, :], tabk, tab_send.at[0], tab_recv.at[0], d_k),
        remote(tab.at[rows_own, lanes(1 - r)], tabr.at[0], tab_send.at[1], tab_recv.at[1], d_y),
        remote(own_part, tabr.at[1], tab_send.at[2], tab_recv.at[2], d_x),
        remote(own_part, tabr.at[2], tab_send.at[3], tab_recv.at[3], d_z1),
        remote(own_part, tabr.at[3], tab_send.at[4], tab_recv.at[4], d_z2),
        remote(own_part, tabr.at[4], tab_send.at[5], tab_recv.at[5], d_k),
    ]

    def tab_step(n):
        tab_moves[n].wait()
        if n == 0:
            tab[rows_own, :] = (
                tab[rows_own, :].astype(wide) + tabk[...].astype(wide)
            ).astype(low_type)
        elif n < 5:
            tab[rows_own, lanes(r)] = (
                tab[rows_own, lanes(r)].astype(wide) + tabr[n - 1].astype(wide)
            ).astype(low_type)
        if n < 5:
            tab_moves[n + 1].start()

    def gh_copy(v):
        return pltpu.make_async_copy(hn.at[:, band(v)], ghead.at[:, band(v)], gh_sem.at[v])

    def head_band(v):
        def rows_block(n, _):
            at = pl.ds(pl.multiple_of(n * 4 * MSLOT, 16), 4 * MSLOT)
            value = nn(pk[n // 2, n % 2].reshape(4 * MSLOT, 2 * half), hn[:, band(v)])
            cols = colb[at, :]
            hit = jnp.where(band_hit(v, cols[:, 1:2]), 1.0, 0.0)
            gch[at, :] = ((jnp.exp(value - cols[:, 0:1]) - hit) * cols[:, 2:3]).astype(low_type)
            return 0

        lax.fori_loop(0, 8, rows_block, 0)
        value = nn(pkt[...], gch[...])
        sq[3, 0:1, 0:128] += jnp.sum(jnp.sum(value * value, axis=0, keepdims=True), axis=1, keepdims=True)
        hn[:, band(v)] = value.astype(low_type)
        gh_copy(v).start()

    def head_ready():
        for n in range(2):
            picked_done(n)
        lax.fori_loop(1, 16, ls_done, 0)

        def to_columns(n, _):
            flip[0:8, :] = lsb[n]
            colb[pl.ds(pl.multiple_of(n * 2 * MSLOT, 16), 2 * MSLOT), :] = jnp.transpose(flip[...])[: 2 * MSLOT]
            return 0

        lax.fori_loop(0, 16, to_columns, 0)

        def turn(n, _):
            rows = pk[n].reshape(8 * MSLOT, 2 * half)
            pkt[:, pl.ds(pl.multiple_of(n * 8 * MSLOT, 128), 8 * MSLOT)] = jnp.transpose(rows)
            return 0

        lax.fori_loop(0, 4, turn, 0)

    def back_step(s, _):
        def work(q, _):
            w = jnp.where(s <= 4, 2 * s - 1 + q, s + 4 + 6 * q)

            @pl.when(jnp.logical_and(w >= 0, w < 4))
            def _():
                back_down(3 - w)

            @pl.when(jnp.logical_and(w >= 4, w < 8))
            def _():
                back_up(7 - w)

            @pl.when(w == 8)
            def _():
                back_output()

            @pl.when(w == 9)
            def _():
                back_attention()

            @pl.when(w == 10)
            def _():
                back_patch()

            return 0

        lax.fori_loop(0, 2, work, 0)

        @pl.when(s < UNITS)
        def _():
            sum_start(sums_moves(s)[0])

        @pl.when(jnp.logical_and(s >= 1, s < UNITS + 1))
        def _():
            sums_one(s - 1)

        @pl.when(jnp.logical_and(s >= 3, s < UNITS + 3))
        def _():
            sums_two(s - 3)

        @pl.when(jnp.logical_and(s >= 5, s < UNITS + 5))
        def _():
            sums_three(s - 5)

        @pl.when(s >= 7)
        def _():
            sums_four(s - 7)

        @pl.when(s == 6)
        def _():
            tab_moves[0].start()
            head_ready()

        for n in range(6):
            @pl.when(s == 7 + 2 * n)
            def _():
                tab_step(n)

        @pl.when(jnp.logical_and(s >= 7, s < 15))
        def _():
            head_band(s - 7)

        return 0

    lax.fori_loop(0, UNITS + 7, back_step, 0)
    gtab_out[rows_own, :] = tab[rows_own, lanes(r)].astype(wide)
    gtab_out[rows_other, :] = tabr[4].astype(wide)
    value = gtab_out[...]
    first_col = jnp.where(c == 0, 1.0, 0.0)
    table_squares = jnp.sum(jnp.sum(value * value, axis=0, keepdims=True), axis=1, keepdims=True)
    line = lax.broadcasted_iota(jnp.int32, (8, 128), 0)
    squares = sq[2, 0:1, 0:128] + (sq[3, 0:1, 0:128] + table_squares) * first_col
    count = (counts[0] + counts[1]).astype(wide) * leader
    fin[r * 16 + c] = jnp.where(
        line == 0, loss_part, jnp.where(line == 1, count, jnp.where(line == 2, squares, 0.0))
    )

    def fin_copy(n, step):
        other = lax.rem(r * 16 + c + step, 32)
        owner = r * 16 + c if n == 0 else lax.rem(r * 16 + c + 32 - step, 32)
        ref = fin.at[owner]
        return remote(ref, ref, fin_send.at[step], fin_recv.at[step], (other // 16, other % 16))

    def fin_start(step, _):
        fin_copy(0, step).start()
        return 0

    def fin_done(step, _):
        fin_copy(0, step).wait_send()
        fin_copy(1, step).wait_recv()
        return 0

    lax.fori_loop(1, 32, fin_start, 0)
    lax.fori_loop(0, UNITS, sums_sent, 0)
    for n in range(2):
        for moves in picked_moves(n):
            sent(moves)
    for v in range(BANDS):
        gh_copy(v).wait()
    lax.fori_loop(1, 32, fin_done, 0)
    totals = jnp.sum(fin[...], axis=0)
    count_total = totals[1:2, :]
    norm_value = jnp.sqrt(totals[2:3, :]) / count_total
    scal_out[0:1, :] = totals[0:1, :] / count_total
    scal_out[1:2, :] = norm_value
    scal_out[2:3, :] = jnp.minimum(1.0, clip_limit / norm_value) / count_total
    scal_out[3:8, :] = jnp.zeros((5, 128), wide)


def step_call(pix, blocks, tab, places, targets, counts, head):
    half = tab.shape[1]
    full = 2 * half
    vocab = head.shape[1]
    slots = 32 * MSLOT
    vm = pltpu.VMEM
    dma = pltpu.SemaphoreType.DMA
    f32, b16 = wide, low_type
    scratch = [
        vm((4, 2, 2, UNITS * UNIT, full), b16),
        vm((2, 8, UNIT, 256), b16),
        vm((8, UNIT, 256), b16),
        vm((16 * UNIT, 256), b16),
        vm((TOK, full), f32),
        vm((TOK, full), f32), vm((TOK, full), f32), vm((TOK, full), f32),
        vm((TOK, full), b16), vm((TOK, full), b16), vm((TOK, full), b16),
        vm((TOK, 3 * full), b16),
        vm((4, TOK, full), f32),
        vm((4, TOK, full), b16),
        vm((full, vocab), b16),
        vm((2, full, 256), f32),
        vm((4, 2, 2, 2 * MSLOT, full), b16),
        vm((MSLOT, full), b16),
        vm((2 * MSLOT, full), b16),
        vm((BANDS, 2 * MSLOT, 512), f32),
        vm((full, slots), b16),
        vm((slots, 512), b16),
        vm((slots, 128), f32),
        vm((4, 8, 256), f32),
        vm((16, 8, 256), f32),
        vm((128, 256), f32),
        vm((256, 128), f32),
        vm((2 * MSLOT, full), f32),
        vm((MSLOT, full), b16), vm((MSLOT, full), b16),
        vm((TOK, full), b16),
        vm((TOK, full), f32),
        vm((8, full), f32),
        vm((4, 4, 2, UNIT, full), b16),
        vm((7, 2, 2, UNIT, half), b16),
        vm((7, 2, UNIT, full), b16),
        vm((7, 2, UNIT, half), b16),
        vm((7, 2, UNIT, half), b16),
        vm((7, 3, UNIT, half), b16),
        vm((224, full), b16),
        vm((112, full), b16),
        vm((5, 112, half), b16),
        vm((32, 8, 128), f32),
        dma((UNITS, 12)), dma((UNITS, 12)),
        dma((2,)), dma((2, 8)), dma((16,)),
        dma((2, 2)),
        dma((2, 12)), dma((2, 12)),
        dma((3,)), dma((3,)),
        dma((16,)), dma((16,)),
        dma((UNITS, 8)), dma((UNITS, 8)),
        dma((6,)), dma((6,)),
        dma((32,)), dma((32,)),
        dma((2,)),
        dma((BANDS,)),
    ]
    in_vmem = pl.BlockSpec(memory_space=pltpu.VMEM)
    return pl.pallas_call(
        step_kernel,
        out_shape=(
            jax.ShapeDtypeStruct((UNITS * UNIT, half), f32),
            jax.ShapeDtypeStruct((224, half), f32),
            jax.ShapeDtypeStruct((full, vocab), b16),
            jax.ShapeDtypeStruct((8, 128), f32),
        ),
        in_specs=[
            *([in_vmem] * 9),
            pl.BlockSpec(memory_space=pltpu.SMEM),
            pl.BlockSpec(memory_space=pl.ANY),
        ],
        out_specs=(in_vmem, in_vmem, pl.BlockSpec(memory_space=pl.ANY), in_vmem),
        scratch_shapes=scratch,
        compiler_params=pltpu.CompilerParams(
            collective_id=0, has_side_effects=True, vmem_limit_bytes=VMEM_LIMIT
        ),
        cost_estimate=pl.CostEstimate(flops=50_000_000_000, bytes_accessed=40_000_000, transcendentals=0),
    )(pix, *blocks, tab, places, targets, counts, head)


def block_path(
    pixels, mask_places, mask_count, targets, step_count,
    patch_weight, vector_table, input_weight, output_weight, upward_weight, downward_weight, head_weight,
    *moments,
):
    weights = (
        patch_weight, vector_table, input_weight, output_weight, upward_weight, downward_weight, head_weight,
    )
    weights = flat(weights)
    blocks = [weights[n] for n in (0, 2, 3, 4, 5)]
    gout, gtab, ghead, scal = step_call(
        pixels.T, blocks, vector_table, mask_places, targets, mask_count, head_weight
    )
    results = adam_call(
        scal, step_count, gout, gtab, ghead, weights, flat(moments[:7]), flat(moments[7:])
    )
    triples = [results[2 + n :: 3] for n in range(3)]
    triples = [unflat(triple) for triple in triples]
    return (*results[:2], *(triple[n] for n in range(7) for triple in triples))


def flat(values):
    patch, table, inward, outward, up, down, head = values
    return (patch, table, inward[0].T, outward[0], up[0].T, down[0], head)


def unflat(values):
    patch, table, inward, outward, up, down, head = values
    return (patch, table, inward.T[None], outward[None], up.T[None], down[None], head)


SMALL = UNITS * UNIT
ROWS = 48
IN_SLOTS = 4
OUT_SLOTS = 3


def adam_kernel(
    scal, step, gout, gtab, ghead, *refs
):
    weights, drifts, powers = refs[:7], refs[7:14], refs[14:21]
    loss_out, norm_out = refs[21:23]
    outs = refs[23:44]
    gbuf, inbuf, outbuf, gsm, insm, outsm, gtb, intb, outtb, in_sem, out_sem, sm_in, sm_out = refs[44:]
    factor = scal[2:3, 0:1]
    count = jnp.full((1, 128), step[0], jnp.int32).astype(wide)[:, 0:1]
    scale_first = 1.0 / (1.0 - jnp.exp(count * math.log(beta_first)))
    scale_second = 1.0 / (1.0 - jnp.exp(count * math.log(beta_second)))
    count_first = scale_first * -learn_rate
    gain_first = factor * (1.0 - beta_first)
    gain_second = factor * factor * (1.0 - beta_second)
    chunks = ghead.shape[0] // ROWS
    states = (weights, drifts, powers)

    def rows_of(n):
        return pl.ds(pl.multiple_of(n * ROWS, ROWS), ROWS)

    def fetch(n):
        slot = lax.rem(n, IN_SLOTS)
        copies = [
            pltpu.make_async_copy(states[m][6].at[rows_of(n)], inbuf.at[slot, m], in_sem.at[slot, m])
            for m in range(3)
        ]
        copies.append(pltpu.make_async_copy(ghead.at[rows_of(n)], gbuf.at[slot], in_sem.at[slot, 3]))
        return copies

    def store(n):
        slot = lax.rem(n, OUT_SLOTS)
        return [
            pltpu.make_async_copy(outbuf.at[slot, m], outs[18 + m].at[rows_of(n)], out_sem.at[slot, m])
            for m in range(3)
        ]

    order = (0, 2, 3, 4, 5)
    small_fetch, small_store = [], []
    start = 0
    for at, n in enumerate(order):
        height = weights[n].shape[0]
        for m in range(3):
            small_fetch.append(
                pltpu.make_async_copy(states[m][n], insm.at[m, start : start + height], sm_in.at[at, m])
            )
            small_store.append(
                pltpu.make_async_copy(outsm.at[m, start : start + height], outs[3 * n + m], sm_out.at[at, m])
            )
        start += height
    for m in range(3):
        small_fetch.append(pltpu.make_async_copy(states[m][1], intb.at[m], sm_in.at[5, m]))
        small_store.append(pltpu.make_async_copy(outtb.at[m], outs[3 + m], sm_out.at[5, m]))
    small_fetch.append(pltpu.make_async_copy(gout, gsm, sm_in.at[6, 0]))
    small_fetch.append(pltpu.make_async_copy(gtab, gtb, sm_in.at[6, 1]))

    def adam(grad, weight, drift, power):
        new_drift = beta_first * drift + gain_first * grad
        new_power = beta_second * power + gain_second * (grad * grad)
        below = jnp.sqrt(new_power * scale_second) + adam_eps
        update = new_drift * count_first / below - (learn_rate * weight_decay) * weight
        return update, new_drift, new_power

    for n in range(IN_SLOTS):
        for copy in fetch(n):
            copy.start()
    for copy in small_fetch:
        copy.start()
    loss_out[...] = scal[0:1, 0:1]
    norm_out[...] = scal[1:2, 0:1]

    def chunk(n, _):
        for copy in fetch(n):
            copy.wait()

        @pl.when(n >= OUT_SLOTS)
        def _():
            for copy in store(n - OUT_SLOTS):
                copy.wait()

        slot, spot = lax.rem(n, IN_SLOTS), lax.rem(n, OUT_SLOTS)

        def part(q, _):
            at = pl.ds(pl.multiple_of(q * 16, 16), 16)
            values = adam(
                gbuf[slot, at, :].astype(wide), inbuf[slot, 0, at, :], inbuf[slot, 1, at, :],
                inbuf[slot, 2, at, :],
            )
            for m in range(3):
                outbuf[spot, m, at, :] = values[m]
            return 0

        lax.fori_loop(0, ROWS // 16, part, 0)
        for copy in store(n):
            copy.start()

        @pl.when(n + IN_SLOTS < chunks)
        def _():
            for copy in fetch(n + IN_SLOTS):
                copy.start()

        @pl.when(n == 2)
        def _():
            for copy in small_fetch:
                copy.wait()

            def small(q, _):
                at = pl.ds(pl.multiple_of(q * UNIT, UNIT), UNIT)
                values = adam(gsm[at, :], insm[0, at, :], insm[1, at, :], insm[2, at, :])
                for m in range(3):
                    outsm[m, at, :] = values[m]
                return 0

            lax.fori_loop(0, UNITS, small, 0)
            values = adam(gtb[0 : intb.shape[1]], intb[0], intb[1], intb[2])
            for m in range(3):
                outtb[m] = values[m]
            for copy in small_store:
                copy.start()

        return 0

    lax.fori_loop(0, chunks, chunk, 0)
    for n in range(chunks - OUT_SLOTS, chunks):
        for copy in store(n):
            copy.wait()
    for copy in small_store:
        copy.wait()


def adam_call(scal, step, gout, gtab, ghead, weights, drifts, powers):
    half = gout.shape[1]
    vocab = ghead.shape[1]
    table = weights[1].shape[0]
    one = jax.ShapeDtypeStruct((1, 1), wide)
    shapes = [jax.ShapeDtypeStruct(value.shape, wide) for value in weights for _ in range(3)]
    in_vmem = pl.BlockSpec(memory_space=pltpu.VMEM)
    anywhere = pl.BlockSpec(memory_space=pl.ANY)
    vm, dma = pltpu.VMEM, pltpu.SemaphoreType.DMA
    results = pl.pallas_call(
        adam_kernel,
        in_specs=[in_vmem, pl.BlockSpec(memory_space=pltpu.SMEM)] + [anywhere] * 24,
        out_specs=[in_vmem] * 2 + [anywhere] * 21,
        out_shape=[one, one] + shapes,
        scratch_shapes=[
            vm((IN_SLOTS, ROWS, vocab), low_type), vm((IN_SLOTS, 3, ROWS, vocab), wide),
            vm((OUT_SLOTS, 3, ROWS, vocab), wide),
            vm((SMALL, half), wide), vm((3, SMALL, half), wide), vm((3, SMALL, half), wide),
            vm(gtab.shape, wide), vm((3, table, half), wide), vm((3, table, half), wide),
            dma((IN_SLOTS, 4)), dma((OUT_SLOTS, 3)), dma((7, 3)), dma((6, 3)),
        ],
        compiler_params=pltpu.CompilerParams(vmem_limit_bytes=VMEM_LIMIT),
        cost_estimate=pl.CostEstimate(flops=60_000_000, bytes_accessed=82_000_000, transcendentals=4_000_000),
    )(scal, step, gout, gtab, ghead, *weights, *drifts, *powers)
    return (results[0].reshape(()), results[1].reshape(()), *results[2:])


def solution(mesh):
    state = (
        P("col", "row"),
        P(None, "row"),
        P(None, "row", "col"),
        P(None, "col", "row"),
        P(None, "row", "col"),
        P(None, "col", "row"),
        P(None, "row"),
    )
    data = (P("row", "col"), P("col", None), P("col"), P("col", None), P())
    outs = (P(), P()) + tuple(spec for spec in state for _ in range(3))
    fits = dict(mesh.shape) == {"row": 2, "col": 16}
    return jax.shard_map(
        block_path if fits else on_device,
        mesh=mesh,
        in_specs=data + state * 3,
        out_specs=outs,
        check_vma=False,
    )
```

```python
import math

import jax
import jax.numpy as jnp
from jax import lax
from jax.experimental import pallas as pl
from jax.experimental.pallas import tpu as pltpu
from jax.sharding import PartitionSpec as P

HEADS = 12
HD = 64
SEQ = 197
MSLOT = 80
BOTH = ("row", "col")

norm_eps = 1e-06
clip_limit = 0.1
learn_rate = 0.01
beta_first = 0.9
beta_second = 0.999
adam_eps = 1e-08
weight_decay = 0.05
low_type = jnp.bfloat16
wide = jnp.float32


def product(left, right):
    return jnp.dot(left, right, preferred_element_type=wide)


def product_nt(left, right):
    return jnp.einsum("ab,cb->ac", left, right, preferred_element_type=wide)


def product_tn(left, right):
    return jnp.einsum("ab,ac->bc", left, right, preferred_element_type=wide)


def norm_forward(values, gain, shift):
    center = jnp.mean(values, axis=1, keepdims=True)
    moved = values - center
    inverse = lax.rsqrt(jnp.mean(moved * moved, axis=1, keepdims=True) + norm_eps)
    scaled = moved * inverse
    return scaled * gain + shift, (scaled, inverse)


def norm_backward(upstream, kept, gain):
    scaled, inverse = kept
    inner = upstream * gain
    downstream = inverse * (
        inner
        - jnp.mean(inner, axis=1, keepdims=True)
        - scaled * jnp.mean(inner * scaled, axis=1, keepdims=True)
    )
    return downstream, jnp.sum(upstream * scaled, axis=0), jnp.sum(upstream, axis=0)


def exact_gelu(values):
    return jax.nn.gelu(values, approximate=False)


def split_heads(grouped):
    images = grouped.shape[0] // SEQ
    pieces = grouped.reshape(images, SEQ, 3, HEADS, HD)
    return pieces[:, :, 0], pieces[:, :, 1], pieces[:, :, 2]


def attention_weights(query, keys):
    scores = jnp.einsum("iqhd,ikhd->ihqk", query, keys, preferred_element_type=wide)
    return jax.nn.softmax(scores * (1.0 / math.sqrt(HD)), axis=-1)


def attend(grouped):
    query, keys, values = split_heads(grouped)
    weights_full = attention_weights(query, keys)
    mixture = jnp.einsum(
        "ihqk,ikhd->iqhd", weights_full.astype(low_type), values, preferred_element_type=wide
    )
    return mixture.reshape(grouped.shape[0], HEADS * HD), weights_full


def attend_back(grouped, weights_full, grad_mixture):
    query, keys, values = split_heads(grouped)
    images = query.shape[0]
    weights_low = weights_full.astype(low_type)
    grad_out = grad_mixture.reshape(images, SEQ, HEADS, HD)
    grad_weights = jnp.einsum("iqhd,ikhd->ihqk", grad_out, values, preferred_element_type=wide)
    grad_values = jnp.einsum("ihqk,iqhd->ikhd", weights_low, grad_out, preferred_element_type=wide)
    centered = grad_weights - jnp.sum(weights_full * grad_weights, axis=-1, keepdims=True)
    grad_scores = (weights_full * centered).astype(low_type)
    scale = 1.0 / math.sqrt(HD)
    grad_query = jnp.einsum("ihqk,ikhd->iqhd", grad_scores, keys, preferred_element_type=wide)
    grad_keys = jnp.einsum("ihqk,iqhd->ikhd", grad_scores, query, preferred_element_type=wide)
    stacked = jnp.stack([grad_query * scale, grad_keys * scale, grad_values], axis=2)
    return stacked.reshape(images * SEQ, 3 * HEADS * HD)


def adam_step(weight, grad, drift, power, factor, step_value):
    scaled = grad * factor
    new_drift = beta_first * drift + (1.0 - beta_first) * scaled
    new_power = beta_second * power + (1.0 - beta_second) * scaled * scaled
    drift_hat = new_drift / (1.0 - jnp.power(beta_first, step_value))
    power_hat = new_power / (1.0 - jnp.power(beta_second, step_value))
    update = -learn_rate * (drift_hat / (jnp.sqrt(power_hat) + adam_eps) + weight_decay * weight)
    return (update, new_drift, new_power)


def on_device(
    pixels,
    mask_places,
    mask_count,
    targets,
    step_count,
    patch_weight,
    vector_table,
    input_weight,
    output_weight,
    upward_weight,
    downward_weight,
    head_weight,
    drift_patch,
    drift_table,
    drift_input,
    drift_output,
    drift_upward,
    drift_downward,
    drift_head,
    power_patch,
    power_table,
    power_input,
    power_output,
    power_upward,
    power_downward,
    power_head,
):
    rows, cols = lax.axis_size("row"), lax.axis_size("col")
    row_index = lax.axis_index("row")
    col_index = lax.axis_index("col")
    images = mask_places.shape[0] // rows
    width = vector_table.shape[1] * rows

    blocks = [
        patch_weight.astype(low_type),
        input_weight[0].astype(low_type).T,
        output_weight[0].astype(low_type),
        upward_weight[0].astype(low_type).T,
        downward_weight[0].astype(low_type),
    ]
    heights = [block.shape[0] for block in blocks]
    gathered = lax.all_gather(jnp.concatenate(blocks, axis=0), BOTH, axis=0, tiled=False)
    gathered = gathered.reshape(rows, cols, sum(heights), -1)

    def whole(index):
        start = sum(heights[:index])
        part = gathered[:, :, start : start + heights[index]]
        return jnp.transpose(part, (1, 2, 0, 3)).reshape(cols * heights[index], width)

    patch_low, input_turned, output_low, upward_turned, downward_low = map(whole, range(5))
    table = lax.all_gather(vector_table, "row", axis=1, tiled=True)

    local_images = pixels.shape[0] // SEQ
    part = pixels.shape[1]
    grid = pixels.reshape(local_images // (rows * images), rows, images, SEQ, part)
    grid = lax.all_to_all(grid, "row", split_axis=1, concat_axis=0, tiled=True)
    grid = grid.reshape(cols, images * SEQ, part)
    grid = lax.all_to_all(grid, "col", split_axis=0, concat_axis=0, tiled=True)
    pixel_own = jnp.transpose(grid, (1, 0, 2)).reshape(images * SEQ, cols * part)

    def own(values):
        return lax.dynamic_slice_in_dim(values, row_index * images, images, axis=0)

    places_own, count_own = own(mask_places), own(mask_count)

    def gains_of(norm_index):
        return (table[SEQ + 2 + 2 * norm_index], table[SEQ + 3 + 2 * norm_index])

    patch_proj = product(pixel_own, patch_low)
    places = jnp.arange(SEQ, dtype=jnp.int32)
    counted_own = jnp.arange(MSLOT, dtype=jnp.int32)[None, :] < count_own[:, None]
    matches = places_own[:, :, None] == places[None, None, :]
    masked = jnp.any(matches & counted_own[:, :, None], axis=1)[:, :, None]
    opening = (places == 0)[None, :, None]
    stream = jnp.where(
        opening,
        table[SEQ],
        jnp.where(masked, table[SEQ + 1], patch_proj.reshape(images, SEQ, -1)),
    )
    stream = (stream + table[:SEQ][None]).reshape(images * SEQ, -1)
    gain_one, shift_one = gains_of(0)
    gain_two, shift_two = gains_of(1)
    final_gain, final_shift = gains_of(2)
    normed_one, stats_one = norm_forward(stream, gain_one, shift_one)
    normed_one = normed_one.astype(low_type)
    grouped = product_nt(normed_one, input_turned).astype(low_type)
    mixture, weights_full = attend(grouped)
    mixture = mixture.astype(low_type)
    stream_mid = stream + product(mixture, output_low)
    normed_two, stats_two = norm_forward(stream_mid, gain_two, shift_two)
    normed_two = normed_two.astype(low_type)
    hidden_pre = product_nt(normed_two, upward_turned)
    hidden_act = exact_gelu(hidden_pre).astype(low_type)
    stream_last = stream_mid + product(hidden_act, downward_low)
    final_out, final_stats = norm_forward(stream_last, final_gain, final_shift)
    selector = matches.astype(low_type)
    picked = jnp.einsum(
        "ims,isd->imd", selector, final_out.astype(low_type).reshape(images, SEQ, -1),
        preferred_element_type=wide,
    ).astype(low_type)

    picked_wide = lax.all_gather(picked.reshape(images * MSLOT, -1), "row", axis=0, tiled=True)
    head_low = head_weight.astype(low_type)
    logits = product(picked_wide, head_low)
    vocab_local = head_weight.shape[1]
    target_local = targets.reshape(-1) - row_index * vocab_local
    target_hits = target_local[:, None] == jnp.arange(vocab_local, dtype=jnp.int32)[None, :]
    chosen = jnp.sum(jnp.where(target_hits, logits, 0.0), axis=1)
    local_top = jnp.max(logits, axis=1)
    local_sum = jnp.sum(jnp.exp(logits - local_top[:, None]), axis=1)
    pair = lax.all_gather(jnp.stack([local_top, local_sum]), "row", axis=0, tiled=False)
    top_value = jnp.max(pair[:, 0], axis=0)
    exp_total = jnp.sum(pair[:, 1] * jnp.exp(pair[:, 0] - top_value), axis=0)
    log_total = top_value + jnp.log(exp_total)
    counted = jnp.arange(MSLOT, dtype=jnp.int32)[None, :] < mask_count[:, None]
    slot_weight = counted.reshape(-1).astype(wide)
    leader_row = (row_index == 0).astype(wide)
    loss_part = jnp.sum(log_total * slot_weight) * leader_row - jnp.sum(chosen * slot_weight)
    count_part = jnp.sum(mask_count.astype(wide)) * leader_row
    grad_logits = (
        (jnp.exp(logits - log_total[:, None]) - target_hits.astype(wide)) * slot_weight[:, None]
    ).astype(low_type)
    grad_head_local = product_tn(picked_wide, grad_logits)
    grad_head = lax.psum(grad_head_local.astype(low_type), "col").astype(wide)
    grad_picked = lax.psum_scatter(
        product_nt(grad_logits, head_low).astype(low_type),
        "row",
        scatter_dimension=0,
        tiled=True,
    )
    grad_final = jnp.einsum(
        "ims,imd->isd", selector, grad_picked.reshape(images, MSLOT, -1),
        preferred_element_type=wide,
    )

    grad_stream, grad_final_gain, grad_final_shift = norm_backward(
        grad_final.reshape(images * SEQ, -1), final_stats, final_gain
    )
    grad_two = grad_stream.astype(low_type)
    grad_downward = product_tn(hidden_act, grad_two)
    grad_act = product_nt(grad_two, downward_low)
    _, gelu_pull = jax.vjp(exact_gelu, hidden_pre)
    grad_pre = gelu_pull(grad_act)[0].astype(low_type)
    grad_upward_turned = product_tn(grad_pre, normed_two)
    grad_normed_two = product(grad_pre, upward_turned)
    grad_mid, grad_gain_two, grad_shift_two = norm_backward(grad_normed_two, stats_two, gain_two)
    grad_mid = grad_mid + grad_stream
    grad_one = grad_mid.astype(low_type)
    grad_output = product_tn(mixture, grad_one)
    grad_mixture = product_nt(grad_one, output_low).astype(low_type)
    grad_grouped = attend_back(grouped, weights_full, grad_mixture).astype(low_type)
    grad_input_turned = product_tn(grad_grouped, normed_one)
    grad_normed_one = product(grad_grouped, input_turned)
    grad_below, grad_gain_one, grad_shift_one = norm_backward(grad_normed_one, stats_one, gain_one)
    grad_grid = (grad_below + grad_mid).reshape(images, SEQ, -1)
    grad_patch = jnp.where(opening | masked, 0.0, grad_grid).reshape(images * SEQ, -1)
    grad_patch_weight = product_tn(pixel_own, grad_patch.astype(low_type))
    lines = [
        jnp.sum(grad_grid, axis=0),
        jnp.sum(grad_grid[:, 0], axis=0)[None],
        jnp.sum(jnp.where(masked, grad_grid, 0.0), axis=(0, 1))[None],
        jnp.stack(
            [grad_gain_one, grad_shift_one, grad_gain_two, grad_shift_two,
             grad_final_gain, grad_final_shift]
        ),
    ]
    table_local = jnp.concatenate(lines, axis=0).astype(low_type)

    def dealt(value, height):
        grid = value.astype(low_type).reshape(cols, height, rows, -1)
        return jnp.transpose(grid, (2, 0, 1, 3)).reshape(rows * cols, height, -1)

    stacked = jnp.concatenate(
        [
            dealt(value, height)
            for value, height in zip(
                [grad_patch_weight, grad_input_turned, grad_output, grad_upward_turned,
                 grad_downward],
                heights,
            )
        ],
        axis=1,
    )
    summed = lax.psum_scatter(stacked, BOTH, scatter_dimension=0, tiled=False).astype(wide)
    starts = [sum(heights[:index]) for index in range(6)]
    pieces = [summed[starts[index] : starts[index + 1]] for index in range(5)]
    grad_table = lax.psum(table_local, BOTH).astype(wide)
    grad_table = lax.dynamic_slice_in_dim(
        grad_table, row_index * vector_table.shape[1], vector_table.shape[1], axis=1
    )
    leader_col = (col_index == 0).astype(wide)
    squares_part = jnp.sum(summed * summed) + leader_col * (
        jnp.sum(grad_table * grad_table) + jnp.sum(grad_head * grad_head)
    )
    loss_total, count_total, squares_total = lax.psum((loss_part, count_part, squares_part), BOTH)
    mean_loss = loss_total / count_total
    grad_norm = jnp.sqrt(squares_total) / count_total
    factor = jnp.minimum(1.0, clip_limit / grad_norm) / count_total
    step_value = step_count[0].astype(wide)
    steps = [
        (patch_weight, pieces[0], drift_patch, power_patch),
        (vector_table, grad_table, drift_table, power_table),
        (input_weight, pieces[1].T[None], drift_input, power_input),
        (output_weight, pieces[2][None], drift_output, power_output),
        (upward_weight, pieces[3].T[None], drift_upward, power_upward),
        (downward_weight, pieces[4][None], drift_downward, power_downward),
        (head_weight, grad_head, drift_head, power_head),
    ]
    results = []
    for weight, grad, drift, power in steps:
        results.extend(adam_step(weight, grad, drift, power, factor, step_value))
    return (mean_loss, grad_norm, *results)


VMEM_LIMIT = 62 * 2**20
TOK = 208
UNIT = 48
UNITS = 13
BANDS = 8
G_FIRST = 7
AHEAD = 4
LAG_A = 1
LAG_B = 3
LAG_C = 4
EYE = pl.DeviceIdType.MESH


def nn(left, right):
    return jnp.dot(left, right, preferred_element_type=wide)


def nt(left, right):
    return lax.dot_general(left, right, (((1,), (1,)), ((), ())), preferred_element_type=wide)


def tn(left, right):
    return lax.dot_general(left, right, (((0,), (0,)), ((), ())), preferred_element_type=wide)


def gelu_parts(values):
    phi_total = 0.5 * (1.0 + lax.erf(values * math.sqrt(0.5)))
    density = jnp.exp(values * values * -0.5) * (1.0 / math.sqrt(2.0 * math.pi))
    return phi_total, density


def normed(values, gain, shift):
    center = jnp.mean(values, axis=1, keepdims=True)
    moved = values - center
    inverse = lax.rsqrt(jnp.mean(moved * moved, axis=1, keepdims=True) + norm_eps)
    scaled = moved * inverse
    return scaled * gain + shift, scaled, inverse


def normed_back(upstream, scaled, inverse, gain):
    inner = upstream * gain
    down = inverse * (
        inner
        - jnp.mean(inner, axis=1, keepdims=True)
        - scaled * jnp.mean(inner * scaled, axis=1, keepdims=True)
    )
    return (
        down,
        jnp.sum(upstream * scaled, axis=0, keepdims=True),
        jnp.sum(upstream, axis=0, keepdims=True),
    )


def step_kernel(
    pix_in, patch_in, input_in, output_in, up_in, down_in, tab_in, places, targets, counts, head_in,
    gout, gtab_out, ghead, scal_out,
    wg, px_out, px_mid, px, tb, st0, st1, st2, n1, n2, mix, qkv, hpre, hact,
    hn, hbuf, pk, pkp, pp, lt, pkt, gch, colb, sq, lsb, flip, tmpa, gpk, gps, gpr, g2b, gacc, gst,
    rk, r1a, r1b, r2a, r2b, rz, tab, tabk, tabr, fin,
    ag_send, ag_recv, px_sem, px_send, px_recv, tb_sem, pk_send, pk_recv, ex_send, ex_recv,
    ls_send, ls_recv, rs_send, rs_recv, tab_send, tab_recv, fin_send, fin_recv, hb_sem, gh_sem, gh_send, gh_recv,
):
    r = lax.axis_index("row")
    c = lax.axis_index("col")
    z, x, k = c // 4, (c // 2) % 2, c % 2
    half = tb.shape[1] // 2
    d_y = (1 - r, c)
    d_x = (r, z * 4 + (1 - x) * 2 + k)
    d_k = (r, z * 4 + x * 2 + 1 - k)

    def d_z(step):
        return (r, lax.rem(z + step, 4) * 4 + x * 2 + k)

    def remote(src, dst, send, recv, device):
        return pltpu.make_async_remote_copy(
            src_ref=src, dst_ref=dst, send_sem=send, recv_sem=recv,
            device_id=device, device_id_type=EYE,
        )

    def lanes(row):
        return pl.ds(pl.multiple_of(row * half, half), half)

    sq[...] = jnp.zeros_like(sq)
    width = px_out.shape[3]
    barrier = pltpu.get_barrier_semaphore()

    def greet(n, _):
        other = lax.rem(r * 16 + c + n, 32)
        pl.semaphore_signal(barrier, inc=1, device_id=(other // 16, other % 16), device_id_type=EYE)
        return 0

    lax.fori_loop(1, 32, greet, 0)

    for n in range(16):
        px_out[n % 2, n // 2, :, 0:SEQ] = pix_in[:, n * SEQ : (n + 1) * SEQ]
        px_out[n % 2, n // 2, :, SEQ:] = jnp.zeros((UNIT, width - SEQ), low_type)
    heights = (UNIT, 3 * UNIT, UNIT, 4 * UNIT, 4 * UNIT)
    blocks = (
        patch_in[...], input_in[...], output_in[...], up_in[...], down_in[...],
    )
    start = 0
    for height, block in zip(heights, blocks):
        wg[z, x, k, start : start + height, lanes(r)] = block.astype(low_type)
        start += height
    tb[0 : tab_in.shape[0], lanes(r)] = tab_in[...]
    tb[tab_in.shape[0] :, lanes(r)] = jnp.zeros((TOK - tab_in.shape[0], half), wide)
    hcopy = lambda n: pltpu.make_async_copy(
        head_in.at[:, pl.ds(pl.multiple_of(n * 256, 256), 256)], hbuf.at[n % 2], hb_sem.at[n % 2]
    )
    hcopy(0).start()
    pl.semaphore_wait(barrier, 31)

    def gather_moves(buf, part, both, send, recv):
        lo, hi = pl.ds(0, 2), pl.ds(2, 2)
        every = slice(None)
        other = lax.rem

        def move(index, out_region, in_region, device):
            out_ref = buf.at[out_region]
            in_ref = buf.at[in_region]
            return (
                remote(out_ref, out_ref, send.at[index], recv.at[index], device),
                remote(in_ref, in_ref, send.at[index], recv.at[index], device),
            )

        first = [
            move(n - 1, (z, x, k) + part(r), (lax.rem(z + 4 - n, 4), x, k) + part(r), d_z(n))
            for n in (1, 2, 3)
        ]
        second = [
            move(3, (lo, x, k) + part(r), (lo, 1 - x, k) + part(r), d_x),
            move(4, (hi, x, k) + part(r), (hi, x, k) + part(1 - r), d_y),
        ]
        pair_one = [move(5, (every, x, k) + part(r), (every, x, 1 - k) + part(r), d_k)]
        third = [
            move(6, (lo, every, k) + part(r), (lo, every, k) + part(1 - r), d_y),
            move(7, (hi, x, k) + both, (hi, 1 - x, k) + both, d_x),
        ]
        pair_two = [
            move(8, (lo, 1 - x, k) + part(r), (lo, 1 - x, 1 - k) + part(r), d_k),
            move(9, (hi, x, k) + part(1 - r), (hi, x, 1 - k) + part(1 - r), d_k),
        ]
        pair_three = [
            move(10, (lo, every, k) + part(1 - r), (lo, every, 1 - k) + part(1 - r), d_k),
            move(11, (hi, 1 - x, k) + both, (hi, 1 - x, 1 - k) + both, d_k),
        ]
        return first, second, pair_one, third, pair_two, pair_three

    def begin(moves):
        for out_copy, _ in moves:
            out_copy.start()

    def landed(moves):
        for _, in_copy in moves:
            in_copy.wait_recv()

    def sent(moves):
        for out_copy, _ in moves:
            out_copy.wait_send()

    def unit_rows(n):
        return pl.ds(pl.multiple_of(n * UNIT, UNIT), UNIT)

    def weight_moves(n):
        rows = unit_rows(n)
        return gather_moves(
            wg, lambda row: (rows, lanes(row)), (rows, slice(None)), ag_send.at[n], ag_recv.at[n]
        )

    late = UNITS - 1

    def late_moves():
        rows = unit_rows(late)
        every = slice(None)

        def move(index, out_region, in_region, device):
            out_ref, in_ref = wg.at[out_region], wg.at[in_region]
            send, recv = ag_send.at[late, index], ag_recv.at[late, index]
            return remote(out_ref, out_ref, send, recv, device), remote(in_ref, in_ref, send, recv, device)

        one = [move(0, (z, x, k, rows, lanes(r)), (z, 1 - x, k, rows, lanes(r)), d_x)]
        two = [move(1, (z, every, k, rows, lanes(r)), (z, every, k, rows, lanes(1 - r)), d_y)]
        three = [
            move(1 + n, (z, every, k, rows, every), (lax.rem(z + 4 - n, 4), every, k, rows, every), d_z(n))
            for n in (1, 2, 3)
        ]
        four = [move(5, (every, every, k, rows, every), (every, every, 1 - k, rows, every), d_k)]
        return one, two, three, four

    def picked_moves(n):
        cut = lanes(n)
        return gather_moves(
            pk, lambda row: (pl.ds(pl.multiple_of(row * MSLOT, 16), MSLOT), cut),
            (slice(None), cut), pk_send.at[n], pk_recv.at[n],
        )

    px_swap = remote(px_out.at[1 - r], px_mid, px_sem.at[0], px_sem.at[1], d_y)

    def px_slot(n):
        return px.at[pl.ds(pl.multiple_of(n * UNIT, UNIT), UNIT)]

    def px_move(part, n):
        target = 8 * (r if part == 0 else 1 - r) + n
        src = px_out.at[r, n] if part == 0 else px_mid.at[n]
        return target, remote(src, px_slot(c), px_send.at[part, n], px_recv.at[c], (r, target))

    def px_start(part):
        def one(n, _):
            target, copy = px_move(part, n)

            @pl.when(target == c)
            def _():
                px[pl.ds(pl.multiple_of(c * UNIT, UNIT), UNIT), :] = (
                    px_out[r, n] if part == 0 else px_mid[n]
                )

            @pl.when(target != c)
            def _():
                copy.start()

            return 0

        lax.fori_loop(0, 8, one, 0)

    def px_done(n, _):
        for part in range(2):
            target, copy = px_move(part, n)

            @pl.when(target != c)
            def _():
                copy.wait_send()

        for source in (n, n + 8):

            @pl.when(source != c)
            def _():
                remote(px_slot(source), px_slot(source), px_send.at[0, n], px_recv.at[source], d_y).wait_recv()

        return 0

    cut_rows = TOK // 2
    own_cut = pl.ds(pl.multiple_of(k * cut_rows, 8), cut_rows)
    other_cut = pl.ds(pl.multiple_of((1 - k) * cut_rows, 8), cut_rows)

    def tb_copy(rows, row, index, device):
        ref = tb.at[rows, lanes(row)]
        return remote(ref, ref, tb_sem.at[index, 0], tb_sem.at[index, 1], device)

    token = lax.broadcasted_iota(jnp.int32, (TOK, 1), 0)
    slot_hit = lax.broadcasted_iota(jnp.int32, (TOK, MSLOT), 0) == places[pl.ds(r, 1), :]
    slot_on = lax.broadcasted_iota(jnp.int32, (TOK, MSLOT), 1) < counts[r]
    selector = jnp.where(slot_hit, 1.0, 0.0)
    masked = jnp.sum(jnp.where(slot_on, selector, 0.0), axis=1, keepdims=True) > 0.5
    opening = token == 0

    def gain(n):
        return tb[SEQ + 2 + 2 * n : SEQ + 3 + 2 * n, :]

    def shift(n):
        return tb[SEQ + 3 + 2 * n : SEQ + 4 + 2 * n, :]

    def square(n):
        return wg[:, :, :, unit_rows(n), :].reshape(16 * UNIT, 2 * half)

    def set_square(n, value):
        wg[:, :, :, unit_rows(n), :] = value.astype(low_type).reshape(4, 2, 2, UNIT, 2 * half)

    def triple():
        return wg[:, :, :, UNIT : 4 * UNIT, :].reshape(48 * UNIT, 2 * half)

    lane_low = lax.broadcasted_iota(jnp.int32, (1, 2 * HD), 1) < HD
    keep_low = jnp.where(lane_low, 1.0, 0.0)
    keep_high = 1.0 - keep_low

    def twice(values):
        return jnp.concatenate(
            [values * keep_low.astype(low_type), values * keep_high.astype(low_type)], axis=0
        )

    def once(values):
        return values[:TOK] * keep_low + values[TOK:] * keep_high

    def pair_lanes(part, p):
        return pl.ds(pl.multiple_of(part * HEADS * HD + p * 2 * HD, 2 * HD), 2 * HD)

    def pair_probs(p):
        query2 = twice(qkv[:, pair_lanes(0, p)])
        key2 = qkv[:, pair_lanes(1, p)]
        scores = nt(query2, key2) * (1.0 / math.sqrt(HD))
        valid = lax.broadcasted_iota(jnp.int32, (1, TOK), 1) < SEQ
        scores = jnp.where(valid, scores, -1e30)
        lifted = jnp.exp(scores - jnp.max(scores, axis=1, keepdims=True))
        return query2, key2, lifted * (1.0 / jnp.sum(lifted, axis=1, keepdims=True))

    def do_patch():
        tb_copy(own_cut, 1 - r, 0, d_y).wait_recv()
        tb_copy(own_cut, 1 - r, 1, d_k).start()
        lax.fori_loop(0, 8, px_done, 0)
        patch = tn(px[...], square(0))[:TOK]
        tb_copy(own_cut, r, 0, d_y).wait_send()
        tb_copy(other_cut, 1 - r, 1, d_k).wait_recv()
        tb_copy(own_cut, 1 - r, 1, d_k).wait_send()
        value = jnp.where(
            opening, tb[SEQ : SEQ + 1, :], jnp.where(masked, tb[SEQ + 1 : SEQ + 2, :], patch)
        )
        value = jnp.where(token < SEQ, value + tb[...], 0.0)
        st0[...] = value
        n1[...] = normed(value, gain(0), shift(0))[0].astype(low_type)

    def do_attention():
        qkv[...] = nt(n1[...], triple()).astype(low_type)

        def one_pair(p, _):
            _, _, probs = pair_probs(p)
            mixed = nn(probs.astype(low_type), qkv[:, pair_lanes(2, p)])
            mix[:, pair_lanes(0, p)] = once(mixed).astype(low_type)
            return 0

        lax.fori_loop(0, HEADS // 2, one_pair, 0)

    def do_output():
        value = st0[...] + nn(mix[...], square(4))
        st1[...] = value
        st2[...] = value
        n2[...] = normed(value, gain(1), shift(1))[0].astype(low_type)

    def do_up(j):
        value = nt(n2[...], square(5 + j))
        hpre[j] = value
        phi_total, _ = gelu_parts(value)
        hact[j] = (value * phi_total).astype(low_type)

    def do_down(j):
        st2[...] += nn(hact[j], square(9 + j))

    begin(late_moves()[0])
    px_swap.start()
    begin(weight_moves(0)[0])
    begin(weight_moves(1)[0])
    px_start(0)
    for n in range(2, AHEAD):
        begin(weight_moves(n)[0])
    tb_copy(own_cut, r, 0, d_y).start()

    def tick(t, _):
        @pl.when(t < late)
        def _():
            first, second, pair_one, _, _, _ = weight_moves(t)
            landed(first)
            begin(second)
            begin(pair_one)

        @pl.when(t == 0)
        def _():
            landed(late_moves()[0])
            begin(late_moves()[1])
            px_swap.wait()
            px_start(1)

        @pl.when(t < late - AHEAD)
        def _():
            begin(weight_moves(t + AHEAD)[0])

        @pl.when(t == late - AHEAD)
        def _():
            landed(late_moves()[1])
            begin(late_moves()[2])

        @pl.when(jnp.logical_and(t >= LAG_A, t < late + LAG_A))
        def _():
            _, second, _, third, pair_two, _ = weight_moves(t - LAG_A)
            landed(second)
            begin(third)
            begin(pair_two)

        @pl.when(t == late + 2)
        def _():
            landed(late_moves()[2])
            begin(late_moves()[3])

        @pl.when(jnp.logical_and(t >= LAG_B, t < late + LAG_B))
        def _():
            _, _, _, third, _, pair_three = weight_moves(t - LAG_B)
            landed(third)
            begin(pair_three)

        @pl.when(jnp.logical_and(t >= LAG_C, t < late + LAG_C))
        def _():
            _, _, pair_one, _, pair_two, pair_three = weight_moves(t - LAG_C)
            landed(pair_one)
            landed(pair_two)
            landed(pair_three)

        @pl.when(t == late + LAG_C)
        def _():
            landed(late_moves()[3])

        @pl.when(t < 2 * BANDS)
        def _():
            @pl.when(t + 1 < 2 * BANDS)
            def _():
                hcopy(t + 1).start()

            hcopy(t).wait()
            hn[:, pl.ds(pl.multiple_of(t * 256, 256), 256)] = hbuf[t % 2].astype(low_type)

        @pl.when(t == LAG_C + 2)
        def _():
            do_patch()

        @pl.when(t == LAG_C + 3)
        def _():
            do_attention()

        @pl.when(t == LAG_C + 4)
        def _():
            do_output()

        @pl.when(jnp.logical_and(t >= LAG_C + 5, t < LAG_C + 9))
        def _():
            do_up(t - LAG_C - 5)

        @pl.when(t >= LAG_C + 9)
        def _():
            do_down(t - LAG_C - 9)

        return 0

    lax.fori_loop(0, UNITS + LAG_C, tick, 0)

    def all_sent(n, _):
        for moves in weight_moves(n):
            sent(moves)
        return 0

    final_out, _, _ = normed(st2[...], gain(2), shift(2))
    picked = tn(selector.astype(low_type), final_out.astype(low_type)).astype(low_type)
    own_rows = pl.ds(pl.multiple_of(r * MSLOT, 16), MSLOT)
    other_rows = pl.ds(pl.multiple_of((1 - r) * MSLOT, 16), MSLOT)
    pp[own_rows, :] = picked
    pk[z, x, k, own_rows, :] = picked

    def swap(index, src, dst, device):
        return remote(src, dst, ex_send.at[index], ex_recv.at[index], device)

    swap_picked = swap(0, pp.at[own_rows, :], pkp, d_y)
    swap_picked.start()
    for n in range(2):
        begin(picked_moves(n)[0])
    lax.fori_loop(0, late, all_sent, 0)
    for moves in late_moves():
        sent(moves)
    flip[...] = jnp.zeros_like(flip)
    flip[0:2, 0:MSLOT] = targets[...].astype(wide)
    info = jnp.transpose(flip[...])
    target_col = jnp.concatenate([info[:MSLOT, 0:1], info[:MSLOT, 1:2]], axis=0)
    slot_line = lax.broadcasted_iota(jnp.int32, (MSLOT, 1), 0)
    weight_col = jnp.concatenate(
        [jnp.where(slot_line < counts[0], 1.0, 0.0), jnp.where(slot_line < counts[1], 1.0, 0.0)], axis=0
    )
    base = (r * (BANDS * 512)).astype(wide)
    band_lane = lax.broadcasted_iota(jnp.int32, (1, 512), 1).astype(wide)

    def band(v):
        return pl.ds(pl.multiple_of(v * 512, 512), 512)

    def band_hit(v, column):
        return (band_lane + (base + (v * 512).astype(wide))) == column

    swap_picked.wait()
    pp[other_rows, :] = pkp[...]

    def picked_second(n):
        first, second, pair_one, _, _, _ = picked_moves(n)
        landed(first)
        begin(second)
        begin(pair_one)

    def picked_third(n):
        _, second, _, third, pair_two, _ = picked_moves(n)
        landed(second)
        begin(third)
        begin(pair_two)

    def picked_last(n):
        _, _, _, third, _, pair_three = picked_moves(n)
        landed(third)
        begin(pair_three)

    def picked_done(n):
        _, _, pair_one, _, pair_two, pair_three = picked_moves(n)
        landed(pair_one)
        landed(pair_two)
        landed(pair_three)

    def logits_band(v, carry):
        top, chosen = carry
        value = nn(pp[...], hn[:, band(v)])
        lt[v] = value
        chosen += jnp.sum(jnp.where(band_hit(v, target_col), value, 0.0), axis=1, keepdims=True)
        return jnp.maximum(top, jnp.max(value, axis=1, keepdims=True)), chosen

    zero_col = jnp.zeros((2 * MSLOT, 1), wide)
    top, chosen = lax.fori_loop(0, BANDS, logits_band, (zero_col - 1e30, zero_col))
    picked_second(0)

    def sum_band(v, total):
        return total + jnp.sum(jnp.exp(lt[v] - top), axis=1, keepdims=True)

    total = lax.fori_loop(0, BANDS, sum_band, zero_col)
    column = lax.broadcasted_iota(jnp.int32, (1, 128), 1)
    tmpa[...] = jnp.zeros_like(tmpa)
    tmpa[0 : 2 * MSLOT, :] = jnp.where(column == 0, top, jnp.where(column == 1, total, 0.0))
    sq[0] = jnp.transpose(tmpa[...])[:8]
    swap_lse = swap(1, sq.at[0], sq.at[1], d_y)
    swap_lse.start()
    picked_second(1)
    picked_third(0)
    swap_lse.wait()
    flip[...] = jnp.zeros_like(flip)
    flip[0:8, :] = sq[1]
    theirs = jnp.transpose(flip[...])[: 2 * MSLOT]
    their_top, their_total = theirs[:, 0:1], theirs[:, 1:2]
    best = jnp.maximum(top, their_top)
    log_total = best + jnp.log(total * jnp.exp(top - best) + their_total * jnp.exp(their_top - best))

    tmpa[0 : 2 * MSLOT, :] = jnp.where(
        column == 0, log_total, jnp.where(column == 1, target_col, jnp.where(column == 2, weight_col, 0.0))
    )
    lsb[c] = jnp.transpose(tmpa[...])[:8]

    def ls_copy(n):
        other = lax.rem(c + n, 16)
        return remote(lsb.at[c], lsb.at[c], ls_send.at[n], ls_recv.at[n], (r, other))

    def ls_in(n):
        other = lax.rem(c + 16 - n, 16)
        return remote(lsb.at[other], lsb.at[other], ls_send.at[n], ls_recv.at[n], (r, other))

    def ls_start(n, _):
        ls_copy(n).start()
        return 0

    def ls_done(n, _):
        ls_copy(n).wait_send()
        ls_in(n).wait_recv()
        return 0

    lax.fori_loop(1, 16, ls_start, 0)
    gpk[...] = jnp.zeros_like(gpk)

    def grad_band(v, _):
        value = jnp.exp(lt[v] - log_total) - jnp.where(band_hit(v, target_col), 1.0, 0.0)
        gpk[...] += nt((value * weight_col).astype(low_type), hn[:, band(v)])
        return 0

    lax.fori_loop(0, BANDS, grad_band, 0)
    gps[...] = gpk[other_rows, :].astype(low_type)
    swap_grad = swap(2, gps, gpr, d_y)
    swap_grad.start()
    picked_third(1)
    picked_last(0)
    leader = jnp.where(r == 0, 1.0, 0.0)
    loss_part = jnp.sum((log_total * leader - chosen) * weight_col, axis=0, keepdims=True)
    swap_grad.wait()
    grad_picked = (gpk[own_rows, :] + gpr[...].astype(wide)).astype(low_type)
    grad_final = nn(selector.astype(low_type), grad_picked)
    _, scaled, inverse = normed(st2[...], gain(2), shift(2))
    grad_last, grad_gain, grad_shift = normed_back(grad_final, scaled, inverse, gain(2))
    st2[...] = grad_last
    g2b[...] = grad_last.astype(low_type)
    gst[4:5, :] = grad_gain
    gst[5:6, :] = grad_shift
    gacc[...] = jnp.zeros_like(gacc)
    picked_last(1)

    def pair_region(n):
        return rk.at[lax.rem(n, 4)]

    def rs_copy(n, index, src, dst, device):
        return remote(src, dst, rs_send.at[n, index], rs_recv.at[n, index], device)

    lo, hi = pl.ds(0, 2), pl.ds(2, 2)

    def sums_moves(n):
        rows = unit_rows(UNITS - 1 - n)
        zero = [rs_copy(n, 0, wg.at[:, :, 1 - k, rows, :], rk.at[lax.rem(n, 4)], d_k)]
        one = [
            rs_copy(n, 1, wg.at[lo, :, k, rows, lanes(1 - r)], r1a.at[lax.rem(n, 7)], d_y),
            rs_copy(n, 2, wg.at[hi, 1 - x, k, rows, :], r1b.at[lax.rem(n, 7)], d_x),
        ]
        two = [
            rs_copy(n, 3, wg.at[lo, 1 - x, k, rows, lanes(r)], r2a.at[lax.rem(n, 7)], d_x),
            rs_copy(n, 4, wg.at[hi, x, k, rows, lanes(1 - r)], r2b.at[lax.rem(n, 7)], d_y),
        ]
        three = [
            rs_copy(n, 4 + m, wg.at[lax.rem(z + m, 4), x, k, rows, lanes(r)], rz.at[lax.rem(n, 7), m - 1], d_z(m))
            for m in (1, 2, 3)
        ]
        return zero, one, two, three

    def sum_start(copies):
        for copy in copies:
            copy.start()

    def sum_land(copies):
        for copy in copies:
            copy.wait_recv()

    def fold(region, value):
        wg[region] = (wg[region].astype(wide) + value.astype(wide)).astype(low_type)

    def sums_one(n):
        rows = unit_rows(UNITS - 1 - n)
        zero, one, _, _ = sums_moves(n)
        sum_land(zero)
        fold((slice(None), slice(None), k, rows, slice(None)), rk[lax.rem(n, 4)])
        sum_start(one)

    def sums_two(n):
        rows = unit_rows(UNITS - 1 - n)
        _, one, two, _ = sums_moves(n)
        sum_land(one)
        fold((lo, slice(None), k, rows, lanes(r)), r1a[lax.rem(n, 7)])
        fold((hi, x, k, rows, slice(None)), r1b[lax.rem(n, 7)])
        sum_start(two)

    def sums_three(n):
        rows = unit_rows(UNITS - 1 - n)
        _, _, two, three = sums_moves(n)
        sum_land(two)
        fold((lo, x, k, rows, lanes(r)), r2a[lax.rem(n, 7)])
        fold((hi, x, k, rows, lanes(r)), r2b[lax.rem(n, 7)])
        sum_start(three)

    def sums_four(n):
        rows = unit_rows(UNITS - 1 - n)
        _, _, _, three = sums_moves(n)
        sum_land(three)
        value = wg[z, x, k, rows, lanes(r)].astype(wide)
        for m in range(3):
            value = value + rz[lax.rem(n, 7), m].astype(wide)
        gout[rows, :] = value
        sq[2, 0:1, 0:128] += jnp.sum(jnp.sum(value * value, axis=0, keepdims=True), axis=1, keepdims=True)

    def sums_sent(n, _):
        for moves in sums_moves(n):
            sent([(copy, None) for copy in moves])
        return 0

    def back_down(j):
        grad_act = nt(g2b[...], square(9 + j))
        value = hpre[j]
        phi_total, density = gelu_parts(value)
        grad_pre = (grad_act * (phi_total + value * density)).astype(low_type)
        set_square(9 + j, tn(hact[j], g2b[...]))
        hact[j] = grad_pre

    def back_up(j):
        gacc[...] += nn(hact[j], square(5 + j))
        set_square(5 + j, tn(hact[j], n2[...]))

    def back_output():
        _, scaled, inverse = normed(st1[...], gain(1), shift(1))
        down, grad_gain, grad_shift = normed_back(gacc[...], scaled, inverse, gain(1))
        gst[2:3, :] = grad_gain
        gst[3:4, :] = grad_shift
        down = down + st2[...]
        st2[...] = down
        g2b[...] = down.astype(low_type)
        grad_mix = nt(g2b[...], square(4)).astype(low_type)
        set_square(4, tn(mix[...], g2b[...]))
        mix[...] = grad_mix

    def back_attention():
        def one_pair(p, _):
            query2, key2, probs = pair_probs(p)
            value2 = qkv[:, pair_lanes(2, p)]
            upstream = twice(mix[:, pair_lanes(0, p)])
            grad_probs = nt(upstream, value2)
            centered = grad_probs - jnp.sum(probs * grad_probs, axis=1, keepdims=True)
            grad_scores = (probs * centered).astype(low_type)
            scale = 1.0 / math.sqrt(HD)
            grad_query = once(nn(grad_scores, key2)) * scale
            grad_key = tn(grad_scores, query2) * scale
            grad_value = tn(probs.astype(low_type), upstream)
            qkv[:, pair_lanes(0, p)] = grad_query.astype(low_type)
            qkv[:, pair_lanes(1, p)] = grad_key.astype(low_type)
            qkv[:, pair_lanes(2, p)] = grad_value.astype(low_type)
            return 0

        lax.fori_loop(0, HEADS // 2, one_pair, 0)
        gacc[...] = nn(qkv[...], triple())
        wg[:, :, :, UNIT : 4 * UNIT, :] = (
            tn(qkv[...], n1[...]).astype(low_type).reshape(4, 2, 2, 3 * UNIT, 2 * half)
        )

    def back_patch():
        _, scaled, inverse = normed(st0[...], gain(0), shift(0))
        down, grad_gain, grad_shift = normed_back(gacc[...], scaled, inverse, gain(0))
        grad = down + st2[...]
        grad_patch = jnp.where(jnp.logical_or(opening, masked), 0.0, grad).astype(low_type)
        set_square(0, nn(px[:, 0:TOK], grad_patch))
        lines = [
            grad[0:1],
            jnp.sum(jnp.where(masked, grad, 0.0), axis=0, keepdims=True),
            grad_gain, grad_shift, gst[2:3, :], gst[3:4, :], gst[4:5, :], gst[5:6, :],
        ]
        for n, line in enumerate(lines):
            grad = jnp.where(token == SEQ + n, line, grad)
        tab[0:TOK, :] = grad.astype(low_type)
        tab[TOK:, :] = jnp.zeros((tab.shape[0] - TOK, tab.shape[1]), low_type)

    tab_half = tab.shape[0] // 2
    rows_own = pl.ds(pl.multiple_of(k * tab_half, 16), tab_half)
    rows_other = pl.ds(pl.multiple_of((1 - k) * tab_half, 16), tab_half)
    d_z1 = (r, (z + 1 - 2 * (z % 2)) * 4 + x * 2 + k)
    d_z2 = (r, lax.rem(z + 2, 4) * 4 + x * 2 + k)
    own_part = tab.at[rows_own, lanes(r)]
    tab_moves = [
        remote(tab.at[rows_other, :], tabk, tab_send.at[0], tab_recv.at[0], d_k),
        remote(tab.at[rows_own, lanes(1 - r)], tabr.at[0], tab_send.at[1], tab_recv.at[1], d_y),
        remote(own_part, tabr.at[1], tab_send.at[2], tab_recv.at[2], d_x),
        remote(own_part, tabr.at[2], tab_send.at[3], tab_recv.at[3], d_z1),
        remote(own_part, tabr.at[3], tab_send.at[4], tab_recv.at[4], d_z2),
        remote(own_part, tabr.at[4], tab_send.at[5], tab_recv.at[5], d_k),
    ]

    def tab_step(n):
        tab_moves[n].wait()
        if n == 0:
            tab[rows_own, :] = (
                tab[rows_own, :].astype(wide) + tabk[...].astype(wide)
            ).astype(low_type)
        elif n < 5:
            tab[rows_own, lanes(r)] = (
                tab[rows_own, lanes(r)].astype(wide) + tabr[n - 1].astype(wide)
            ).astype(low_type)
        if n < 5:
            tab_moves[n + 1].start()

    def gh_moves(n):
        own, other = band(k * (BANDS // 2) + n), band((1 - k) * (BANDS // 2) + n)
        keep = pltpu.make_async_copy(hn.at[:, own], ghead.at[:, own], gh_sem.at[n])
        give = remote(hn.at[:, own], ghead.at[:, own], gh_send.at[n], gh_recv.at[n], d_k)
        take = remote(hn.at[:, other], ghead.at[:, other], gh_send.at[n], gh_recv.at[n], d_k)
        return keep, give, take

    def head_logits(n):
        v = k * (BANDS // 2) + n

        def rows_block(m, _):
            at = pl.ds(pl.multiple_of(m * 8 * MSLOT, 128), 8 * MSLOT)
            value = nn(pk[m].reshape(8 * MSLOT, 2 * half), hn[:, band(v)])
            cols = colb[at, :]
            hit = jnp.where(band_hit(v, cols[:, 1:2]), 1.0, 0.0)
            gch[at, :] = ((jnp.exp(value - cols[:, 0:1]) - hit) * cols[:, 2:3]).astype(low_type)
            return 0

        lax.fori_loop(0, 4, rows_block, 0)

    def head_grad(n):
        value = nn(pkt[...], gch[...])
        sq[3, 0:1, 0:128] += jnp.sum(jnp.sum(value * value, axis=0, keepdims=True), axis=1, keepdims=True)
        hn[:, band(k * (BANDS // 2) + n)] = value.astype(low_type)
        keep, give, _ = gh_moves(n)
        keep.start()
        give.start()

    def head_ready():
        for n in range(2):
            picked_done(n)
        lax.fori_loop(1, 16, ls_done, 0)

        def to_columns(n, _):
            flip[0:8, :] = lsb[n]
            colb[pl.ds(pl.multiple_of(n * 2 * MSLOT, 16), 2 * MSLOT), :] = jnp.transpose(flip[...])[: 2 * MSLOT]
            return 0

        lax.fori_loop(0, 16, to_columns, 0)

        def turn(n, _):
            rows = pk[n].reshape(8 * MSLOT, 2 * half)
            pkt[:, pl.ds(pl.multiple_of(n * 8 * MSLOT, 128), 8 * MSLOT)] = jnp.transpose(rows)
            return 0

        lax.fori_loop(0, 4, turn, 0)

    def back_step(s, _):
        def work(q, _):
            w = jnp.where(s <= 4, 2 * s - 1 + q, s + 4 + 6 * q)

            @pl.when(jnp.logical_and(w >= 0, w < 4))
            def _():
                back_down(3 - w)

            @pl.when(jnp.logical_and(w >= 4, w < 8))
            def _():
                back_up(7 - w)

            @pl.when(w == 8)
            def _():
                back_output()

            @pl.when(w == 9)
            def _():
                back_attention()

            @pl.when(w == 10)
            def _():
                back_patch()

            return 0

        lax.fori_loop(0, 2, work, 0)

        @pl.when(s < UNITS)
        def _():
            sum_start(sums_moves(s)[0])

        @pl.when(jnp.logical_and(s >= 1, s < UNITS + 1))
        def _():
            sums_one(s - 1)

        @pl.when(jnp.logical_and(s >= 3, s < UNITS + 3))
        def _():
            sums_two(s - 3)

        @pl.when(jnp.logical_and(s >= 5, s < UNITS + 5))
        def _():
            sums_three(s - 5)

        @pl.when(s >= 7)
        def _():
            sums_four(s - 7)

        @pl.when(s == 2)
        def _():
            head_ready()

        @pl.when(s == 6)
        def _():
            tab_moves[0].start()

        for n in range(6):
            @pl.when(s == 7 + 2 * n)
            def _():
                tab_step(n)

        @pl.when(jnp.logical_and(s >= G_FIRST, s < G_FIRST + BANDS))
        def _():
            @pl.when((s - G_FIRST) % 2 == 0)
            def _():
                head_logits((s - G_FIRST) // 2)

            @pl.when((s - G_FIRST) % 2 == 1)
            def _():
                head_grad((s - G_FIRST) // 2)

        return 0

    lax.fori_loop(0, UNITS + 7, back_step, 0)
    gtab_out[rows_own, :] = tab[rows_own, lanes(r)].astype(wide)
    gtab_out[rows_other, :] = tabr[4].astype(wide)
    value = gtab_out[...]
    first_col = jnp.where(c == 0, 1.0, 0.0)
    first_chip = jnp.where(c < 2, 1.0, 0.0)
    table_squares = jnp.sum(jnp.sum(value * value, axis=0, keepdims=True), axis=1, keepdims=True)
    line = lax.broadcasted_iota(jnp.int32, (8, 128), 0)
    squares = sq[2, 0:1, 0:128] + sq[3, 0:1, 0:128] * first_chip + table_squares * first_col
    count = (counts[0] + counts[1]).astype(wide) * leader
    fin[r * 16 + c] = jnp.where(
        line == 0, loss_part, jnp.where(line == 1, count, jnp.where(line == 2, squares, 0.0))
    )

    def fin_copy(n, step):
        other = lax.rem(r * 16 + c + step, 32)
        owner = r * 16 + c if n == 0 else lax.rem(r * 16 + c + 32 - step, 32)
        ref = fin.at[owner]
        return remote(ref, ref, fin_send.at[step], fin_recv.at[step], (other // 16, other % 16))

    def fin_start(step, _):
        fin_copy(0, step).start()
        return 0

    def fin_done(step, _):
        fin_copy(0, step).wait_send()
        fin_copy(1, step).wait_recv()
        return 0

    lax.fori_loop(1, 32, fin_start, 0)
    lax.fori_loop(0, UNITS, sums_sent, 0)
    for n in range(2):
        for moves in picked_moves(n):
            sent(moves)
    for n in range(BANDS // 2):
        keep, give, take = gh_moves(n)
        keep.wait()
        give.wait_send()
        take.wait_recv()
    lax.fori_loop(1, 32, fin_done, 0)
    totals = jnp.sum(fin[...], axis=0)
    count_total = totals[1:2, :]
    norm_value = jnp.sqrt(totals[2:3, :]) / count_total
    scal_out[0:1, :] = totals[0:1, :] / count_total
    scal_out[1:2, :] = norm_value
    scal_out[2:3, :] = jnp.minimum(1.0, clip_limit / norm_value) / count_total
    scal_out[3:8, :] = jnp.zeros((5, 128), wide)


def step_call(pix, blocks, tab, places, targets, counts, head):
    half = tab.shape[1]
    full = 2 * half
    vocab = head.shape[1]
    slots = 32 * MSLOT
    vm = pltpu.VMEM
    dma = pltpu.SemaphoreType.DMA
    f32, b16 = wide, low_type
    scratch = [
        vm((4, 2, 2, UNITS * UNIT, full), b16),
        vm((2, 8, UNIT, 256), b16),
        vm((8, UNIT, 256), b16),
        vm((16 * UNIT, 256), b16),
        vm((TOK, full), f32),
        vm((TOK, full), f32), vm((TOK, full), f32), vm((TOK, full), f32),
        vm((TOK, full), b16), vm((TOK, full), b16), vm((TOK, full), b16),
        vm((TOK, 3 * full), b16),
        vm((4, TOK, full), f32),
        vm((4, TOK, full), b16),
        vm((full, vocab), b16),
        vm((2, full, 256), f32),
        vm((4, 2, 2, 2 * MSLOT, full), b16),
        vm((MSLOT, full), b16),
        vm((2 * MSLOT, full), b16),
        vm((BANDS, 2 * MSLOT, 512), f32),
        vm((full, slots), b16),
        vm((slots, 512), b16),
        vm((slots, 128), f32),
        vm((4, 8, 256), f32),
        vm((16, 8, 256), f32),
        vm((128, 256), f32),
        vm((256, 128), f32),
        vm((2 * MSLOT, full), f32),
        vm((MSLOT, full), b16), vm((MSLOT, full), b16),
        vm((TOK, full), b16),
        vm((TOK, full), f32),
        vm((8, full), f32),
        vm((4, 4, 2, UNIT, full), b16),
        vm((7, 2, 2, UNIT, half), b16),
        vm((7, 2, UNIT, full), b16),
        vm((7, 2, UNIT, half), b16),
        vm((7, 2, UNIT, half), b16),
        vm((7, 3, UNIT, half), b16),
        vm((224, full), b16),
        vm((112, full), b16),
        vm((5, 112, half), b16),
        vm((32, 8, 128), f32),
        dma((UNITS, 12)), dma((UNITS, 12)),
        dma((2,)), dma((2, 8)), dma((16,)),
        dma((2, 2)),
        dma((2, 12)), dma((2, 12)),
        dma((3,)), dma((3,)),
        dma((16,)), dma((16,)),
        dma((UNITS, 8)), dma((UNITS, 8)),
        dma((6,)), dma((6,)),
        dma((32,)), dma((32,)),
        dma((2,)),
        dma((BANDS // 2,)), dma((BANDS // 2,)), dma((BANDS // 2,)),
    ]
    in_vmem = pl.BlockSpec(memory_space=pltpu.VMEM)
    return pl.pallas_call(
        step_kernel,
        out_shape=(
            jax.ShapeDtypeStruct((UNITS * UNIT, half), f32),
            jax.ShapeDtypeStruct((224, half), f32),
            jax.ShapeDtypeStruct((full, vocab), b16),
            jax.ShapeDtypeStruct((8, 128), f32),
        ),
        in_specs=[
            *([in_vmem] * 9),
            pl.BlockSpec(memory_space=pltpu.SMEM),
            pl.BlockSpec(memory_space=pl.ANY),
        ],
        out_specs=(in_vmem, in_vmem, pl.BlockSpec(memory_space=pl.ANY), in_vmem),
        scratch_shapes=scratch,
        compiler_params=pltpu.CompilerParams(
            collective_id=0, has_side_effects=True, vmem_limit_bytes=VMEM_LIMIT
        ),
        cost_estimate=pl.CostEstimate(flops=50_000_000_000, bytes_accessed=40_000_000, transcendentals=0),
    )(pix, *blocks, tab, places, targets, counts, head)


def block_path(
    pixels, mask_places, mask_count, targets, step_count,
    patch_weight, vector_table, input_weight, output_weight, upward_weight, downward_weight, head_weight,
    *moments,
):
    weights = (
        patch_weight, vector_table, input_weight, output_weight, upward_weight, downward_weight, head_weight,
    )
    weights = flat(weights)
    blocks = [weights[n] for n in (0, 2, 3, 4, 5)]
    gout, gtab, ghead, scal = step_call(
        pixels.T, blocks, vector_table, mask_places, targets, mask_count, head_weight
    )
    results = adam_call(
        scal, step_count, gout, gtab, ghead, weights, flat(moments[:7]), flat(moments[7:])
    )
    triples = [results[2 + n :: 3] for n in range(3)]
    triples = [unflat(triple) for triple in triples]
    return (*results[:2], *(triple[n] for n in range(7) for triple in triples))


def flat(values):
    patch, table, inward, outward, up, down, head = values
    return (patch, table, inward[0].T, outward[0], up[0].T, down[0], head)


def unflat(values):
    patch, table, inward, outward, up, down, head = values
    return (patch, table, inward.T[None], outward[None], up.T[None], down[None], head)


SMALL = UNITS * UNIT
ROWS = 48
IN_SLOTS = 4
OUT_SLOTS = 3


def adam_kernel(
    scal, step, gout, gtab, ghead, *refs
):
    weights, drifts, powers = refs[:7], refs[7:14], refs[14:21]
    loss_out, norm_out = refs[21:23]
    outs = refs[23:44]
    gbuf, inbuf, outbuf, gsm, insm, outsm, gtb, intb, outtb, in_sem, out_sem, sm_in, sm_out = refs[44:]
    factor = scal[2:3, 0:1]
    count = jnp.full((1, 128), step[0], jnp.int32).astype(wide)[:, 0:1]
    scale_first = 1.0 / (1.0 - jnp.exp(count * math.log(beta_first)))
    scale_second = 1.0 / (1.0 - jnp.exp(count * math.log(beta_second)))
    count_first = scale_first * -learn_rate
    gain_first = factor * (1.0 - beta_first)
    gain_second = factor * factor * (1.0 - beta_second)
    chunks = ghead.shape[0] // ROWS
    states = (weights, drifts, powers)

    def rows_of(n):
        return pl.ds(pl.multiple_of(n * ROWS, ROWS), ROWS)

    def fetch(n):
        slot = lax.rem(n, IN_SLOTS)
        copies = [
            pltpu.make_async_copy(states[m][6].at[rows_of(n)], inbuf.at[slot, m], in_sem.at[slot, m])
            for m in range(3)
        ]
        copies.append(pltpu.make_async_copy(ghead.at[rows_of(n)], gbuf.at[slot], in_sem.at[slot, 3]))
        return copies

    def store(n):
        slot = lax.rem(n, OUT_SLOTS)
        return [
            pltpu.make_async_copy(outbuf.at[slot, m], outs[18 + m].at[rows_of(n)], out_sem.at[slot, m])
            for m in range(3)
        ]

    order = (0, 2, 3, 4, 5)
    small_fetch, small_store = [], []
    start = 0
    for at, n in enumerate(order):
        height = weights[n].shape[0]
        for m in range(3):
            small_fetch.append(
                pltpu.make_async_copy(states[m][n], insm.at[m, start : start + height], sm_in.at[at, m])
            )
            small_store.append(
                pltpu.make_async_copy(outsm.at[m, start : start + height], outs[3 * n + m], sm_out.at[at, m])
            )
        start += height
    for m in range(3):
        small_fetch.append(pltpu.make_async_copy(states[m][1], intb.at[m], sm_in.at[5, m]))
        small_store.append(pltpu.make_async_copy(outtb.at[m], outs[3 + m], sm_out.at[5, m]))
    small_fetch.append(pltpu.make_async_copy(gout, gsm, sm_in.at[6, 0]))
    small_fetch.append(pltpu.make_async_copy(gtab, gtb, sm_in.at[6, 1]))

    def adam(grad, weight, drift, power):
        new_drift = beta_first * drift + gain_first * grad
        new_power = beta_second * power + gain_second * (grad * grad)
        below = jnp.sqrt(new_power * scale_second) + adam_eps
        update = new_drift * count_first / below - (learn_rate * weight_decay) * weight
        return update, new_drift, new_power

    for n in range(IN_SLOTS):
        for copy in fetch(n):
            copy.start()
    for copy in small_fetch:
        copy.start()
    loss_out[...] = scal[0:1, 0:1]
    norm_out[...] = scal[1:2, 0:1]

    def chunk(n, _):
        for copy in fetch(n):
            copy.wait()

        @pl.when(n >= OUT_SLOTS)
        def _():
            for copy in store(n - OUT_SLOTS):
                copy.wait()

        slot, spot = lax.rem(n, IN_SLOTS), lax.rem(n, OUT_SLOTS)

        def part(q, _):
            at = pl.ds(pl.multiple_of(q * 16, 16), 16)
            values = adam(
                gbuf[slot, at, :].astype(wide), inbuf[slot, 0, at, :], inbuf[slot, 1, at, :],
                inbuf[slot, 2, at, :],
            )
            for m in range(3):
                outbuf[spot, m, at, :] = values[m]
            return 0

        lax.fori_loop(0, ROWS // 16, part, 0)
        for copy in store(n):
            copy.start()

        @pl.when(n + IN_SLOTS < chunks)
        def _():
            for copy in fetch(n + IN_SLOTS):
                copy.start()

        @pl.when(n == 2)
        def _():
            for copy in small_fetch:
                copy.wait()

            def small(q, _):
                at = pl.ds(pl.multiple_of(q * UNIT, UNIT), UNIT)
                values = adam(gsm[at, :], insm[0, at, :], insm[1, at, :], insm[2, at, :])
                for m in range(3):
                    outsm[m, at, :] = values[m]
                return 0

            lax.fori_loop(0, UNITS, small, 0)
            values = adam(gtb[0 : intb.shape[1]], intb[0], intb[1], intb[2])
            for m in range(3):
                outtb[m] = values[m]
            for copy in small_store:
                copy.start()

        return 0

    lax.fori_loop(0, chunks, chunk, 0)
    for n in range(chunks - OUT_SLOTS, chunks):
        for copy in store(n):
            copy.wait()
    for copy in small_store:
        copy.wait()


def adam_call(scal, step, gout, gtab, ghead, weights, drifts, powers):
    half = gout.shape[1]
    vocab = ghead.shape[1]
    table = weights[1].shape[0]
    one = jax.ShapeDtypeStruct((1, 1), wide)
    shapes = [jax.ShapeDtypeStruct(value.shape, wide) for value in weights for _ in range(3)]
    in_vmem = pl.BlockSpec(memory_space=pltpu.VMEM)
    anywhere = pl.BlockSpec(memory_space=pl.ANY)
    vm, dma = pltpu.VMEM, pltpu.SemaphoreType.DMA
    results = pl.pallas_call(
        adam_kernel,
        in_specs=[in_vmem, pl.BlockSpec(memory_space=pltpu.SMEM)] + [anywhere] * 24,
        out_specs=[in_vmem] * 2 + [anywhere] * 21,
        out_shape=[one, one] + shapes,
        scratch_shapes=[
            vm((IN_SLOTS, ROWS, vocab), low_type), vm((IN_SLOTS, 3, ROWS, vocab), wide),
            vm((OUT_SLOTS, 3, ROWS, vocab), wide),
            vm((SMALL, half), wide), vm((3, SMALL, half), wide), vm((3, SMALL, half), wide),
            vm(gtab.shape, wide), vm((3, table, half), wide), vm((3, table, half), wide),
            dma((IN_SLOTS, 4)), dma((OUT_SLOTS, 3)), dma((7, 3)), dma((6, 3)),
        ],
        compiler_params=pltpu.CompilerParams(vmem_limit_bytes=VMEM_LIMIT),
        cost_estimate=pl.CostEstimate(flops=60_000_000, bytes_accessed=82_000_000, transcendentals=4_000_000),
    )(scal, step, gout, gtab, ghead, *weights, *drifts, *powers)
    return (results[0].reshape(()), results[1].reshape(()), *results[2:])


def solution(mesh):
    state = (
        P("col", "row"),
        P(None, "row"),
        P(None, "row", "col"),
        P(None, "col", "row"),
        P(None, "row", "col"),
        P(None, "col", "row"),
        P(None, "row"),
    )
    data = (P("row", "col"), P("col", None), P("col"), P("col", None), P())
    outs = (P(), P()) + tuple(spec for spec in state for _ in range(3))
    fits = dict(mesh.shape) == {"row": 2, "col": 16}
    return jax.shard_map(
        block_path if fits else on_device,
        mesh=mesh,
        in_specs=data + state * 3,
        out_specs=outs,
        check_vma=False,
    )
```

```python
import math

import jax
import jax.numpy as jnp
from jax import lax
from jax.experimental import pallas as pl
from jax.experimental.pallas import tpu as pltpu
from jax.sharding import PartitionSpec as P

HEADS = 12
HD = 64
SEQ = 197
MSLOT = 80
BOTH = ("row", "col")

norm_eps = 1e-06
clip_limit = 0.1
learn_rate = 0.01
beta_first = 0.9
beta_second = 0.999
adam_eps = 1e-08
weight_decay = 0.05
low_type = jnp.bfloat16
wide = jnp.float32


def product(left, right):
    return jnp.dot(left, right, preferred_element_type=wide)


def product_nt(left, right):
    return jnp.einsum("ab,cb->ac", left, right, preferred_element_type=wide)


def product_tn(left, right):
    return jnp.einsum("ab,ac->bc", left, right, preferred_element_type=wide)


def norm_forward(values, gain, shift):
    center = jnp.mean(values, axis=1, keepdims=True)
    moved = values - center
    inverse = lax.rsqrt(jnp.mean(moved * moved, axis=1, keepdims=True) + norm_eps)
    scaled = moved * inverse
    return scaled * gain + shift, (scaled, inverse)


def norm_backward(upstream, kept, gain):
    scaled, inverse = kept
    inner = upstream * gain
    downstream = inverse * (
        inner
        - jnp.mean(inner, axis=1, keepdims=True)
        - scaled * jnp.mean(inner * scaled, axis=1, keepdims=True)
    )
    return downstream, jnp.sum(upstream * scaled, axis=0), jnp.sum(upstream, axis=0)


def exact_gelu(values):
    return jax.nn.gelu(values, approximate=False)


def split_heads(grouped):
    images = grouped.shape[0] // SEQ
    pieces = grouped.reshape(images, SEQ, 3, HEADS, HD)
    return pieces[:, :, 0], pieces[:, :, 1], pieces[:, :, 2]


def attention_weights(query, keys):
    scores = jnp.einsum("iqhd,ikhd->ihqk", query, keys, preferred_element_type=wide)
    return jax.nn.softmax(scores * (1.0 / math.sqrt(HD)), axis=-1)


def attend(grouped):
    query, keys, values = split_heads(grouped)
    weights_full = attention_weights(query, keys)
    mixture = jnp.einsum(
        "ihqk,ikhd->iqhd", weights_full.astype(low_type), values, preferred_element_type=wide
    )
    return mixture.reshape(grouped.shape[0], HEADS * HD), weights_full


def attend_back(grouped, weights_full, grad_mixture):
    query, keys, values = split_heads(grouped)
    images = query.shape[0]
    weights_low = weights_full.astype(low_type)
    grad_out = grad_mixture.reshape(images, SEQ, HEADS, HD)
    grad_weights = jnp.einsum("iqhd,ikhd->ihqk", grad_out, values, preferred_element_type=wide)
    grad_values = jnp.einsum("ihqk,iqhd->ikhd", weights_low, grad_out, preferred_element_type=wide)
    centered = grad_weights - jnp.sum(weights_full * grad_weights, axis=-1, keepdims=True)
    grad_scores = (weights_full * centered).astype(low_type)
    scale = 1.0 / math.sqrt(HD)
    grad_query = jnp.einsum("ihqk,ikhd->iqhd", grad_scores, keys, preferred_element_type=wide)
    grad_keys = jnp.einsum("ihqk,iqhd->ikhd", grad_scores, query, preferred_element_type=wide)
    stacked = jnp.stack([grad_query * scale, grad_keys * scale, grad_values], axis=2)
    return stacked.reshape(images * SEQ, 3 * HEADS * HD)


def adam_step(weight, grad, drift, power, factor, step_value):
    scaled = grad * factor
    new_drift = beta_first * drift + (1.0 - beta_first) * scaled
    new_power = beta_second * power + (1.0 - beta_second) * scaled * scaled
    drift_hat = new_drift / (1.0 - jnp.power(beta_first, step_value))
    power_hat = new_power / (1.0 - jnp.power(beta_second, step_value))
    update = -learn_rate * (drift_hat / (jnp.sqrt(power_hat) + adam_eps) + weight_decay * weight)
    return (update, new_drift, new_power)


def on_device(
    pixels,
    mask_places,
    mask_count,
    targets,
    step_count,
    patch_weight,
    vector_table,
    input_weight,
    output_weight,
    upward_weight,
    downward_weight,
    head_weight,
    drift_patch,
    drift_table,
    drift_input,
    drift_output,
    drift_upward,
    drift_downward,
    drift_head,
    power_patch,
    power_table,
    power_input,
    power_output,
    power_upward,
    power_downward,
    power_head,
):
    rows, cols = lax.axis_size("row"), lax.axis_size("col")
    row_index = lax.axis_index("row")
    col_index = lax.axis_index("col")
    images = mask_places.shape[0] // rows
    width = vector_table.shape[1] * rows

    blocks = [
        patch_weight.astype(low_type),
        input_weight[0].astype(low_type).T,
        output_weight[0].astype(low_type),
        upward_weight[0].astype(low_type).T,
        downward_weight[0].astype(low_type),
    ]
    heights = [block.shape[0] for block in blocks]
    gathered = lax.all_gather(jnp.concatenate(blocks, axis=0), BOTH, axis=0, tiled=False)
    gathered = gathered.reshape(rows, cols, sum(heights), -1)

    def whole(index):
        start = sum(heights[:index])
        part = gathered[:, :, start : start + heights[index]]
        return jnp.transpose(part, (1, 2, 0, 3)).reshape(cols * heights[index], width)

    patch_low, input_turned, output_low, upward_turned, downward_low = map(whole, range(5))
    table = lax.all_gather(vector_table, "row", axis=1, tiled=True)

    local_images = pixels.shape[0] // SEQ
    part = pixels.shape[1]
    grid = pixels.reshape(local_images // (rows * images), rows, images, SEQ, part)
    grid = lax.all_to_all(grid, "row", split_axis=1, concat_axis=0, tiled=True)
    grid = grid.reshape(cols, images * SEQ, part)
    grid = lax.all_to_all(grid, "col", split_axis=0, concat_axis=0, tiled=True)
    pixel_own = jnp.transpose(grid, (1, 0, 2)).reshape(images * SEQ, cols * part)

    def own(values):
        return lax.dynamic_slice_in_dim(values, row_index * images, images, axis=0)

    places_own, count_own = own(mask_places), own(mask_count)

    def gains_of(norm_index):
        return (table[SEQ + 2 + 2 * norm_index], table[SEQ + 3 + 2 * norm_index])

    patch_proj = product(pixel_own, patch_low)
    places = jnp.arange(SEQ, dtype=jnp.int32)
    counted_own = jnp.arange(MSLOT, dtype=jnp.int32)[None, :] < count_own[:, None]
    matches = places_own[:, :, None] == places[None, None, :]
    masked = jnp.any(matches & counted_own[:, :, None], axis=1)[:, :, None]
    opening = (places == 0)[None, :, None]
    stream = jnp.where(
        opening,
        table[SEQ],
        jnp.where(masked, table[SEQ + 1], patch_proj.reshape(images, SEQ, -1)),
    )
    stream = (stream + table[:SEQ][None]).reshape(images * SEQ, -1)
    gain_one, shift_one = gains_of(0)
    gain_two, shift_two = gains_of(1)
    final_gain, final_shift = gains_of(2)
    normed_one, stats_one = norm_forward(stream, gain_one, shift_one)
    normed_one = normed_one.astype(low_type)
    grouped = product_nt(normed_one, input_turned).astype(low_type)
    mixture, weights_full = attend(grouped)
    mixture = mixture.astype(low_type)
    stream_mid = stream + product(mixture, output_low)
    normed_two, stats_two = norm_forward(stream_mid, gain_two, shift_two)
    normed_two = normed_two.astype(low_type)
    hidden_pre = product_nt(normed_two, upward_turned)
    hidden_act = exact_gelu(hidden_pre).astype(low_type)
    stream_last = stream_mid + product(hidden_act, downward_low)
    final_out, final_stats = norm_forward(stream_last, final_gain, final_shift)
    selector = matches.astype(low_type)
    picked = jnp.einsum(
        "ims,isd->imd", selector, final_out.astype(low_type).reshape(images, SEQ, -1),
        preferred_element_type=wide,
    ).astype(low_type)

    picked_wide = lax.all_gather(picked.reshape(images * MSLOT, -1), "row", axis=0, tiled=True)
    head_low = head_weight.astype(low_type)
    logits = product(picked_wide, head_low)
    vocab_local = head_weight.shape[1]
    target_local = targets.reshape(-1) - row_index * vocab_local
    target_hits = target_local[:, None] == jnp.arange(vocab_local, dtype=jnp.int32)[None, :]
    chosen = jnp.sum(jnp.where(target_hits, logits, 0.0), axis=1)
    local_top = jnp.max(logits, axis=1)
    local_sum = jnp.sum(jnp.exp(logits - local_top[:, None]), axis=1)
    pair = lax.all_gather(jnp.stack([local_top, local_sum]), "row", axis=0, tiled=False)
    top_value = jnp.max(pair[:, 0], axis=0)
    exp_total = jnp.sum(pair[:, 1] * jnp.exp(pair[:, 0] - top_value), axis=0)
    log_total = top_value + jnp.log(exp_total)
    counted = jnp.arange(MSLOT, dtype=jnp.int32)[None, :] < mask_count[:, None]
    slot_weight = counted.reshape(-1).astype(wide)
    leader_row = (row_index == 0).astype(wide)
    loss_part = jnp.sum(log_total * slot_weight) * leader_row - jnp.sum(chosen * slot_weight)
    count_part = jnp.sum(mask_count.astype(wide)) * leader_row
    grad_logits = (
        (jnp.exp(logits - log_total[:, None]) - target_hits.astype(wide)) * slot_weight[:, None]
    ).astype(low_type)
    grad_head_local = product_tn(picked_wide, grad_logits)
    grad_head = lax.psum(grad_head_local.astype(low_type), "col").astype(wide)
    grad_picked = lax.psum_scatter(
        product_nt(grad_logits, head_low).astype(low_type),
        "row",
        scatter_dimension=0,
        tiled=True,
    )
    grad_final = jnp.einsum(
        "ims,imd->isd", selector, grad_picked.reshape(images, MSLOT, -1),
        preferred_element_type=wide,
    )

    grad_stream, grad_final_gain, grad_final_shift = norm_backward(
        grad_final.reshape(images * SEQ, -1), final_stats, final_gain
    )
    grad_two = grad_stream.astype(low_type)
    grad_downward = product_tn(hidden_act, grad_two)
    grad_act = product_nt(grad_two, downward_low)
    _, gelu_pull = jax.vjp(exact_gelu, hidden_pre)
    grad_pre = gelu_pull(grad_act)[0].astype(low_type)
    grad_upward_turned = product_tn(grad_pre, normed_two)
    grad_normed_two = product(grad_pre, upward_turned)
    grad_mid, grad_gain_two, grad_shift_two = norm_backward(grad_normed_two, stats_two, gain_two)
    grad_mid = grad_mid + grad_stream
    grad_one = grad_mid.astype(low_type)
    grad_output = product_tn(mixture, grad_one)
    grad_mixture = product_nt(grad_one, output_low).astype(low_type)
    grad_grouped = attend_back(grouped, weights_full, grad_mixture).astype(low_type)
    grad_input_turned = product_tn(grad_grouped, normed_one)
    grad_normed_one = product(grad_grouped, input_turned)
    grad_below, grad_gain_one, grad_shift_one = norm_backward(grad_normed_one, stats_one, gain_one)
    grad_grid = (grad_below + grad_mid).reshape(images, SEQ, -1)
    grad_patch = jnp.where(opening | masked, 0.0, grad_grid).reshape(images * SEQ, -1)
    grad_patch_weight = product_tn(pixel_own, grad_patch.astype(low_type))
    lines = [
        jnp.sum(grad_grid, axis=0),
        jnp.sum(grad_grid[:, 0], axis=0)[None],
        jnp.sum(jnp.where(masked, grad_grid, 0.0), axis=(0, 1))[None],
        jnp.stack(
            [grad_gain_one, grad_shift_one, grad_gain_two, grad_shift_two,
             grad_final_gain, grad_final_shift]
        ),
    ]
    table_local = jnp.concatenate(lines, axis=0).astype(low_type)

    def dealt(value, height):
        grid = value.astype(low_type).reshape(cols, height, rows, -1)
        return jnp.transpose(grid, (2, 0, 1, 3)).reshape(rows * cols, height, -1)

    stacked = jnp.concatenate(
        [
            dealt(value, height)
            for value, height in zip(
                [grad_patch_weight, grad_input_turned, grad_output, grad_upward_turned,
                 grad_downward],
                heights,
            )
        ],
        axis=1,
    )
    summed = lax.psum_scatter(stacked, BOTH, scatter_dimension=0, tiled=False).astype(wide)
    starts = [sum(heights[:index]) for index in range(6)]
    pieces = [summed[starts[index] : starts[index + 1]] for index in range(5)]
    grad_table = lax.psum(table_local, BOTH).astype(wide)
    grad_table = lax.dynamic_slice_in_dim(
        grad_table, row_index * vector_table.shape[1], vector_table.shape[1], axis=1
    )
    leader_col = (col_index == 0).astype(wide)
    squares_part = jnp.sum(summed * summed) + leader_col * (
        jnp.sum(grad_table * grad_table) + jnp.sum(grad_head * grad_head)
    )
    loss_total, count_total, squares_total = lax.psum((loss_part, count_part, squares_part), BOTH)
    mean_loss = loss_total / count_total
    grad_norm = jnp.sqrt(squares_total) / count_total
    factor = jnp.minimum(1.0, clip_limit / grad_norm) / count_total
    step_value = step_count[0].astype(wide)
    steps = [
        (patch_weight, pieces[0], drift_patch, power_patch),
        (vector_table, grad_table, drift_table, power_table),
        (input_weight, pieces[1].T[None], drift_input, power_input),
        (output_weight, pieces[2][None], drift_output, power_output),
        (upward_weight, pieces[3].T[None], drift_upward, power_upward),
        (downward_weight, pieces[4][None], drift_downward, power_downward),
        (head_weight, grad_head, drift_head, power_head),
    ]
    results = []
    for weight, grad, drift, power in steps:
        results.extend(adam_step(weight, grad, drift, power, factor, step_value))
    return (mean_loss, grad_norm, *results)


VMEM_LIMIT = 62 * 2**20
TOK = 208
UNIT = 48
UNITS = 13
BANDS = 8
G_FIRST = 7
AHEAD = 2
LAG_A = 1
LAG_B = 3
LAG_C = 4
EYE = pl.DeviceIdType.MESH


def nn(left, right):
    return jnp.dot(left, right, preferred_element_type=wide)


def nt(left, right):
    return lax.dot_general(left, right, (((1,), (1,)), ((), ())), preferred_element_type=wide)


def tn(left, right):
    return lax.dot_general(left, right, (((0,), (0,)), ((), ())), preferred_element_type=wide)


def gelu_parts(values):
    phi_total = 0.5 * (1.0 + lax.erf(values * math.sqrt(0.5)))
    density = jnp.exp(values * values * -0.5) * (1.0 / math.sqrt(2.0 * math.pi))
    return phi_total, density


def normed(values, gain, shift):
    center = jnp.mean(values, axis=1, keepdims=True)
    moved = values - center
    inverse = lax.rsqrt(jnp.mean(moved * moved, axis=1, keepdims=True) + norm_eps)
    scaled = moved * inverse
    return scaled * gain + shift, scaled, inverse


def normed_back(upstream, scaled, inverse, gain):
    inner = upstream * gain
    down = inverse * (
        inner
        - jnp.mean(inner, axis=1, keepdims=True)
        - scaled * jnp.mean(inner * scaled, axis=1, keepdims=True)
    )
    return (
        down,
        jnp.sum(upstream * scaled, axis=0, keepdims=True),
        jnp.sum(upstream, axis=0, keepdims=True),
    )


def step_kernel(
    pix_in, patch_in, input_in, output_in, up_in, down_in, tab_in, places, targets, counts, head_in, drift_in, power_in,
    gout, gtab_out, ghead, scal_out, head_low, drift_low, power_low,
    wg, px_out, px_mid, px, tb, st0, st1, st2, n1, n2, mix, qkv, hpre, hact,
    hn, hbuf, pk, pkp, pp, lt, pkt, gch, colb, sq, lsb, flip, tmpa, gpk, gps, gpr, g2b, gacc, gst,
    rk, r1a, r1b, r2a, r2b, rz, tab, tabk, tabr, fin,
    ag_send, ag_recv, px_sem, px_send, px_recv, tb_sem, pk_send, pk_recv, ex_send, ex_recv,
    ls_send, ls_recv, rs_send, rs_recv, tab_send, tab_recv, fin_send, fin_recv, hb_sem, st_sem, gh_sem, gh_send, gh_recv,
):
    r = lax.axis_index("row")
    c = lax.axis_index("col")
    z, x, k = c // 4, (c // 2) % 2, c % 2
    half = tb.shape[1] // 2
    d_y = (1 - r, c)
    d_x = (r, z * 4 + (1 - x) * 2 + k)
    d_k = (r, z * 4 + x * 2 + 1 - k)

    def d_z(step):
        return (r, lax.rem(z + step, 4) * 4 + x * 2 + k)

    def remote(src, dst, send, recv, device):
        return pltpu.make_async_remote_copy(
            src_ref=src, dst_ref=dst, send_sem=send, recv_sem=recv,
            device_id=device, device_id_type=EYE,
        )

    def lanes(row):
        return pl.ds(pl.multiple_of(row * half, half), half)

    sq[...] = jnp.zeros_like(sq)
    width = px_out.shape[3]
    barrier = pltpu.get_barrier_semaphore()

    def greet(n, _):
        other = lax.rem(r * 16 + c + n, 32)
        pl.semaphore_signal(barrier, inc=1, device_id=(other // 16, other % 16), device_id_type=EYE)
        return 0

    lax.fori_loop(1, 32, greet, 0)

    for n in range(16):
        px_out[n % 2, n // 2, :, 0:SEQ] = pix_in[:, n * SEQ : (n + 1) * SEQ]
        px_out[n % 2, n // 2, :, SEQ:] = jnp.zeros((UNIT, width - SEQ), low_type)
    heights = (UNIT, 3 * UNIT, UNIT, 4 * UNIT, 4 * UNIT)
    blocks = (
        patch_in[...], input_in[...], output_in[...], up_in[...], down_in[...],
    )
    start = 0
    for height, block in zip(heights, blocks):
        wg[z, x, k, start : start + height, lanes(r)] = block.astype(low_type)
        start += height
    tb[0 : tab_in.shape[0], lanes(r)] = tab_in[...]
    tb[tab_in.shape[0] :, lanes(r)] = jnp.zeros((TOK - tab_in.shape[0], half), wide)
    wide_states = (head_in, drift_in, power_in)
    low_states = (head_low, drift_low, power_low)

    def state_rows(b):
        return pl.ds(pl.multiple_of(b * UNIT, UNIT), UNIT)

    def state_in(a, b):
        return pltpu.make_async_copy(wide_states[a].at[state_rows(b)], hbuf.at[a], hb_sem.at[a])

    wide_part = pkt.shape[1]
    rest_part = hn.shape[1] - wide_part

    def state_out(a, b):
        rows = state_rows(b)
        if a == 0:
            return [pltpu.make_async_copy(hn.at[rows], head_low.at[rows], st_sem.at[0])]
        first = pkt.at[UNIT * (a - 1) : UNIT * a]
        second = pkt.at[UNIT * (a + 1) : UNIT * (a + 2), 0:rest_part]
        low = low_states[a]
        return [
            pltpu.make_async_copy(first, low.at[rows, 0:wide_part], st_sem.at[a]),
            pltpu.make_async_copy(second, low.at[rows, wide_part:], st_sem.at[a + 2]),
        ]

    for a in range(3):
        state_in(a, 0).start()
    pl.semaphore_wait(barrier, 31)

    def gather_moves(buf, part, both, send, recv):
        lo, hi = pl.ds(0, 2), pl.ds(2, 2)
        every = slice(None)
        other = lax.rem

        def move(index, out_region, in_region, device):
            out_ref = buf.at[out_region]
            in_ref = buf.at[in_region]
            return (
                remote(out_ref, out_ref, send.at[index], recv.at[index], device),
                remote(in_ref, in_ref, send.at[index], recv.at[index], device),
            )

        first = [
            move(n - 1, (z, x, k) + part(r), (lax.rem(z + 4 - n, 4), x, k) + part(r), d_z(n))
            for n in (1, 2, 3)
        ]
        second = [
            move(3, (lo, x, k) + part(r), (lo, 1 - x, k) + part(r), d_x),
            move(4, (hi, x, k) + part(r), (hi, x, k) + part(1 - r), d_y),
        ]
        pair_one = [move(5, (every, x, k) + part(r), (every, x, 1 - k) + part(r), d_k)]
        third = [
            move(6, (lo, every, k) + part(r), (lo, every, k) + part(1 - r), d_y),
            move(7, (hi, x, k) + both, (hi, 1 - x, k) + both, d_x),
        ]
        pair_two = [
            move(8, (lo, 1 - x, k) + part(r), (lo, 1 - x, 1 - k) + part(r), d_k),
            move(9, (hi, x, k) + part(1 - r), (hi, x, 1 - k) + part(1 - r), d_k),
        ]
        pair_three = [
            move(10, (lo, every, k) + part(1 - r), (lo, every, 1 - k) + part(1 - r), d_k),
            move(11, (hi, 1 - x, k) + both, (hi, 1 - x, 1 - k) + both, d_k),
        ]
        return first, second, pair_one, third, pair_two, pair_three

    def begin(moves):
        for out_copy, _ in moves:
            out_copy.start()

    def landed(moves):
        for _, in_copy in moves:
            in_copy.wait_recv()

    def sent(moves):
        for out_copy, _ in moves:
            out_copy.wait_send()

    def unit_rows(n):
        return pl.ds(pl.multiple_of(n * UNIT, UNIT), UNIT)

    def weight_moves(n):
        rows = unit_rows(n)
        return gather_moves(
            wg, lambda row: (rows, lanes(row)), (rows, slice(None)), ag_send.at[n], ag_recv.at[n]
        )

    late = UNITS - 1

    def late_moves():
        rows = unit_rows(late)
        every = slice(None)

        def move(index, out_region, in_region, device):
            out_ref, in_ref = wg.at[out_region], wg.at[in_region]
            send, recv = ag_send.at[late, index], ag_recv.at[late, index]
            return remote(out_ref, out_ref, send, recv, device), remote(in_ref, in_ref, send, recv, device)

        one = [move(0, (z, x, k, rows, lanes(r)), (z, 1 - x, k, rows, lanes(r)), d_x)]
        two = [move(1, (z, every, k, rows, lanes(r)), (z, every, k, rows, lanes(1 - r)), d_y)]
        three = [
            move(1 + n, (z, every, k, rows, every), (lax.rem(z + 4 - n, 4), every, k, rows, every), d_z(n))
            for n in (1, 2, 3)
        ]
        four = [move(5, (every, every, k, rows, every), (every, every, 1 - k, rows, every), d_k)]
        return one, two, three, four

    def picked_moves(n):
        cut = lanes(n)
        return gather_moves(
            pk, lambda row: (pl.ds(pl.multiple_of(row * MSLOT, 16), MSLOT), cut),
            (slice(None), cut), pk_send.at[n], pk_recv.at[n],
        )

    px_swap = remote(px_out.at[1 - r], px_mid, px_sem.at[0], px_sem.at[1], d_y)

    def px_slot(n):
        return px.at[pl.ds(pl.multiple_of(n * UNIT, UNIT), UNIT)]

    def px_move(part, n):
        target = 8 * (r if part == 0 else 1 - r) + n
        src = px_out.at[r, n] if part == 0 else px_mid.at[n]
        return target, remote(src, px_slot(c), px_send.at[part, n], px_recv.at[c], (r, target))

    def px_start(part):
        def one(n, _):
            target, copy = px_move(part, n)

            @pl.when(target == c)
            def _():
                px[pl.ds(pl.multiple_of(c * UNIT, UNIT), UNIT), :] = (
                    px_out[r, n] if part == 0 else px_mid[n]
                )

            @pl.when(target != c)
            def _():
                copy.start()

            return 0

        lax.fori_loop(0, 8, one, 0)

    def px_done(n, _):
        for part in range(2):
            target, copy = px_move(part, n)

            @pl.when(target != c)
            def _():
                copy.wait_send()

        for source in (n, n + 8):

            @pl.when(source != c)
            def _():
                remote(px_slot(source), px_slot(source), px_send.at[0, n], px_recv.at[source], d_y).wait_recv()

        return 0

    cut_rows = TOK // 2
    own_cut = pl.ds(pl.multiple_of(k * cut_rows, 8), cut_rows)
    other_cut = pl.ds(pl.multiple_of((1 - k) * cut_rows, 8), cut_rows)

    def tb_copy(rows, row, index, device):
        ref = tb.at[rows, lanes(row)]
        return remote(ref, ref, tb_sem.at[index, 0], tb_sem.at[index, 1], device)

    token = lax.broadcasted_iota(jnp.int32, (TOK, 1), 0)
    slot_hit = lax.broadcasted_iota(jnp.int32, (TOK, MSLOT), 0) == places[pl.ds(r, 1), :]
    slot_on = lax.broadcasted_iota(jnp.int32, (TOK, MSLOT), 1) < counts[r]
    selector = jnp.where(slot_hit, 1.0, 0.0)
    masked = jnp.sum(jnp.where(slot_on, selector, 0.0), axis=1, keepdims=True) > 0.5
    opening = token == 0

    def gain(n):
        return tb[SEQ + 2 + 2 * n : SEQ + 3 + 2 * n, :]

    def shift(n):
        return tb[SEQ + 3 + 2 * n : SEQ + 4 + 2 * n, :]

    def square(n):
        return wg[:, :, :, unit_rows(n), :].reshape(16 * UNIT, 2 * half)

    def set_square(n, value):
        wg[:, :, :, unit_rows(n), :] = value.astype(low_type).reshape(4, 2, 2, UNIT, 2 * half)

    def triple():
        return wg[:, :, :, UNIT : 4 * UNIT, :].reshape(48 * UNIT, 2 * half)

    lane_low = lax.broadcasted_iota(jnp.int32, (1, 2 * HD), 1) < HD
    keep_low = jnp.where(lane_low, 1.0, 0.0)
    keep_high = 1.0 - keep_low

    def twice(values):
        return jnp.concatenate(
            [values * keep_low.astype(low_type), values * keep_high.astype(low_type)], axis=0
        )

    def once(values):
        return values[:TOK] * keep_low + values[TOK:] * keep_high

    def pair_lanes(part, p):
        return pl.ds(pl.multiple_of(part * HEADS * HD + p * 2 * HD, 2 * HD), 2 * HD)

    def pair_probs(p):
        query2 = twice(qkv[:, pair_lanes(0, p)])
        key2 = qkv[:, pair_lanes(1, p)]
        scores = nt(query2, key2) * (1.0 / math.sqrt(HD))
        valid = lax.broadcasted_iota(jnp.int32, (1, TOK), 1) < SEQ
        scores = jnp.where(valid, scores, -1e30)
        lifted = jnp.exp(scores - jnp.max(scores, axis=1, keepdims=True))
        return query2, key2, lifted * (1.0 / jnp.sum(lifted, axis=1, keepdims=True))

    def do_patch():
        tb_copy(own_cut, 1 - r, 0, d_y).wait_recv()
        tb_copy(own_cut, 1 - r, 1, d_k).start()
        lax.fori_loop(0, 8, px_done, 0)
        patch = tn(px[...], square(0))[:TOK]
        tb_copy(own_cut, r, 0, d_y).wait_send()
        tb_copy(other_cut, 1 - r, 1, d_k).wait_recv()
        tb_copy(own_cut, 1 - r, 1, d_k).wait_send()
        value = jnp.where(
            opening, tb[SEQ : SEQ + 1, :], jnp.where(masked, tb[SEQ + 1 : SEQ + 2, :], patch)
        )
        value = jnp.where(token < SEQ, value + tb[...], 0.0)
        st0[...] = value
        n1[...] = normed(value, gain(0), shift(0))[0].astype(low_type)

    def do_attention():
        qkv[...] = nt(n1[...], triple()).astype(low_type)

        def one_pair(p, _):
            _, _, probs = pair_probs(p)
            mixed = nn(probs.astype(low_type), qkv[:, pair_lanes(2, p)])
            mix[:, pair_lanes(0, p)] = once(mixed).astype(low_type)
            return 0

        lax.fori_loop(0, HEADS // 2, one_pair, 0)

    def do_output():
        value = st0[...] + nn(mix[...], square(4))
        st1[...] = value
        st2[...] = value
        n2[...] = normed(value, gain(1), shift(1))[0].astype(low_type)

    def do_up(j):
        value = nt(n2[...], square(5 + j))
        hpre[j] = value
        phi_total, _ = gelu_parts(value)
        hact[j] = (value * phi_total).astype(low_type)

    def do_down(j):
        st2[...] += nn(hact[j], square(9 + j))

    begin(late_moves()[0])
    px_swap.start()
    begin(weight_moves(0)[0])
    begin(weight_moves(1)[0])
    px_start(0)
    for n in range(2, AHEAD):
        begin(weight_moves(n)[0])
    tb_copy(own_cut, r, 0, d_y).start()

    def tick(t, _):
        @pl.when(t < late)
        def _():
            first, second, pair_one, _, _, _ = weight_moves(t)
            landed(first)
            begin(second)
            begin(pair_one)

        @pl.when(t == 0)
        def _():
            landed(late_moves()[0])
            begin(late_moves()[1])
            px_swap.wait()
            px_start(1)

        @pl.when(t < late - AHEAD)
        def _():
            begin(weight_moves(t + AHEAD)[0])

        @pl.when(t == late - AHEAD)
        def _():
            landed(late_moves()[1])
            begin(late_moves()[2])

        @pl.when(jnp.logical_and(t >= LAG_A, t < late + LAG_A))
        def _():
            _, second, _, third, pair_two, _ = weight_moves(t - LAG_A)
            landed(second)
            begin(third)
            begin(pair_two)

        @pl.when(t == late + 2)
        def _():
            landed(late_moves()[2])
            begin(late_moves()[3])

        @pl.when(jnp.logical_and(t >= LAG_B, t < late + LAG_B))
        def _():
            _, _, _, third, _, pair_three = weight_moves(t - LAG_B)
            landed(third)
            begin(pair_three)

        @pl.when(jnp.logical_and(t >= LAG_C, t < late + LAG_C))
        def _():
            _, _, pair_one, _, pair_two, pair_three = weight_moves(t - LAG_C)
            landed(pair_one)
            landed(pair_two)
            landed(pair_three)

        @pl.when(t == late + LAG_C)
        def _():
            landed(late_moves()[3])

        @pl.when(t < 16)
        def _():
            for a in range(3):
                state_in(a, t).wait()

                @pl.when(t >= 1)
                def _():
                    for copy in state_out(a, t - 1):
                        copy.wait()

                value = hbuf[a].astype(low_type)
                if a == 0:
                    hn[state_rows(t), :] = value
                else:
                    pkt[UNIT * (a - 1) : UNIT * a, :] = value[:, :wide_part]
                    pkt[UNIT * (a + 1) : UNIT * (a + 2), 0:rest_part] = value[:, wide_part:]
                for copy in state_out(a, t):
                    copy.start()

                @pl.when(t + 1 < 16)
                def _():
                    state_in(a, t + 1).start()

        @pl.when(t == LAG_C + 2)
        def _():
            do_patch()

        @pl.when(t == LAG_C + 3)
        def _():
            do_attention()

        @pl.when(t == LAG_C + 4)
        def _():
            do_output()

        @pl.when(jnp.logical_and(t >= LAG_C + 5, t < LAG_C + 9))
        def _():
            do_up(t - LAG_C - 5)

        @pl.when(t >= LAG_C + 9)
        def _():
            do_down(t - LAG_C - 9)

        return 0

    lax.fori_loop(0, UNITS + LAG_C, tick, 0)

    def all_sent(n, _):
        for moves in weight_moves(n):
            sent(moves)
        return 0

    for a in range(3):
        for copy in state_out(a, 15):
            copy.wait()

    final_out, _, _ = normed(st2[...], gain(2), shift(2))
    picked = tn(selector.astype(low_type), final_out.astype(low_type)).astype(low_type)
    own_rows = pl.ds(pl.multiple_of(r * MSLOT, 16), MSLOT)
    other_rows = pl.ds(pl.multiple_of((1 - r) * MSLOT, 16), MSLOT)
    pp[own_rows, :] = picked
    pk[z, x, k, own_rows, :] = picked

    def swap(index, src, dst, device):
        return remote(src, dst, ex_send.at[index], ex_recv.at[index], device)

    swap_picked = swap(0, pp.at[own_rows, :], pkp, d_y)
    swap_picked.start()
    for n in range(2):
        begin(picked_moves(n)[0])
    lax.fori_loop(0, late, all_sent, 0)
    for moves in late_moves():
        sent(moves)
    flip[...] = jnp.zeros_like(flip)
    flip[0:2, 0:MSLOT] = targets[...].astype(wide)
    info = jnp.transpose(flip[...])
    target_col = jnp.concatenate([info[:MSLOT, 0:1], info[:MSLOT, 1:2]], axis=0)
    slot_line = lax.broadcasted_iota(jnp.int32, (MSLOT, 1), 0)
    weight_col = jnp.concatenate(
        [jnp.where(slot_line < counts[0], 1.0, 0.0), jnp.where(slot_line < counts[1], 1.0, 0.0)], axis=0
    )
    base = (r * (BANDS * 512)).astype(wide)
    band_lane = lax.broadcasted_iota(jnp.int32, (1, 512), 1).astype(wide)

    def band(v):
        return pl.ds(pl.multiple_of(v * 512, 512), 512)

    def band_hit(v, column):
        return (band_lane + (base + (v * 512).astype(wide))) == column

    swap_picked.wait()
    pp[other_rows, :] = pkp[...]

    def picked_second(n):
        first, second, pair_one, _, _, _ = picked_moves(n)
        landed(first)
        begin(second)
        begin(pair_one)

    def picked_third(n):
        _, second, _, third, pair_two, _ = picked_moves(n)
        landed(second)
        begin(third)
        begin(pair_two)

    def picked_last(n):
        _, _, _, third, _, pair_three = picked_moves(n)
        landed(third)
        begin(pair_three)

    def picked_done(n):
        _, _, pair_one, _, pair_two, pair_three = picked_moves(n)
        landed(pair_one)
        landed(pair_two)
        landed(pair_three)

    def logits_band(v, carry):
        top, chosen = carry
        value = nn(pp[...], hn[:, band(v)])
        lt[v] = value
        chosen += jnp.sum(jnp.where(band_hit(v, target_col), value, 0.0), axis=1, keepdims=True)
        return jnp.maximum(top, jnp.max(value, axis=1, keepdims=True)), chosen

    zero_col = jnp.zeros((2 * MSLOT, 1), wide)
    top, chosen = lax.fori_loop(0, BANDS, logits_band, (zero_col - 1e30, zero_col))
    picked_second(0)

    def sum_band(v, total):
        return total + jnp.sum(jnp.exp(lt[v] - top), axis=1, keepdims=True)

    total = lax.fori_loop(0, BANDS, sum_band, zero_col)
    column = lax.broadcasted_iota(jnp.int32, (1, 128), 1)
    tmpa[...] = jnp.zeros_like(tmpa)
    tmpa[0 : 2 * MSLOT, :] = jnp.where(column == 0, top, jnp.where(column == 1, total, 0.0))
    sq[0] = jnp.transpose(tmpa[...])[:8]
    swap_lse = swap(1, sq.at[0], sq.at[1], d_y)
    swap_lse.start()
    picked_second(1)
    picked_third(0)
    swap_lse.wait()
    flip[...] = jnp.zeros_like(flip)
    flip[0:8, :] = sq[1]
    theirs = jnp.transpose(flip[...])[: 2 * MSLOT]
    their_top, their_total = theirs[:, 0:1], theirs[:, 1:2]
    best = jnp.maximum(top, their_top)
    log_total = best + jnp.log(total * jnp.exp(top - best) + their_total * jnp.exp(their_top - best))

    tmpa[0 : 2 * MSLOT, :] = jnp.where(
        column == 0, log_total, jnp.where(column == 1, target_col, jnp.where(column == 2, weight_col, 0.0))
    )
    lsb[c] = jnp.transpose(tmpa[...])[:8]

    def ls_copy(n):
        other = lax.rem(c + n, 16)
        return remote(lsb.at[c], lsb.at[c], ls_send.at[n], ls_recv.at[n], (r, other))

    def ls_in(n):
        other = lax.rem(c + 16 - n, 16)
        return remote(lsb.at[other], lsb.at[other], ls_send.at[n], ls_recv.at[n], (r, other))

    def ls_start(n, _):
        ls_copy(n).start()
        return 0

    def ls_done(n, _):
        ls_copy(n).wait_send()
        ls_in(n).wait_recv()
        return 0

    lax.fori_loop(1, 16, ls_start, 0)
    gpk[...] = jnp.zeros_like(gpk)

    def grad_band(v, _):
        value = jnp.exp(lt[v] - log_total) - jnp.where(band_hit(v, target_col), 1.0, 0.0)
        gpk[...] += nt((value * weight_col).astype(low_type), hn[:, band(v)])
        return 0

    lax.fori_loop(0, BANDS, grad_band, 0)
    gps[...] = gpk[other_rows, :].astype(low_type)
    swap_grad = swap(2, gps, gpr, d_y)
    swap_grad.start()
    picked_third(1)
    picked_last(0)
    leader = jnp.where(r == 0, 1.0, 0.0)
    loss_part = jnp.sum((log_total * leader - chosen) * weight_col, axis=0, keepdims=True)
    swap_grad.wait()
    grad_picked = (gpk[own_rows, :] + gpr[...].astype(wide)).astype(low_type)
    grad_final = nn(selector.astype(low_type), grad_picked)
    _, scaled, inverse = normed(st2[...], gain(2), shift(2))
    grad_last, grad_gain, grad_shift = normed_back(grad_final, scaled, inverse, gain(2))
    st2[...] = grad_last
    g2b[...] = grad_last.astype(low_type)
    gst[4:5, :] = grad_gain
    gst[5:6, :] = grad_shift
    gacc[...] = jnp.zeros_like(gacc)
    picked_last(1)

    def pair_region(n):
        return rk.at[lax.rem(n, 4)]

    def rs_copy(n, index, src, dst, device):
        return remote(src, dst, rs_send.at[n, index], rs_recv.at[n, index], device)

    lo, hi = pl.ds(0, 2), pl.ds(2, 2)

    def sums_moves(n):
        rows = unit_rows(UNITS - 1 - n)
        zero = [rs_copy(n, 0, wg.at[:, :, 1 - k, rows, :], rk.at[lax.rem(n, 4)], d_k)]
        one = [
            rs_copy(n, 1, wg.at[lo, :, k, rows, lanes(1 - r)], r1a.at[lax.rem(n, 7)], d_y),
            rs_copy(n, 2, wg.at[hi, 1 - x, k, rows, :], r1b.at[lax.rem(n, 7)], d_x),
        ]
        two = [
            rs_copy(n, 3, wg.at[lo, 1 - x, k, rows, lanes(r)], r2a.at[lax.rem(n, 7)], d_x),
            rs_copy(n, 4, wg.at[hi, x, k, rows, lanes(1 - r)], r2b.at[lax.rem(n, 7)], d_y),
        ]
        three = [
            rs_copy(n, 4 + m, wg.at[lax.rem(z + m, 4), x, k, rows, lanes(r)], rz.at[lax.rem(n, 7), m - 1], d_z(m))
            for m in (1, 2, 3)
        ]
        return zero, one, two, three

    def sum_start(copies):
        for copy in copies:
            copy.start()

    def sum_land(copies):
        for copy in copies:
            copy.wait_recv()

    def fold(region, value):
        wg[region] = (wg[region].astype(wide) + value.astype(wide)).astype(low_type)

    def sums_one(n):
        rows = unit_rows(UNITS - 1 - n)
        zero, one, _, _ = sums_moves(n)
        sum_land(zero)
        fold((slice(None), slice(None), k, rows, slice(None)), rk[lax.rem(n, 4)])
        sum_start(one)

    def sums_two(n):
        rows = unit_rows(UNITS - 1 - n)
        _, one, two, _ = sums_moves(n)
        sum_land(one)
        fold((lo, slice(None), k, rows, lanes(r)), r1a[lax.rem(n, 7)])
        fold((hi, x, k, rows, slice(None)), r1b[lax.rem(n, 7)])
        sum_start(two)

    def sums_three(n):
        rows = unit_rows(UNITS - 1 - n)
        _, _, two, three = sums_moves(n)
        sum_land(two)
        fold((lo, x, k, rows, lanes(r)), r2a[lax.rem(n, 7)])
        fold((hi, x, k, rows, lanes(r)), r2b[lax.rem(n, 7)])
        sum_start(three)

    def sums_four(n):
        rows = unit_rows(UNITS - 1 - n)
        _, _, _, three = sums_moves(n)
        sum_land(three)
        value = wg[z, x, k, rows, lanes(r)].astype(wide)
        for m in range(3):
            value = value + rz[lax.rem(n, 7), m].astype(wide)
        gout[rows, :] = value
        sq[2, 0:1, 0:128] += jnp.sum(jnp.sum(value * value, axis=0, keepdims=True), axis=1, keepdims=True)

    def sums_sent(n, _):
        for moves in sums_moves(n):
            sent([(copy, None) for copy in moves])
        return 0

    def back_down(j):
        grad_act = nt(g2b[...], square(9 + j))
        value = hpre[j]
        phi_total, density = gelu_parts(value)
        grad_pre = (grad_act * (phi_total + value * density)).astype(low_type)
        set_square(9 + j, tn(hact[j], g2b[...]))
        hact[j] = grad_pre

    def back_up(j):
        gacc[...] += nn(hact[j], square(5 + j))
        set_square(5 + j, tn(hact[j], n2[...]))

    def back_output():
        _, scaled, inverse = normed(st1[...], gain(1), shift(1))
        down, grad_gain, grad_shift = normed_back(gacc[...], scaled, inverse, gain(1))
        gst[2:3, :] = grad_gain
        gst[3:4, :] = grad_shift
        down = down + st2[...]
        st2[...] = down
        g2b[...] = down.astype(low_type)
        grad_mix = nt(g2b[...], square(4)).astype(low_type)
        set_square(4, tn(mix[...], g2b[...]))
        mix[...] = grad_mix

    def back_attention():
        def one_pair(p, _):
            query2, key2, probs = pair_probs(p)
            value2 = qkv[:, pair_lanes(2, p)]
            upstream = twice(mix[:, pair_lanes(0, p)])
            grad_probs = nt(upstream, value2)
            centered = grad_probs - jnp.sum(probs * grad_probs, axis=1, keepdims=True)
            grad_scores = (probs * centered).astype(low_type)
            scale = 1.0 / math.sqrt(HD)
            grad_query = once(nn(grad_scores, key2)) * scale
            grad_key = tn(grad_scores, query2) * scale
            grad_value = tn(probs.astype(low_type), upstream)
            qkv[:, pair_lanes(0, p)] = grad_query.astype(low_type)
            qkv[:, pair_lanes(1, p)] = grad_key.astype(low_type)
            qkv[:, pair_lanes(2, p)] = grad_value.astype(low_type)
            return 0

        lax.fori_loop(0, HEADS // 2, one_pair, 0)
        gacc[...] = nn(qkv[...], triple())
        wg[:, :, :, UNIT : 4 * UNIT, :] = (
            tn(qkv[...], n1[...]).astype(low_type).reshape(4, 2, 2, 3 * UNIT, 2 * half)
        )

    def back_patch():
        _, scaled, inverse = normed(st0[...], gain(0), shift(0))
        down, grad_gain, grad_shift = normed_back(gacc[...], scaled, inverse, gain(0))
        grad = down + st2[...]
        grad_patch = jnp.where(jnp.logical_or(opening, masked), 0.0, grad).astype(low_type)
        set_square(0, nn(px[:, 0:TOK], grad_patch))
        lines = [
            grad[0:1],
            jnp.sum(jnp.where(masked, grad, 0.0), axis=0, keepdims=True),
            grad_gain, grad_shift, gst[2:3, :], gst[3:4, :], gst[4:5, :], gst[5:6, :],
        ]
        for n, line in enumerate(lines):
            grad = jnp.where(token == SEQ + n, line, grad)
        tab[0:TOK, :] = grad.astype(low_type)
        tab[TOK:, :] = jnp.zeros((tab.shape[0] - TOK, tab.shape[1]), low_type)

    tab_half = tab.shape[0] // 2
    rows_own = pl.ds(pl.multiple_of(k * tab_half, 16), tab_half)
    rows_other = pl.ds(pl.multiple_of((1 - k) * tab_half, 16), tab_half)
    d_z1 = (r, (z + 1 - 2 * (z % 2)) * 4 + x * 2 + k)
    d_z2 = (r, lax.rem(z + 2, 4) * 4 + x * 2 + k)
    own_part = tab.at[rows_own, lanes(r)]
    tab_moves = [
        remote(tab.at[rows_other, :], tabk, tab_send.at[0], tab_recv.at[0], d_k),
        remote(tab.at[rows_own, lanes(1 - r)], tabr.at[0], tab_send.at[1], tab_recv.at[1], d_y),
        remote(own_part, tabr.at[1], tab_send.at[2], tab_recv.at[2], d_x),
        remote(own_part, tabr.at[2], tab_send.at[3], tab_recv.at[3], d_z1),
        remote(own_part, tabr.at[3], tab_send.at[4], tab_recv.at[4], d_z2),
        remote(own_part, tabr.at[4], tab_send.at[5], tab_recv.at[5], d_k),
    ]

    def tab_step(n):
        tab_moves[n].wait()
        if n == 0:
            tab[rows_own, :] = (
                tab[rows_own, :].astype(wide) + tabk[...].astype(wide)
            ).astype(low_type)
        elif n < 5:
            tab[rows_own, lanes(r)] = (
                tab[rows_own, lanes(r)].astype(wide) + tabr[n - 1].astype(wide)
            ).astype(low_type)
        if n < 5:
            tab_moves[n + 1].start()

    def gh_moves(n):
        own, other = band(k * (BANDS // 2) + n), band((1 - k) * (BANDS // 2) + n)
        keep = pltpu.make_async_copy(hn.at[:, own], ghead.at[:, own], gh_sem.at[n])
        give = remote(hn.at[:, own], ghead.at[:, own], gh_send.at[n], gh_recv.at[n], d_k)
        take = remote(hn.at[:, other], ghead.at[:, other], gh_send.at[n], gh_recv.at[n], d_k)
        return keep, give, take

    def head_logits(n):
        v = k * (BANDS // 2) + n

        def rows_block(m, _):
            at = pl.ds(pl.multiple_of(m * 8 * MSLOT, 128), 8 * MSLOT)
            value = nn(pk[m].reshape(8 * MSLOT, 2 * half), hn[:, band(v)])
            cols = colb[at, :]
            hit = jnp.where(band_hit(v, cols[:, 1:2]), 1.0, 0.0)
            gch[at, :] = ((jnp.exp(value - cols[:, 0:1]) - hit) * cols[:, 2:3]).astype(low_type)
            return 0

        lax.fori_loop(0, 4, rows_block, 0)

    def head_grad(n):
        value = nn(pkt[...], gch[...])
        sq[3, 0:1, 0:128] += jnp.sum(jnp.sum(value * value, axis=0, keepdims=True), axis=1, keepdims=True)
        hn[:, band(k * (BANDS // 2) + n)] = value.astype(low_type)
        keep, give, _ = gh_moves(n)
        keep.start()
        give.start()

    def head_ready():
        for n in range(2):
            picked_done(n)
        lax.fori_loop(1, 16, ls_done, 0)

        def to_columns(n, _):
            flip[0:8, :] = lsb[n]
            colb[pl.ds(pl.multiple_of(n * 2 * MSLOT, 16), 2 * MSLOT), :] = jnp.transpose(flip[...])[: 2 * MSLOT]
            return 0

        lax.fori_loop(0, 16, to_columns, 0)

        def turn(n, _):
            rows = pk[n].reshape(8 * MSLOT, 2 * half)
            pkt[:, pl.ds(pl.multiple_of(n * 8 * MSLOT, 128), 8 * MSLOT)] = jnp.transpose(rows)
            return 0

        lax.fori_loop(0, 4, turn, 0)

    def back_step(s, _):
        def work(q, _):
            w = jnp.where(s <= 4, 2 * s - 1 + q, s + 4 + 6 * q)

            @pl.when(jnp.logical_and(w >= 0, w < 4))
            def _():
                back_down(3 - w)

            @pl.when(jnp.logical_and(w >= 4, w < 8))
            def _():
                back_up(7 - w)

            @pl.when(w == 8)
            def _():
                back_output()

            @pl.when(w == 9)
            def _():
                back_attention()

            @pl.when(w == 10)
            def _():
                back_patch()

            return 0

        lax.fori_loop(0, 2, work, 0)

        @pl.when(s < UNITS)
        def _():
            sum_start(sums_moves(s)[0])

        @pl.when(jnp.logical_and(s >= 1, s < UNITS + 1))
        def _():
            sums_one(s - 1)

        @pl.when(jnp.logical_and(s >= 3, s < UNITS + 3))
        def _():
            sums_two(s - 3)

        @pl.when(jnp.logical_and(s >= 5, s < UNITS + 5))
        def _():
            sums_three(s - 5)

        @pl.when(s >= 7)
        def _():
            sums_four(s - 7)

        @pl.when(s == 2)
        def _():
            head_ready()

        @pl.when(s == 6)
        def _():
            tab_moves[0].start()

        for n in range(6):
            @pl.when(s == 7 + 2 * n)
            def _():
                tab_step(n)

        @pl.when(jnp.logical_and(s >= G_FIRST, s < G_FIRST + BANDS))
        def _():
            @pl.when((s - G_FIRST) % 2 == 0)
            def _():
                head_logits((s - G_FIRST) // 2)

            @pl.when((s - G_FIRST) % 2 == 1)
            def _():
                head_grad((s - G_FIRST) // 2)

        return 0

    lax.fori_loop(0, UNITS + 7, back_step, 0)
    gtab_out[rows_own, :] = tab[rows_own, lanes(r)].astype(wide)
    gtab_out[rows_other, :] = tabr[4].astype(wide)
    value = gtab_out[...]
    first_col = jnp.where(c == 0, 1.0, 0.0)
    first_chip = jnp.where(c < 2, 1.0, 0.0)
    table_squares = jnp.sum(jnp.sum(value * value, axis=0, keepdims=True), axis=1, keepdims=True)
    line = lax.broadcasted_iota(jnp.int32, (8, 128), 0)
    squares = sq[2, 0:1, 0:128] + sq[3, 0:1, 0:128] * first_chip + table_squares * first_col
    count = (counts[0] + counts[1]).astype(wide) * leader
    fin[r * 16 + c] = jnp.where(
        line == 0, loss_part, jnp.where(line == 1, count, jnp.where(line == 2, squares, 0.0))
    )

    def fin_copy(n, step):
        other = lax.rem(r * 16 + c + step, 32)
        owner = r * 16 + c if n == 0 else lax.rem(r * 16 + c + 32 - step, 32)
        ref = fin.at[owner]
        return remote(ref, ref, fin_send.at[step], fin_recv.at[step], (other // 16, other % 16))

    def fin_start(step, _):
        fin_copy(0, step).start()
        return 0

    def fin_done(step, _):
        fin_copy(0, step).wait_send()
        fin_copy(1, step).wait_recv()
        return 0

    lax.fori_loop(1, 32, fin_start, 0)
    lax.fori_loop(0, UNITS, sums_sent, 0)
    for n in range(2):
        for moves in picked_moves(n):
            sent(moves)
    for n in range(BANDS // 2):
        keep, give, take = gh_moves(n)
        keep.wait()
        give.wait_send()
        take.wait_recv()
    lax.fori_loop(1, 32, fin_done, 0)
    totals = jnp.sum(fin[...], axis=0)
    count_total = totals[1:2, :]
    norm_value = jnp.sqrt(totals[2:3, :]) / count_total
    scal_out[0:1, :] = totals[0:1, :] / count_total
    scal_out[1:2, :] = norm_value
    scal_out[2:3, :] = jnp.minimum(1.0, clip_limit / norm_value) / count_total
    scal_out[3:8, :] = jnp.zeros((5, 128), wide)


def step_call(pix, blocks, tab, places, targets, counts, head, drift, power):
    half = tab.shape[1]
    full = 2 * half
    vocab = head.shape[1]
    slots = 32 * MSLOT
    vm = pltpu.VMEM
    dma = pltpu.SemaphoreType.DMA
    f32, b16 = wide, low_type
    scratch = [
        vm((4, 2, 2, UNITS * UNIT, full), b16),
        vm((2, 8, UNIT, 256), b16),
        vm((8, UNIT, 256), b16),
        vm((16 * UNIT, 256), b16),
        vm((TOK, full), f32),
        vm((TOK, full), f32), vm((TOK, full), f32), vm((TOK, full), f32),
        vm((TOK, full), b16), vm((TOK, full), b16), vm((TOK, full), b16),
        vm((TOK, 3 * full), b16),
        vm((4, TOK, full), f32),
        vm((4, TOK, full), b16),
        vm((full, vocab), b16),
        vm((3, UNIT, vocab), f32),
        vm((4, 2, 2, 2 * MSLOT, full), b16),
        vm((MSLOT, full), b16),
        vm((2 * MSLOT, full), b16),
        vm((BANDS, 2 * MSLOT, 512), f32),
        vm((full, slots), b16),
        vm((slots, 512), b16),
        vm((slots, 128), f32),
        vm((4, 8, 256), f32),
        vm((16, 8, 256), f32),
        vm((128, 256), f32),
        vm((256, 128), f32),
        vm((2 * MSLOT, full), f32),
        vm((MSLOT, full), b16), vm((MSLOT, full), b16),
        vm((TOK, full), b16),
        vm((TOK, full), f32),
        vm((8, full), f32),
        vm((4, 4, 2, UNIT, full), b16),
        vm((7, 2, 2, UNIT, half), b16),
        vm((7, 2, UNIT, full), b16),
        vm((7, 2, UNIT, half), b16),
        vm((7, 2, UNIT, half), b16),
        vm((7, 3, UNIT, half), b16),
        vm((224, full), b16),
        vm((112, full), b16),
        vm((5, 112, half), b16),
        vm((32, 8, 128), f32),
        dma((UNITS, 12)), dma((UNITS, 12)),
        dma((2,)), dma((2, 8)), dma((16,)),
        dma((2, 2)),
        dma((2, 12)), dma((2, 12)),
        dma((3,)), dma((3,)),
        dma((16,)), dma((16,)),
        dma((UNITS, 8)), dma((UNITS, 8)),
        dma((6,)), dma((6,)),
        dma((32,)), dma((32,)),
        dma((3,)), dma((5,)),
        dma((BANDS // 2,)), dma((BANDS // 2,)), dma((BANDS // 2,)),
    ]
    in_vmem = pl.BlockSpec(memory_space=pltpu.VMEM)
    return pl.pallas_call(
        step_kernel,
        out_shape=(
            jax.ShapeDtypeStruct((UNITS * UNIT, half), f32),
            jax.ShapeDtypeStruct((224, half), f32),
            jax.ShapeDtypeStruct((full, vocab), b16),
            jax.ShapeDtypeStruct((8, 128), f32),
            *([jax.ShapeDtypeStruct((full, vocab), b16)] * 3),
        ),
        in_specs=[
            *([in_vmem] * 9),
            pl.BlockSpec(memory_space=pltpu.SMEM),
            *([pl.BlockSpec(memory_space=pl.ANY)] * 3),
        ],
        out_specs=(
            in_vmem, in_vmem, pl.BlockSpec(memory_space=pl.ANY), in_vmem,
            *([pl.BlockSpec(memory_space=pl.ANY)] * 3),
        ),
        scratch_shapes=scratch,
        compiler_params=pltpu.CompilerParams(
            collective_id=0, has_side_effects=True, vmem_limit_bytes=VMEM_LIMIT
        ),
        cost_estimate=pl.CostEstimate(flops=50_000_000_000, bytes_accessed=40_000_000, transcendentals=0),
    )(pix, *blocks, tab, places, targets, counts, head, drift, power)


def block_path(
    pixels, mask_places, mask_count, targets, step_count,
    patch_weight, vector_table, input_weight, output_weight, upward_weight, downward_weight, head_weight,
    *moments,
):
    weights = (
        patch_weight, vector_table, input_weight, output_weight, upward_weight, downward_weight, head_weight,
    )
    weights = flat(weights)
    blocks = [weights[n] for n in (0, 2, 3, 4, 5)]
    drifts, powers = flat(moments[:7]), flat(moments[7:])
    gout, gtab, ghead, scal, *low = step_call(
        pixels.T, blocks, vector_table, mask_places, targets, mask_count, head_weight, drifts[6], powers[6]
    )
    states = [(*group[:6], value) for group, value in zip((weights, drifts, powers), low)]
    results = adam_call(scal, step_count, gout, gtab, ghead, *states)
    triples = [results[2 + n :: 3] for n in range(3)]
    triples = [unflat(triple) for triple in triples]
    return (*results[:2], *(triple[n] for n in range(7) for triple in triples))


def flat(values):
    patch, table, inward, outward, up, down, head = values
    return (patch, table, inward[0].T, outward[0], up[0].T, down[0], head)


def unflat(values):
    patch, table, inward, outward, up, down, head = values
    return (patch, table, inward.T[None], outward[None], up.T[None], down[None], head)


SMALL = UNITS * UNIT
ROWS = 48
IN_SLOTS = 4
OUT_SLOTS = 3


def adam_kernel(
    scal, step, gout, gtab, ghead, *refs
):
    weights, drifts, powers = refs[:7], refs[7:14], refs[14:21]
    loss_out, norm_out = refs[21:23]
    outs = refs[23:44]
    gbuf, inbuf, outbuf, gsm, insm, outsm, gtb, intb, outtb, in_sem, out_sem, sm_in, sm_out = refs[44:]
    factor = scal[2:3, 0:1]
    count = jnp.full((1, 128), step[0], jnp.int32).astype(wide)[:, 0:1]
    scale_first = 1.0 / (1.0 - jnp.exp(count * math.log(beta_first)))
    scale_second = 1.0 / (1.0 - jnp.exp(count * math.log(beta_second)))
    count_first = scale_first * -learn_rate
    gain_first = factor * (1.0 - beta_first)
    gain_second = factor * factor * (1.0 - beta_second)
    chunks = ghead.shape[0] // ROWS
    states = (weights, drifts, powers)

    def rows_of(n):
        return pl.ds(pl.multiple_of(n * ROWS, ROWS), ROWS)

    def fetch(n):
        slot = lax.rem(n, IN_SLOTS)
        copies = [
            pltpu.make_async_copy(states[m][6].at[rows_of(n)], inbuf.at[slot, m], in_sem.at[slot, m])
            for m in range(3)
        ]
        copies.append(pltpu.make_async_copy(ghead.at[rows_of(n)], gbuf.at[slot], in_sem.at[slot, 3]))
        return copies

    def store(n):
        slot = lax.rem(n, OUT_SLOTS)
        return [
            pltpu.make_async_copy(outbuf.at[slot, m], outs[18 + m].at[rows_of(n)], out_sem.at[slot, m])
            for m in range(3)
        ]

    order = (0, 2, 3, 4, 5)
    small_fetch, small_store = [], []
    start = 0
    for at, n in enumerate(order):
        height = weights[n].shape[0]
        for m in range(3):
            small_fetch.append(
                pltpu.make_async_copy(states[m][n], insm.at[m, start : start + height], sm_in.at[at, m])
            )
            small_store.append(
                pltpu.make_async_copy(outsm.at[m, start : start + height], outs[3 * n + m], sm_out.at[at, m])
            )
        start += height
    for m in range(3):
        small_fetch.append(pltpu.make_async_copy(states[m][1], intb.at[m], sm_in.at[5, m]))
        small_store.append(pltpu.make_async_copy(outtb.at[m], outs[3 + m], sm_out.at[5, m]))
    small_fetch.append(pltpu.make_async_copy(gout, gsm, sm_in.at[6, 0]))
    small_fetch.append(pltpu.make_async_copy(gtab, gtb, sm_in.at[6, 1]))

    def adam(grad, weight, drift, power):
        new_drift = beta_first * drift + gain_first * grad
        new_power = beta_second * power + gain_second * (grad * grad)
        below = jnp.sqrt(new_power * scale_second) + adam_eps
        update = new_drift * count_first / below - (learn_rate * weight_decay) * weight
        return update, new_drift, new_power

    for n in range(IN_SLOTS):
        for copy in fetch(n):
            copy.start()
    for copy in small_fetch:
        copy.start()
    loss_out[...] = scal[0:1, 0:1]
    norm_out[...] = scal[1:2, 0:1]

    def chunk(n, _):
        for copy in fetch(n):
            copy.wait()

        @pl.when(n >= OUT_SLOTS)
        def _():
            for copy in store(n - OUT_SLOTS):
                copy.wait()

        slot, spot = lax.rem(n, IN_SLOTS), lax.rem(n, OUT_SLOTS)

        def part(q, _):
            at = pl.ds(pl.multiple_of(q * 16, 16), 16)
            values = adam(
                gbuf[slot, at, :].astype(wide), *(inbuf[slot, m, at, :].astype(wide) for m in range(3))
            )
            for m in range(3):
                outbuf[spot, m, at, :] = values[m]
            return 0

        lax.fori_loop(0, ROWS // 16, part, 0)
        for copy in store(n):
            copy.start()

        @pl.when(n + IN_SLOTS < chunks)
        def _():
            for copy in fetch(n + IN_SLOTS):
                copy.start()

        @pl.when(n == 2)
        def _():
            for copy in small_fetch:
                copy.wait()

            def small(q, _):
                at = pl.ds(pl.multiple_of(q * UNIT, UNIT), UNIT)
                values = adam(gsm[at, :], insm[0, at, :], insm[1, at, :], insm[2, at, :])
                for m in range(3):
                    outsm[m, at, :] = values[m]
                return 0

            lax.fori_loop(0, UNITS, small, 0)
            values = adam(gtb[0 : intb.shape[1]], intb[0], intb[1], intb[2])
            for m in range(3):
                outtb[m] = values[m]
            for copy in small_store:
                copy.start()

        return 0

    lax.fori_loop(0, chunks, chunk, 0)
    for n in range(chunks - OUT_SLOTS, chunks):
        for copy in store(n):
            copy.wait()
    for copy in small_store:
        copy.wait()


def adam_call(scal, step, gout, gtab, ghead, weights, drifts, powers):
    half = gout.shape[1]
    vocab = ghead.shape[1]
    table = weights[1].shape[0]
    one = jax.ShapeDtypeStruct((1, 1), wide)
    shapes = [jax.ShapeDtypeStruct(value.shape, wide) for value in weights for _ in range(3)]
    in_vmem = pl.BlockSpec(memory_space=pltpu.VMEM)
    anywhere = pl.BlockSpec(memory_space=pl.ANY)
    vm, dma = pltpu.VMEM, pltpu.SemaphoreType.DMA
    results = pl.pallas_call(
        adam_kernel,
        in_specs=[in_vmem, pl.BlockSpec(memory_space=pltpu.SMEM)] + [anywhere] * 24,
        out_specs=[in_vmem] * 2 + [anywhere] * 21,
        out_shape=[one, one] + shapes,
        scratch_shapes=[
            vm((IN_SLOTS, ROWS, vocab), low_type), vm((IN_SLOTS, 3, ROWS, vocab), low_type),
            vm((OUT_SLOTS, 3, ROWS, vocab), wide),
            vm((SMALL, half), wide), vm((3, SMALL, half), wide), vm((3, SMALL, half), wide),
            vm(gtab.shape, wide), vm((3, table, half), wide), vm((3, table, half), wide),
            dma((IN_SLOTS, 4)), dma((OUT_SLOTS, 3)), dma((7, 3)), dma((6, 3)),
        ],
        compiler_params=pltpu.CompilerParams(vmem_limit_bytes=VMEM_LIMIT),
        cost_estimate=pl.CostEstimate(flops=60_000_000, bytes_accessed=82_000_000, transcendentals=4_000_000),
    )(scal, step, gout, gtab, ghead, *weights, *drifts, *powers)
    return (results[0].reshape(()), results[1].reshape(()), *results[2:])


def solution(mesh):
    state = (
        P("col", "row"),
        P(None, "row"),
        P(None, "row", "col"),
        P(None, "col", "row"),
        P(None, "row", "col"),
        P(None, "col", "row"),
        P(None, "row"),
    )
    data = (P("row", "col"), P("col", None), P("col"), P("col", None), P())
    outs = (P(), P()) + tuple(spec for spec in state for _ in range(3))
    fits = dict(mesh.shape) == {"row": 2, "col": 16}
    return jax.shard_map(
        block_path if fits else on_device,
        mesh=mesh,
        in_specs=data + state * 3,
        out_specs=outs,
        check_vma=False,
    )
```

```python
import math

import jax
import jax.numpy as jnp
from jax import lax
from jax.experimental import pallas as pl
from jax.experimental.pallas import tpu as pltpu
from jax.sharding import PartitionSpec as P

HEADS = 12
HD = 64
SEQ = 197
MSLOT = 80
BOTH = ("row", "col")

norm_eps = 1e-06
clip_limit = 0.1
learn_rate = 0.01
beta_first = 0.9
beta_second = 0.999
adam_eps = 1e-08
weight_decay = 0.05
low_type = jnp.bfloat16
wide = jnp.float32


def product(left, right):
    return jnp.dot(left, right, preferred_element_type=wide)


def product_nt(left, right):
    return jnp.einsum("ab,cb->ac", left, right, preferred_element_type=wide)


def product_tn(left, right):
    return jnp.einsum("ab,ac->bc", left, right, preferred_element_type=wide)


def norm_forward(values, gain, shift):
    center = jnp.mean(values, axis=1, keepdims=True)
    moved = values - center
    inverse = lax.rsqrt(jnp.mean(moved * moved, axis=1, keepdims=True) + norm_eps)
    scaled = moved * inverse
    return scaled * gain + shift, (scaled, inverse)


def norm_backward(upstream, kept, gain):
    scaled, inverse = kept
    inner = upstream * gain
    downstream = inverse * (
        inner
        - jnp.mean(inner, axis=1, keepdims=True)
        - scaled * jnp.mean(inner * scaled, axis=1, keepdims=True)
    )
    return downstream, jnp.sum(upstream * scaled, axis=0), jnp.sum(upstream, axis=0)


def exact_gelu(values):
    return jax.nn.gelu(values, approximate=False)


def split_heads(grouped):
    images = grouped.shape[0] // SEQ
    pieces = grouped.reshape(images, SEQ, 3, HEADS, HD)
    return pieces[:, :, 0], pieces[:, :, 1], pieces[:, :, 2]


def attention_weights(query, keys):
    scores = jnp.einsum("iqhd,ikhd->ihqk", query, keys, preferred_element_type=wide)
    return jax.nn.softmax(scores * (1.0 / math.sqrt(HD)), axis=-1)


def attend(grouped):
    query, keys, values = split_heads(grouped)
    weights_full = attention_weights(query, keys)
    mixture = jnp.einsum(
        "ihqk,ikhd->iqhd", weights_full.astype(low_type), values, preferred_element_type=wide
    )
    return mixture.reshape(grouped.shape[0], HEADS * HD), weights_full


def attend_back(grouped, weights_full, grad_mixture):
    query, keys, values = split_heads(grouped)
    images = query.shape[0]
    weights_low = weights_full.astype(low_type)
    grad_out = grad_mixture.reshape(images, SEQ, HEADS, HD)
    grad_weights = jnp.einsum("iqhd,ikhd->ihqk", grad_out, values, preferred_element_type=wide)
    grad_values = jnp.einsum("ihqk,iqhd->ikhd", weights_low, grad_out, preferred_element_type=wide)
    centered = grad_weights - jnp.sum(weights_full * grad_weights, axis=-1, keepdims=True)
    grad_scores = (weights_full * centered).astype(low_type)
    scale = 1.0 / math.sqrt(HD)
    grad_query = jnp.einsum("ihqk,ikhd->iqhd", grad_scores, keys, preferred_element_type=wide)
    grad_keys = jnp.einsum("ihqk,iqhd->ikhd", grad_scores, query, preferred_element_type=wide)
    stacked = jnp.stack([grad_query * scale, grad_keys * scale, grad_values], axis=2)
    return stacked.reshape(images * SEQ, 3 * HEADS * HD)


def adam_step(weight, grad, drift, power, factor, step_value):
    scaled = grad * factor
    new_drift = beta_first * drift + (1.0 - beta_first) * scaled
    new_power = beta_second * power + (1.0 - beta_second) * scaled * scaled
    drift_hat = new_drift / (1.0 - jnp.power(beta_first, step_value))
    power_hat = new_power / (1.0 - jnp.power(beta_second, step_value))
    update = -learn_rate * (drift_hat / (jnp.sqrt(power_hat) + adam_eps) + weight_decay * weight)
    return (update, new_drift, new_power)


def on_device(
    pixels,
    mask_places,
    mask_count,
    targets,
    step_count,
    patch_weight,
    vector_table,
    input_weight,
    output_weight,
    upward_weight,
    downward_weight,
    head_weight,
    drift_patch,
    drift_table,
    drift_input,
    drift_output,
    drift_upward,
    drift_downward,
    drift_head,
    power_patch,
    power_table,
    power_input,
    power_output,
    power_upward,
    power_downward,
    power_head,
):
    rows, cols = lax.axis_size("row"), lax.axis_size("col")
    row_index = lax.axis_index("row")
    col_index = lax.axis_index("col")
    images = mask_places.shape[0] // rows
    width = vector_table.shape[1] * rows

    blocks = [
        patch_weight.astype(low_type),
        input_weight[0].astype(low_type).T,
        output_weight[0].astype(low_type),
        upward_weight[0].astype(low_type).T,
        downward_weight[0].astype(low_type),
    ]
    heights = [block.shape[0] for block in blocks]
    gathered = lax.all_gather(jnp.concatenate(blocks, axis=0), BOTH, axis=0, tiled=False)
    gathered = gathered.reshape(rows, cols, sum(heights), -1)

    def whole(index):
        start = sum(heights[:index])
        part = gathered[:, :, start : start + heights[index]]
        return jnp.transpose(part, (1, 2, 0, 3)).reshape(cols * heights[index], width)

    patch_low, input_turned, output_low, upward_turned, downward_low = map(whole, range(5))
    table = lax.all_gather(vector_table, "row", axis=1, tiled=True)

    local_images = pixels.shape[0] // SEQ
    part = pixels.shape[1]
    grid = pixels.reshape(local_images // (rows * images), rows, images, SEQ, part)
    grid = lax.all_to_all(grid, "row", split_axis=1, concat_axis=0, tiled=True)
    grid = grid.reshape(cols, images * SEQ, part)
    grid = lax.all_to_all(grid, "col", split_axis=0, concat_axis=0, tiled=True)
    pixel_own = jnp.transpose(grid, (1, 0, 2)).reshape(images * SEQ, cols * part)

    def own(values):
        return lax.dynamic_slice_in_dim(values, row_index * images, images, axis=0)

    places_own, count_own = own(mask_places), own(mask_count)

    def gains_of(norm_index):
        return (table[SEQ + 2 + 2 * norm_index], table[SEQ + 3 + 2 * norm_index])

    patch_proj = product(pixel_own, patch_low)
    places = jnp.arange(SEQ, dtype=jnp.int32)
    counted_own = jnp.arange(MSLOT, dtype=jnp.int32)[None, :] < count_own[:, None]
    matches = places_own[:, :, None] == places[None, None, :]
    masked = jnp.any(matches & counted_own[:, :, None], axis=1)[:, :, None]
    opening = (places == 0)[None, :, None]
    stream = jnp.where(
        opening,
        table[SEQ],
        jnp.where(masked, table[SEQ + 1], patch_proj.reshape(images, SEQ, -1)),
    )
    stream = (stream + table[:SEQ][None]).reshape(images * SEQ, -1)
    gain_one, shift_one = gains_of(0)
    gain_two, shift_two = gains_of(1)
    final_gain, final_shift = gains_of(2)
    normed_one, stats_one = norm_forward(stream, gain_one, shift_one)
    normed_one = normed_one.astype(low_type)
    grouped = product_nt(normed_one, input_turned).astype(low_type)
    mixture, weights_full = attend(grouped)
    mixture = mixture.astype(low_type)
    stream_mid = stream + product(mixture, output_low)
    normed_two, stats_two = norm_forward(stream_mid, gain_two, shift_two)
    normed_two = normed_two.astype(low_type)
    hidden_pre = product_nt(normed_two, upward_turned)
    hidden_act = exact_gelu(hidden_pre).astype(low_type)
    stream_last = stream_mid + product(hidden_act, downward_low)
    final_out, final_stats = norm_forward(stream_last, final_gain, final_shift)
    selector = matches.astype(low_type)
    picked = jnp.einsum(
        "ims,isd->imd", selector, final_out.astype(low_type).reshape(images, SEQ, -1),
        preferred_element_type=wide,
    ).astype(low_type)

    picked_wide = lax.all_gather(picked.reshape(images * MSLOT, -1), "row", axis=0, tiled=True)
    head_low = head_weight.astype(low_type)
    logits = product(picked_wide, head_low)
    vocab_local = head_weight.shape[1]
    target_local = targets.reshape(-1) - row_index * vocab_local
    target_hits = target_local[:, None] == jnp.arange(vocab_local, dtype=jnp.int32)[None, :]
    chosen = jnp.sum(jnp.where(target_hits, logits, 0.0), axis=1)
    local_top = jnp.max(logits, axis=1)
    local_sum = jnp.sum(jnp.exp(logits - local_top[:, None]), axis=1)
    pair = lax.all_gather(jnp.stack([local_top, local_sum]), "row", axis=0, tiled=False)
    top_value = jnp.max(pair[:, 0], axis=0)
    exp_total = jnp.sum(pair[:, 1] * jnp.exp(pair[:, 0] - top_value), axis=0)
    log_total = top_value + jnp.log(exp_total)
    counted = jnp.arange(MSLOT, dtype=jnp.int32)[None, :] < mask_count[:, None]
    slot_weight = counted.reshape(-1).astype(wide)
    leader_row = (row_index == 0).astype(wide)
    loss_part = jnp.sum(log_total * slot_weight) * leader_row - jnp.sum(chosen * slot_weight)
    count_part = jnp.sum(mask_count.astype(wide)) * leader_row
    grad_logits = (
        (jnp.exp(logits - log_total[:, None]) - target_hits.astype(wide)) * slot_weight[:, None]
    ).astype(low_type)
    grad_head_local = product_tn(picked_wide, grad_logits)
    grad_head = lax.psum(grad_head_local.astype(low_type), "col").astype(wide)
    grad_picked = lax.psum_scatter(
        product_nt(grad_logits, head_low).astype(low_type),
        "row",
        scatter_dimension=0,
        tiled=True,
    )
    grad_final = jnp.einsum(
        "ims,imd->isd", selector, grad_picked.reshape(images, MSLOT, -1),
        preferred_element_type=wide,
    )

    grad_stream, grad_final_gain, grad_final_shift = norm_backward(
        grad_final.reshape(images * SEQ, -1), final_stats, final_gain
    )
    grad_two = grad_stream.astype(low_type)
    grad_downward = product_tn(hidden_act, grad_two)
    grad_act = product_nt(grad_two, downward_low)
    _, gelu_pull = jax.vjp(exact_gelu, hidden_pre)
    grad_pre = gelu_pull(grad_act)[0].astype(low_type)
    grad_upward_turned = product_tn(grad_pre, normed_two)
    grad_normed_two = product(grad_pre, upward_turned)
    grad_mid, grad_gain_two, grad_shift_two = norm_backward(grad_normed_two, stats_two, gain_two)
    grad_mid = grad_mid + grad_stream
    grad_one = grad_mid.astype(low_type)
    grad_output = product_tn(mixture, grad_one)
    grad_mixture = product_nt(grad_one, output_low).astype(low_type)
    grad_grouped = attend_back(grouped, weights_full, grad_mixture).astype(low_type)
    grad_input_turned = product_tn(grad_grouped, normed_one)
    grad_normed_one = product(grad_grouped, input_turned)
    grad_below, grad_gain_one, grad_shift_one = norm_backward(grad_normed_one, stats_one, gain_one)
    grad_grid = (grad_below + grad_mid).reshape(images, SEQ, -1)
    grad_patch = jnp.where(opening | masked, 0.0, grad_grid).reshape(images * SEQ, -1)
    grad_patch_weight = product_tn(pixel_own, grad_patch.astype(low_type))
    lines = [
        jnp.sum(grad_grid, axis=0),
        jnp.sum(grad_grid[:, 0], axis=0)[None],
        jnp.sum(jnp.where(masked, grad_grid, 0.0), axis=(0, 1))[None],
        jnp.stack(
            [grad_gain_one, grad_shift_one, grad_gain_two, grad_shift_two,
             grad_final_gain, grad_final_shift]
        ),
    ]
    table_local = jnp.concatenate(lines, axis=0).astype(low_type)

    def dealt(value, height):
        grid = value.astype(low_type).reshape(cols, height, rows, -1)
        return jnp.transpose(grid, (2, 0, 1, 3)).reshape(rows * cols, height, -1)

    stacked = jnp.concatenate(
        [
            dealt(value, height)
            for value, height in zip(
                [grad_patch_weight, grad_input_turned, grad_output, grad_upward_turned,
                 grad_downward],
                heights,
            )
        ],
        axis=1,
    )
    summed = lax.psum_scatter(stacked, BOTH, scatter_dimension=0, tiled=False).astype(wide)
    starts = [sum(heights[:index]) for index in range(6)]
    pieces = [summed[starts[index] : starts[index + 1]] for index in range(5)]
    grad_table = lax.psum(table_local, BOTH).astype(wide)
    grad_table = lax.dynamic_slice_in_dim(
        grad_table, row_index * vector_table.shape[1], vector_table.shape[1], axis=1
    )
    leader_col = (col_index == 0).astype(wide)
    squares_part = jnp.sum(summed * summed) + leader_col * (
        jnp.sum(grad_table * grad_table) + jnp.sum(grad_head * grad_head)
    )
    loss_total, count_total, squares_total = lax.psum((loss_part, count_part, squares_part), BOTH)
    mean_loss = loss_total / count_total
    grad_norm = jnp.sqrt(squares_total) / count_total
    factor = jnp.minimum(1.0, clip_limit / grad_norm) / count_total
    step_value = step_count[0].astype(wide)
    steps = [
        (patch_weight, pieces[0], drift_patch, power_patch),
        (vector_table, grad_table, drift_table, power_table),
        (input_weight, pieces[1].T[None], drift_input, power_input),
        (output_weight, pieces[2][None], drift_output, power_output),
        (upward_weight, pieces[3].T[None], drift_upward, power_upward),
        (downward_weight, pieces[4][None], drift_downward, power_downward),
        (head_weight, grad_head, drift_head, power_head),
    ]
    results = []
    for weight, grad, drift, power in steps:
        results.extend(adam_step(weight, grad, drift, power, factor, step_value))
    return (mean_loss, grad_norm, *results)


VMEM_LIMIT = 62 * 2**20
TOK = 208
UNIT = 48
UNITS = 13
BANDS = 8
G_FIRST = 7
AHEAD = 2
LAG_A = 1
LAG_B = 3
LAG_C = 4
EYE = pl.DeviceIdType.MESH


def nn(left, right):
    return jnp.dot(left, right, preferred_element_type=wide)


def nt(left, right):
    return lax.dot_general(left, right, (((1,), (1,)), ((), ())), preferred_element_type=wide)


def tn(left, right):
    return lax.dot_general(left, right, (((0,), (0,)), ((), ())), preferred_element_type=wide)


def gelu_parts(values):
    phi_total = 0.5 * (1.0 + lax.erf(values * math.sqrt(0.5)))
    density = jnp.exp(values * values * -0.5) * (1.0 / math.sqrt(2.0 * math.pi))
    return phi_total, density


def normed(values, gain, shift):
    center = jnp.mean(values, axis=1, keepdims=True)
    moved = values - center
    inverse = lax.rsqrt(jnp.mean(moved * moved, axis=1, keepdims=True) + norm_eps)
    scaled = moved * inverse
    return scaled * gain + shift, scaled, inverse


def normed_back(upstream, scaled, inverse, gain):
    inner = upstream * gain
    down = inverse * (
        inner
        - jnp.mean(inner, axis=1, keepdims=True)
        - scaled * jnp.mean(inner * scaled, axis=1, keepdims=True)
    )
    return (
        down,
        jnp.sum(upstream * scaled, axis=0, keepdims=True),
        jnp.sum(upstream, axis=0, keepdims=True),
    )


def step_kernel(
    pix_in, patch_in, input_in, output_in, up_in, down_in, tab_in, places, targets, counts, head_in, drift_in, power_in,
    gout, gtab_out, ghead, scal_out, head_low, drift_low, power_low,
    wg, px_out, px_mid, px, tb, st0, st1, st2, n1, n2, mix, qkv, hpre, hact,
    hn, hbuf, pk, pkp, pp, lt, pkt, gch, colb, sq, lsb, flip, tmpa, gpk, gps, gpr, g2b, gacc, gst,
    rk, r1a, r1b, r2a, r2b, rz, tab, tabk, tabr, fin,
    ag_send, ag_recv, px_sem, px_send, px_recv, tb_sem, pk_send, pk_recv, ex_send, ex_recv,
    ls_send, ls_recv, rs_send, rs_recv, tab_send, tab_recv, fin_send, fin_recv, hb_sem, st_sem, gh_sem, gh_send, gh_recv,
):
    r = lax.axis_index("row")
    c = lax.axis_index("col")
    z, x, k = c // 4, (c // 2) % 2, c % 2
    half = tb.shape[1] // 2
    d_y = (1 - r, c)
    d_x = (r, z * 4 + (1 - x) * 2 + k)
    d_k = (r, z * 4 + x * 2 + 1 - k)

    def d_z(step):
        return (r, lax.rem(z + step, 4) * 4 + x * 2 + k)

    def remote(src, dst, send, recv, device):
        return pltpu.make_async_remote_copy(
            src_ref=src, dst_ref=dst, send_sem=send, recv_sem=recv,
            device_id=device, device_id_type=EYE,
        )

    def lanes(row):
        return pl.ds(pl.multiple_of(row * half, half), half)

    sq[...] = jnp.zeros_like(sq)
    width = px_out.shape[3]
    barrier = pltpu.get_barrier_semaphore()

    def greet(n, _):
        other = lax.rem(r * 16 + c + n, 32)
        pl.semaphore_signal(barrier, inc=1, device_id=(other // 16, other % 16), device_id_type=EYE)
        return 0

    lax.fori_loop(1, 32, greet, 0)

    for n in range(16):
        px_out[n % 2, n // 2, :, 0:SEQ] = pix_in[:, n * SEQ : (n + 1) * SEQ]
        px_out[n % 2, n // 2, :, SEQ:] = jnp.zeros((UNIT, width - SEQ), low_type)
    heights = (UNIT, 3 * UNIT, UNIT, 4 * UNIT, 4 * UNIT)
    blocks = (
        patch_in[...], input_in[...], output_in[...], up_in[...], down_in[...],
    )
    start = 0
    for height, block in zip(heights, blocks):
        wg[z, x, k, start : start + height, lanes(r)] = block.astype(low_type)
        start += height
    tb[0 : tab_in.shape[0], lanes(r)] = tab_in[...]
    tb[tab_in.shape[0] :, lanes(r)] = jnp.zeros((TOK - tab_in.shape[0], half), wide)
    wide_states = (head_in, drift_in, power_in)
    low_states = (head_low, drift_low, power_low)

    def state_rows(b):
        return pl.ds(pl.multiple_of(b * UNIT, UNIT), UNIT)

    def state_in(a, b):
        return pltpu.make_async_copy(wide_states[a].at[state_rows(b)], hbuf.at[a], hb_sem.at[a])

    wide_part = pkt.shape[1]
    rest_part = hn.shape[1] - wide_part

    def state_out(a, b):
        rows = state_rows(b)
        if a == 0:
            return [pltpu.make_async_copy(hn.at[rows], head_low.at[rows], st_sem.at[0])]
        first = pkt.at[UNIT * (a - 1) : UNIT * a]
        second = pkt.at[UNIT * (a + 1) : UNIT * (a + 2), 0:rest_part]
        low = low_states[a]
        return [
            pltpu.make_async_copy(first, low.at[rows, 0:wide_part], st_sem.at[a]),
            pltpu.make_async_copy(second, low.at[rows, wide_part:], st_sem.at[a + 2]),
        ]

    for a in range(3):
        state_in(a, 0).start()
    pl.semaphore_wait(barrier, 31)

    def gather_moves(buf, part, both, send, recv):
        lo, hi = pl.ds(0, 2), pl.ds(2, 2)
        every = slice(None)
        other = lax.rem

        def move(index, out_region, in_region, device):
            out_ref = buf.at[out_region]
            in_ref = buf.at[in_region]
            return (
                remote(out_ref, out_ref, send.at[index], recv.at[index], device),
                remote(in_ref, in_ref, send.at[index], recv.at[index], device),
            )

        first = [
            move(n - 1, (z, x, k) + part(r), (lax.rem(z + 4 - n, 4), x, k) + part(r), d_z(n))
            for n in (1, 2, 3)
        ]
        second = [
            move(3, (lo, x, k) + part(r), (lo, 1 - x, k) + part(r), d_x),
            move(4, (hi, x, k) + part(r), (hi, x, k) + part(1 - r), d_y),
        ]
        pair_one = [move(5, (every, x, k) + part(r), (every, x, 1 - k) + part(r), d_k)]
        third = [
            move(6, (lo, every, k) + part(r), (lo, every, k) + part(1 - r), d_y),
            move(7, (hi, x, k) + both, (hi, 1 - x, k) + both, d_x),
        ]
        pair_two = [
            move(8, (lo, 1 - x, k) + part(r), (lo, 1 - x, 1 - k) + part(r), d_k),
            move(9, (hi, x, k) + part(1 - r), (hi, x, 1 - k) + part(1 - r), d_k),
        ]
        pair_three = [
            move(10, (lo, every, k) + part(1 - r), (lo, every, 1 - k) + part(1 - r), d_k),
            move(11, (hi, 1 - x, k) + both, (hi, 1 - x, 1 - k) + both, d_k),
        ]
        return first, second, pair_one, third, pair_two, pair_three

    def begin(moves):
        for out_copy, _ in moves:
            out_copy.start()

    def landed(moves):
        for _, in_copy in moves:
            in_copy.wait_recv()

    def sent(moves):
        for out_copy, _ in moves:
            out_copy.wait_send()

    def unit_rows(n):
        return pl.ds(pl.multiple_of(n * UNIT, UNIT), UNIT)

    def weight_moves(n):
        rows = unit_rows(n)
        return gather_moves(
            wg, lambda row: (rows, lanes(row)), (rows, slice(None)), ag_send.at[n], ag_recv.at[n]
        )

    late = UNITS - 1

    def late_moves():
        rows = unit_rows(late)
        every = slice(None)

        def move(index, out_region, in_region, device):
            out_ref, in_ref = wg.at[out_region], wg.at[in_region]
            send, recv = ag_send.at[late, index], ag_recv.at[late, index]
            return remote(out_ref, out_ref, send, recv, device), remote(in_ref, in_ref, send, recv, device)

        one = [move(0, (z, x, k, rows, lanes(r)), (z, 1 - x, k, rows, lanes(r)), d_x)]
        two = [move(1, (z, every, k, rows, lanes(r)), (z, every, k, rows, lanes(1 - r)), d_y)]
        three = [
            move(1 + n, (z, every, k, rows, every), (lax.rem(z + 4 - n, 4), every, k, rows, every), d_z(n))
            for n in (1, 2, 3)
        ]
        four = [move(5, (every, every, k, rows, every), (every, every, 1 - k, rows, every), d_k)]
        return one, two, three, four

    def picked_moves(n):
        cut = lanes(n)
        return gather_moves(
            pk, lambda row: (pl.ds(pl.multiple_of(row * MSLOT, 16), MSLOT), cut),
            (slice(None), cut), pk_send.at[n], pk_recv.at[n],
        )

    px_swap = remote(px_out.at[1 - r], px_mid, px_sem.at[0], px_sem.at[1], d_y)

    def px_slot(n):
        return px.at[pl.ds(pl.multiple_of(n * UNIT, UNIT), UNIT)]

    def px_move(part, n):
        target = 8 * (r if part == 0 else 1 - r) + n
        src = px_out.at[r, n] if part == 0 else px_mid.at[n]
        return target, remote(src, px_slot(c), px_send.at[part, n], px_recv.at[c], (r, target))

    def px_start(part):
        def one(n, _):
            target, copy = px_move(part, n)

            @pl.when(target == c)
            def _():
                px[pl.ds(pl.multiple_of(c * UNIT, UNIT), UNIT), :] = (
                    px_out[r, n] if part == 0 else px_mid[n]
                )

            @pl.when(target != c)
            def _():
                copy.start()

            return 0

        lax.fori_loop(0, 8, one, 0)

    def px_done(n, _):
        for part in range(2):
            target, copy = px_move(part, n)

            @pl.when(target != c)
            def _():
                copy.wait_send()

        for source in (n, n + 8):

            @pl.when(source != c)
            def _():
                remote(px_slot(source), px_slot(source), px_send.at[0, n], px_recv.at[source], d_y).wait_recv()

        return 0

    cut_rows = TOK // 2
    own_cut = pl.ds(pl.multiple_of(k * cut_rows, 8), cut_rows)
    other_cut = pl.ds(pl.multiple_of((1 - k) * cut_rows, 8), cut_rows)

    def tb_copy(rows, row, index, device):
        ref = tb.at[rows, lanes(row)]
        return remote(ref, ref, tb_sem.at[index, 0], tb_sem.at[index, 1], device)

    token = lax.broadcasted_iota(jnp.int32, (TOK, 1), 0)
    slot_hit = lax.broadcasted_iota(jnp.int32, (TOK, MSLOT), 0) == places[pl.ds(r, 1), :]
    slot_on = lax.broadcasted_iota(jnp.int32, (TOK, MSLOT), 1) < counts[r]
    selector = jnp.where(slot_hit, 1.0, 0.0)
    masked = jnp.sum(jnp.where(slot_on, selector, 0.0), axis=1, keepdims=True) > 0.5
    opening = token == 0

    def gain(n):
        return tb[SEQ + 2 + 2 * n : SEQ + 3 + 2 * n, :]

    def shift(n):
        return tb[SEQ + 3 + 2 * n : SEQ + 4 + 2 * n, :]

    def square(n):
        return wg[:, :, :, unit_rows(n), :].reshape(16 * UNIT, 2 * half)

    def set_square(n, value):
        wg[:, :, :, unit_rows(n), :] = value.astype(low_type).reshape(4, 2, 2, UNIT, 2 * half)

    def triple():
        return wg[:, :, :, UNIT : 4 * UNIT, :].reshape(48 * UNIT, 2 * half)

    lane_low = lax.broadcasted_iota(jnp.int32, (1, 2 * HD), 1) < HD
    keep_low = jnp.where(lane_low, 1.0, 0.0)
    keep_high = 1.0 - keep_low

    def twice(values):
        return jnp.concatenate(
            [values * keep_low.astype(low_type), values * keep_high.astype(low_type)], axis=0
        )

    def once(values):
        return values[:TOK] * keep_low + values[TOK:] * keep_high

    def pair_lanes(part, p):
        return pl.ds(pl.multiple_of(part * HEADS * HD + p * 2 * HD, 2 * HD), 2 * HD)

    def pair_probs(p):
        query2 = twice(qkv[:, pair_lanes(0, p)])
        key2 = qkv[:, pair_lanes(1, p)]
        scores = nt(query2, key2) * (1.0 / math.sqrt(HD))
        valid = lax.broadcasted_iota(jnp.int32, (1, TOK), 1) < SEQ
        scores = jnp.where(valid, scores, -1e30)
        lifted = jnp.exp(scores - jnp.max(scores, axis=1, keepdims=True))
        return query2, key2, lifted * (1.0 / jnp.sum(lifted, axis=1, keepdims=True))

    def do_patch():
        tb_copy(own_cut, 1 - r, 0, d_y).wait_recv()
        tb_copy(own_cut, 1 - r, 1, d_k).start()
        lax.fori_loop(0, 8, px_done, 0)
        patch = tn(px[...], square(0))[:TOK]
        tb_copy(own_cut, r, 0, d_y).wait_send()
        tb_copy(other_cut, 1 - r, 1, d_k).wait_recv()
        tb_copy(own_cut, 1 - r, 1, d_k).wait_send()
        value = jnp.where(
            opening, tb[SEQ : SEQ + 1, :], jnp.where(masked, tb[SEQ + 1 : SEQ + 2, :], patch)
        )
        value = jnp.where(token < SEQ, value + tb[...], 0.0)
        st0[...] = value
        n1[...] = normed(value, gain(0), shift(0))[0].astype(low_type)

    def do_attention():
        qkv[...] = nt(n1[...], triple()).astype(low_type)

        def one_pair(p, _):
            _, _, probs = pair_probs(p)
            mixed = nn(probs.astype(low_type), qkv[:, pair_lanes(2, p)])
            mix[:, pair_lanes(0, p)] = once(mixed).astype(low_type)
            return 0

        lax.fori_loop(0, HEADS // 2, one_pair, 0)

    def do_output():
        value = st0[...] + nn(mix[...], square(4))
        st1[...] = value
        st2[...] = value
        n2[...] = normed(value, gain(1), shift(1))[0].astype(low_type)

    def do_up(j):
        value = nt(n2[...], square(5 + j))
        hpre[j] = value
        phi_total, _ = gelu_parts(value)
        hact[j] = (value * phi_total).astype(low_type)

    def do_down(j):
        st2[...] += nn(hact[j], square(9 + j))

    begin(late_moves()[0])
    px_swap.start()
    begin(weight_moves(0)[0])
    begin(weight_moves(1)[0])
    px_start(0)
    for n in range(2, AHEAD):
        begin(weight_moves(n)[0])
    tb_copy(own_cut, r, 0, d_y).start()

    def tick(t, _):
        @pl.when(t < late)
        def _():
            first, second, pair_one, _, _, _ = weight_moves(t)
            landed(first)
            begin(second)
            begin(pair_one)

        @pl.when(t == 0)
        def _():
            landed(late_moves()[0])
            begin(late_moves()[1])
            px_swap.wait()
            px_start(1)

        @pl.when(t < late - AHEAD)
        def _():
            begin(weight_moves(t + AHEAD)[0])

        @pl.when(t == late - AHEAD)
        def _():
            landed(late_moves()[1])
            begin(late_moves()[2])

        @pl.when(jnp.logical_and(t >= LAG_A, t < late + LAG_A))
        def _():
            _, second, _, third, pair_two, _ = weight_moves(t - LAG_A)
            landed(second)
            begin(third)
            begin(pair_two)

        @pl.when(t == late + 2)
        def _():
            landed(late_moves()[2])
            begin(late_moves()[3])

        @pl.when(jnp.logical_and(t >= LAG_B, t < late + LAG_B))
        def _():
            _, _, _, third, _, pair_three = weight_moves(t - LAG_B)
            landed(third)
            begin(pair_three)

        @pl.when(jnp.logical_and(t >= LAG_C, t < late + LAG_C))
        def _():
            _, _, pair_one, _, pair_two, pair_three = weight_moves(t - LAG_C)
            landed(pair_one)
            landed(pair_two)
            landed(pair_three)

        @pl.when(t == late + LAG_C)
        def _():
            landed(late_moves()[3])

        @pl.when(t < 16)
        def _():
            for a in range(3):
                state_in(a, t).wait()

                @pl.when(t >= 1)
                def _():
                    for copy in state_out(a, t - 1):
                        copy.wait()

                value = hbuf[a].astype(low_type)
                if a == 0:
                    hn[state_rows(t), :] = value
                else:
                    pkt[UNIT * (a - 1) : UNIT * a, :] = value[:, :wide_part]
                    pkt[UNIT * (a + 1) : UNIT * (a + 2), 0:rest_part] = value[:, wide_part:]
                for copy in state_out(a, t):
                    copy.start()

                @pl.when(t + 1 < 16)
                def _():
                    state_in(a, t + 1).start()

        @pl.when(t == LAG_C + 2)
        def _():
            do_patch()

        @pl.when(t == LAG_C + 3)
        def _():
            do_attention()

        @pl.when(t == LAG_C + 4)
        def _():
            do_output()

        @pl.when(jnp.logical_and(t >= LAG_C + 5, t < LAG_C + 9))
        def _():
            do_up(t - LAG_C - 5)

        @pl.when(t >= LAG_C + 9)
        def _():
            do_down(t - LAG_C - 9)

        return 0

    lax.fori_loop(0, UNITS + LAG_C, tick, 0)

    def all_sent(n, _):
        for moves in weight_moves(n):
            sent(moves)
        return 0

    for a in range(3):
        for copy in state_out(a, 15):
            copy.wait()

    final_out, _, _ = normed(st2[...], gain(2), shift(2))
    picked = tn(selector.astype(low_type), final_out.astype(low_type)).astype(low_type)
    own_rows = pl.ds(pl.multiple_of(r * MSLOT, 16), MSLOT)
    other_rows = pl.ds(pl.multiple_of((1 - r) * MSLOT, 16), MSLOT)
    pp[own_rows, :] = picked
    pk[z, x, k, own_rows, :] = picked

    def swap(index, src, dst, device):
        return remote(src, dst, ex_send.at[index], ex_recv.at[index], device)

    swap_picked = swap(0, pp.at[own_rows, :], pkp, d_y)
    swap_picked.start()
    for n in range(2):
        begin(picked_moves(n)[0])
    lax.fori_loop(0, late, all_sent, 0)
    for moves in late_moves():
        sent(moves)
    flip[...] = jnp.zeros_like(flip)
    flip[0:2, 0:MSLOT] = targets[...].astype(wide)
    info = jnp.transpose(flip[...])
    target_col = jnp.concatenate([info[:MSLOT, 0:1], info[:MSLOT, 1:2]], axis=0)
    slot_line = lax.broadcasted_iota(jnp.int32, (MSLOT, 1), 0)
    weight_col = jnp.concatenate(
        [jnp.where(slot_line < counts[0], 1.0, 0.0), jnp.where(slot_line < counts[1], 1.0, 0.0)], axis=0
    )
    base = (r * (BANDS * 512)).astype(wide)
    band_lane = lax.broadcasted_iota(jnp.int32, (1, 512), 1).astype(wide)

    def band(v):
        return pl.ds(pl.multiple_of(v * 512, 512), 512)

    def band_hit(v, column):
        return (band_lane + (base + (v * 512).astype(wide))) == column

    swap_picked.wait()
    pp[other_rows, :] = pkp[...]

    def picked_second(n):
        first, second, pair_one, _, _, _ = picked_moves(n)
        landed(first)
        begin(second)
        begin(pair_one)

    def picked_third(n):
        _, second, _, third, pair_two, _ = picked_moves(n)
        landed(second)
        begin(third)
        begin(pair_two)

    def picked_last(n):
        _, _, _, third, _, pair_three = picked_moves(n)
        landed(third)
        begin(pair_three)

    def picked_done(n):
        _, _, pair_one, _, pair_two, pair_three = picked_moves(n)
        landed(pair_one)
        landed(pair_two)
        landed(pair_three)

    def logits_band(v, carry):
        top, chosen = carry
        value = nn(pp[...], hn[:, band(v)])
        lt[v] = value
        chosen += jnp.sum(jnp.where(band_hit(v, target_col), value, 0.0), axis=1, keepdims=True)
        return jnp.maximum(top, jnp.max(value, axis=1, keepdims=True)), chosen

    zero_col = jnp.zeros((2 * MSLOT, 1), wide)
    top, chosen = lax.fori_loop(0, BANDS, logits_band, (zero_col - 1e30, zero_col))
    picked_second(0)

    def sum_band(v, total):
        return total + jnp.sum(jnp.exp(lt[v] - top), axis=1, keepdims=True)

    total = lax.fori_loop(0, BANDS, sum_band, zero_col)
    column = lax.broadcasted_iota(jnp.int32, (1, 128), 1)
    tmpa[...] = jnp.zeros_like(tmpa)
    tmpa[0 : 2 * MSLOT, :] = jnp.where(column == 0, top, jnp.where(column == 1, total, 0.0))
    sq[0] = jnp.transpose(tmpa[...])[:8]
    swap_lse = swap(1, sq.at[0], sq.at[1], d_y)
    swap_lse.start()
    picked_second(1)
    picked_third(0)
    swap_lse.wait()
    flip[...] = jnp.zeros_like(flip)
    flip[0:8, :] = sq[1]
    theirs = jnp.transpose(flip[...])[: 2 * MSLOT]
    their_top, their_total = theirs[:, 0:1], theirs[:, 1:2]
    best = jnp.maximum(top, their_top)
    log_total = best + jnp.log(total * jnp.exp(top - best) + their_total * jnp.exp(their_top - best))

    tmpa[0 : 2 * MSLOT, :] = jnp.where(
        column == 0, log_total, jnp.where(column == 1, target_col, jnp.where(column == 2, weight_col, 0.0))
    )
    lsb[c] = jnp.transpose(tmpa[...])[:8]

    def ls_copy(n):
        other = lax.rem(c + n, 16)
        return remote(lsb.at[c], lsb.at[c], ls_send.at[n], ls_recv.at[n], (r, other))

    def ls_in(n):
        other = lax.rem(c + 16 - n, 16)
        return remote(lsb.at[other], lsb.at[other], ls_send.at[n], ls_recv.at[n], (r, other))

    def ls_start(n, _):
        ls_copy(n).start()
        return 0

    def ls_done(n, _):
        ls_copy(n).wait_send()
        ls_in(n).wait_recv()
        return 0

    lax.fori_loop(1, 16, ls_start, 0)
    gpk[...] = jnp.zeros_like(gpk)

    def grad_band(v, _):
        value = jnp.exp(lt[v] - log_total) - jnp.where(band_hit(v, target_col), 1.0, 0.0)
        gpk[...] += nt((value * weight_col).astype(low_type), hn[:, band(v)])
        return 0

    lax.fori_loop(0, BANDS, grad_band, 0)
    gps[...] = gpk[other_rows, :].astype(low_type)
    swap_grad = swap(2, gps, gpr, d_y)
    swap_grad.start()
    leader = jnp.where(r == 0, 1.0, 0.0)
    loss_part = jnp.sum((log_total * leader - chosen) * weight_col, axis=0, keepdims=True)
    swap_grad.wait()
    picked_third(1)
    grad_picked = (gpk[own_rows, :] + gpr[...].astype(wide)).astype(low_type)
    grad_final = nn(selector.astype(low_type), grad_picked)
    _, scaled, inverse = normed(st2[...], gain(2), shift(2))
    grad_last, grad_gain, grad_shift = normed_back(grad_final, scaled, inverse, gain(2))
    st2[...] = grad_last
    g2b[...] = grad_last.astype(low_type)
    gst[4:5, :] = grad_gain
    gst[5:6, :] = grad_shift
    gacc[...] = jnp.zeros_like(gacc)

    def pair_region(n):
        return rk.at[lax.rem(n, 4)]

    def rs_copy(n, index, src, dst, device):
        return remote(src, dst, rs_send.at[n, index], rs_recv.at[n, index], device)

    lo, hi = pl.ds(0, 2), pl.ds(2, 2)

    def sums_moves(n):
        rows = unit_rows(UNITS - 1 - n)
        zero = [rs_copy(n, 0, wg.at[:, :, 1 - k, rows, :], rk.at[lax.rem(n, 4)], d_k)]
        one = [
            rs_copy(n, 1, wg.at[lo, :, k, rows, lanes(1 - r)], r1a.at[lax.rem(n, 7)], d_y),
            rs_copy(n, 2, wg.at[hi, 1 - x, k, rows, :], r1b.at[lax.rem(n, 7)], d_x),
        ]
        two = [
            rs_copy(n, 3, wg.at[lo, 1 - x, k, rows, lanes(r)], r2a.at[lax.rem(n, 7)], d_x),
            rs_copy(n, 4, wg.at[hi, x, k, rows, lanes(1 - r)], r2b.at[lax.rem(n, 7)], d_y),
        ]
        three = [
            rs_copy(n, 4 + m, wg.at[lax.rem(z + m, 4), x, k, rows, lanes(r)], rz.at[lax.rem(n, 7), m - 1], d_z(m))
            for m in (1, 2, 3)
        ]
        return zero, one, two, three

    def sum_start(copies):
        for copy in copies:
            copy.start()

    def sum_land(copies):
        for copy in copies:
            copy.wait_recv()

    def fold(region, value):
        wg[region] = (wg[region].astype(wide) + value.astype(wide)).astype(low_type)

    def sums_one(n):
        rows = unit_rows(UNITS - 1 - n)
        zero, one, _, _ = sums_moves(n)
        sum_land(zero)
        fold((slice(None), slice(None), k, rows, slice(None)), rk[lax.rem(n, 4)])
        sum_start(one)

    def sums_two(n):
        rows = unit_rows(UNITS - 1 - n)
        _, one, two, _ = sums_moves(n)
        sum_land(one)
        fold((lo, slice(None), k, rows, lanes(r)), r1a[lax.rem(n, 7)])
        fold((hi, x, k, rows, slice(None)), r1b[lax.rem(n, 7)])
        sum_start(two)

    def sums_three(n):
        rows = unit_rows(UNITS - 1 - n)
        _, _, two, three = sums_moves(n)
        sum_land(two)
        fold((lo, x, k, rows, lanes(r)), r2a[lax.rem(n, 7)])
        fold((hi, x, k, rows, lanes(r)), r2b[lax.rem(n, 7)])
        sum_start(three)

    def sums_four(n):
        rows = unit_rows(UNITS - 1 - n)
        _, _, _, three = sums_moves(n)
        sum_land(three)
        value = wg[z, x, k, rows, lanes(r)].astype(wide)
        for m in range(3):
            value = value + rz[lax.rem(n, 7), m].astype(wide)
        gout[rows, :] = value
        sq[2, 0:1, 0:128] += jnp.sum(jnp.sum(value * value, axis=0, keepdims=True), axis=1, keepdims=True)

    def sums_sent(n, _):
        for moves in sums_moves(n):
            sent([(copy, None) for copy in moves])
        return 0

    def back_down(j):
        grad_act = nt(g2b[...], square(9 + j))
        value = hpre[j]
        phi_total, density = gelu_parts(value)
        grad_pre = (grad_act * (phi_total + value * density)).astype(low_type)
        set_square(9 + j, tn(hact[j], g2b[...]))
        hact[j] = grad_pre

    def back_up(j):
        gacc[...] += nn(hact[j], square(5 + j))
        set_square(5 + j, tn(hact[j], n2[...]))

    def back_output():
        _, scaled, inverse = normed(st1[...], gain(1), shift(1))
        down, grad_gain, grad_shift = normed_back(gacc[...], scaled, inverse, gain(1))
        gst[2:3, :] = grad_gain
        gst[3:4, :] = grad_shift
        down = down + st2[...]
        st2[...] = down
        g2b[...] = down.astype(low_type)
        grad_mix = nt(g2b[...], square(4)).astype(low_type)
        set_square(4, tn(mix[...], g2b[...]))
        mix[...] = grad_mix

    def back_attention():
        def one_pair(p, _):
            query2, key2, probs = pair_probs(p)
            value2 = qkv[:, pair_lanes(2, p)]
            upstream = twice(mix[:, pair_lanes(0, p)])
            grad_probs = nt(upstream, value2)
            centered = grad_probs - jnp.sum(probs * grad_probs, axis=1, keepdims=True)
            grad_scores = (probs * centered).astype(low_type)
            scale = 1.0 / math.sqrt(HD)
            grad_query = once(nn(grad_scores, key2)) * scale
            grad_key = tn(grad_scores, query2) * scale
            grad_value = tn(probs.astype(low_type), upstream)
            qkv[:, pair_lanes(0, p)] = grad_query.astype(low_type)
            qkv[:, pair_lanes(1, p)] = grad_key.astype(low_type)
            qkv[:, pair_lanes(2, p)] = grad_value.astype(low_type)
            return 0

        lax.fori_loop(0, HEADS // 2, one_pair, 0)
        gacc[...] = nn(qkv[...], triple())
        wg[:, :, :, UNIT : 4 * UNIT, :] = (
            tn(qkv[...], n1[...]).astype(low_type).reshape(4, 2, 2, 3 * UNIT, 2 * half)
        )

    def back_patch():
        _, scaled, inverse = normed(st0[...], gain(0), shift(0))
        down, grad_gain, grad_shift = normed_back(gacc[...], scaled, inverse, gain(0))
        grad = down + st2[...]
        grad_patch = jnp.where(jnp.logical_or(opening, masked), 0.0, grad).astype(low_type)
        set_square(0, nn(px[:, 0:TOK], grad_patch))
        lines = [
            grad[0:1],
            jnp.sum(jnp.where(masked, grad, 0.0), axis=0, keepdims=True),
            grad_gain, grad_shift, gst[2:3, :], gst[3:4, :], gst[4:5, :], gst[5:6, :],
        ]
        for n, line in enumerate(lines):
            grad = jnp.where(token == SEQ + n, line, grad)
        tab[0:TOK, :] = grad.astype(low_type)
        tab[TOK:, :] = jnp.zeros((tab.shape[0] - TOK, tab.shape[1]), low_type)

    tab_half = tab.shape[0] // 2
    rows_own = pl.ds(pl.multiple_of(k * tab_half, 16), tab_half)
    rows_other = pl.ds(pl.multiple_of((1 - k) * tab_half, 16), tab_half)
    d_z1 = (r, (z + 1 - 2 * (z % 2)) * 4 + x * 2 + k)
    d_z2 = (r, lax.rem(z + 2, 4) * 4 + x * 2 + k)
    own_part = tab.at[rows_own, lanes(r)]
    tab_moves = [
        remote(tab.at[rows_other, :], tabk, tab_send.at[0], tab_recv.at[0], d_k),
        remote(tab.at[rows_own, lanes(1 - r)], tabr.at[0], tab_send.at[1], tab_recv.at[1], d_y),
        remote(own_part, tabr.at[1], tab_send.at[2], tab_recv.at[2], d_x),
        remote(own_part, tabr.at[2], tab_send.at[3], tab_recv.at[3], d_z1),
        remote(own_part, tabr.at[3], tab_send.at[4], tab_recv.at[4], d_z2),
        remote(own_part, tabr.at[4], tab_send.at[5], tab_recv.at[5], d_k),
    ]

    def tab_step(n):
        tab_moves[n].wait()
        if n == 0:
            tab[rows_own, :] = (
                tab[rows_own, :].astype(wide) + tabk[...].astype(wide)
            ).astype(low_type)
        elif n < 5:
            tab[rows_own, lanes(r)] = (
                tab[rows_own, lanes(r)].astype(wide) + tabr[n - 1].astype(wide)
            ).astype(low_type)
        if n < 5:
            tab_moves[n + 1].start()

    def gh_moves(n):
        own, other = band(k * (BANDS // 2) + n), band((1 - k) * (BANDS // 2) + n)
        keep = pltpu.make_async_copy(hn.at[:, own], ghead.at[:, own], gh_sem.at[n])
        give = remote(hn.at[:, own], ghead.at[:, own], gh_send.at[n], gh_recv.at[n], d_k)
        take = remote(hn.at[:, other], ghead.at[:, other], gh_send.at[n], gh_recv.at[n], d_k)
        return keep, give, take

    def head_logits(n):
        v = k * (BANDS // 2) + n

        def rows_block(m, _):
            at = pl.ds(pl.multiple_of(m * 8 * MSLOT, 128), 8 * MSLOT)
            value = nn(pk[m].reshape(8 * MSLOT, 2 * half), hn[:, band(v)])
            cols = colb[at, :]
            hit = jnp.where(band_hit(v, cols[:, 1:2]), 1.0, 0.0)
            gch[at, :] = ((jnp.exp(value - cols[:, 0:1]) - hit) * cols[:, 2:3]).astype(low_type)
            return 0

        lax.fori_loop(0, 4, rows_block, 0)

    def head_grad(n):
        value = nn(pkt[...], gch[...])
        sq[3, 0:1, 0:128] += jnp.sum(jnp.sum(value * value, axis=0, keepdims=True), axis=1, keepdims=True)
        hn[:, band(k * (BANDS // 2) + n)] = value.astype(low_type)
        keep, give, _ = gh_moves(n)
        keep.start()
        give.start()

    def head_ready():
        for n in range(2):
            picked_done(n)
        lax.fori_loop(1, 16, ls_done, 0)

        def to_columns(n, _):
            flip[0:8, :] = lsb[n]
            colb[pl.ds(pl.multiple_of(n * 2 * MSLOT, 16), 2 * MSLOT), :] = jnp.transpose(flip[...])[: 2 * MSLOT]
            return 0

        lax.fori_loop(0, 16, to_columns, 0)

        def turn(n, _):
            rows = pk[n].reshape(8 * MSLOT, 2 * half)
            pkt[:, pl.ds(pl.multiple_of(n * 8 * MSLOT, 128), 8 * MSLOT)] = jnp.transpose(rows)
            return 0

        lax.fori_loop(0, 4, turn, 0)

    def back_step(s, _):
        def work(q, _):
            w = jnp.where(s == 0, 15 * q, jnp.where(s <= 4, 2 * s - 1 + q, s + 4 + 6 * q))

            @pl.when(jnp.logical_and(w >= 0, w < 4))
            def _():
                back_down(3 - w)

            @pl.when(jnp.logical_and(w >= 4, w < 8))
            def _():
                back_up(7 - w)

            @pl.when(w == 8)
            def _():
                back_output()

            @pl.when(w == 9)
            def _():
                back_attention()

            @pl.when(w == 10)
            def _():
                back_patch()

            @pl.when(jnp.logical_and(q == 0, s < UNITS))
            def _():
                sum_start(sums_moves(s)[0])

            @pl.when(jnp.logical_and(q == 0, jnp.logical_and(s >= 1, s < UNITS + 1)))
            def _():
                sums_one(s - 1)

            return 0

        lax.fori_loop(0, 2, work, 0)

        @pl.when(jnp.logical_and(s >= 3, s < UNITS + 3))
        def _():
            sums_two(s - 3)

        @pl.when(jnp.logical_and(s >= 5, s < UNITS + 5))
        def _():
            sums_three(s - 5)

        @pl.when(s >= 7)
        def _():
            sums_four(s - 7)

        for n in range(2):
            @pl.when(s == n)
            def _():
                picked_last(n)

        @pl.when(s == 4)
        def _():
            head_ready()

        @pl.when(s == 6)
        def _():
            tab_moves[0].start()

        for n in range(6):
            @pl.when(s == 7 + 2 * n)
            def _():
                tab_step(n)

        @pl.when(jnp.logical_and(s >= G_FIRST, s < G_FIRST + BANDS))
        def _():
            @pl.when((s - G_FIRST) % 2 == 0)
            def _():
                head_logits((s - G_FIRST) // 2)

            @pl.when((s - G_FIRST) % 2 == 1)
            def _():
                head_grad((s - G_FIRST) // 2)

        return 0

    lax.fori_loop(0, UNITS + 7, back_step, 0)
    gtab_out[rows_own, :] = tab[rows_own, lanes(r)].astype(wide)
    gtab_out[rows_other, :] = tabr[4].astype(wide)
    value = gtab_out[...]
    first_col = jnp.where(c == 0, 1.0, 0.0)
    first_chip = jnp.where(c < 2, 1.0, 0.0)
    table_squares = jnp.sum(jnp.sum(value * value, axis=0, keepdims=True), axis=1, keepdims=True)
    line = lax.broadcasted_iota(jnp.int32, (8, 128), 0)
    squares = sq[2, 0:1, 0:128] + sq[3, 0:1, 0:128] * first_chip + table_squares * first_col
    count = (counts[0] + counts[1]).astype(wide) * leader
    fin[r * 16 + c] = jnp.where(
        line == 0, loss_part, jnp.where(line == 1, count, jnp.where(line == 2, squares, 0.0))
    )

    def fin_copy(n, step):
        other = lax.rem(r * 16 + c + step, 32)
        owner = r * 16 + c if n == 0 else lax.rem(r * 16 + c + 32 - step, 32)
        ref = fin.at[owner]
        return remote(ref, ref, fin_send.at[step], fin_recv.at[step], (other // 16, other % 16))

    def fin_start(step, _):
        fin_copy(0, step).start()
        return 0

    def fin_done(step, _):
        fin_copy(0, step).wait_send()
        fin_copy(1, step).wait_recv()
        return 0

    lax.fori_loop(1, 32, fin_start, 0)
    lax.fori_loop(0, UNITS, sums_sent, 0)
    for n in range(2):
        for moves in picked_moves(n):
            sent(moves)
    for n in range(BANDS // 2):
        keep, give, take = gh_moves(n)
        keep.wait()
        give.wait_send()
        take.wait_recv()
    lax.fori_loop(1, 32, fin_done, 0)
    totals = jnp.sum(fin[...], axis=0)
    count_total = totals[1:2, :]
    norm_value = jnp.sqrt(totals[2:3, :]) / count_total
    scal_out[0:1, :] = totals[0:1, :] / count_total
    scal_out[1:2, :] = norm_value
    scal_out[2:3, :] = jnp.minimum(1.0, clip_limit / norm_value) / count_total
    scal_out[3:8, :] = jnp.zeros((5, 128), wide)


def step_call(pix, blocks, tab, places, targets, counts, head, drift, power):
    half = tab.shape[1]
    full = 2 * half
    vocab = head.shape[1]
    slots = 32 * MSLOT
    vm = pltpu.VMEM
    dma = pltpu.SemaphoreType.DMA
    f32, b16 = wide, low_type
    scratch = [
        vm((4, 2, 2, UNITS * UNIT, full), b16),
        vm((2, 8, UNIT, 256), b16),
        vm((8, UNIT, 256), b16),
        vm((16 * UNIT, 256), b16),
        vm((TOK, full), f32),
        vm((TOK, full), f32), vm((TOK, full), f32), vm((TOK, full), f32),
        vm((TOK, full), b16), vm((TOK, full), b16), vm((TOK, full), b16),
        vm((TOK, 3 * full), b16),
        vm((4, TOK, full), f32),
        vm((4, TOK, full), b16),
        vm((full, vocab), b16),
        vm((3, UNIT, vocab), f32),
        vm((4, 2, 2, 2 * MSLOT, full), b16),
        vm((MSLOT, full), b16),
        vm((2 * MSLOT, full), b16),
        vm((BANDS, 2 * MSLOT, 512), f32),
        vm((full, slots), b16),
        vm((slots, 512), b16),
        vm((slots, 128), f32),
        vm((4, 8, 256), f32),
        vm((16, 8, 256), f32),
        vm((128, 256), f32),
        vm((256, 128), f32),
        vm((2 * MSLOT, full), f32),
        vm((MSLOT, full), b16), vm((MSLOT, full), b16),
        vm((TOK, full), b16),
        vm((TOK, full), f32),
        vm((8, full), f32),
        vm((4, 4, 2, UNIT, full), b16),
        vm((7, 2, 2, UNIT, half), b16),
        vm((7, 2, UNIT, full), b16),
        vm((7, 2, UNIT, half), b16),
        vm((7, 2, UNIT, half), b16),
        vm((7, 3, UNIT, half), b16),
        vm((224, full), b16),
        vm((112, full), b16),
        vm((5, 112, half), b16),
        vm((32, 8, 128), f32),
        dma((UNITS, 12)), dma((UNITS, 12)),
        dma((2,)), dma((2, 8)), dma((16,)),
        dma((2, 2)),
        dma((2, 12)), dma((2, 12)),
        dma((3,)), dma((3,)),
        dma((16,)), dma((16,)),
        dma((UNITS, 8)), dma((UNITS, 8)),
        dma((6,)), dma((6,)),
        dma((32,)), dma((32,)),
        dma((3,)), dma((5,)),
        dma((BANDS // 2,)), dma((BANDS // 2,)), dma((BANDS // 2,)),
    ]
    in_vmem = pl.BlockSpec(memory_space=pltpu.VMEM)
    return pl.pallas_call(
        step_kernel,
        out_shape=(
            jax.ShapeDtypeStruct((UNITS * UNIT, half), f32),
            jax.ShapeDtypeStruct((224, half), f32),
            jax.ShapeDtypeStruct((full, vocab), b16),
            jax.ShapeDtypeStruct((8, 128), f32),
            *([jax.ShapeDtypeStruct((full, vocab), b16)] * 3),
        ),
        in_specs=[
            *([in_vmem] * 9),
            pl.BlockSpec(memory_space=pltpu.SMEM),
            *([pl.BlockSpec(memory_space=pl.ANY)] * 3),
        ],
        out_specs=(
            in_vmem, in_vmem, pl.BlockSpec(memory_space=pl.ANY), in_vmem,
            *([pl.BlockSpec(memory_space=pl.ANY)] * 3),
        ),
        scratch_shapes=scratch,
        compiler_params=pltpu.CompilerParams(
            collective_id=0, has_side_effects=True, vmem_limit_bytes=VMEM_LIMIT
        ),
        cost_estimate=pl.CostEstimate(flops=50_000_000_000, bytes_accessed=40_000_000, transcendentals=0),
    )(pix, *blocks, tab, places, targets, counts, head, drift, power)


def block_path(
    pixels, mask_places, mask_count, targets, step_count,
    patch_weight, vector_table, input_weight, output_weight, upward_weight, downward_weight, head_weight,
    *moments,
):
    weights = (
        patch_weight, vector_table, input_weight, output_weight, upward_weight, downward_weight, head_weight,
    )
    weights = flat(weights)
    blocks = [weights[n] for n in (0, 2, 3, 4, 5)]
    drifts, powers = flat(moments[:7]), flat(moments[7:])
    gout, gtab, ghead, scal, *low = step_call(
        pixels.T, blocks, vector_table, mask_places, targets, mask_count, head_weight, drifts[6], powers[6]
    )
    states = [(*group[:6], value) for group, value in zip((weights, drifts, powers), low)]
    results = adam_call(scal, step_count, gout, gtab, ghead, *states)
    triples = [results[2 + n :: 3] for n in range(3)]
    triples = [unflat(triple) for triple in triples]
    return (*results[:2], *(triple[n] for n in range(7) for triple in triples))


def flat(values):
    patch, table, inward, outward, up, down, head = values
    return (patch, table, inward[0].T, outward[0], up[0].T, down[0], head)


def unflat(values):
    patch, table, inward, outward, up, down, head = values
    return (patch, table, inward.T[None], outward[None], up.T[None], down[None], head)


SMALL = UNITS * UNIT
ROWS = 48
IN_SLOTS = 4
OUT_SLOTS = 3


def adam_kernel(
    scal, step, gout, gtab, ghead, *refs
):
    weights, drifts, powers = refs[:7], refs[7:14], refs[14:21]
    loss_out, norm_out = refs[21:23]
    outs = refs[23:44]
    gbuf, inbuf, outbuf, gsm, insm, outsm, gtb, intb, outtb, in_sem, out_sem, sm_in, sm_out = refs[44:]
    factor = scal[2:3, 0:1]
    count = jnp.full((1, 128), step[0], jnp.int32).astype(wide)[:, 0:1]
    scale_first = 1.0 / (1.0 - jnp.exp(count * math.log(beta_first)))
    scale_second = 1.0 / (1.0 - jnp.exp(count * math.log(beta_second)))
    count_first = scale_first * -learn_rate
    gain_first = factor * (1.0 - beta_first)
    gain_second = factor * factor * (1.0 - beta_second)
    chunks = ghead.shape[0] // ROWS
    states = (weights, drifts, powers)

    def rows_of(n):
        return pl.ds(pl.multiple_of(n * ROWS, ROWS), ROWS)

    def fetch(n):
        slot = lax.rem(n, IN_SLOTS)
        copies = [
            pltpu.make_async_copy(states[m][6].at[rows_of(n)], inbuf.at[slot, m], in_sem.at[slot, m])
            for m in range(3)
        ]
        copies.append(pltpu.make_async_copy(ghead.at[rows_of(n)], gbuf.at[slot], in_sem.at[slot, 3]))
        return copies

    def store(n):
        slot = lax.rem(n, OUT_SLOTS)
        return [
            pltpu.make_async_copy(outbuf.at[slot, m], outs[18 + m].at[rows_of(n)], out_sem.at[slot, m])
            for m in range(3)
        ]

    order = (0, 2, 3, 4, 5)
    small_fetch, small_store = [], []
    start = 0
    for at, n in enumerate(order):
        height = weights[n].shape[0]
        for m in range(3):
            small_fetch.append(
                pltpu.make_async_copy(states[m][n], insm.at[m, start : start + height], sm_in.at[at, m])
            )
            small_store.append(
                pltpu.make_async_copy(outsm.at[m, start : start + height], outs[3 * n + m], sm_out.at[at, m])
            )
        start += height
    for m in range(3):
        small_fetch.append(pltpu.make_async_copy(states[m][1], intb.at[m], sm_in.at[5, m]))
        small_store.append(pltpu.make_async_copy(outtb.at[m], outs[3 + m], sm_out.at[5, m]))
    small_fetch.append(pltpu.make_async_copy(gout, gsm, sm_in.at[6, 0]))
    small_fetch.append(pltpu.make_async_copy(gtab, gtb, sm_in.at[6, 1]))

    def adam(grad, weight, drift, power):
        new_drift = beta_first * drift + gain_first * grad
        new_power = beta_second * power + gain_second * (grad * grad)
        below = jnp.sqrt(new_power * scale_second) + adam_eps
        update = new_drift * count_first / below - (learn_rate * weight_decay) * weight
        return update, new_drift, new_power

    for n in range(IN_SLOTS):
        for copy in fetch(n):
            copy.start()
    for copy in small_fetch:
        copy.start()
    loss_out[...] = scal[0:1, 0:1]
    norm_out[...] = scal[1:2, 0:1]

    def chunk(n, _):
        for copy in fetch(n):
            copy.wait()

        @pl.when(n >= OUT_SLOTS)
        def _():
            for copy in store(n - OUT_SLOTS):
                copy.wait()

        slot, spot = lax.rem(n, IN_SLOTS), lax.rem(n, OUT_SLOTS)

        def part(q, _):
            at = pl.ds(pl.multiple_of(q * 16, 16), 16)
            values = adam(
                gbuf[slot, at, :].astype(wide), *(inbuf[slot, m, at, :].astype(wide) for m in range(3))
            )
            for m in range(3):
                outbuf[spot, m, at, :] = values[m]
            return 0

        lax.fori_loop(0, ROWS // 16, part, 0)
        for copy in store(n):
            copy.start()

        @pl.when(n + IN_SLOTS < chunks)
        def _():
            for copy in fetch(n + IN_SLOTS):
                copy.start()

        @pl.when(n == 2)
        def _():
            for copy in small_fetch:
                copy.wait()

            def small(q, _):
                at = pl.ds(pl.multiple_of(q * UNIT, UNIT), UNIT)
                values = adam(gsm[at, :], insm[0, at, :], insm[1, at, :], insm[2, at, :])
                for m in range(3):
                    outsm[m, at, :] = values[m]
                return 0

            lax.fori_loop(0, UNITS, small, 0)
            values = adam(gtb[0 : intb.shape[1]], intb[0], intb[1], intb[2])
            for m in range(3):
                outtb[m] = values[m]
            for copy in small_store:
                copy.start()

        return 0

    lax.fori_loop(0, chunks, chunk, 0)
    for n in range(chunks - OUT_SLOTS, chunks):
        for copy in store(n):
            copy.wait()
    for copy in small_store:
        copy.wait()


def adam_call(scal, step, gout, gtab, ghead, weights, drifts, powers):
    half = gout.shape[1]
    vocab = ghead.shape[1]
    table = weights[1].shape[0]
    one = jax.ShapeDtypeStruct((1, 1), wide)
    shapes = [jax.ShapeDtypeStruct(value.shape, wide) for value in weights for _ in range(3)]
    in_vmem = pl.BlockSpec(memory_space=pltpu.VMEM)
    anywhere = pl.BlockSpec(memory_space=pl.ANY)
    vm, dma = pltpu.VMEM, pltpu.SemaphoreType.DMA
    results = pl.pallas_call(
        adam_kernel,
        in_specs=[in_vmem, pl.BlockSpec(memory_space=pltpu.SMEM)] + [anywhere] * 24,
        out_specs=[in_vmem] * 2 + [anywhere] * 21,
        out_shape=[one, one] + shapes,
        scratch_shapes=[
            vm((IN_SLOTS, ROWS, vocab), low_type), vm((IN_SLOTS, 3, ROWS, vocab), low_type),
            vm((OUT_SLOTS, 3, ROWS, vocab), wide),
            vm((SMALL, half), wide), vm((3, SMALL, half), wide), vm((3, SMALL, half), wide),
            vm(gtab.shape, wide), vm((3, table, half), wide), vm((3, table, half), wide),
            dma((IN_SLOTS, 4)), dma((OUT_SLOTS, 3)), dma((7, 3)), dma((6, 3)),
        ],
        compiler_params=pltpu.CompilerParams(vmem_limit_bytes=VMEM_LIMIT),
        cost_estimate=pl.CostEstimate(flops=60_000_000, bytes_accessed=82_000_000, transcendentals=4_000_000),
    )(scal, step, gout, gtab, ghead, *weights, *drifts, *powers)
    return (results[0].reshape(()), results[1].reshape(()), *results[2:])


def solution(mesh):
    state = (
        P("col", "row"),
        P(None, "row"),
        P(None, "row", "col"),
        P(None, "col", "row"),
        P(None, "row", "col"),
        P(None, "col", "row"),
        P(None, "row"),
    )
    data = (P("row", "col"), P("col", None), P("col"), P("col", None), P())
    outs = (P(), P()) + tuple(spec for spec in state for _ in range(3))
    fits = dict(mesh.shape) == {"row": 2, "col": 16}
    return jax.shard_map(
        block_path if fits else on_device,
        mesh=mesh,
        in_specs=data + state * 3,
        out_specs=outs,
        check_vma=False,
    )
```

```python
import math

import jax
import jax.numpy as jnp
from jax import lax
from jax.experimental import pallas as pl
from jax.experimental.pallas import tpu as pltpu
from jax.sharding import PartitionSpec as P

HEADS = 12
HD = 64
SEQ = 197
MSLOT = 80
BOTH = ("row", "col")

norm_eps = 1e-06
clip_limit = 0.1
learn_rate = 0.01
beta_first = 0.9
beta_second = 0.999
adam_eps = 1e-08
weight_decay = 0.05
low_type = jnp.bfloat16
wide = jnp.float32


def product(left, right):
    return jnp.dot(left, right, preferred_element_type=wide)


def product_nt(left, right):
    return jnp.einsum("ab,cb->ac", left, right, preferred_element_type=wide)


def product_tn(left, right):
    return jnp.einsum("ab,ac->bc", left, right, preferred_element_type=wide)


def norm_forward(values, gain, shift):
    center = jnp.mean(values, axis=1, keepdims=True)
    moved = values - center
    inverse = lax.rsqrt(jnp.mean(moved * moved, axis=1, keepdims=True) + norm_eps)
    scaled = moved * inverse
    return scaled * gain + shift, (scaled, inverse)


def norm_backward(upstream, kept, gain):
    scaled, inverse = kept
    inner = upstream * gain
    downstream = inverse * (
        inner
        - jnp.mean(inner, axis=1, keepdims=True)
        - scaled * jnp.mean(inner * scaled, axis=1, keepdims=True)
    )
    return downstream, jnp.sum(upstream * scaled, axis=0), jnp.sum(upstream, axis=0)


def exact_gelu(values):
    return jax.nn.gelu(values, approximate=False)


def split_heads(grouped):
    images = grouped.shape[0] // SEQ
    pieces = grouped.reshape(images, SEQ, 3, HEADS, HD)
    return pieces[:, :, 0], pieces[:, :, 1], pieces[:, :, 2]


def attention_weights(query, keys):
    scores = jnp.einsum("iqhd,ikhd->ihqk", query, keys, preferred_element_type=wide)
    return jax.nn.softmax(scores * (1.0 / math.sqrt(HD)), axis=-1)


def attend(grouped):
    query, keys, values = split_heads(grouped)
    weights_full = attention_weights(query, keys)
    mixture = jnp.einsum(
        "ihqk,ikhd->iqhd", weights_full.astype(low_type), values, preferred_element_type=wide
    )
    return mixture.reshape(grouped.shape[0], HEADS * HD), weights_full


def attend_back(grouped, weights_full, grad_mixture):
    query, keys, values = split_heads(grouped)
    images = query.shape[0]
    weights_low = weights_full.astype(low_type)
    grad_out = grad_mixture.reshape(images, SEQ, HEADS, HD)
    grad_weights = jnp.einsum("iqhd,ikhd->ihqk", grad_out, values, preferred_element_type=wide)
    grad_values = jnp.einsum("ihqk,iqhd->ikhd", weights_low, grad_out, preferred_element_type=wide)
    centered = grad_weights - jnp.sum(weights_full * grad_weights, axis=-1, keepdims=True)
    grad_scores = (weights_full * centered).astype(low_type)
    scale = 1.0 / math.sqrt(HD)
    grad_query = jnp.einsum("ihqk,ikhd->iqhd", grad_scores, keys, preferred_element_type=wide)
    grad_keys = jnp.einsum("ihqk,iqhd->ikhd", grad_scores, query, preferred_element_type=wide)
    stacked = jnp.stack([grad_query * scale, grad_keys * scale, grad_values], axis=2)
    return stacked.reshape(images * SEQ, 3 * HEADS * HD)


def adam_step(weight, grad, drift, power, factor, step_value):
    scaled = grad * factor
    new_drift = beta_first * drift + (1.0 - beta_first) * scaled
    new_power = beta_second * power + (1.0 - beta_second) * scaled * scaled
    drift_hat = new_drift / (1.0 - jnp.power(beta_first, step_value))
    power_hat = new_power / (1.0 - jnp.power(beta_second, step_value))
    update = -learn_rate * (drift_hat / (jnp.sqrt(power_hat) + adam_eps) + weight_decay * weight)
    return (update, new_drift, new_power)


def on_device(
    pixels,
    mask_places,
    mask_count,
    targets,
    step_count,
    patch_weight,
    vector_table,
    input_weight,
    output_weight,
    upward_weight,
    downward_weight,
    head_weight,
    drift_patch,
    drift_table,
    drift_input,
    drift_output,
    drift_upward,
    drift_downward,
    drift_head,
    power_patch,
    power_table,
    power_input,
    power_output,
    power_upward,
    power_downward,
    power_head,
):
    rows, cols = lax.axis_size("row"), lax.axis_size("col")
    row_index = lax.axis_index("row")
    col_index = lax.axis_index("col")
    images = mask_places.shape[0] // rows
    width = vector_table.shape[1] * rows

    blocks = [
        patch_weight.astype(low_type),
        input_weight[0].astype(low_type).T,
        output_weight[0].astype(low_type),
        upward_weight[0].astype(low_type).T,
        downward_weight[0].astype(low_type),
    ]
    heights = [block.shape[0] for block in blocks]
    gathered = lax.all_gather(jnp.concatenate(blocks, axis=0), BOTH, axis=0, tiled=False)
    gathered = gathered.reshape(rows, cols, sum(heights), -1)

    def whole(index):
        start = sum(heights[:index])
        part = gathered[:, :, start : start + heights[index]]
        return jnp.transpose(part, (1, 2, 0, 3)).reshape(cols * heights[index], width)

    patch_low, input_turned, output_low, upward_turned, downward_low = map(whole, range(5))
    table = lax.all_gather(vector_table, "row", axis=1, tiled=True)

    local_images = pixels.shape[0] // SEQ
    part = pixels.shape[1]
    grid = pixels.reshape(local_images // (rows * images), rows, images, SEQ, part)
    grid = lax.all_to_all(grid, "row", split_axis=1, concat_axis=0, tiled=True)
    grid = grid.reshape(cols, images * SEQ, part)
    grid = lax.all_to_all(grid, "col", split_axis=0, concat_axis=0, tiled=True)
    pixel_own = jnp.transpose(grid, (1, 0, 2)).reshape(images * SEQ, cols * part)

    def own(values):
        return lax.dynamic_slice_in_dim(values, row_index * images, images, axis=0)

    places_own, count_own = own(mask_places), own(mask_count)

    def gains_of(norm_index):
        return (table[SEQ + 2 + 2 * norm_index], table[SEQ + 3 + 2 * norm_index])

    patch_proj = product(pixel_own, patch_low)
    places = jnp.arange(SEQ, dtype=jnp.int32)
    counted_own = jnp.arange(MSLOT, dtype=jnp.int32)[None, :] < count_own[:, None]
    matches = places_own[:, :, None] == places[None, None, :]
    masked = jnp.any(matches & counted_own[:, :, None], axis=1)[:, :, None]
    opening = (places == 0)[None, :, None]
    stream = jnp.where(
        opening,
        table[SEQ],
        jnp.where(masked, table[SEQ + 1], patch_proj.reshape(images, SEQ, -1)),
    )
    stream = (stream + table[:SEQ][None]).reshape(images * SEQ, -1)
    gain_one, shift_one = gains_of(0)
    gain_two, shift_two = gains_of(1)
    final_gain, final_shift = gains_of(2)
    normed_one, stats_one = norm_forward(stream, gain_one, shift_one)
    normed_one = normed_one.astype(low_type)
    grouped = product_nt(normed_one, input_turned).astype(low_type)
    mixture, weights_full = attend(grouped)
    mixture = mixture.astype(low_type)
    stream_mid = stream + product(mixture, output_low)
    normed_two, stats_two = norm_forward(stream_mid, gain_two, shift_two)
    normed_two = normed_two.astype(low_type)
    hidden_pre = product_nt(normed_two, upward_turned)
    hidden_act = exact_gelu(hidden_pre).astype(low_type)
    stream_last = stream_mid + product(hidden_act, downward_low)
    final_out, final_stats = norm_forward(stream_last, final_gain, final_shift)
    selector = matches.astype(low_type)
    picked = jnp.einsum(
        "ims,isd->imd", selector, final_out.astype(low_type).reshape(images, SEQ, -1),
        preferred_element_type=wide,
    ).astype(low_type)

    picked_wide = lax.all_gather(picked.reshape(images * MSLOT, -1), "row", axis=0, tiled=True)
    head_low = head_weight.astype(low_type)
    logits = product(picked_wide, head_low)
    vocab_local = head_weight.shape[1]
    target_local = targets.reshape(-1) - row_index * vocab_local
    target_hits = target_local[:, None] == jnp.arange(vocab_local, dtype=jnp.int32)[None, :]
    chosen = jnp.sum(jnp.where(target_hits, logits, 0.0), axis=1)
    local_top = jnp.max(logits, axis=1)
    local_sum = jnp.sum(jnp.exp(logits - local_top[:, None]), axis=1)
    pair = lax.all_gather(jnp.stack([local_top, local_sum]), "row", axis=0, tiled=False)
    top_value = jnp.max(pair[:, 0], axis=0)
    exp_total = jnp.sum(pair[:, 1] * jnp.exp(pair[:, 0] - top_value), axis=0)
    log_total = top_value + jnp.log(exp_total)
    counted = jnp.arange(MSLOT, dtype=jnp.int32)[None, :] < mask_count[:, None]
    slot_weight = counted.reshape(-1).astype(wide)
    leader_row = (row_index == 0).astype(wide)
    loss_part = jnp.sum(log_total * slot_weight) * leader_row - jnp.sum(chosen * slot_weight)
    count_part = jnp.sum(mask_count.astype(wide)) * leader_row
    grad_logits = (
        (jnp.exp(logits - log_total[:, None]) - target_hits.astype(wide)) * slot_weight[:, None]
    ).astype(low_type)
    grad_head_local = product_tn(picked_wide, grad_logits)
    grad_head = lax.psum(grad_head_local.astype(low_type), "col").astype(wide)
    grad_picked = lax.psum_scatter(
        product_nt(grad_logits, head_low).astype(low_type),
        "row",
        scatter_dimension=0,
        tiled=True,
    )
    grad_final = jnp.einsum(
        "ims,imd->isd", selector, grad_picked.reshape(images, MSLOT, -1),
        preferred_element_type=wide,
    )

    grad_stream, grad_final_gain, grad_final_shift = norm_backward(
        grad_final.reshape(images * SEQ, -1), final_stats, final_gain
    )
    grad_two = grad_stream.astype(low_type)
    grad_downward = product_tn(hidden_act, grad_two)
    grad_act = product_nt(grad_two, downward_low)
    _, gelu_pull = jax.vjp(exact_gelu, hidden_pre)
    grad_pre = gelu_pull(grad_act)[0].astype(low_type)
    grad_upward_turned = product_tn(grad_pre, normed_two)
    grad_normed_two = product(grad_pre, upward_turned)
    grad_mid, grad_gain_two, grad_shift_two = norm_backward(grad_normed_two, stats_two, gain_two)
    grad_mid = grad_mid + grad_stream
    grad_one = grad_mid.astype(low_type)
    grad_output = product_tn(mixture, grad_one)
    grad_mixture = product_nt(grad_one, output_low).astype(low_type)
    grad_grouped = attend_back(grouped, weights_full, grad_mixture).astype(low_type)
    grad_input_turned = product_tn(grad_grouped, normed_one)
    grad_normed_one = product(grad_grouped, input_turned)
    grad_below, grad_gain_one, grad_shift_one = norm_backward(grad_normed_one, stats_one, gain_one)
    grad_grid = (grad_below + grad_mid).reshape(images, SEQ, -1)
    grad_patch = jnp.where(opening | masked, 0.0, grad_grid).reshape(images * SEQ, -1)
    grad_patch_weight = product_tn(pixel_own, grad_patch.astype(low_type))
    lines = [
        jnp.sum(grad_grid, axis=0),
        jnp.sum(grad_grid[:, 0], axis=0)[None],
        jnp.sum(jnp.where(masked, grad_grid, 0.0), axis=(0, 1))[None],
        jnp.stack(
            [grad_gain_one, grad_shift_one, grad_gain_two, grad_shift_two,
             grad_final_gain, grad_final_shift]
        ),
    ]
    table_local = jnp.concatenate(lines, axis=0).astype(low_type)

    def dealt(value, height):
        grid = value.astype(low_type).reshape(cols, height, rows, -1)
        return jnp.transpose(grid, (2, 0, 1, 3)).reshape(rows * cols, height, -1)

    stacked = jnp.concatenate(
        [
            dealt(value, height)
            for value, height in zip(
                [grad_patch_weight, grad_input_turned, grad_output, grad_upward_turned,
                 grad_downward],
                heights,
            )
        ],
        axis=1,
    )
    summed = lax.psum_scatter(stacked, BOTH, scatter_dimension=0, tiled=False).astype(wide)
    starts = [sum(heights[:index]) for index in range(6)]
    pieces = [summed[starts[index] : starts[index + 1]] for index in range(5)]
    grad_table = lax.psum(table_local, BOTH).astype(wide)
    grad_table = lax.dynamic_slice_in_dim(
        grad_table, row_index * vector_table.shape[1], vector_table.shape[1], axis=1
    )
    leader_col = (col_index == 0).astype(wide)
    squares_part = jnp.sum(summed * summed) + leader_col * (
        jnp.sum(grad_table * grad_table) + jnp.sum(grad_head * grad_head)
    )
    loss_total, count_total, squares_total = lax.psum((loss_part, count_part, squares_part), BOTH)
    mean_loss = loss_total / count_total
    grad_norm = jnp.sqrt(squares_total) / count_total
    factor = jnp.minimum(1.0, clip_limit / grad_norm) / count_total
    step_value = step_count[0].astype(wide)
    steps = [
        (patch_weight, pieces[0], drift_patch, power_patch),
        (vector_table, grad_table, drift_table, power_table),
        (input_weight, pieces[1].T[None], drift_input, power_input),
        (output_weight, pieces[2][None], drift_output, power_output),
        (upward_weight, pieces[3].T[None], drift_upward, power_upward),
        (downward_weight, pieces[4][None], drift_downward, power_downward),
        (head_weight, grad_head, drift_head, power_head),
    ]
    results = []
    for weight, grad, drift, power in steps:
        results.extend(adam_step(weight, grad, drift, power, factor, step_value))
    return (mean_loss, grad_norm, *results)


VMEM_LIMIT = 62 * 2**20
TOK = 208
UNIT = 48
UNITS = 13
BANDS = 8
G_FIRST = 7
AHEAD = 2
LAG_A = 1
LAG_B = 3
LAG_C = 4
EYE = pl.DeviceIdType.MESH


def nn(left, right):
    return jnp.dot(left, right, preferred_element_type=wide)


def nt(left, right):
    return lax.dot_general(left, right, (((1,), (1,)), ((), ())), preferred_element_type=wide)


def tn(left, right):
    return lax.dot_general(left, right, (((0,), (0,)), ((), ())), preferred_element_type=wide)


def gelu_parts(values):
    phi_total = 0.5 * (1.0 + lax.erf(values * math.sqrt(0.5)))
    density = jnp.exp(values * values * -0.5) * (1.0 / math.sqrt(2.0 * math.pi))
    return phi_total, density


def normed(values, gain, shift):
    center = jnp.mean(values, axis=1, keepdims=True)
    moved = values - center
    inverse = lax.rsqrt(jnp.mean(moved * moved, axis=1, keepdims=True) + norm_eps)
    scaled = moved * inverse
    return scaled * gain + shift, scaled, inverse


def normed_back(upstream, scaled, inverse, gain):
    inner = upstream * gain
    down = inverse * (
        inner
        - jnp.mean(inner, axis=1, keepdims=True)
        - scaled * jnp.mean(inner * scaled, axis=1, keepdims=True)
    )
    return (
        down,
        jnp.sum(upstream * scaled, axis=0, keepdims=True),
        jnp.sum(upstream, axis=0, keepdims=True),
    )


def step_kernel(
    pix_in, patch_in, input_in, output_in, up_in, down_in, tab_in, places, targets, counts, head_in, drift_in, power_in,
    gout, gtab_out, ghead, scal_out, head_low, drift_low, power_low,
    wg, px_out, px_mid, px, tb, st0, st1, st2, n1, n2, mix, qkv, hpre, hact,
    hn, hbuf, pk, pkp, pp, lt, pkt, gch, colb, sq, lsb, flip, tmpa, gpk, gps, gpr, g2b, gacc, gst,
    rk, r1a, r1b, r2a, r2b, rz, tab, tabk, tabr, fin,
    ag_send, ag_recv, px_sem, px_send, px_recv, tb_sem, pk_send, pk_recv, ex_send, ex_recv,
    ls_send, ls_recv, rs_send, rs_recv, tab_send, tab_recv, fin_send, fin_recv, hb_sem, st_sem, gh_sem, gh_send, gh_recv,
):
    r = lax.axis_index("row")
    c = lax.axis_index("col")
    z, x, k = c // 4, (c // 2) % 2, c % 2
    half = tb.shape[1] // 2
    d_y = (1 - r, c)
    d_x = (r, z * 4 + (1 - x) * 2 + k)
    d_k = (r, z * 4 + x * 2 + 1 - k)

    def d_z(step):
        return (r, lax.rem(z + step, 4) * 4 + x * 2 + k)

    def remote(src, dst, send, recv, device):
        return pltpu.make_async_remote_copy(
            src_ref=src, dst_ref=dst, send_sem=send, recv_sem=recv,
            device_id=device, device_id_type=EYE,
        )

    def lanes(row):
        return pl.ds(pl.multiple_of(row * half, half), half)

    sq[...] = jnp.zeros_like(sq)
    width = px_out.shape[3]
    barrier = pltpu.get_barrier_semaphore()

    def greet(n, _):
        other = lax.rem(r * 16 + c + n, 32)
        pl.semaphore_signal(barrier, inc=1, device_id=(other // 16, other % 16), device_id_type=EYE)
        return 0

    lax.fori_loop(1, 32, greet, 0)

    for n in range(16):
        px_out[n % 2, n // 2, :, 0:SEQ] = pix_in[:, n * SEQ : (n + 1) * SEQ]
        px_out[n % 2, n // 2, :, SEQ:] = jnp.zeros((UNIT, width - SEQ), low_type)
    heights = (UNIT, 3 * UNIT, UNIT, 4 * UNIT, 4 * UNIT)
    blocks = (
        patch_in[...], input_in[...], output_in[...], up_in[...], down_in[...],
    )
    start = 0
    for height, block in zip(heights, blocks):
        wg[z, x, k, start : start + height, lanes(r)] = block.astype(low_type)
        start += height
    tb[0 : tab_in.shape[0], lanes(r)] = tab_in[...]
    tb[tab_in.shape[0] :, lanes(r)] = jnp.zeros((TOK - tab_in.shape[0], half), wide)
    wide_states = (head_in, drift_in, power_in)
    low_states = (head_low, drift_low, power_low)

    def state_rows(b):
        return pl.ds(pl.multiple_of(b * UNIT, UNIT), UNIT)

    def state_in(a, b):
        return pltpu.make_async_copy(wide_states[a].at[state_rows(b)], hbuf.at[a], hb_sem.at[a])

    wide_part = pkt.shape[1]
    rest_part = hn.shape[1] - wide_part

    def state_out(a, b):
        rows = state_rows(b)
        if a == 0:
            return [pltpu.make_async_copy(hn.at[rows], head_low.at[rows], st_sem.at[0])]
        first = pkt.at[UNIT * (a - 1) : UNIT * a]
        second = pkt.at[UNIT * (a + 1) : UNIT * (a + 2), 0:rest_part]
        low = low_states[a]
        return [
            pltpu.make_async_copy(first, low.at[rows, 0:wide_part], st_sem.at[a]),
            pltpu.make_async_copy(second, low.at[rows, wide_part:], st_sem.at[a + 2]),
        ]

    for a in range(3):
        state_in(a, 0).start()
    pl.semaphore_wait(barrier, 31)

    def gather_moves(buf, part, both, send, recv):
        lo, hi = pl.ds(0, 2), pl.ds(2, 2)
        every = slice(None)
        other = lax.rem

        def move(index, out_region, in_region, device):
            out_ref = buf.at[out_region]
            in_ref = buf.at[in_region]
            return (
                remote(out_ref, out_ref, send.at[index], recv.at[index], device),
                remote(in_ref, in_ref, send.at[index], recv.at[index], device),
            )

        first = [
            move(n - 1, (z, x, k) + part(r), (lax.rem(z + 4 - n, 4), x, k) + part(r), d_z(n))
            for n in (1, 2, 3)
        ]
        second = [
            move(3, (lo, x, k) + part(r), (lo, 1 - x, k) + part(r), d_x),
            move(4, (hi, x, k) + part(r), (hi, x, k) + part(1 - r), d_y),
        ]
        pair_one = [move(5, (every, x, k) + part(r), (every, x, 1 - k) + part(r), d_k)]
        third = [
            move(6, (lo, every, k) + part(r), (lo, every, k) + part(1 - r), d_y),
            move(7, (hi, x, k) + both, (hi, 1 - x, k) + both, d_x),
        ]
        pair_two = [
            move(8, (lo, 1 - x, k) + part(r), (lo, 1 - x, 1 - k) + part(r), d_k),
            move(9, (hi, x, k) + part(1 - r), (hi, x, 1 - k) + part(1 - r), d_k),
        ]
        pair_three = [
            move(10, (lo, every, k) + part(1 - r), (lo, every, 1 - k) + part(1 - r), d_k),
            move(11, (hi, 1 - x, k) + both, (hi, 1 - x, 1 - k) + both, d_k),
        ]
        return first, second, pair_one, third, pair_two, pair_three

    def begin(moves):
        for out_copy, _ in moves:
            out_copy.start()

    def landed(moves):
        for _, in_copy in moves:
            in_copy.wait_recv()

    def sent(moves):
        for out_copy, _ in moves:
            out_copy.wait_send()

    def unit_rows(n):
        return pl.ds(pl.multiple_of(n * UNIT, UNIT), UNIT)

    def weight_moves(n):
        rows = unit_rows(n)
        return gather_moves(
            wg, lambda row: (rows, lanes(row)), (rows, slice(None)), ag_send.at[n], ag_recv.at[n]
        )

    late = UNITS - 1

    def late_moves():
        rows = unit_rows(late)
        every = slice(None)

        def move(index, out_region, in_region, device):
            out_ref, in_ref = wg.at[out_region], wg.at[in_region]
            send, recv = ag_send.at[late, index], ag_recv.at[late, index]
            return remote(out_ref, out_ref, send, recv, device), remote(in_ref, in_ref, send, recv, device)

        one = [move(0, (z, x, k, rows, lanes(r)), (z, 1 - x, k, rows, lanes(r)), d_x)]
        two = [move(1, (z, every, k, rows, lanes(r)), (z, every, k, rows, lanes(1 - r)), d_y)]
        three = [
            move(1 + n, (z, every, k, rows, every), (lax.rem(z + 4 - n, 4), every, k, rows, every), d_z(n))
            for n in (1, 2, 3)
        ]
        four = [move(5, (every, every, k, rows, every), (every, every, 1 - k, rows, every), d_k)]
        return one, two, three, four

    def picked_moves(n):
        cut = lanes(n)
        return gather_moves(
            pk, lambda row: (pl.ds(pl.multiple_of(row * MSLOT, 16), MSLOT), cut),
            (slice(None), cut), pk_send.at[n], pk_recv.at[n],
        )

    px_swap = remote(px_out.at[1 - r], px_mid, px_sem.at[0], px_sem.at[1], d_y)

    def px_slot(n):
        return px.at[pl.ds(pl.multiple_of(n * UNIT, UNIT), UNIT)]

    def px_move(part, n):
        target = 8 * (r if part == 0 else 1 - r) + n
        src = px_out.at[r, n] if part == 0 else px_mid.at[n]
        return target, remote(src, px_slot(c), px_send.at[part, n], px_recv.at[c], (r, target))

    def px_start(part):
        def one(n, _):
            target, copy = px_move(part, n)

            @pl.when(target == c)
            def _():
                px[pl.ds(pl.multiple_of(c * UNIT, UNIT), UNIT), :] = (
                    px_out[r, n] if part == 0 else px_mid[n]
                )

            @pl.when(target != c)
            def _():
                copy.start()

            return 0

        lax.fori_loop(0, 8, one, 0)

    def px_done(n, _):
        for part in range(2):
            target, copy = px_move(part, n)

            @pl.when(target != c)
            def _():
                copy.wait_send()

        for source in (n, n + 8):

            @pl.when(source != c)
            def _():
                remote(px_slot(source), px_slot(source), px_send.at[0, n], px_recv.at[source], d_y).wait_recv()

        return 0

    cut_rows = TOK // 2
    own_cut = pl.ds(pl.multiple_of(k * cut_rows, 8), cut_rows)
    other_cut = pl.ds(pl.multiple_of((1 - k) * cut_rows, 8), cut_rows)

    def tb_copy(rows, row, index, device):
        ref = tb.at[rows, lanes(row)]
        return remote(ref, ref, tb_sem.at[index, 0], tb_sem.at[index, 1], device)

    token = lax.broadcasted_iota(jnp.int32, (TOK, 1), 0)
    slot_hit = lax.broadcasted_iota(jnp.int32, (TOK, MSLOT), 0) == places[pl.ds(r, 1), :]
    slot_on = lax.broadcasted_iota(jnp.int32, (TOK, MSLOT), 1) < counts[r]
    selector = jnp.where(slot_hit, 1.0, 0.0)
    masked = jnp.sum(jnp.where(slot_on, selector, 0.0), axis=1, keepdims=True) > 0.5
    opening = token == 0

    def gain(n):
        return tb[SEQ + 2 + 2 * n : SEQ + 3 + 2 * n, :]

    def shift(n):
        return tb[SEQ + 3 + 2 * n : SEQ + 4 + 2 * n, :]

    def square(n):
        return wg[:, :, :, unit_rows(n), :].reshape(16 * UNIT, 2 * half)

    def set_square(n, value):
        wg[:, :, :, unit_rows(n), :] = value.astype(low_type).reshape(4, 2, 2, UNIT, 2 * half)

    def triple():
        return wg[:, :, :, UNIT : 4 * UNIT, :].reshape(48 * UNIT, 2 * half)

    lane_low = lax.broadcasted_iota(jnp.int32, (1, 2 * HD), 1) < HD
    keep_low = jnp.where(lane_low, 1.0, 0.0)
    keep_high = 1.0 - keep_low

    def twice(values):
        return jnp.concatenate(
            [values * keep_low.astype(low_type), values * keep_high.astype(low_type)], axis=0
        )

    def once(values):
        return values[:TOK] * keep_low + values[TOK:] * keep_high

    def pair_lanes(part, p):
        return pl.ds(pl.multiple_of(part * HEADS * HD + p * 2 * HD, 2 * HD), 2 * HD)

    def pair_probs(p):
        query2 = twice(qkv[:, pair_lanes(0, p)])
        key2 = qkv[:, pair_lanes(1, p)]
        scores = nt(query2, key2) * (1.0 / math.sqrt(HD))
        valid = lax.broadcasted_iota(jnp.int32, (1, TOK), 1) < SEQ
        scores = jnp.where(valid, scores, -1e30)
        lifted = jnp.exp(scores - jnp.max(scores, axis=1, keepdims=True))
        return query2, key2, lifted * (1.0 / jnp.sum(lifted, axis=1, keepdims=True))

    def do_patch():
        tb_copy(own_cut, 1 - r, 0, d_y).wait_recv()
        tb_copy(own_cut, 1 - r, 1, d_k).start()
        lax.fori_loop(0, 8, px_done, 0)
        patch = tn(px[...], square(0))[:TOK]
        tb_copy(own_cut, r, 0, d_y).wait_send()
        tb_copy(other_cut, 1 - r, 1, d_k).wait_recv()
        tb_copy(own_cut, 1 - r, 1, d_k).wait_send()
        value = jnp.where(
            opening, tb[SEQ : SEQ + 1, :], jnp.where(masked, tb[SEQ + 1 : SEQ + 2, :], patch)
        )
        value = jnp.where(token < SEQ, value + tb[...], 0.0)
        st0[...] = value
        n1[...] = normed(value, gain(0), shift(0))[0].astype(low_type)

    def do_attention():
        qkv[...] = nt(n1[...], triple()).astype(low_type)

        def one_pair(p, _):
            _, _, probs = pair_probs(p)
            mixed = nn(probs.astype(low_type), qkv[:, pair_lanes(2, p)])
            mix[:, pair_lanes(0, p)] = once(mixed).astype(low_type)
            return 0

        lax.fori_loop(0, HEADS // 2, one_pair, 0)

    def do_output():
        value = st0[...] + nn(mix[...], square(4))
        st1[...] = value
        st2[...] = value
        n2[...] = normed(value, gain(1), shift(1))[0].astype(low_type)

    def do_up(j):
        value = nt(n2[...], square(5 + j))
        hpre[j] = value
        phi_total, _ = gelu_parts(value)
        hact[j] = (value * phi_total).astype(low_type)

    def do_down(j):
        st2[...] += nn(hact[j], square(9 + j))

    begin(late_moves()[0])
    px_swap.start()
    begin(weight_moves(0)[0])
    begin(weight_moves(1)[0])
    px_start(0)
    for n in range(2, AHEAD):
        begin(weight_moves(n)[0])
    tb_copy(own_cut, r, 0, d_y).start()

    def tick(t, _):
        @pl.when(t < late)
        def _():
            first, second, pair_one, _, _, _ = weight_moves(t)
            landed(first)
            begin(second)
            begin(pair_one)

        @pl.when(t == 0)
        def _():
            landed(late_moves()[0])
            begin(late_moves()[1])
            px_swap.wait()
            px_start(1)

        @pl.when(t < late - AHEAD)
        def _():
            begin(weight_moves(t + AHEAD)[0])

        @pl.when(t == late - AHEAD)
        def _():
            landed(late_moves()[1])
            begin(late_moves()[2])

        @pl.when(jnp.logical_and(t >= LAG_A, t < late + LAG_A))
        def _():
            _, second, _, third, pair_two, _ = weight_moves(t - LAG_A)
            landed(second)
            begin(third)
            begin(pair_two)

        @pl.when(t == late + 2)
        def _():
            landed(late_moves()[2])
            begin(late_moves()[3])

        @pl.when(jnp.logical_and(t >= LAG_B, t < late + LAG_B))
        def _():
            _, _, _, third, _, pair_three = weight_moves(t - LAG_B)
            landed(third)
            begin(pair_three)

        @pl.when(jnp.logical_and(t >= LAG_C, t < late + LAG_C))
        def _():
            _, _, pair_one, _, pair_two, pair_three = weight_moves(t - LAG_C)
            landed(pair_one)
            landed(pair_two)
            landed(pair_three)

        @pl.when(t == late + LAG_C)
        def _():
            landed(late_moves()[3])

        @pl.when(t < 16)
        def _():
            for a in range(3):
                state_in(a, t).wait()

                @pl.when(t >= 1)
                def _():
                    for copy in state_out(a, t - 1):
                        copy.wait()

                value = hbuf[a].astype(low_type)
                if a == 0:
                    hn[state_rows(t), :] = value
                else:
                    pkt[UNIT * (a - 1) : UNIT * a, :] = value[:, :wide_part]
                    pkt[UNIT * (a + 1) : UNIT * (a + 2), 0:rest_part] = value[:, wide_part:]
                for copy in state_out(a, t):
                    copy.start()

                @pl.when(t + 1 < 16)
                def _():
                    state_in(a, t + 1).start()

        @pl.when(t == LAG_C + 2)
        def _():
            do_patch()

        @pl.when(t == LAG_C + 3)
        def _():
            do_attention()

        @pl.when(t == LAG_C + 4)
        def _():
            do_output()

        @pl.when(jnp.logical_and(t >= LAG_C + 5, t < LAG_C + 9))
        def _():
            do_up(t - LAG_C - 5)

        @pl.when(t >= LAG_C + 9)
        def _():
            do_down(t - LAG_C - 9)

        return 0

    lax.fori_loop(0, UNITS + LAG_C, tick, 0)

    def all_sent(n, _):
        for moves in weight_moves(n):
            sent(moves)
        return 0

    for a in range(3):
        for copy in state_out(a, 15):
            copy.wait()

    final_out, _, _ = normed(st2[...], gain(2), shift(2))
    picked = tn(selector.astype(low_type), final_out.astype(low_type)).astype(low_type)
    own_rows = pl.ds(pl.multiple_of(r * MSLOT, 16), MSLOT)
    other_rows = pl.ds(pl.multiple_of((1 - r) * MSLOT, 16), MSLOT)
    pp[own_rows, :] = picked
    pk[z, x, k, own_rows, :] = picked

    def swap(index, src, dst, device):
        return remote(src, dst, ex_send.at[index], ex_recv.at[index], device)

    swap_picked = swap(0, pp.at[own_rows, :], pkp, d_y)
    swap_picked.start()
    for n in range(2):
        begin(picked_moves(n)[0])
    lax.fori_loop(0, late, all_sent, 0)
    for moves in late_moves():
        sent(moves)
    flip[...] = jnp.zeros_like(flip)
    flip[0:2, 0:MSLOT] = targets[...].astype(wide)
    info = jnp.transpose(flip[...])
    target_col = jnp.concatenate([info[:MSLOT, 0:1], info[:MSLOT, 1:2]], axis=0)
    slot_line = lax.broadcasted_iota(jnp.int32, (MSLOT, 1), 0)
    weight_col = jnp.concatenate(
        [jnp.where(slot_line < counts[0], 1.0, 0.0), jnp.where(slot_line < counts[1], 1.0, 0.0)], axis=0
    )
    base = (r * (BANDS * 512)).astype(wide)
    band_lane = lax.broadcasted_iota(jnp.int32, (1, 512), 1).astype(wide)

    def band(v):
        return pl.ds(pl.multiple_of(v * 512, 512), 512)

    def band_hit(v, column):
        return (band_lane + (base + (v * 512).astype(wide))) == column

    swap_picked.wait()
    pp[other_rows, :] = pkp[...]

    def picked_second(n):
        first, second, pair_one, _, _, _ = picked_moves(n)
        landed(first)
        begin(second)
        begin(pair_one)

    def picked_third(n):
        _, second, _, third, pair_two, _ = picked_moves(n)
        landed(second)
        begin(third)
        begin(pair_two)

    def picked_last(n):
        _, _, _, third, _, pair_three = picked_moves(n)
        landed(third)
        begin(pair_three)

    def picked_done(n):
        _, _, pair_one, _, pair_two, pair_three = picked_moves(n)
        landed(pair_one)
        landed(pair_two)
        landed(pair_three)

    def logits_band(v, carry):
        top, chosen = carry
        value = nn(pp[...], hn[:, band(v)])
        lt[v] = value
        chosen += jnp.sum(jnp.where(band_hit(v, target_col), value, 0.0), axis=1, keepdims=True)
        return jnp.maximum(top, jnp.max(value, axis=1, keepdims=True)), chosen

    zero_col = jnp.zeros((2 * MSLOT, 1), wide)
    top, chosen = lax.fori_loop(0, BANDS, logits_band, (zero_col - 1e30, zero_col))
    picked_second(0)

    def sum_band(v, total):
        return total + jnp.sum(jnp.exp(lt[v] - top), axis=1, keepdims=True)

    total = lax.fori_loop(0, BANDS, sum_band, zero_col)
    column = lax.broadcasted_iota(jnp.int32, (1, 128), 1)
    tmpa[...] = jnp.zeros_like(tmpa)
    tmpa[0 : 2 * MSLOT, :] = jnp.where(column == 0, top, jnp.where(column == 1, total, 0.0))
    sq[0] = jnp.transpose(tmpa[...])[:8]
    swap_lse = swap(1, sq.at[0], sq.at[1], d_y)
    swap_lse.start()
    picked_second(1)
    picked_third(0)
    swap_lse.wait()
    flip[...] = jnp.zeros_like(flip)
    flip[0:8, :] = sq[1]
    theirs = jnp.transpose(flip[...])[: 2 * MSLOT]
    their_top, their_total = theirs[:, 0:1], theirs[:, 1:2]
    best = jnp.maximum(top, their_top)
    log_total = best + jnp.log(total * jnp.exp(top - best) + their_total * jnp.exp(their_top - best))

    tmpa[0 : 2 * MSLOT, :] = jnp.where(
        column == 0, log_total, jnp.where(column == 1, target_col, jnp.where(column == 2, weight_col, 0.0))
    )
    lsb[c] = jnp.transpose(tmpa[...])[:8]

    def ls_copy(n):
        other = lax.rem(c + n, 16)
        return remote(lsb.at[c], lsb.at[c], ls_send.at[n], ls_recv.at[n], (r, other))

    def ls_in(n):
        other = lax.rem(c + 16 - n, 16)
        return remote(lsb.at[other], lsb.at[other], ls_send.at[n], ls_recv.at[n], (r, other))

    def ls_start(n, _):
        ls_copy(n).start()
        return 0

    def ls_done(n, _):
        ls_copy(n).wait_send()
        ls_in(n).wait_recv()
        return 0

    lax.fori_loop(1, 16, ls_start, 0)
    gpk[...] = jnp.zeros_like(gpk)

    def grad_band(v, _):
        value = jnp.exp(lt[v] - log_total) - jnp.where(band_hit(v, target_col), 1.0, 0.0)
        gpk[...] += nt((value * weight_col).astype(low_type), hn[:, band(v)])
        return 0

    lax.fori_loop(0, BANDS, grad_band, 0)
    gps[...] = gpk[other_rows, :].astype(low_type)
    swap_grad = swap(2, gps, gpr, d_y)
    swap_grad.start()
    leader = jnp.where(r == 0, 1.0, 0.0)
    loss_part = jnp.sum((log_total * leader - chosen) * weight_col, axis=0, keepdims=True)
    swap_grad.wait()
    picked_third(1)
    grad_picked = (gpk[own_rows, :] + gpr[...].astype(wide)).astype(low_type)
    grad_final = nn(selector.astype(low_type), grad_picked)
    _, scaled, inverse = normed(st2[...], gain(2), shift(2))
    grad_last, grad_gain, grad_shift = normed_back(grad_final, scaled, inverse, gain(2))
    st2[...] = grad_last
    g2b[...] = grad_last.astype(low_type)
    gst[4:5, :] = grad_gain
    gst[5:6, :] = grad_shift
    gacc[...] = jnp.zeros_like(gacc)

    def pair_region(n):
        return rk.at[lax.rem(n, 4)]

    def rs_copy(n, index, src, dst, device):
        return remote(src, dst, rs_send.at[n, index], rs_recv.at[n, index], device)

    lo, hi = pl.ds(0, 2), pl.ds(2, 2)

    def sums_moves(n):
        rows = unit_rows(UNITS - 1 - n)
        zero = [rs_copy(n, 0, wg.at[:, :, 1 - k, rows, :], rk.at[lax.rem(n, 4)], d_k)]
        one = [
            rs_copy(n, 1, wg.at[lo, :, k, rows, lanes(1 - r)], r1a.at[lax.rem(n, 7)], d_y),
            rs_copy(n, 2, wg.at[hi, 1 - x, k, rows, :], r1b.at[lax.rem(n, 7)], d_x),
        ]
        two = [
            rs_copy(n, 3, wg.at[lo, 1 - x, k, rows, lanes(r)], r2a.at[lax.rem(n, 7)], d_x),
            rs_copy(n, 4, wg.at[hi, x, k, rows, lanes(1 - r)], r2b.at[lax.rem(n, 7)], d_y),
        ]
        three = [
            rs_copy(n, 4 + m, wg.at[lax.rem(z + m, 4), x, k, rows, lanes(r)], rz.at[lax.rem(n, 7), m - 1], d_z(m))
            for m in (1, 2, 3)
        ]
        return zero, one, two, three

    def sum_start(copies):
        for copy in copies:
            copy.start()

    def sum_land(copies):
        for copy in copies:
            copy.wait_recv()

    def fold(region, value):
        wg[region] = (wg[region].astype(wide) + value.astype(wide)).astype(low_type)

    def sums_one(n):
        rows = unit_rows(UNITS - 1 - n)
        zero, one, _, _ = sums_moves(n)
        sum_land(zero)
        fold((slice(None), slice(None), k, rows, slice(None)), rk[lax.rem(n, 4)])
        sum_start(one)

    def sums_two(n):
        rows = unit_rows(UNITS - 1 - n)
        _, one, two, _ = sums_moves(n)
        sum_land(one)
        fold((lo, slice(None), k, rows, lanes(r)), r1a[lax.rem(n, 7)])
        fold((hi, x, k, rows, slice(None)), r1b[lax.rem(n, 7)])
        sum_start(two)

    def sums_three(n):
        rows = unit_rows(UNITS - 1 - n)
        _, _, two, three = sums_moves(n)
        sum_land(two)
        fold((lo, x, k, rows, lanes(r)), r2a[lax.rem(n, 7)])
        fold((hi, x, k, rows, lanes(r)), r2b[lax.rem(n, 7)])
        sum_start(three)

    def sums_four(n):
        rows = unit_rows(UNITS - 1 - n)
        _, _, _, three = sums_moves(n)
        sum_land(three)
        value = wg[z, x, k, rows, lanes(r)].astype(wide)
        for m in range(3):
            value = value + rz[lax.rem(n, 7), m].astype(wide)
        gout[rows, :] = value
        sq[2, 0:1, 0:128] += jnp.sum(jnp.sum(value * value, axis=0, keepdims=True), axis=1, keepdims=True)

    def sums_sent(n, _):
        for moves in sums_moves(n):
            sent([(copy, None) for copy in moves])
        return 0

    def back_down(j):
        grad_act = nt(g2b[...], square(9 + j))
        value = hpre[j]
        phi_total, density = gelu_parts(value)
        grad_pre = (grad_act * (phi_total + value * density)).astype(low_type)
        set_square(9 + j, tn(hact[j], g2b[...]))
        hact[j] = grad_pre

    def back_up(j):
        gacc[...] += nn(hact[j], square(5 + j))
        set_square(5 + j, tn(hact[j], n2[...]))

    def back_output():
        _, scaled, inverse = normed(st1[...], gain(1), shift(1))
        down, grad_gain, grad_shift = normed_back(gacc[...], scaled, inverse, gain(1))
        gst[2:3, :] = grad_gain
        gst[3:4, :] = grad_shift
        down = down + st2[...]
        st2[...] = down
        g2b[...] = down.astype(low_type)
        grad_mix = nt(g2b[...], square(4)).astype(low_type)
        set_square(4, tn(mix[...], g2b[...]))
        mix[...] = grad_mix

    def back_attention():
        def one_pair(p, _):
            query2, key2, probs = pair_probs(p)
            value2 = qkv[:, pair_lanes(2, p)]
            upstream = twice(mix[:, pair_lanes(0, p)])
            grad_probs = nt(upstream, value2)
            centered = grad_probs - jnp.sum(probs * grad_probs, axis=1, keepdims=True)
            grad_scores = (probs * centered).astype(low_type)
            scale = 1.0 / math.sqrt(HD)
            grad_query = once(nn(grad_scores, key2)) * scale
            grad_key = tn(grad_scores, query2) * scale
            grad_value = tn(probs.astype(low_type), upstream)
            qkv[:, pair_lanes(0, p)] = grad_query.astype(low_type)
            qkv[:, pair_lanes(1, p)] = grad_key.astype(low_type)
            qkv[:, pair_lanes(2, p)] = grad_value.astype(low_type)
            return 0

        lax.fori_loop(0, HEADS // 2, one_pair, 0)
        gacc[...] = nn(qkv[...], triple())
        wg[:, :, :, UNIT : 4 * UNIT, :] = (
            tn(qkv[...], n1[...]).astype(low_type).reshape(4, 2, 2, 3 * UNIT, 2 * half)
        )

    def back_patch():
        _, scaled, inverse = normed(st0[...], gain(0), shift(0))
        down, grad_gain, grad_shift = normed_back(gacc[...], scaled, inverse, gain(0))
        grad = down + st2[...]
        grad_patch = jnp.where(jnp.logical_or(opening, masked), 0.0, grad).astype(low_type)
        set_square(0, nn(px[:, 0:TOK], grad_patch))
        lines = [
            grad[0:1],
            jnp.sum(jnp.where(masked, grad, 0.0), axis=0, keepdims=True),
            grad_gain, grad_shift, gst[2:3, :], gst[3:4, :], gst[4:5, :], gst[5:6, :],
        ]
        for n, line in enumerate(lines):
            grad = jnp.where(token == SEQ + n, line, grad)
        tab[0:TOK, :] = grad.astype(low_type)
        tab[TOK:, :] = jnp.zeros((tab.shape[0] - TOK, tab.shape[1]), low_type)

    tab_half = tab.shape[0] // 2
    rows_own = pl.ds(pl.multiple_of(k * tab_half, 16), tab_half)
    rows_other = pl.ds(pl.multiple_of((1 - k) * tab_half, 16), tab_half)
    d_z1 = (r, (z + 1 - 2 * (z % 2)) * 4 + x * 2 + k)
    d_z2 = (r, lax.rem(z + 2, 4) * 4 + x * 2 + k)
    own_part = tab.at[rows_own, lanes(r)]
    tab_moves = [
        remote(tab.at[rows_other, :], tabk, tab_send.at[0], tab_recv.at[0], d_k),
        remote(tab.at[rows_own, lanes(1 - r)], tabr.at[0], tab_send.at[1], tab_recv.at[1], d_y),
        remote(own_part, tabr.at[1], tab_send.at[2], tab_recv.at[2], d_x),
        remote(own_part, tabr.at[2], tab_send.at[3], tab_recv.at[3], d_z1),
        remote(own_part, tabr.at[3], tab_send.at[4], tab_recv.at[4], d_z2),
        remote(own_part, tabr.at[4], tab_send.at[5], tab_recv.at[5], d_k),
    ]

    def tab_step(n):
        tab_moves[n].wait()
        if n == 0:
            tab[rows_own, :] = (
                tab[rows_own, :].astype(wide) + tabk[...].astype(wide)
            ).astype(low_type)
        elif n < 5:
            tab[rows_own, lanes(r)] = (
                tab[rows_own, lanes(r)].astype(wide) + tabr[n - 1].astype(wide)
            ).astype(low_type)
        if n < 5:
            tab_moves[n + 1].start()

    def gh_moves(n):
        own, other = band(k * (BANDS // 2) + n), band((1 - k) * (BANDS // 2) + n)
        keep = pltpu.make_async_copy(hn.at[:, own], ghead.at[:, own], gh_sem.at[n])
        give = remote(hn.at[:, own], ghead.at[:, own], gh_send.at[n], gh_recv.at[n], d_k)
        take = remote(hn.at[:, other], ghead.at[:, other], gh_send.at[n], gh_recv.at[n], d_k)
        return keep, give, take

    def head_logits(n):
        v = k * (BANDS // 2) + n

        def rows_block(m, _):
            at = pl.ds(pl.multiple_of(m * 8 * MSLOT, 128), 8 * MSLOT)
            value = nn(pk[m].reshape(8 * MSLOT, 2 * half), hn[:, band(v)])
            cols = colb[at, :]
            hit = jnp.where(band_hit(v, cols[:, 1:2]), 1.0, 0.0)
            gch[at, :] = ((jnp.exp(value - cols[:, 0:1]) - hit) * cols[:, 2:3]).astype(low_type)
            return 0

        lax.fori_loop(0, 4, rows_block, 0)

    def head_grad(n):
        value = nn(pkt[...], gch[...])
        sq[3, 0:1, 0:128] += jnp.sum(jnp.sum(value * value, axis=0, keepdims=True), axis=1, keepdims=True)
        hn[:, band(k * (BANDS // 2) + n)] = value.astype(low_type)
        keep, give, _ = gh_moves(n)
        keep.start()
        give.start()

    def head_ready():
        for n in range(2):
            picked_done(n)
        lax.fori_loop(1, 16, ls_done, 0)

        def to_columns(n, _):
            flip[0:8, :] = lsb[n]
            colb[pl.ds(pl.multiple_of(n * 2 * MSLOT, 16), 2 * MSLOT), :] = jnp.transpose(flip[...])[: 2 * MSLOT]
            return 0

        lax.fori_loop(0, 16, to_columns, 0)

        def turn(n, _):
            rows = pk[n].reshape(8 * MSLOT, 2 * half)
            pkt[:, pl.ds(pl.multiple_of(n * 8 * MSLOT, 128), 8 * MSLOT)] = jnp.transpose(rows)
            return 0

        lax.fori_loop(0, 4, turn, 0)

    def back_step(s, _):
        def work(q, _):
            w = jnp.where(s == 0, 15 * q, jnp.where(s <= 4, 2 * s - 1 + q, s + 4 + 6 * q))

            @pl.when(jnp.logical_and(w >= 0, w < 4))
            def _():
                back_down(3 - w)

            @pl.when(jnp.logical_and(w >= 4, w < 8))
            def _():
                back_up(7 - w)

            @pl.when(w == 8)
            def _():
                back_output()

            @pl.when(w == 9)
            def _():
                back_attention()

            @pl.when(w == 10)
            def _():
                back_patch()

            @pl.when(jnp.logical_and(q == 0, s < UNITS))
            def _():
                sum_start(sums_moves(s)[0])

            @pl.when(jnp.logical_and(q == 0, jnp.logical_and(s >= 1, s < UNITS + 1)))
            def _():
                sums_one(s - 1)

            return 0

        lax.fori_loop(0, 2, work, 0)

        @pl.when(jnp.logical_and(s >= 3, s < UNITS + 3))
        def _():
            sums_two(s - 3)

        @pl.when(jnp.logical_and(s >= 5, s < UNITS + 5))
        def _():
            sums_three(s - 5)

        @pl.when(s >= 6)
        def _():
            sums_four(s - 6)

        for n in range(2):
            @pl.when(s == n)
            def _():
                picked_last(n)

        @pl.when(s == 4)
        def _():
            head_ready()

        @pl.when(s == 6)
        def _():
            tab_moves[0].start()

        for n in range(6):
            @pl.when(s == 7 + 2 * n)
            def _():
                tab_step(n)

        @pl.when(jnp.logical_and(s >= G_FIRST, s < G_FIRST + BANDS))
        def _():
            @pl.when((s - G_FIRST) % 2 == 0)
            def _():
                head_logits((s - G_FIRST) // 2)

            @pl.when((s - G_FIRST) % 2 == 1)
            def _():
                head_grad((s - G_FIRST) // 2)

        return 0

    lax.fori_loop(0, UNITS + 6, back_step, 0)
    gtab_out[rows_own, :] = tab[rows_own, lanes(r)].astype(wide)
    gtab_out[rows_other, :] = tabr[4].astype(wide)
    value = gtab_out[...]
    first_col = jnp.where(c == 0, 1.0, 0.0)
    first_chip = jnp.where(c < 2, 1.0, 0.0)
    table_squares = jnp.sum(jnp.sum(value * value, axis=0, keepdims=True), axis=1, keepdims=True)
    line = lax.broadcasted_iota(jnp.int32, (8, 128), 0)
    squares = sq[2, 0:1, 0:128] + sq[3, 0:1, 0:128] * first_chip + table_squares * first_col
    count = (counts[0] + counts[1]).astype(wide) * leader
    fin[r * 16 + c] = jnp.where(
        line == 0, loss_part, jnp.where(line == 1, count, jnp.where(line == 2, squares, 0.0))
    )

    def fin_copy(n, step):
        other = lax.rem(r * 16 + c + step, 32)
        owner = r * 16 + c if n == 0 else lax.rem(r * 16 + c + 32 - step, 32)
        ref = fin.at[owner]
        return remote(ref, ref, fin_send.at[step], fin_recv.at[step], (other // 16, other % 16))

    def fin_start(step, _):
        fin_copy(0, step).start()
        return 0

    def fin_done(step, _):
        fin_copy(0, step).wait_send()
        fin_copy(1, step).wait_recv()
        return 0

    lax.fori_loop(1, 32, fin_start, 0)
    lax.fori_loop(0, UNITS, sums_sent, 0)
    for n in range(2):
        for moves in picked_moves(n):
            sent(moves)
    for n in range(BANDS // 2):
        keep, give, take = gh_moves(n)
        keep.wait()
        give.wait_send()
        take.wait_recv()
    lax.fori_loop(1, 32, fin_done, 0)
    totals = jnp.sum(fin[...], axis=0)
    count_total = totals[1:2, :]
    norm_value = jnp.sqrt(totals[2:3, :]) / count_total
    scal_out[0:1, :] = totals[0:1, :] / count_total
    scal_out[1:2, :] = norm_value
    scal_out[2:3, :] = jnp.minimum(1.0, clip_limit / norm_value) / count_total
    scal_out[3:8, :] = jnp.zeros((5, 128), wide)


def step_call(pix, blocks, tab, places, targets, counts, head, drift, power):
    half = tab.shape[1]
    full = 2 * half
    vocab = head.shape[1]
    slots = 32 * MSLOT
    vm = pltpu.VMEM
    dma = pltpu.SemaphoreType.DMA
    f32, b16 = wide, low_type
    scratch = [
        vm((4, 2, 2, UNITS * UNIT, full), b16),
        vm((2, 8, UNIT, 256), b16),
        vm((8, UNIT, 256), b16),
        vm((16 * UNIT, 256), b16),
        vm((TOK, full), f32),
        vm((TOK, full), f32), vm((TOK, full), f32), vm((TOK, full), f32),
        vm((TOK, full), b16), vm((TOK, full), b16), vm((TOK, full), b16),
        vm((TOK, 3 * full), b16),
        vm((4, TOK, full), f32),
        vm((4, TOK, full), b16),
        vm((full, vocab), b16),
        vm((3, UNIT, vocab), f32),
        vm((4, 2, 2, 2 * MSLOT, full), b16),
        vm((MSLOT, full), b16),
        vm((2 * MSLOT, full), b16),
        vm((BANDS, 2 * MSLOT, 512), f32),
        vm((full, slots), b16),
        vm((slots, 512), b16),
        vm((slots, 128), f32),
        vm((4, 8, 256), f32),
        vm((16, 8, 256), f32),
        vm((128, 256), f32),
        vm((256, 128), f32),
        vm((2 * MSLOT, full), f32),
        vm((MSLOT, full), b16), vm((MSLOT, full), b16),
        vm((TOK, full), b16),
        vm((TOK, full), f32),
        vm((8, full), f32),
        vm((4, 4, 2, UNIT, full), b16),
        vm((7, 2, 2, UNIT, half), b16),
        vm((7, 2, UNIT, full), b16),
        vm((7, 2, UNIT, half), b16),
        vm((7, 2, UNIT, half), b16),
        vm((7, 3, UNIT, half), b16),
        vm((224, full), b16),
        vm((112, full), b16),
        vm((5, 112, half), b16),
        vm((32, 8, 128), f32),
        dma((UNITS, 12)), dma((UNITS, 12)),
        dma((2,)), dma((2, 8)), dma((16,)),
        dma((2, 2)),
        dma((2, 12)), dma((2, 12)),
        dma((3,)), dma((3,)),
        dma((16,)), dma((16,)),
        dma((UNITS, 8)), dma((UNITS, 8)),
        dma((6,)), dma((6,)),
        dma((32,)), dma((32,)),
        dma((3,)), dma((5,)),
        dma((BANDS // 2,)), dma((BANDS // 2,)), dma((BANDS // 2,)),
    ]
    in_vmem = pl.BlockSpec(memory_space=pltpu.VMEM)
    return pl.pallas_call(
        step_kernel,
        out_shape=(
            jax.ShapeDtypeStruct((UNITS * UNIT, half), f32),
            jax.ShapeDtypeStruct((224, half), f32),
            jax.ShapeDtypeStruct((full, vocab), b16),
            jax.ShapeDtypeStruct((8, 128), f32),
            *([jax.ShapeDtypeStruct((full, vocab), b16)] * 3),
        ),
        in_specs=[
            *([in_vmem] * 9),
            pl.BlockSpec(memory_space=pltpu.SMEM),
            *([pl.BlockSpec(memory_space=pl.ANY)] * 3),
        ],
        out_specs=(
            in_vmem, in_vmem, pl.BlockSpec(memory_space=pl.ANY), in_vmem,
            *([pl.BlockSpec(memory_space=pl.ANY)] * 3),
        ),
        scratch_shapes=scratch,
        compiler_params=pltpu.CompilerParams(
            collective_id=0, has_side_effects=True, vmem_limit_bytes=VMEM_LIMIT
        ),
        cost_estimate=pl.CostEstimate(flops=50_000_000_000, bytes_accessed=40_000_000, transcendentals=0),
    )(pix, *blocks, tab, places, targets, counts, head, drift, power)


def block_path(
    pixels, mask_places, mask_count, targets, step_count,
    patch_weight, vector_table, input_weight, output_weight, upward_weight, downward_weight, head_weight,
    *moments,
):
    weights = (
        patch_weight, vector_table, input_weight, output_weight, upward_weight, downward_weight, head_weight,
    )
    weights = flat(weights)
    blocks = [weights[n] for n in (0, 2, 3, 4, 5)]
    drifts, powers = flat(moments[:7]), flat(moments[7:])
    gout, gtab, ghead, scal, *low = step_call(
        pixels.T, blocks, vector_table, mask_places, targets, mask_count, head_weight, drifts[6], powers[6]
    )
    states = [(*group[:6], value) for group, value in zip((weights, drifts, powers), low)]
    results = adam_call(scal, step_count, gout, gtab, ghead, *states)
    triples = [results[2 + n :: 3] for n in range(3)]
    triples = [unflat(triple) for triple in triples]
    return (*results[:2], *(triple[n] for n in range(7) for triple in triples))


def flat(values):
    patch, table, inward, outward, up, down, head = values
    return (patch, table, inward[0].T, outward[0], up[0].T, down[0], head)


def unflat(values):
    patch, table, inward, outward, up, down, head = values
    return (patch, table, inward.T[None], outward[None], up.T[None], down[None], head)


SMALL = UNITS * UNIT
ROWS = 48
IN_SLOTS = 4
OUT_SLOTS = 3


def adam_kernel(
    scal, step, gout, gtab, ghead, *refs
):
    weights, drifts, powers = refs[:7], refs[7:14], refs[14:21]
    loss_out, norm_out = refs[21:23]
    outs = refs[23:44]
    gbuf, inbuf, outbuf, gsm, insm, outsm, gtb, intb, outtb, in_sem, out_sem, sm_in, sm_out = refs[44:]
    factor = scal[2:3, 0:1]
    count = jnp.full((1, 128), step[0], jnp.int32).astype(wide)[:, 0:1]
    scale_first = 1.0 / (1.0 - jnp.exp(count * math.log(beta_first)))
    scale_second = 1.0 / (1.0 - jnp.exp(count * math.log(beta_second)))
    count_first = scale_first * -learn_rate
    gain_first = factor * (1.0 - beta_first)
    gain_second = factor * factor * (1.0 - beta_second)
    chunks = ghead.shape[0] // ROWS
    states = (weights, drifts, powers)

    def rows_of(n):
        return pl.ds(pl.multiple_of(n * ROWS, ROWS), ROWS)

    def fetch(n):
        slot = lax.rem(n, IN_SLOTS)
        copies = [
            pltpu.make_async_copy(states[m][6].at[rows_of(n)], inbuf.at[slot, m], in_sem.at[slot, m])
            for m in range(3)
        ]
        copies.append(pltpu.make_async_copy(ghead.at[rows_of(n)], gbuf.at[slot], in_sem.at[slot, 3]))
        return copies

    def store(n):
        slot = lax.rem(n, OUT_SLOTS)
        return [
            pltpu.make_async_copy(outbuf.at[slot, m], outs[18 + m].at[rows_of(n)], out_sem.at[slot, m])
            for m in range(3)
        ]

    order = (0, 2, 3, 4, 5)
    small_fetch, small_store = [], []
    start = 0
    for at, n in enumerate(order):
        height = weights[n].shape[0]
        for m in range(3):
            small_fetch.append(
                pltpu.make_async_copy(states[m][n], insm.at[m, start : start + height], sm_in.at[at, m])
            )
            small_store.append(
                pltpu.make_async_copy(outsm.at[m, start : start + height], outs[3 * n + m], sm_out.at[at, m])
            )
        start += height
    for m in range(3):
        small_fetch.append(pltpu.make_async_copy(states[m][1], intb.at[m], sm_in.at[5, m]))
        small_store.append(pltpu.make_async_copy(outtb.at[m], outs[3 + m], sm_out.at[5, m]))
    small_fetch.append(pltpu.make_async_copy(gout, gsm, sm_in.at[6, 0]))
    small_fetch.append(pltpu.make_async_copy(gtab, gtb, sm_in.at[6, 1]))

    def adam(grad, weight, drift, power):
        new_drift = beta_first * drift + gain_first * grad
        new_power = beta_second * power + gain_second * (grad * grad)
        below = jnp.sqrt(new_power * scale_second) + adam_eps
        update = new_drift * count_first / below - (learn_rate * weight_decay) * weight
        return update, new_drift, new_power

    for n in range(IN_SLOTS):
        for copy in fetch(n):
            copy.start()
    for copy in small_fetch:
        copy.start()
    loss_out[...] = scal[0:1, 0:1]
    norm_out[...] = scal[1:2, 0:1]

    def chunk(n, _):
        for copy in fetch(n):
            copy.wait()

        @pl.when(n >= OUT_SLOTS)
        def _():
            for copy in store(n - OUT_SLOTS):
                copy.wait()

        slot, spot = lax.rem(n, IN_SLOTS), lax.rem(n, OUT_SLOTS)

        def part(q, _):
            at = pl.ds(pl.multiple_of(q * 16, 16), 16)
            values = adam(
                gbuf[slot, at, :].astype(wide), *(inbuf[slot, m, at, :].astype(wide) for m in range(3))
            )
            for m in range(3):
                outbuf[spot, m, at, :] = values[m]
            return 0

        lax.fori_loop(0, ROWS // 16, part, 0)
        for copy in store(n):
            copy.start()

        @pl.when(n + IN_SLOTS < chunks)
        def _():
            for copy in fetch(n + IN_SLOTS):
                copy.start()

        @pl.when(n == 2)
        def _():
            for copy in small_fetch:
                copy.wait()

            def small(q, _):
                at = pl.ds(pl.multiple_of(q * UNIT, UNIT), UNIT)
                values = adam(gsm[at, :], insm[0, at, :], insm[1, at, :], insm[2, at, :])
                for m in range(3):
                    outsm[m, at, :] = values[m]
                return 0

            lax.fori_loop(0, UNITS, small, 0)
            values = adam(gtb[0 : intb.shape[1]], intb[0], intb[1], intb[2])
            for m in range(3):
                outtb[m] = values[m]
            for copy in small_store:
                copy.start()

        return 0

    lax.fori_loop(0, chunks, chunk, 0)
    for n in range(chunks - OUT_SLOTS, chunks):
        for copy in store(n):
            copy.wait()
    for copy in small_store:
        copy.wait()


def adam_call(scal, step, gout, gtab, ghead, weights, drifts, powers):
    half = gout.shape[1]
    vocab = ghead.shape[1]
    table = weights[1].shape[0]
    one = jax.ShapeDtypeStruct((1, 1), wide)
    shapes = [jax.ShapeDtypeStruct(value.shape, wide) for value in weights for _ in range(3)]
    in_vmem = pl.BlockSpec(memory_space=pltpu.VMEM)
    anywhere = pl.BlockSpec(memory_space=pl.ANY)
    vm, dma = pltpu.VMEM, pltpu.SemaphoreType.DMA
    results = pl.pallas_call(
        adam_kernel,
        in_specs=[in_vmem, pl.BlockSpec(memory_space=pltpu.SMEM)] + [anywhere] * 24,
        out_specs=[in_vmem] * 2 + [anywhere] * 21,
        out_shape=[one, one] + shapes,
        scratch_shapes=[
            vm((IN_SLOTS, ROWS, vocab), low_type), vm((IN_SLOTS, 3, ROWS, vocab), low_type),
            vm((OUT_SLOTS, 3, ROWS, vocab), wide),
            vm((SMALL, half), wide), vm((3, SMALL, half), wide), vm((3, SMALL, half), wide),
            vm(gtab.shape, wide), vm((3, table, half), wide), vm((3, table, half), wide),
            dma((IN_SLOTS, 4)), dma((OUT_SLOTS, 3)), dma((7, 3)), dma((6, 3)),
        ],
        compiler_params=pltpu.CompilerParams(vmem_limit_bytes=VMEM_LIMIT),
        cost_estimate=pl.CostEstimate(flops=60_000_000, bytes_accessed=82_000_000, transcendentals=4_000_000),
    )(scal, step, gout, gtab, ghead, *weights, *drifts, *powers)
    return (results[0].reshape(()), results[1].reshape(()), *results[2:])


def solution(mesh):
    state = (
        P("col", "row"),
        P(None, "row"),
        P(None, "row", "col"),
        P(None, "col", "row"),
        P(None, "row", "col"),
        P(None, "col", "row"),
        P(None, "row"),
    )
    data = (P("row", "col"), P("col", None), P("col"), P("col", None), P())
    outs = (P(), P()) + tuple(spec for spec in state for _ in range(3))
    fits = dict(mesh.shape) == {"row": 2, "col": 16}
    return jax.shard_map(
        block_path if fits else on_device,
        mesh=mesh,
        in_specs=data + state * 3,
        out_specs=outs,
        check_vma=False,
    )
```
